32 devices in a mesh: dp: 2 (over y), fsdp: 16 (over z, x, core).
Axes of the slice: x: 2, y: 2, z: 4, core: 2. Of those that a mesh axis runs over, the one named last changes fastest.
Arguments:
- hidden: bfloat16 [64, 512, 768], P(('dp', 'fsdp')), may hold values from -6 to 6
- grad_out: bfloat16 [64, 512, 768], P(('dp', 'fsdp')), may hold values from -6 to 6
- past_states: bfloat16 [64, 512, 768], P(('dp', 'fsdp')), may hold values from -6 to 6
- old_coeffs: bfloat16 [64, 512, 768], P(('dp', 'fsdp')), may hold values from -6 to 6
- fresh_flags: int32 [64], P(('dp', 'fsdp')), may hold values 0 or 1
- ridge_map: bfloat16 [512, 1024], replicated, may hold values from -0.1875 to 0.1875
- gain_attn: bfloat16 [768], P(('dp', 'fsdp')), may hold values from 0.25 to 1.75
- shift_attn: bfloat16 [768], P(('dp', 'fsdp')), may hold values from -1.75 to 1.75
- qkv_weight: bfloat16 [768, 2304], P(('dp', 'fsdp')), may hold values from -0.21875 to 0.21875
- qv_bias: bfloat16 [1536], P(('dp', 'fsdp')), may hold values from -1.75 to 1.75
- out_weight: bfloat16 [768, 768], P(('dp', 'fsdp')), may hold values from -0.4375 to 0.4375
- out_bias: bfloat16 [768], P(('dp', 'fsdp')), may hold values from -1.75 to 1.75
- gain_mlp: bfloat16 [768], P(('dp', 'fsdp')), may hold values from 0.25 to 1.75
- shift_mlp: bfloat16 [768], P(('dp', 'fsdp')), may hold values from -1.75 to 1.75
- up_weight: bfloat16 [768, 3072], P(('dp', 'fsdp')), may hold values from -0.21875 to 0.21875
- up_bias: bfloat16 [3072], P(('dp', 'fsdp')), may hold values from -1.75 to 1.75
- down_weight: bfloat16 [3072, 768], P(('dp', 'fsdp')), may hold values from -0.109375 to 0.109375
- down_bias: bfloat16 [768], P(('dp', 'fsdp')), may hold values from -1.75 to 1.75
- mean_weight: bfloat16 [512, 12], P(('dp', 'fsdp')), may hold values from -0.25 to 0.25
- width_weight: bfloat16 [512, 12], P(('dp', 'fsdp')), may hold values from -0.25 to 0.25
Outputs:
- output: bfloat16 [64, 512, 768], P(('dp', 'fsdp'))
- grad_input: bfloat16 [64, 512, 768], P(('dp', 'fsdp'))
- grad_gain_attn: float32 [768], P(('dp', 'fsdp'))
- grad_shift_attn: float32 [768], P(('dp', 'fsdp'))
- grad_qkv_weight: float32 [768, 2304], P(('dp', 'fsdp'))
- grad_qv_bias: float32 [1536], P(('dp', 'fsdp'))
- grad_out_weight: float32 [768, 768], P(('dp', 'fsdp'))
- grad_out_bias: float32 [768], P(('dp', 'fsdp'))
- grad_gain_mlp: float32 [768], P(('dp', 'fsdp'))
- grad_shift_mlp: float32 [768], P(('dp', 'fsdp'))
- grad_up_weight: float32 [768, 3072], P(('dp', 'fsdp'))
- grad_up_bias: float32 [3072], P(('dp', 'fsdp'))
- grad_down_weight: float32 [3072, 768], P(('dp', 'fsdp'))
- grad_down_bias: float32 [768], P(('dp', 'fsdp'))
- grad_mean_weight: float32 [512, 12], P(('dp', 'fsdp'))
- grad_width_weight: float32 [512, 12], P(('dp', 'fsdp'))
The draws below stay inside these ranges and needn't reach their ends.
All inputs are finite; a program needn't handle non-finite values. No bound on the sum of `fresh_flags` on one device may be relied on, other than what follows from the above.
Results may differ from the reference program's by a relative error of at most 0.014.
The reference program's roundings to bfloat16 on the way count: a program that leaves them out, or rounds other values in their place, can miss the bound.
Values may be sent and summed in bfloat16 or wider, within the bound.
A program may use at most 192 MiB of HBM per device.

```python
import math
import jax
import jax.numpy as jnp
from jax import lax

D = 768
HEADS = 12
FF = 3072
NB = 512
NS = 512
SEQ_LEN = 512
SEQS = 64


def with_ends(entries, own_key, smallest, largest):
    extent = entries.shape
    place = [jax.random.randint(jax.random.fold_in(own_key, axis), (), 0, extent[axis]) for axis in range(len(extent))]
    entries = entries.at[tuple(place)].set(smallest)
    longest = extent.index(max(extent))
    place[longest] = (place[longest] + 1) % extent[longest]
    return entries.at[tuple(place)].set(largest)


def shard_levels(key, dims, pieces, least, high):
    gain = 1.0
    for dim, blocks in pieces:
        steps = jax.random.uniform(jax.random.fold_in(jax.random.fold_in(key, 6), dim), (blocks,), jnp.float32, least / len(pieces), high / len(pieces))
        gain = gain * jnp.repeat(jnp.exp(steps), dims[dim] // blocks).reshape((-1,) + (1,) * (len(dims) - 1 - dim))
    return gain


def gaussian(rng, shape, spread, reach, split=(), held_as=jnp.bfloat16):
    factor_of = shard_levels(rng, shape, split, -0.22, 0.18) if split else 1.0
    result = jax.random.normal(rng, shape, jnp.float32) * spread * factor_of
    return jnp.minimum(jnp.maximum(result, -reach), reach).astype(held_as)


def setup_inputs(seed: int = 0) -> dict:
    seeds = jax.random.split(jax.random.key(seed), 21)
    hidden = gaussian(seeds[0], (SEQS, SEQ_LEN, D), 1.0, 6.0, ((0, 32),))
    grad_out = gaussian(seeds[1], (SEQS, SEQ_LEN, D), 1.0, 6.0, ((0, 32),))
    past_states = gaussian(seeds[2], (SEQS, SEQ_LEN, D), 1.0, 6.0, ((0, 32),))
    old_coeffs = gaussian(seeds[3], (SEQS, NB, D), 1.0, 6.0, ((0, 32),))
    fresh_flags = with_ends((jax.random.randint(seeds[4], (SEQS,), 0, 4) < 1).astype(jnp.int32), jax.random.fold_in(seeds[4], 1), 0, 1)
    ridge_map = gaussian(seeds[5], (NB, NS + SEQ_LEN), (NS + SEQ_LEN) ** -0.5, 0.1875)
    gain_attn = jnp.clip(1.0 + 0.15 * jax.random.normal(seeds[6], (D,), jnp.float32), 0.25, 1.75).astype(jnp.bfloat16)
    shift_attn = gaussian(seeds[7], (D,), 0.3, 1.75, ((0, 32),))
    qkv_weight = gaussian(seeds[8], (D, 3 * D), D ** -0.5, 0.21875, ((0, 32),))
    qv_bias = gaussian(seeds[9], (2 * D,), 0.3, 1.75, ((0, 32),))
    out_weight = gaussian(seeds[10], (D, D), (D // 4) ** -0.5, 0.4375, ((0, 32),))
    out_bias = gaussian(seeds[11], (D,), 0.3, 1.75, ((0, 32),))
    gain_mlp = jnp.clip(1.0 + 0.15 * jax.random.normal(seeds[12], (D,), jnp.float32), 0.25, 1.75).astype(jnp.bfloat16)
    shift_mlp = gaussian(seeds[13], (D,), 0.3, 1.75, ((0, 32),))
    up_weight = gaussian(seeds[14], (D, FF), D ** -0.5, 0.21875, ((0, 32),))
    up_bias = gaussian(seeds[15], (FF,), 0.3, 1.75, ((0, 32),))
    down_weight = gaussian(seeds[16], (FF, D), FF ** -0.5, 0.109375, ((0, 32),))
    down_bias = gaussian(seeds[17], (D,), 0.3, 1.75, ((0, 32),))
    mean_weight = gaussian(seeds[18], (NB, HEADS), NB ** -0.5, 0.25, ((0, 32),))
    width_weight = gaussian(seeds[19], (NB, HEADS), NB ** -0.5, 0.25, ((0, 32),))
    return dict(hidden=hidden, grad_out=grad_out, past_states=past_states, old_coeffs=old_coeffs, fresh_flags=fresh_flags, ridge_map=ridge_map, gain_attn=gain_attn, shift_attn=shift_attn, qkv_weight=qkv_weight, qv_bias=qv_bias, out_weight=out_weight, out_bias=out_bias, gain_mlp=gain_mlp, shift_mlp=shift_mlp, up_weight=up_weight, up_bias=up_bias, down_weight=down_weight, down_bias=down_bias, mean_weight=mean_weight, width_weight=width_weight)


@jax.custom_vjp
def low(v):
    return lax.optimization_barrier(v.astype(jnp.bfloat16)).astype(jnp.float32)

@jax.custom_vjp
def low_back(v):
    return v

def low_keep(v):
    return (low(v), None)

def low_pass(kept, grad):
    return (grad,)

def back_keep(v):
    return (v, None)

def back_low(kept, grad):
    return (low(grad),)
low.defvjp(low_keep, low_pass)
low_back.defvjp(back_keep, back_low)
epsilon = 1e-05
highest = lax.Precision.HIGHEST

def layer_norm(values, scale_vec, shift_vec):
    centred = values - lax.optimization_barrier(jnp.mean(values, axis=-1, keepdims=True))
    variance = lax.optimization_barrier(jnp.mean(centred * centred, axis=-1, keepdims=True))
    return centred * lax.rsqrt(variance + epsilon) * scale_vec + shift_vec

def basis_tables(basis_count, sample_count):
    centers = (jnp.arange(basis_count, dtype=jnp.float32) + 0.5) / basis_count
    points = (jnp.arange(sample_count, dtype=jnp.float32) + 0.5) / sample_count
    offsets = (points[:, None] - centers[None, :]) * basis_count
    return (centers, jnp.exp(-0.5 * offsets * offsets))

def memory_weights(logits, mean_weight, width_weight, centers):
    basis_count = centers.shape[0]
    centre = jax.nn.sigmoid(lax.optimization_barrier(jnp.sum(logits * mean_weight[:, None, :], axis=-1)))
    variance = (jax.nn.softplus(lax.optimization_barrier(jnp.sum(logits * width_weight[:, None, :], axis=-1))) + 0.5) * 0.02
    distance = centre[..., None] - centers
    return 1.0 / basis_count * lax.rsqrt(variance)[..., None] * jnp.exp(-0.5 * distance * distance / variance[..., None])

def block(hidden, coeffs, params, centers):
    gain_attn, shift_attn, qkv_weight, qv_bias, out_weight, out_bias, gain_mlp, shift_mlp, up_weight, up_bias, down_weight, down_bias, mean_weight, width_weight = params
    length, width_dim = hidden.shape
    heads = mean_weight.shape[1]
    head_dim = width_dim // heads
    basis_count = coeffs.shape[0]
    factor = 1.0 / math.sqrt(head_dim)
    normed = low(layer_norm(hidden, gain_attn, shift_attn))
    bias_row = jnp.concatenate([qv_bias[:width_dim], jnp.zeros((width_dim,), qv_bias.dtype), qv_bias[width_dim:]])
    qkv = low(low_back(jnp.matmul(normed, qkv_weight, precision=highest) + bias_row))
    qkv = qkv.reshape(length, 3, heads, head_dim)
    queries = qkv[:, 0]
    key_rows = qkv[:, 1]
    value_rows = qkv[:, 2]
    memory = low(low_back(jnp.matmul(coeffs, qkv_weight[:, width_dim:], precision=highest)))
    memory = memory.reshape(basis_count, 2, heads, head_dim)
    scores = low_back(jnp.einsum('qhe,khe->hqk', queries, key_rows, precision=highest) * factor)
    positions = jnp.arange(length)
    causal = positions[:, None] >= positions[None, :]
    scores = jnp.where(causal, scores, -1e+30)
    probs = low(jax.nn.softmax(scores, axis=-1))
    logits = low_back(jnp.einsum('qhe,jhe->hqj', queries, memory[:, 0], precision=highest) * factor)
    basis = low(memory_weights(logits, mean_weight.T, width_weight.T, centers))
    attended = jnp.einsum('hqk,khe->qhe', probs, value_rows, precision=highest) + jnp.einsum('hqj,jhe->qhe', basis, memory[:, 1], precision=highest)
    merged = low(low_back(attended.reshape(length, width_dim)))
    mid = hidden + low_back(jnp.matmul(merged, out_weight, precision=highest) + out_bias)
    normed_two = low(layer_norm(mid, gain_mlp, shift_mlp))
    up_pre = low_back(jnp.matmul(normed_two, up_weight, precision=highest) + up_bias)
    act = low(jax.nn.gelu(up_pre, approximate=True))
    return mid + jnp.matmul(act, down_weight, precision=highest) + down_bias

def reference(hidden, grad_out, past_states, old_coeffs, fresh_flags, ridge_map, gain_attn, shift_attn, qkv_weight, qv_bias, out_weight, out_bias, gain_mlp, shift_mlp, up_weight, up_bias, down_weight, down_bias, mean_weight, width_weight):
    params = tuple((weight_arg.astype(jnp.float32) for weight_arg in (gain_attn, shift_attn, qkv_weight, qv_bias, out_weight, out_bias, gain_mlp, shift_mlp, up_weight, up_bias, down_weight, down_bias, mean_weight, width_weight)))
    centers, sampled = basis_tables(NB, NS)
    ridge_full = ridge_map.astype(jnp.float32)
    group = math.gcd(SEQS, max(1, 4096 // SEQ_LEN))
    rounds = SEQS // group

    def regroup(array):
        return array.reshape((rounds, group) + array.shape[1:])

    def one_group(totals, group_items):
        states, cotangent, past_rows, old_rows, flag_rows = group_items
        keep_mask = (1 - flag_rows).astype(jnp.float32)
        old_kept = old_rows.astype(jnp.float32) * keep_mask[:, None, None]
        past_full = past_rows.astype(jnp.float32)

        def forward(inputs, weights):
            sampled_low = low(sampled)
            old_signal = low(jnp.einsum('ij,sjd->sid', sampled_low, old_kept, precision=highest))
            signal = jnp.concatenate([old_signal, past_full], axis=1)
            coeffs = low(jnp.einsum('jt,std->sjd', ridge_full, signal, precision=highest))
            return jax.vmap(lambda row_block, coeff_block: block(row_block, coeff_block, weights, centers))(inputs, coeffs)
        outputs, backward = jax.vjp(forward, states.astype(jnp.float32), params)
        grad_states, grad_params = backward(cotangent.astype(jnp.float32))
        totals = jax.tree.map(jnp.add, totals, grad_params)
        return (totals, (outputs.astype(jnp.bfloat16), grad_states.astype(jnp.bfloat16)))
    zero_grads = jax.tree.map(jnp.zeros_like, params)
    totals, (outputs, grad_states) = lax.scan(one_group, zero_grads, (regroup(hidden), regroup(grad_out), regroup(past_states), regroup(old_coeffs), regroup(fresh_flags)))
    output = outputs.reshape(hidden.shape)
    grad_input = grad_states.reshape(hidden.shape)
    return (output, grad_input, totals[0], totals[1], totals[2], totals[3], totals[4], totals[5], totals[6], totals[7], totals[8], totals[9], totals[10], totals[11], totals[12], totals[13])
```

```python
import math

import jax
import jax.numpy as jnp
from jax import lax
from jax.experimental import pallas as pl
from jax.experimental.pallas import tpu as pltpu
from jax.sharding import PartitionSpec as P

EPS = 1e-05
LOG2E = 1.4426950408889634
BF = jnp.bfloat16
F32 = jnp.float32
AXES = ("dp", "fsdp")
VMEM_BYTES = 60 * 1024 * 1024


def dot_nn(a, b):
    return lax.dot_general(a, b, (((1,), (0,)), ((), ())), preferred_element_type=F32)


def dot_nt(a, b):
    return lax.dot_general(a, b, (((1,), (1,)), ((), ())), preferred_element_type=F32)


def dot_tn(a, b):
    return lax.dot_general(a, b, (((0,), (0,)), ((), ())), preferred_element_type=F32)


def split_high_low(x):
    high = x.astype(BF)
    return high, (x - high.astype(F32)).astype(BF)


def iota(shape, dim):
    return lax.broadcasted_iota(jnp.int32, shape, dim)


def head_masks(pair_lanes, head_dim):
    lane = iota((1, pair_lanes), 1)
    return [((lane // head_dim) == h).astype(F32).astype(BF) for h in range(pair_lanes // head_dim)]


def norm_parts(x):
    mean = jnp.mean(x, axis=-1, keepdims=True)
    centred = x - mean
    variance = jnp.mean(centred * centred, axis=-1, keepdims=True)
    inv = lax.rsqrt(variance + EPS)
    return centred * inv, inv


def norm_back(grad, unit, inv, gain):
    g = grad * gain
    return inv * (g - jnp.mean(g, axis=-1, keepdims=True) - unit * jnp.mean(g * unit, axis=-1, keepdims=True))


MESH = pl.DeviceIdType.MESH


class Place:
    def __init__(self):
        self.y = lax.axis_index("dp")
        f = lax.axis_index("fsdp")
        self.z, self.x, self.c = f // 4, (f // 2) % 2, f % 2

    def at(self, y=None, z=None, x=None, c=None):
        y, z, x, c = (b if a is None else a for a, b in ((y, self.y), (z, self.z), (x, self.x), (c, self.c)))
        return (y, z * 4 + x * 2 + c)

    def far_z(self, s):
        return (self.z + s) % 4

    def others(self):
        return [self.at(c=1 - self.c), self.at(x=1 - self.x), self.at(y=1 - self.y)] + [
            self.at(z=self.far_z(s)) for s in (1, 2, 3)]

    def layer(self):
        return [self.at(y=(self.y + d // 4) % 2, x=(self.x + d // 2) % 2, c=(self.c + d) % 2) for d in range(1, 8)] + [
            self.at(z=self.far_z(s)) for s in (1, 2, 3)]

    def greet(self, devices):
        barrier = pltpu.get_barrier_semaphore()
        for d in devices:
            pl.semaphore_signal(barrier, inc=1, device_id=d, device_id_type=MESH)
        pl.semaphore_wait(barrier, len(devices))


class Weight:
    def __init__(self, index, rows, half, parts):
        self.index, self.rows, self.half, self.parts = index, rows, half, parts

    def where(self, part, c=None):
        r0, rn, c0, cn = self.parts[part]
        if c is None:
            return pl.ds(r0, rn), pl.ds(c0, cn)
        return pl.ds(r0, rn), pl.ds(pl.multiple_of(c * self.half + c0, 128), cn)

    def columns(self, c):
        return pl.ds(pl.multiple_of(c * self.half, 128), self.half)


def split_columns(n):
    first = (n // 128 + 1) // 2 * 128
    return first


def weight_table(width, ff, devices):
    chip = 2 * width // devices
    chip_ff = 2 * ff // devices
    items = []
    for i, n in enumerate((3 * width, width, ff)):
        half = n // 2
        first = split_columns(half)
        items.append(Weight(i, chip, half, ((0, chip, 0, first), (0, chip, first, half - first))))
    half = width // 2
    items.append(Weight(3, chip_ff, half, ((0, chip_ff // 2, 0, half), (chip_ff // 2, chip_ff // 2, 0, half))))
    return items


def nested(conds, act):
    if not conds:
        act()
        return

    @pl.when(conds[0]())
    def _():
        nested(conds[1:], act)


class Started:
    def __init__(self, send, recv):
        self.send, self.recv, self.live = send, recv, {}

    def go(self, name, src, dst, slot, dev):
        copy = pltpu.make_async_remote_copy(
            src_ref=src, dst_ref=dst, send_sem=self.send.at[slot], recv_sem=self.recv.at[slot],
            device_id=dev, device_id_type=MESH)
        copy.start()
        self.live.setdefault(name, []).append(copy)

    def arrived(self, name):
        for copy in self.live[name]:
            copy.wait_recv()

    def left(self, name=None):
        for key in list(self.live) if name is None else [name]:
            for copy in self.live.pop(key):
                copy.wait_send()


class Gather:
    SLOTS = 2 * 23

    def __init__(self, place, send, recv, base, w, full):
        self.p, self.send, self.recv, self.base, self.w, self.full = place, send, recv, base, w, full
        self.begun = []

    def ref(self, part, y, z, x):
        if part is None:
            return self.full.at[y, z, x, :, self.w.columns(self.p.c)]
        r, c = self.w.where(part, self.p.c)
        return self.full.at[y, z, x, r, c]

    def go(self, src, dst, send, recv, dev, conds, like):
        pltpu.make_async_remote_copy(
            src_ref=src, dst_ref=dst, send_sem=self.send.at[self.base + send()], recv_sem=self.recv.at[self.base + recv],
            device_id=dev, device_id_type=MESH).start()
        self.begun.append((send, conds, like))

    def wait(self, ref, slot):
        pltpu.make_async_remote_copy(
            src_ref=ref, dst_ref=ref, send_sem=self.send.at[self.base], recv_sem=self.recv.at[self.base + slot],
            device_id=self.p.at(c=1 - self.p.c), device_id_type=MESH).wait_recv()

    def left(self):
        for send, conds, like in self.begun:
            def act():
                pltpu.make_async_remote_copy(
                    src_ref=like(), dst_ref=like(), send_sem=self.send.at[self.base + send()], recv_sem=self.recv.at[self.base],
                    device_id=self.p.at(c=1 - self.p.c), device_id_type=MESH).wait_send()

            nested(conds, act)

    def along(self, j, act):
        here = self.p.z
        for z, cond, toward in ((lambda: here - j, lambda: here >= j, 1), (lambda: here + j, lambda: here + j <= 3, -1)):
            nested((cond,), lambda: act(z, (cond,), toward))

    def pass_z(self, src, dst, z, toward, conds, like):
        p = self.p
        more = (lambda: p.z <= 2) if toward == 1 else (lambda: p.z >= 1)
        nested((more,), lambda: self.go(
            src, dst, lambda: z() + (0 if toward == 1 else 4), z(), p.at(z=p.z + toward), conds + (more,), like))

    def partner(self, part, step):
        p = self.p
        return p.at(x=1 - p.x) if (part + step) % 2 == 0 else p.at(y=1 - p.y)

    def behind(self, part):
        p = self.p
        return (p.y, 1 - p.x) if part == 0 else (1 - p.y, p.x)

    def own_z(self):
        return self.p.z

    def one(self, part):
        return self.ref(part, 0, 0, 0)

    def start(self, block):
        p = self.p
        for toward in (1, -1):
            self.pass_z(block, self.ref(None, p.y, p.z, p.x), self.own_z, toward, (), lambda: self.one(None))
        for part in (0, 1):
            self.onward(part, self.own_z, block.at[self.w.where(part)], ())

    def onward(self, part, z, src, conds):
        p = self.p
        dst = self.ref(part, p.y, z(), p.x)
        o = part * 23
        like = lambda: self.one(part)
        self.go(src, dst, lambda: o + 8 + z(), o + 8 + z(), self.partner(part, 0), conds, like)
        self.go(src, dst, lambda: o + 12 + z(), o + 12 + z(), self.partner(part, 1), conds, like)

    def on_z(self, j):
        def act(z, conds, toward):
            whole = self.ref(None, self.p.y, z(), self.p.x)
            self.wait(whole, z())
            self.pass_z(whole, whole, z, toward, conds, lambda: self.one(None))
            for part in (0, 1):
                self.onward(part, z, self.ref(part, self.p.y, z(), self.p.x), conds)

        self.along(j, act)

    def on_second(self, j):
        def act(z, conds, toward):
            for part in (0, 1):
                self.second_on(part, z, conds)

        if j == 0:
            act(self.own_z, (), 0)
        else:
            self.along(j, act)

    def second_on(self, part, z, conds):
        y, x = self.behind(part)
        ref = self.ref(part, y, z(), x)
        o = part * 23
        self.wait(ref, o + 8 + z())
        self.go(ref, ref, lambda: o + 16 + z(), o + 16 + z(), self.partner(part, 1), conds, lambda: self.one(part))

    def core(self, step):
        p = self.p
        for part in (0, 1):
            o = part * 23
            if step == 2:
                for z in range(4):
                    y, x = (1 - p.y, p.x) if part == 0 else (p.y, 1 - p.x)
                    self.wait(self.ref(part, y, z, x), o + 12 + z)
                    self.wait(self.ref(part, 1 - p.y, z, 1 - p.x), o + 16 + z)
            self.go_core(lambda part=part: self.of_step(part, step), o + 20 + step)

    def of_step(self, part, step):
        p = self.p
        if step == 0:
            y, x = p.y, p.x
        elif step == 1:
            y, x = self.behind(part)
        else:
            y, x = (1 - p.y, slice(None)) if part == 0 else (slice(None), 1 - p.x)
        return self.ref(part, y, slice(None), x)

    def go_core(self, make, slot):
        self.go(make(), make(), lambda: slot, slot, self.p.at(c=1 - self.p.c), (), make)

    def finish(self):
        p = self.p
        for part in (0, 1):
            r, c = self.w.where(part, 1 - p.c)
            for step in range(3):
                if step == 2:
                    ref = self.full.at[1 - p.y, :, :, r, c] if part == 0 else self.full.at[:, :, 1 - p.x, r, c]
                else:
                    y, x = (p.y, p.x) if step == 0 else self.behind(part)
                    ref = self.full.at[y, :, x, r, c]
                self.wait(ref, part * 23 + 20 + step)


class LateGather(Gather):
    def start(self, block):
        for part in (0, 1):
            self.onward(part, self.own_z, block.at[self.w.where(part)], ())

    def on_third(self):
        p = self.p
        for part in (0, 1):
            o = part * 23
            y, x = (1 - p.y, p.x) if part == 0 else (p.y, 1 - p.x)
            self.wait(self.ref(part, y, p.z, x), o + 12 + p.z)
            self.wait(self.ref(part, 1 - p.y, p.z, 1 - p.x), o + 16 + p.z)
        ref = self.layer(p.z)
        for toward in (1, -1):
            self.pass_z(ref, ref, self.own_z, toward, (), lambda: self.layer(0))

    def layer(self, z):
        return self.ref(None, slice(None), z, slice(None))

    def on_z(self, j):
        def act(z, conds, toward):
            ref = self.layer(z())
            self.wait(ref, z())
            self.pass_z(ref, ref, z, toward, conds, lambda: self.layer(0))

        self.along(j, act)

    def core(self):
        self.go_core(lambda: self.ref(None, slice(None), slice(None), slice(None)), 20)

    def finish(self):
        self.wait(self.full.at[:, :, :, :, self.w.columns(1 - self.p.c)], 20)


def middle_body(
    att, hidden, gout, wout, wup, wdown, vecs, ubias, vsum, usum,
    x_t, dout, mid, x, acc, gacc, act_s, slope_s, outs, local, sem, put_down, put_up, hook,
):
    output_h, gmid_h, gatt_h, dout_h = outs
    tokens, width = hidden.shape
    ff = wup.shape[1]
    block = 256
    blocks = tokens // block
    chunk = ubias.shape[1]
    chunks = ff // chunk
    out_bias, gain, shift, down_bias = (vecs[i:i + 1, :] for i in (4, 5, 6, 7))

    def enter(i, _):
        r = pl.ds(pl.multiple_of(i * block, block), block)
        m = hidden[r, :].astype(F32) + dot_nn(att[r, :], wout[...]) + out_bias
        mid[r, :] = m
        unit, _ = norm_parts(m)
        y = (unit * gain + shift).astype(BF)
        x[r, :] = y
        x_t[:, r] = y.T
        acc[r, :] = jnp.zeros((block, width), F32)
        gacc[r, :] = jnp.zeros((block, width), F32)
        hook("enter", i)
        return 0

    lax.fori_loop(0, blocks, enter, 0)
    hook("entered", 0)

    def chunk_of(i):
        return (i % 2) * 2 + i // 2

    def first(i):
        j = chunk_of(i)
        c = pl.ds(pl.multiple_of(j * chunk, chunk), chunk)
        slot = i % 2
        w_up = wup[:, c]
        bias = ubias[pl.ds(j, 1), :]
        for b in range(blocks):
            r = slice(b * block, (b + 1) * block)
            u = dot_nn(x[r, :], w_up) + bias
            u2 = u * u
            th = jnp.tanh(u * (0.7978845608028654 + 0.7978845608028654 * 0.044715 * u2))
            half_one = 0.5 + 0.5 * th
            act_s[slot, r, :] = (u * half_one).astype(BF)
            slope = half_one + (0.5 * u) * (1.0 - th * th) * (
                0.7978845608028654 + 3 * 0.7978845608028654 * 0.044715 * u2)
            slope_s[slot, r, :] = slope.astype(BF)
        for k in range(2):
            part = slice(k * chunk // 2, (k + 1) * chunk // 2)
            put_down(i, k, dot_tn(act_s[slot, :, part], gout[...]).astype(BF))
        hook("first", i)

    def second(i):
        j = chunk_of(i)
        c = pl.ds(pl.multiple_of(j * chunk, chunk), chunk)
        slot = i % 2
        w_up, w_down = wup[:, c], wdown[c, :]
        colsum = jnp.zeros((1, chunk), F32)
        for b in range(blocks):
            r = slice(b * block, (b + 1) * block)
            gu = (dot_nt(gout[r, :], w_down) * slope_s[slot, r, :].astype(F32)).astype(BF)
            colsum = colsum + jnp.sum(gu.astype(F32), axis=0, keepdims=True)
            slope_s[slot, r, :] = gu
            acc[r, :] += dot_nn(act_s[slot, r, :], w_down)
            gacc[r, :] += dot_nt(gu, w_up)
        usum[pl.ds(j, 1), :] = colsum
        hook("middle", i)
        for k in range(2):
            part = slice(k * width // 2, (k + 1) * width // 2)
            put_up(i, k, dot_nn(x_t[part, :], slope_s[slot]).astype(BF))
        hook("second", i)

    def ahead(i, _):
        first(i)
        return 0

    lax.fori_loop(0, 2, ahead, 0)
    hook("ready", 0)
    usum[...] = jnp.zeros_like(usum)

    def both(i, _):
        second(i)

        @pl.when(i + 2 < chunks)
        def _():
            first(i + 2)

        hook("both", i)
        return 0

    lax.fori_loop(0, chunks, both, 0)
    vsum[...] = jnp.zeros_like(vsum)

    def rows_out(i):
        r = pl.ds(pl.multiple_of(i * block, block), block)
        return (pltpu.make_async_copy(act_s.at[0, r, :], output_h.at[r, :], local.at[sem + 1 + 3 * i]),
                pltpu.make_async_copy(mid.at[r, :], gmid_h.at[r, :], local.at[sem + 2 + 3 * i]),
                pltpu.make_async_copy(act_s.at[1, r, :], gatt_h.at[r, :], local.at[sem + 3 + 3 * i]))

    def leave(i, _):
        r = pl.ds(pl.multiple_of(i * block, block), block)
        m = mid[r, :]
        act_s[0, r, :] = (m + acc[r, :] + down_bias).astype(BF)
        unit, inv = norm_parts(m)
        g = gacc[r, :]
        go = gout[r, :].astype(F32)
        gm = go + norm_back(g, unit, inv, gain)
        mid[r, :] = gm
        gp = gm.astype(BF)
        x[r, :] = gp
        act_s[1, r, :] = dot_nt(gp, wout[...]).astype(BF)
        for copy in rows_out(i):
            copy.start()
        vsum[0:1, :] += jnp.sum(go, axis=0, keepdims=True)
        vsum[1:2, :] += jnp.sum(g * unit, axis=0, keepdims=True)
        vsum[2:3, :] += jnp.sum(g, axis=0, keepdims=True)
        vsum[3:4, :] += jnp.sum(gp.astype(F32), axis=0, keepdims=True)
        hook("leave", i)
        return 0

    lax.fori_loop(0, blocks, leave, 0)
    for j in range(width // 256):
        c = slice(j * 256, (j + 1) * 256)
        dout[:, c] = dot_tn(att[...], x[:, c]).astype(BF)
    final = pltpu.make_async_copy(dout, dout_h, local.at[sem])
    final.start()
    hook("end", 0)
    for i in range(blocks):
        for copy in rows_out(i):
            copy.wait()
    final.wait()


def middle_scratch(tokens, width, chunk):
    return [
        pltpu.VMEM((tokens, width), F32),
        pltpu.VMEM((tokens, width), BF),
        pltpu.VMEM((tokens, width), F32),
        pltpu.VMEM((tokens, width), F32),
        pltpu.VMEM((2, tokens, chunk), BF),
        pltpu.VMEM((2, tokens, chunk), BF),
    ]


def middle_call(att, hidden, gout, wout, wup, wdown, vecs, ubias):
    tokens, width = att.shape
    ff = wup.shape[1]
    chunk = ubias.shape[1]
    vm = pl.BlockSpec(memory_space=pltpu.VMEM)
    anyw = pl.BlockSpec(memory_space=pl.ANY)
    shapes = (
        jax.ShapeDtypeStruct((tokens, width), BF),
        jax.ShapeDtypeStruct((tokens, width), F32),
        jax.ShapeDtypeStruct((tokens, width), BF),
        jax.ShapeDtypeStruct((width, width), BF),
        jax.ShapeDtypeStruct((width, ff), BF),
        jax.ShapeDtypeStruct((ff, width), BF),
        jax.ShapeDtypeStruct((8, width), F32),
        jax.ShapeDtypeStruct((8, chunk), F32),
    )

    def kernel(att, hidden, gout, wout, wup, wdown, vecs, ubias, o, gm, ga, do, du, dd, vsum, usum, *scratch):
        def place(i):
            return ((i % 2) * 2 + i // 2) * chunk

        def put_down(i, k, v):
            dd[pl.ds(pl.multiple_of(place(i) + k * chunk // 2, chunk // 2), chunk // 2), :] = v

        def put_up(i, k, v):
            du[k * width // 2:(k + 1) * width // 2, pl.ds(pl.multiple_of(place(i), chunk), chunk)] = v

        middle_body(att, hidden, gout, wout, wup, wdown, vecs, ubias, vsum, usum, *scratch[:-1], (o, gm, ga, do), scratch[-1], 0,
                    put_down, put_up, lambda where, i: None)

    return pl.pallas_call(
        kernel,
        out_shape=shapes,
        in_specs=[vm] * 8,
        out_specs=[anyw] * 4 + [vm] * 4,
        scratch_shapes=[pltpu.VMEM((width, tokens), BF), pltpu.VMEM((width, width), BF)] + middle_scratch(tokens, width, chunk) + [pltpu.SemaphoreType.DMA((1 + 3 * (tokens // 256),))],
        compiler_params=pltpu.CompilerParams(vmem_limit_bytes=58 * 1024 * 1024),
        name="middle",
    )(att, hidden.reshape(tokens, width), gout.reshape(tokens, width), wout, wup, wdown, vecs, ubias)


class EarlyReduce:
    SLOTS = 20

    def __init__(self, place, send, recv, g_d, g_u, away_d, away_u, r1_d, r1_u, r2_d, r2_y, r2_x, r3_d):
        self.p, self.send, self.recv = place, send, recv
        self.g_d, self.g_u, self.away_d, self.away_u = g_d, g_u, away_d, away_u
        self.r1_d, self.r1_u, self.r2_d, self.r2_y, self.r2_x, self.r3_d = r1_d, r1_u, r2_d, r2_y, r2_x, r3_d
        self.n = g_d.shape[-1]
        self.h = g_d.shape[-2] // 2

    def copy(self, src, dst, slot, dev):
        return pltpu.make_async_remote_copy(
            src_ref=src, dst_ref=dst, send_sem=self.send.at[slot], recv_sem=self.recv.at[slot], device_id=dev, device_id_type=MESH)

    def mate(self):
        return self.p.at(c=1 - self.p.c)

    def sides(self, v):
        low, high = v[..., :self.n], v[..., self.n:]
        return jnp.where(self.p.c == 0, low, high), jnp.where(self.p.c == 0, high, low)

    def down_core(self, i):
        return self.copy(self.away_d.at[i % 2], self.r1_d.at[i // 2, i % 2], i, self.mate())

    def put_down(self, i, k, v):
        if k == 0:
            @pl.when(i >= 2)
            def _():
                self.down_core(i - 2).wait_send()

        keep, give = self.sides(v.reshape(2, 2 * self.h, 2 * self.n))
        self.g_d[i // 2, i % 2, k] = keep
        self.away_d[i % 2, k] = give

    def down_second(self, t):
        p = self.p
        a, b = pl.ds(0, self.h), pl.ds(self.h, self.h)
        return (self.copy(self.g_d.at[t, 1 - p.y, :, :, a, :], self.r2_d.at[t, 0], 8 + 2 * t, p.at(y=1 - p.y)),
                self.copy(self.g_d.at[t, :, :, 1 - p.x, b, :], self.r2_d.at[t, 1], 9 + 2 * t, p.at(x=1 - p.x)))

    def down_third(self, t):
        p = self.p
        a, b = pl.ds(0, self.h), pl.ds(self.h, self.h)
        return (self.copy(self.g_d.at[t, p.y, :, 1 - p.x, a, :], self.r3_d.at[t, 0], 12 + 2 * t, p.at(x=1 - p.x)),
                self.copy(self.g_d.at[t, 1 - p.y, :, p.x, b, :], self.r3_d.at[t, 1], 13 + 2 * t, p.at(y=1 - p.y)))

    def down_add_core(self, t):
        for y in (0, 1):
            self.down_core(2 * t + y).wait_recv()

        def step(i, _):
            at = (t, i // 4, (i // 2) % 2, i % 2)
            self.g_d[at] = self.g_d[at] + self.r1_d[at]
            return 0

        lax.fori_loop(0, 8, step, 0)
        for copy in self.down_second(t):
            copy.start()

    def down_add_second(self, t):
        p, h = self.p, self.h
        for copy in self.down_second(t):
            copy.wait_recv()

        def step(i, _):
            u, v = i // 2, i % 2
            at, to = (t, p.y, u, v, slice(0, h)), (t, 0, u, v)
            self.g_d[at] = self.g_d[at] + self.r2_d[to]
            at, to = (t, u, v, p.x, slice(h, 2 * h)), (t, 1, u, v)
            self.g_d[at] = self.g_d[at] + self.r2_d[to]
            return 0

        lax.fori_loop(0, 4, step, 0)
        for copy in self.down_third(t):
            copy.start()

    def down_add_third(self, t):
        p, h = self.p, self.h
        for copy in self.down_third(t):
            copy.wait_recv()
        for z in (0, 1):
            for part in (0, 1):
                rows = slice(part * h, (part + 1) * h)
                at = (t, p.y, z, p.x, rows)
                self.g_d[at] = self.g_d[at] + self.r3_d[t, part, z]

    def up_core(self, i):
        return self.copy(self.away_u.at[i % 2], self.r1_u.at[i], 4 + i, self.mate())

    def rows_u(self):
        return self.g_u.shape[-2]

    def put_up(self, i, k, v):
        if k == 0:
            @pl.when(i >= 2)
            def _():
                self.up_core(i - 2).wait_send()

        keep, give = self.sides(v)
        c = pl.ds(pl.multiple_of((i // 2) * self.n, 128), self.n)
        self.g_u[i % 2, k, :, :, :, c] = keep.reshape(4, 2, self.rows_u(), self.n)
        self.away_u[i % 2, k] = give.reshape(4, 2, self.rows_u(), self.n)

    def up_second(self, i):
        p = self.p
        t = i % 2
        c = pl.ds((i // 2) * self.n, self.n)
        if t == 0:
            return self.copy(self.g_u.at[0, 1 - p.y, :, :, :, c], self.r2_y.at[i // 2], 16 + i, p.at(y=1 - p.y))
        return self.copy(self.g_u.at[1, :, :, 1 - p.x, :, c], self.r2_x.at[i // 2], 16 + i, p.at(x=1 - p.x))

    def up_add_core(self, i):
        self.up_core(i).wait_recv()
        c = slice((i // 2) * self.n, (i // 2 + 1) * self.n)

        def step(b, _):
            at = (b // 8, (b // 2) % 4, b % 2)
            here = (i % 2,) + at + (slice(None), c)
            self.g_u[here] = self.g_u[here] + self.r1_u[(i,) + at]
            return 0

        lax.fori_loop(0, 16, step, 0)
        self.up_second(i).start()

    def up_add_second(self, i):
        p = self.p
        self.up_second(i).wait_recv()
        c = slice((i // 2) * self.n, (i // 2 + 1) * self.n)

        def step(b, _):
            if i % 2 == 0:
                here, got = (0, p.y, b // 2, b % 2, slice(None), c), self.r2_y[i // 2, b // 2, b % 2]
            else:
                here, got = (1, b // 4, b % 4, p.x, slice(None), c), self.r2_x[i // 2, b // 4, b % 4]
            self.g_u[here] = self.g_u[here] + got
            return 0

        lax.fori_loop(0, 8, step, 0)

    def left(self):
        for i in (2, 3):
            self.down_core(i).wait_send()
            self.up_core(i).wait_send()
        for t in (0, 1):
            for copy in self.down_second(t) + self.down_third(t):
                copy.wait_send()
        for i in range(4):
            self.up_second(i).wait_send()


def forward_coeffs(s, flags, past, old, ridge, coeffs, coef_t):
    length, basis = past.shape[1], ridge.shape[0]
    samples = ridge.shape[1] - length
    brows = slice(s * basis, (s + 1) * basis)
    diff = (iota((samples, basis), 0) - iota((samples, basis), 1)).astype(F32)
    sampled = jnp.exp(-0.5 * diff * diff).astype(BF)
    keep = (1 - flags[s]).astype(F32)
    old_signal = (dot_nn(sampled, old[s]) * keep).astype(BF)
    co = (dot_nn(ridge[:, :samples], old_signal) + dot_nn(ridge[:, samples:], past[s])).astype(BF)
    coeffs[brows, :] = co
    coef_t[:, brows] = co.T


def forward_projections(s, half, heads, length, basis, hidden, vecs, wmat, wqkv, normed, norm_t, coeffs, qkv, mem, ublk, proj, head_par):
    width = hidden.shape[1]
    hd = width // heads
    rows = slice(s * length, (s + 1) * length)
    brows = slice(s * basis, (s + 1) * basis)
    step = width // 3
    if half == 0:
        unit, _ = norm_parts(hidden[rows, :].astype(F32))
        nrm = (unit * vecs[0:1, :] + vecs[1:2, :]).astype(BF)
        normed[...] = nrm
        norm_t[:, rows] = nrm.T
    for j in range(9) if half == 0 else ():
        cols = slice(j * step, (j + 1) * step)
        y = dot_nn(normed[...], wqkv[:, cols])
        if j < 3:
            y = y + vecs[2:3, cols]
        elif j >= 6:
            y = y + vecs[3:4, (j - 6) * step:(j - 5) * step]
        qkv[rows, cols] = y.astype(BF)
    if half == 0:
        return
    for j in range(6):
        cols = slice(j * step, (j + 1) * step)
        wcols = slice(width + j * step, width + (j + 1) * step)
        mem[brows, cols] = dot_nn(coeffs[brows, :], wqkv[:, wcols]).astype(BF)
    raw = dot_tn(wmat[...], mem[brows, 0:width])[0:32, :]
    own = (iota((32, width), 0) % 16) == (iota((32, width), 1) // hd)
    u = jnp.where(own, raw, 0.0) * (1.0 / math.sqrt(hd))
    ublk[s] = u
    u_hi, u_lo = split_high_low(u)
    q = qkv[rows, 0:width]
    pr = dot_nt(u_hi, q) + dot_nt(u_lo, q)
    proj[s] = pr
    basis_rows(pr, heads, basis, head_par)


def basis_rows(pr, heads, basis, head_par):
    centre = 1.0 / (1.0 + jnp.exp(-pr[0:16]))
    wide = pr[16:32]
    soft = jnp.maximum(wide, 0.0) + jnp.log(1.0 + jnp.exp(-jnp.abs(wide)))
    variance = (soft + 0.5) * 0.02
    inv_root = lax.rsqrt(variance)
    root = inv_root * math.sqrt(0.5 * LOG2E)
    shift_log = jnp.log(inv_root) * LOG2E - math.log2(basis)
    for h in range(heads):
        head_par[h, 0:1, :] = root[h:h + 1]
        head_par[h, 1:2, :] = centre[h:h + 1] * root[h:h + 1]
        head_par[h, 2:3, :] = shift_log[h:h + 1]
    return centre, wide, variance, root


def forward_heads(s, first, last, heads, length, basis, width, qkv, mem, att, lse, head_par, att_t):
    hd = width // heads
    half = length // 2
    rows = slice(s * length, (s + 1) * length)
    brows = slice(s * basis, (s + 1) * basis)
    masks = head_masks(2 * hd, hd)
    scale = LOG2E / math.sqrt(hd)

    def pair(p, _):
        c0 = pl.multiple_of(p * (2 * hd), 2 * hd)
        q = qkv[rows, pl.ds(c0, 2 * hd)]
        k = qkv[rows, pl.ds(pl.multiple_of(width + c0, 2 * hd), 2 * hd)]
        v_t = qkv[rows, pl.ds(pl.multiple_of(2 * width + c0, 2 * hd), 2 * hd)].T
        mv_t = mem[brows, pl.ds(pl.multiple_of(width + c0, 2 * hd), 2 * hd)].T
        cent = ((iota((basis, 1), 0).astype(F32) + 0.5) / basis)
        for h in range(2):
            head = p * 2 + h
            km = k * masks[h]
            lanes = slice(h * hd, (h + 1) * hd)
            for b in range(2):
                cols = slice(b * half, (b + 1) * half)
                depth = (b + 1) * half
                sc = dot_nt(km[:depth], q[cols]) * scale
                allowed = iota((depth, half), 0) <= iota((depth, half), 1) + b * half
                sc = jnp.where(allowed, sc, -1e30)
                top = jnp.max(sc, axis=0, keepdims=True)
                e = jnp.exp2(sc - top)
                total = jnp.sum(e, axis=0, keepdims=True)
                out = dot_nn(v_t[lanes, :depth], e.astype(BF)) / total
                lse[s, head, :, cols] = top + jnp.log(total) * LOG2E
                t = cent * head_par[head, 0:1, cols] - head_par[head, 1:2, cols]
                bas = jnp.exp2(head_par[head, 2:3, cols] - t * t).astype(BF)
                out = out + dot_nn(mv_t[lanes, :], bas)
                att_t[lanes, cols] = out
        att[rows, pl.ds(c0, 2 * hd)] = att_t[...].T.astype(BF)
        return 0

    lax.fori_loop(first, last, pair, 0)


def unpack_small(small, wmat, vecs, ubias, devices, width, ff):
    flat = small.reshape(devices * 32, 128)
    wmat[...] = small.reshape(devices, 32, 128)[:, 0:16, :].reshape(devices * 16, 128)
    every = flat[...]

    def spread(row, offset, each, n):
        pick = (iota((devices, devices * 32), 1) == iota((devices, devices * 32), 0) * 32 + row)
        mine = dot_nn(pick.astype(F32).astype(BF), every).astype(BF)
        place = iota((128, n), 0) == iota((128, n), 1) % each + offset
        wide = dot_nn(mine, place.astype(F32).astype(BF))
        own = iota((devices, n), 1) // each == iota((devices, n), 0)
        return jnp.sum(jnp.where(own, wide, 0.0), axis=0, keepdims=True)

    e = width // devices
    vecs[0:1, :] = spread(16, 0, e, width)
    vecs[1:2, :] = spread(16, e, e, width)
    both = spread(17, 2 * e, 2 * e, 2 * width)
    vecs[2:3, :] = both[:, :width]
    vecs[3:4, :] = both[:, width:]
    vecs[4:5, :] = spread(16, 2 * e, e, width)
    vecs[5:6, :] = spread(16, 3 * e, e, width)
    vecs[6:7, :] = spread(17, 0, e, width)
    vecs[7:8, :] = spread(17, e, e, width)
    up = spread(18, 0, ff // devices, ff)
    chunk = ubias.shape[1]
    ubias[...] = jnp.zeros_like(ubias)
    for j in range(ff // chunk):
        ubias[j:j + 1, :] = up[:, j * chunk:(j + 1) * chunk]


FIRST_STEPS = (
    "#0", "qz1", "qs0", "os0", "qz2", "qs1", "+0", "qz3", "ug", "own", "ot", "qc0", "#1", "qs2", "+1", "qs3", "qc1",
    "uz1", "us0", "oz1", "+2", "uz2", "us1", "oz2", "qc2",
)
LATER_STEPS = (
    ("uz3", "us2", "dg", "oz3", "oc"), ("us3", "uc0", "uc1"), ("dz1",), ("ds0",), ("dz2",), ("ds1",), ("dz3",), ("dc0",),
    (), ("ds2",), (), ("uc2",), ("ds3",), ("dc1",),
)


def forward_kernel(
    heads, devices,
    flags, hidden_h, past_h, old_h, ridge_h, gout_h, small, qkv_s, out_s, up_s, down_s,
    norm_h, coef_h, qkv_h, mem_h, output_h, gmid_h, gatt_h, dout_h, gu_h, gd_h, wq_h,
    lse, ublk, proj, wmat, vecs, vsum, usum,
    hidden, gout, att, wq, wo, wu, wd, ubias,
    wide_s, wide_r, block, block_d, sfull, early, send, recv, local, early_send, early_recv,
):
    place = Place()
    p = place
    tokens, width = hidden.shape
    seqs, length = past_h.shape[0], past_h.shape[1]
    basis = ridge_h.shape[0]
    ff = up_s.shape[1]
    t_qkv, t_out, t_up, t_down = weight_table(width, ff, devices)
    st = Started(send, recv)
    n = Gather.SLOTS
    g_qkv = Gather(place, send, recv, 0, t_qkv, wq)
    g_up = Gather(place, send, recv, n, t_up, wu)
    g_down = Gather(place, send, recv, 2 * n, t_down, wd)
    g_out = LateGather(place, send, recv, 3 * n, t_out, wo)
    base = 4 * n
    nh = wide_r.shape[1]
    blocks = {
        "q": block.at[:, 0:t_qkv.half], "o": block.at[:, t_qkv.half:t_qkv.half + t_out.half],
        "u": block.at[:, t_qkv.half + t_out.half:nh], "d": block_d}
    gather_of = {"q": g_qkv, "o": g_out, "u": g_up, "d": g_down}

    def pass_on(word):
        g, what, n = gather_of[word[0]], word[1], word[2:]
        if what == "g":
            g.start(blocks[word[0]])
        elif what == "z":
            g.on_z(int(n))
        elif what == "s":
            g.on_second(int(n))
        elif what == "t":
            g.on_third()
        elif what == "f":
            g.finish()
        elif n:
            g.core(int(n))
        else:
            g.core()

    stores = []

    def store(src, dst, rows=None):
        i = len(stores)

        def make():
            a, b = (src, dst) if rows is None else (src.at[rows, :], dst.at[rows, :])
            return pltpu.make_async_copy(a, b, local.at[9 + i])

        make().start()
        stores.append(make)

    def attention(norm_t, coef_t, qkv, mem, past, old, ridge, normed, coeffs, head_par, att_t):
        forward_attention(
            heads, devices, place, (flags, hidden_h, past_h, old_h, ridge_h, gout_h, small, qkv_s, out_s, up_s, down_s),
            (t_qkv, t_out, t_up, t_down), st, (g_qkv, g_up, g_down, g_out), base, store, blocks, pass_on,
            (norm_h, coef_h, qkv_h, mem_h, wq_h),
            lse, ublk, proj, wmat, vecs, hidden, gout, norm_t, coef_t, qkv, mem, att, wq, ubias,
            wide_s, wide_r, block, block_d, sfull, local,
            past, old, ridge, normed, coeffs, head_par, att_t)
        for make in stores:
            make().wait()

    pl.run_scoped(
        attention,
        pltpu.VMEM((width, tokens), BF),
        pltpu.VMEM((width, seqs * basis), BF),
        pltpu.VMEM((tokens, 3 * width), BF),
        pltpu.VMEM((seqs * basis, 2 * width), BF),
        pltpu.VMEM(past_h.shape, BF),
        pltpu.VMEM(old_h.shape, BF),
        pltpu.VMEM(ridge_h.shape, BF),
        pltpu.VMEM((length, width), BF),
        pltpu.VMEM((seqs * basis, width), BF),
        pltpu.VMEM((heads, 8, length), F32),
        pltpu.VMEM((2 * (width // heads), length), F32),
    )

    er = EarlyReduce(place, early_send, early_recv, *early)
    sem = 9 + 2 * seqs + 3

    def hook(where, i):
        def at(n, *acts):
            @pl.when(i == n)
            def _():
                for act, arg in acts:
                    act(arg)

        if where == "first":
            er.down_core(i).start()
        elif where == "entered":
            pass_on("uf")
        elif where == "ready":
            for word in ("dc2", "df"):
                pass_on(word)
        elif where == "second":
            er.up_core(i).start()
            at(0, (er.down_add_core, 0))
            at(1, (er.down_add_second, 0))
        elif where == "middle":
            at(2, (er.down_add_core, 1))
            at(3, (er.up_add_core, 2), (er.down_add_third, 0))
        elif where == "both":
            at(0, (er.up_add_core, 0))
            at(1, (er.up_add_core, 1))
        elif where == "leave":
            at(0, (er.up_add_core, 3), (er.down_add_second, 1))
            at(2, (er.up_add_second, 0), (er.up_add_second, 1))
        elif where == "end":
            er.up_add_second(2)
            er.down_add_third(1)
            er.up_add_second(3)

    wflat = wq.reshape(width, 3 * width)

    def feed_forward(*scratch):
        middle_body(
            att, hidden, gout, wo.reshape(width, width), wu.reshape(width, ff), wd.reshape(ff, width), vecs, ubias, vsum, usum,
            wflat.at[:, 0:tokens], wflat.at[:, tokens:tokens + width], *scratch, (output_h, gmid_h, gatt_h, dout_h), local, sem, er.put_down, er.put_up, hook)
        out = [pltpu.make_async_copy(er.g_u, gu_h, local.at[sem + 14])] + [
            pltpu.make_async_copy(er.g_d.at[t, p.y, :, p.x], gd_h.at[2 * t:2 * t + 2], local.at[sem + 15 + t]) for t in (0, 1)]
        for copy in out:
            copy.start()
        er.left()
        for g in (g_up, g_down, g_out):
            g.left()
        for copy in out:
            copy.wait()

    pl.run_scoped(feed_forward, *middle_scratch(tokens, width, ubias.shape[1]))


def forward_attention(
    heads, devices, place, inputs, table, st, gathers, base, store, blocks, pass_on, outs,
    lse, ublk, proj, wmat, vecs, hidden, gout, norm_t, coef_t, qkv, mem, att, wq, ubias,
    wide_s, wide_r, block, block_d, sfull, local,
    past, old, ridge, normed, coeffs, head_par, att_t,
):
    p = place
    flags, hidden_h, past_h, old_h, ridge_h, gout_h, small, qkv_s, out_s, up_s, down_s = inputs
    t_qkv, t_out, t_up, t_down = table
    g_qkv, g_up, g_down, g_out = gathers
    norm_h, coef_h, qkv_h, mem_h, wq_h = outs
    tokens, width = hidden.shape
    seqs, length = past.shape[0], past.shape[1]
    basis = ridge.shape[0]
    ff = up_s.shape[1]
    loads = []
    for i, (src, dst) in enumerate(((ridge_h, ridge), (old_h, old), (past_h, past), (hidden_h, hidden), (gout_h, gout))):
        copy = pltpu.make_async_copy(src, dst, local.at[i])
        copy.start()
        loads.append(copy)
    pos = 0
    for half in range(2):
        for ref, w in ((qkv_s, t_qkv), (out_s, t_out), (up_s, t_up)):
            wide_s[:, pos:pos + w.half] = ref[:, half * w.half:(half + 1) * w.half].astype(F32)
            pos += w.half
    nh = pos // 2
    sfull[p.y, p.z, p.x, p.c] = small[...]
    ed = down_s.shape[0]
    hd_cols = width // 2
    block_d[pl.ds(pl.multiple_of(p.c * ed, 16), ed), :] = down_s[:, pl.ds(pl.multiple_of(p.c * hd_cols, 128), hd_cols)]

    place.greet(place.others())
    mate = p.at(c=1 - p.c)
    there = pl.multiple_of((1 - p.c) * nh, 128)
    st.go("wide", wide_s.at[:, pl.ds(there, t_qkv.half)], wide_r.at[:, 0:t_qkv.half], base, mate)
    st.go("wide2", wide_s.at[:, pl.ds(pl.multiple_of(there + t_qkv.half, 128), nh - t_qkv.half)], wide_r.at[:, t_qkv.half:nh], base + 8, mate)
    ref = sfull.at[p.y, p.z, p.x, p.c]
    st.go("s0", ref, ref, base + 1, mate)
    st.go("down", down_s.at[:, pl.ds(pl.multiple_of((1 - p.c) * hd_cols, 128), hd_cols)],
          block_d.at[pl.ds(pl.multiple_of(p.c * ed, 16), ed), :], base + 2, mate)

    def make_block(c0, cn):
        mine = wide_s[:, pl.ds(pl.multiple_of(p.c * nh + c0, 128), cn)]
        other = wide_r[:, c0:c0 + cn]
        block[:, c0:c0 + cn] = jnp.concatenate(
            [jnp.where(p.c == 0, mine, other), jnp.where(p.c == 0, other, mine)], axis=0).astype(BF)

    b_qkv, b_out, b_up = blocks["q"], blocks["o"], blocks["u"]
    own = []

    def keep_own(g, src, i):
        copy = pltpu.make_async_copy(src, g.full.at[p.y, p.z, p.x, :, g.w.columns(p.c)], local.at[i])
        copy.start()
        own.append(copy)

    st.arrived("wide")
    make_block(0, t_qkv.half)
    g_qkv.start(b_qkv)
    st.arrived("s0")
    ref = sfull.at[p.y, p.z, p.x]
    for s in (1, 2, 3):
        st.go("sz", ref, ref, base + 2 + s, p.at(z=p.far_z(s)))
    st.arrived("wide2")
    make_block(t_qkv.half, nh - t_qkv.half)
    g_out.start(b_out)
    st.arrived("down")
    for i, (g, src) in enumerate(((g_qkv, b_qkv), (g_out, b_out), (g_up, b_up), (g_down, block_d))):
        keep_own(g, src, 5 + i)
    loads[0].wait()
    loads[1].wait()
    loads[2].wait()
    def small_step(i):
        if i == 0:
            st.arrived("sz")
            ref = sfull.at[p.y, :, p.x]
            st.go("sx", ref, ref, base + 6, p.at(x=1 - p.x))
        elif i == 1:
            st.arrived("sx")
            ref = sfull.at[p.y]
            st.go("sy", ref, ref, base + 7, p.at(y=1 - p.y))
        else:
            st.arrived("sy")
            unpack_small(sfull, wmat, vecs, ubias, devices, width, ff)

    def own_in_place():
        for copy in own:
            copy.wait()

    def perform(word):
        if word == "own":
            own_in_place()
        elif word[0] == "#":
            forward_coeffs(int(word[1]), flags, past, old, ridge, coeffs, coef_t)
        elif word[0] == "+":
            small_step(int(word[1]))
        else:
            pass_on(word)

    for word in FIRST_STEPS:
        perform(word)
    loads[3].wait()
    g_qkv.finish()
    wflat = wq.reshape(width, 3 * width)
    store(wq, wq_h)
    store(coef_t, coef_h)

    def project(s, half):
        forward_projections(s, half, heads, length, basis, hidden, vecs, wmat, wflat, normed, norm_t, coeffs, qkv, mem, ublk, proj, head_par)

    def attend(s, a, b):
        forward_heads(s, a, b, heads, length, basis, width, qkv, mem, att, lse, head_par, att_t)

    events = iter(LATER_STEPS)

    def step(count=1):
        for _ in range(count):
            for word in next(events, ()):
                perform(word)

    pairs = heads // 2
    for s in range(seqs):
        project(s, 0)
        step()
        project(s, 1)
        store(qkv, qkv_h, slice(s * length, (s + 1) * length))
        store(mem, mem_h, slice(s * basis, (s + 1) * basis))
        if s == seqs - 1:
            store(norm_t, norm_h)
        step()
        for a in range(pairs):
            attend(s, a, a + 1)
            step()
    step(99)
    g_out.finish()
    loads[4].wait()
    st.left()
    g_qkv.left()


def forward_call(heads, devices, flags, hidden, past, old, ridge, gout, small, qkv_s, out_s, up_s, down_s):
    seqs, length, width = hidden.shape
    basis = ridge.shape[0]
    tokens = seqs * length
    ff = up_s.shape[1]
    chip = 2 * width // devices
    chip_ff = 2 * ff // devices
    vm = pl.BlockSpec(memory_space=pltpu.VMEM)
    anyw = pl.BlockSpec(memory_space=pl.ANY)
    full = (2, 4, 2, chip, 3 * width)
    n = width // 2
    far = [
        ((width, tokens), BF), ((width, seqs * basis), BF), ((tokens, 3 * width), BF), ((seqs * basis, 2 * width), BF),
        ((tokens, width), BF), ((tokens, width), F32), ((tokens, width), BF),
        ((width, width), BF), ((2, 2, 4, 2, chip, 2 * n), BF), ((4, chip_ff, n), BF), (full, BF)]
    near = [
        ((seqs, heads, 1, length), F32), ((seqs, 32, width), F32), ((seqs, 32, length), F32),
        ((basis, 128), BF), ((8, width), F32), ((8, width), F32), ((8, width), F32)]
    nh = (4 * width + ff) // 2
    slots = 4 * Gather.SLOTS + 9
    return pl.pallas_call(
        lambda *refs: forward_kernel(heads, devices, *refs),
        out_shape=tuple(jax.ShapeDtypeStruct(*m) for m in far + near),
        in_specs=[pl.BlockSpec(memory_space=pltpu.SMEM)] + [anyw] * 5 + [vm] * 5,
        out_specs=[anyw] * len(far) + [vm] * len(near),
        scratch_shapes=[
            pltpu.VMEM((tokens, width), BF),
            pltpu.VMEM((tokens, width), BF),
            pltpu.VMEM((tokens, width), BF),
            pltpu.VMEM(full, BF),
            pltpu.VMEM((2, 4, 2, chip, width), BF),
            pltpu.VMEM((2, 4, 2, chip, ff), BF),
            pltpu.VMEM((2, 4, 2, chip_ff, width), BF),
            pltpu.VMEM((8, width), F32),
            pltpu.VMEM((width // devices, 2 * nh), F32),
            pltpu.VMEM((width // devices, nh), F32),
            pltpu.VMEM((chip, nh), BF),
            pltpu.VMEM((chip_ff, width // 2), BF),
            pltpu.VMEM((2, 4, 2, 2, 32, 128), BF),
            [pltpu.VMEM(shape, BF) for shape in (
                (2, 2, 2, 2, chip_ff, n), (2, 2, 4, 2, chip, 2 * n), (2, 2, 2, chip_ff, n), (2, 2, 4, 2, chip, n),
                (2, 2, 2, 2, chip_ff, n), (4, 2, 4, 2, chip, n),
                (2, 2, 2, 2, chip_ff // 2, n), (2, 4, 2, chip, n), (2, 2, 4, chip, n), (2, 2, 2, chip_ff // 2, n))],
            pltpu.SemaphoreType.DMA((slots,)),
            pltpu.SemaphoreType.DMA((slots,)),
            pltpu.SemaphoreType.DMA((9 + 2 * seqs + 3 + 17,)),
            pltpu.SemaphoreType.DMA((EarlyReduce.SLOTS,)),
            pltpu.SemaphoreType.DMA((EarlyReduce.SLOTS,)),
        ],
        compiler_params=pltpu.CompilerParams(vmem_limit_bytes=61 * 1024 * 1024, collective_id=0, has_side_effects=True),
        name="forward",
    )(flags, hidden.reshape(tokens, width), past, old, ridge, gout.reshape(tokens, width), small, qkv_s, out_s, up_s, down_s)


def forward_plain_call(heads, flags, hidden, past, old, ridge, wmat, vecs, wqkv):
    seqs, length, width = hidden.shape
    basis = ridge.shape[0]
    tokens = seqs * length
    vm = pl.BlockSpec(memory_space=pltpu.VMEM)

    def kernel(
        flags, hidden, past, old, ridge, wmat, vecs, wqkv,
        norm_t, coef_t, qkv, mem, att, lse, ublk, proj, normed, coeffs, head_par, att_t,
    ):
        for s in range(seqs):
            forward_coeffs(s, flags, past, old, ridge, coeffs, coef_t)
            for half in (0, 1):
                forward_projections(s, half, heads, length, basis, hidden, vecs, wmat, wqkv, normed, norm_t, coeffs, qkv, mem, ublk, proj, head_par)
            forward_heads(s, 0, heads // 2, heads, length, basis, width, qkv, mem, att, lse, head_par, att_t)

    shapes = (
        jax.ShapeDtypeStruct((width, tokens), BF),
        jax.ShapeDtypeStruct((width, seqs * basis), BF),
        jax.ShapeDtypeStruct((tokens, 3 * width), BF),
        jax.ShapeDtypeStruct((seqs * basis, 2 * width), BF),
        jax.ShapeDtypeStruct((tokens, width), BF),
        jax.ShapeDtypeStruct((seqs, heads, 1, length), F32),
        jax.ShapeDtypeStruct((seqs, 32, width), F32),
        jax.ShapeDtypeStruct((seqs, 32, length), F32),
    )
    return pl.pallas_call(
        kernel,
        out_shape=shapes,
        in_specs=[pl.BlockSpec(memory_space=pltpu.SMEM)] + [vm] * 7,
        out_specs=[vm] * 8,
        scratch_shapes=[
            pltpu.VMEM((length, width), BF),
            pltpu.VMEM((seqs * basis, width), BF),
            pltpu.VMEM((heads, 8, length), F32),
            pltpu.VMEM((2 * (width // heads), length), F32),
        ],
        compiler_params=pltpu.CompilerParams(vmem_limit_bytes=VMEM_BYTES),
        name="forward_plain",
    )(flags, hidden.reshape(tokens, width), past, old, ridge, wmat, vecs, wqkv)


def backward_heads(s, p, first, heads, length, basis, width, qkv, mem, gatt, lse, head_par, grows, dq_t, gqkv, gmem):
    hd = width // heads
    half = length // 2
    rows = slice(s * length, (s + 1) * length)
    brows = slice(s * basis, (s + 1) * basis)
    masks = head_masks(2 * hd, hd)
    scale = LOG2E / math.sqrt(hd)
    c0 = pl.multiple_of(p * (2 * hd), 2 * hd)
    c1 = pl.multiple_of(width + c0, 2 * hd)
    c2 = pl.multiple_of(2 * width + c0, 2 * hd)
    here = pl.multiple_of((p - first) * (2 * hd), 2 * hd)
    wide = gmem.shape[1] // 2
    q = qkv[rows, pl.ds(c0, 2 * hd)]
    k = qkv[rows, pl.ds(c1, 2 * hd)]
    v = qkv[rows, pl.ds(c2, 2 * hd)]
    mv = mem[brows, pl.ds(c1, 2 * hd)]
    ga = gatt[rows, pl.ds(c0, 2 * hd)]
    k_t = k.T
    cent = ((iota((basis, 1), 0).astype(F32) + 0.5) / basis)
    dv = [0.0, 0.0]
    dk = [0.0, 0.0]
    dmv = 0.0
    for h in range(2):
        head = p * 2 + h
        km, vm, mvm, gam, qm = (a * masks[h] for a in (k, v, mv, ga, q))
        lanes = slice(h * hd, (h + 1) * hd)
        for b in range(2):
            cols = slice(b * half, (b + 1) * half)
            depth = (b + 1) * half
            sc = dot_nt(km[:depth], q[cols]) * scale
            pr = jnp.exp2(sc - lse[s, head, :, cols])
            allowed = iota((depth, half), 0) <= iota((depth, half), 1) + b * half
            pr = jnp.where(allowed, pr, 0.0)
            dp = dot_nt(vm[:depth], ga[cols])
            inner = jnp.sum(pr * dp, axis=0, keepdims=True)
            ds = (pr * (dp - inner)).astype(BF)
            pb = pr.astype(BF)
            dvb = dot_nn(pb, gam[cols])
            dkb = dot_nn(ds, qm[cols])
            dq_t[pl.ds(pl.multiple_of(here + h * hd, hd), hd), cols] = dot_nn(k_t[lanes, :depth], ds)
            for i in range(b + 1):
                part = slice(i * half, (i + 1) * half)
                dv[i] = dv[i] + dvb[part]
                dk[i] = dk[i] + dkb[part]
            t = cent * head_par[head, 0:1, cols] - head_par[head, 1:2, cols]
            bas = jnp.exp2(head_par[head, 2:3, cols] - t * t)
            e = dot_nt(mvm, ga[cols]) * bas
            et = e * t
            grows[0, pl.ds(head, 1), cols] = jnp.sum(e, axis=0, keepdims=True)
            grows[1, pl.ds(head, 1), cols] = jnp.sum(et, axis=0, keepdims=True)
            grows[2, pl.ds(head, 1), cols] = jnp.sum(et * t, axis=0, keepdims=True)
            dmv = dmv + dot_nn(bas.astype(BF), gam[cols])
    for i in range(2):
        out_rows = slice(s * length + i * half, s * length + (i + 1) * half)
        gqkv[out_rows, pl.ds(c1, 2 * hd)] = (dk[i] * (1.0 / math.sqrt(hd))).astype(BF)
        gqkv[out_rows, pl.ds(c2, 2 * hd)] = dv[i].astype(BF)
    gmem[brows, pl.ds(pl.multiple_of(wide + here, 2 * hd), 2 * hd)] = dmv.astype(BF)


def backward_finish(s, start, heads, rows_of, qkv, mem, ublk, grows, dq_t, wmat, gqkv, gmem, msum):
    centre, wide, variance, root = rows_of
    n, length = dq_t.shape
    width = ublk.shape[2]
    basis = wmat.shape[0]
    hd = width // heads
    rows = slice(s * length, (s + 1) * length)
    brows = slice(s * basis, (s + 1) * basis)
    cols = slice(start, start + n)
    inv_var = 1.0 / variance
    s0, s1, s2 = grows[0], grows[1], grows[2]
    to_centre = s1 * (inv_var / root) * centre * (1.0 - centre)
    wide_slope = 0.02 / (1.0 + jnp.exp(-wide))
    to_wide = (-0.5 * s0 * inv_var + s2 * (0.5 * inv_var * inv_var) / (root * root)) * wide_slope
    head = iota((16, length), 0)
    live = (head >= start // hd) & (head < (start + n) // hd)
    g = jnp.concatenate([jnp.where(live, to_centre, 0.0), jnp.where(live, to_wide, 0.0)], axis=0)
    g_hi, g_lo = split_high_low(g)
    u_hi, u_lo = split_high_low(ublk[s, :, cols])
    dqm = dot_tn(u_hi, g_hi) + dot_tn(u_hi, g_lo) + dot_tn(u_lo, g_hi)
    total = dq_t[...] * (1.0 / math.sqrt(hd)) + dqm
    gqkv[rows, cols] = total.T.astype(BF)
    q = qkv[rows, cols]
    own = (iota((32, n), 0) % 16) == (iota((32, n), 1) + start) // hd
    r = dot_nn(g_hi, q) + dot_nn(g_lo, q)
    r = jnp.where(own, r, 0.0) * (1.0 / math.sqrt(hd))
    r_hi, r_lo = split_high_low(r)
    w = wmat[...][:, 0:32]
    gmem[brows, 0:n] = (dot_nn(w, r_hi) + dot_nn(w, r_lo)).astype(BF)
    mk = mem[brows, cols]
    add = dot_nt(r_hi, mk) + dot_nt(r_lo, mk)
    if msum.shape[0] == 32:
        msum[...] += add
    else:
        some, at = n // hd, start // hd
        msum[...] += jnp.concatenate([add[at:at + some], add[16 + at:16 + at + some]], axis=0)


def backward_input(r, width, hid, gm, gqkv, wqkv, vecs, gin, vsum):
    g = dot_nt(gqkv[r, :], wqkv[...])
    unit, inv = norm_parts(hid.astype(F32))
    gin[...] = (gm + norm_back(g, unit, inv, vecs[0:1, :])).astype(BF)
    vsum[0:1, :] += jnp.sum(g * unit, axis=0, keepdims=True)
    vsum[1:2, :] += jnp.sum(g, axis=0, keepdims=True)


def bias_sums(width, gqkv, out):
    out[0:1, :] = jnp.sum(gqkv[:, 0:width].astype(F32), axis=0, keepdims=True)
    out[1:2, :] = jnp.sum(gqkv[:, 2 * width:3 * width].astype(F32), axis=0, keepdims=True)


def backward_plain_call(heads, hidden, norm_t, coef_t, qkv, mem, gatt, gmid, lse, ublk, proj, wmat, vecs, wqkv):
    seqs, length, width = hidden.shape
    tokens = seqs * length
    brows = coef_t.shape[1]
    basis = brows // seqs
    vm = pl.BlockSpec(memory_space=pltpu.VMEM)

    def kernel(
        hidden, norm_t, coef_t, qkv, mem, gatt, gmid, lse, ublk, proj, wmat, vecs, wqkv,
        gin, dqkv, vsum, msum, gqkv, gmem, head_par, grows, dq_t,
    ):
        vsum[...] = jnp.zeros_like(vsum)
        msum[...] = jnp.zeros_like(msum)
        grows[...] = jnp.zeros_like(grows)
        for s in range(seqs):
            rows_of = basis_rows(proj[s], heads, basis, head_par)

            def pair(p, _):
                backward_heads(s, p, 0, heads, length, basis, width, qkv, mem, gatt, lse, head_par, grows, dq_t, gqkv, gmem)
                return 0

            lax.fori_loop(0, heads // 2, pair, 0)
            backward_finish(s, 0, heads, rows_of, qkv, mem, ublk, grows, dq_t, wmat, gqkv, gmem, msum)
        step = width // 3
        for j in range(9):
            c = slice(j * step, (j + 1) * step)
            y = dot_nn(norm_t[...], gqkv[:, c])
            if j >= 3:
                y = y + dot_nn(coef_t[...], gmem[:, (j - 3) * step:(j - 2) * step])
            dqkv[:, c] = y.astype(BF)

        def last(i, _):
            r = pl.ds(pl.multiple_of(i * 256, 256), 256)
            backward_input(r, width, hidden[r, :], gmid[r, :], gqkv, wqkv, vecs, gin.at[r, :], vsum.at[2:4, :])
            return 0

        lax.fori_loop(0, tokens // 256, last, 0)
        bias_sums(width, gqkv, vsum)

    shapes = (
        jax.ShapeDtypeStruct((tokens, width), BF),
        jax.ShapeDtypeStruct((width, 3 * width), BF),
        jax.ShapeDtypeStruct((8, width), F32),
        jax.ShapeDtypeStruct((32, basis), F32),
    )
    return pl.pallas_call(
        kernel,
        out_shape=shapes,
        in_specs=[vm] * 13,
        out_specs=[vm] * 4,
        scratch_shapes=[
            pltpu.VMEM((tokens, 3 * width), BF),
            pltpu.VMEM((brows, 2 * width), BF),
            pltpu.VMEM((heads, 8, length), F32),
            pltpu.VMEM((3, 16, length), F32),
            pltpu.VMEM((width, length), F32),
        ],
        compiler_params=pltpu.CompilerParams(vmem_limit_bytes=VMEM_BYTES),
        name="backward_plain",
    )(hidden.reshape(tokens, width), norm_t, coef_t, qkv, mem, gatt, gmid, lse, ublk, proj, wmat, vecs, wqkv)


class Reduce:
    SLOTS = 13

    def __init__(self, place, started, name, base, parts, bufs):
        self.p, self.s, self.name, self.base, self.parts = place, started, name, base, parts
        self.g, self.r1, self.r2, self.r3, self.r4, self.f = bufs

    def where(self, part):
        r0, rn, c0, cn = self.parts[part]
        return pl.ds(r0, rn), pl.ds(c0, cn)

    def core(self, *pieces):
        for i, (src, rows) in enumerate(pieces):
            self.s.go((self.name, 1), src, self.r1.at[:, :, :, rows, :], self.base + i, self.p.at(c=1 - self.p.c))

    def second(self):
        p = self.p
        self.s.arrived((self.name, 1))

        def step(i, _):
            at = (i // 8, (i // 2) % 4, i % 2)
            self.g[at] = self.g[at] + self.r1[at]
            return 0

        lax.fori_loop(0, 16, step, 0)
        for part in (0, 1):
            r, c = self.where(part)
            if part == 0:
                self.s.go((self.name, 2), self.g.at[1 - p.y, :, :, r, c], self.r2[0], self.base + 2, p.at(y=1 - p.y))
            else:
                self.s.go((self.name, 2), self.g.at[:, :, 1 - p.x, r, c], self.r2[1], self.base + 3, p.at(x=1 - p.x))

    def third(self):
        p = self.p
        self.s.arrived((self.name, 2))
        r, c = self.where(0)
        r_b, c_b = self.where(1)

        def step(i, _):
            z, k = i // 2, i % 2
            self.g[p.y, z, k, r, c] = self.g[p.y, z, k, r, c] + self.r2[0][z, k]
            self.g[k, z, p.x, r_b, c_b] = self.g[k, z, p.x, r_b, c_b] + self.r2[1][k, z]
            return 0

        lax.fori_loop(0, 8, step, 0)
        for part in (0, 1):
            self.send_third(part)

    def send_third(self, part):
        p = self.p
        r, c = self.where(part)
        if part == 0:
            self.s.go((self.name, 3), self.g.at[p.y, :, 1 - p.x, r, c], self.r3[0], self.base + 4, p.at(x=1 - p.x))
        else:
            self.s.go((self.name, 3), self.g.at[1 - p.y, :, p.x, r, c], self.r3[1], self.base + 5, p.at(y=1 - p.y))

    def along(self):
        p = self.p
        self.s.arrived((self.name, 3))

        def step(z, _):
            for part in self.parts:
                r, c = self.where(part)
                self.g[p.y, z, p.x, r, c] = self.g[p.y, z, p.x, r, c] + self.r3[part][z]
            return 0

        lax.fori_loop(0, 4, step, 0)
        self.send_along()

    def summand(self, z):
        p = self.p
        return self.g.at[z] if len(self.g.shape) == 3 else self.g.at[p.y, z, p.x]

    def send_along(self):
        p = self.p
        for s in (1, 2, 3):
            to = p.far_z(s)
            self.s.go((self.name, 4), self.summand(to), self.r4.at[s - 1], self.base + 5 + s, p.at(z=to))

    def last(self, out, segments):
        p = self.p
        self.s.arrived((self.name, 4))
        own = self.summand(p.z)[...].astype(F32)
        self.f[...] = (own + self.r4[0].astype(F32)) + (self.r4[1].astype(F32) + self.r4[2].astype(F32))
        n = self.f.shape[0] // 2
        theirs = pl.ds(pl.multiple_of((1 - p.c) * n, 8), n)
        mine = pl.ds(pl.multiple_of(p.c * n, 8), n)
        for i, (c0, to, cn) in enumerate(segments):
            there = out.at[:, pl.ds(pl.multiple_of(to, 128), cn)]
            self.s.go((self.name, 5), self.f.at[theirs, pl.ds(c0, cn)], there, self.base + 9 + i, p.at(c=1 - p.c))
            there[...] = self.f[mine, c0:c0 + cn]

    def done(self):
        self.s.arrived((self.name, 5))


class Everywhere:
    SLOTS = 10

    def __init__(self, place, started, name, slot, held, got):
        self.p, self.s, self.name, self.slot, self.held, self.got = place, started, name, slot, held, got

    def start(self, step):
        p = self.p
        if step == 0:
            for d in range(1, 8):
                to = p.at(y=(p.y + d // 4) % 2, x=(p.x + d // 2) % 2, c=(p.c + d) % 2)
                self.s.go((self.name, 0), self.held.at[0], self.got.at[d - 1], self.slot + d - 1, to)
        else:
            for s in (1, 2, 3):
                self.s.go((self.name, 1), self.held.at[1], self.got.at[6 + s], self.slot + 6 + s, p.at(z=p.far_z(s)))

    def add(self, step):
        self.s.arrived((self.name, step))
        first = 0 if step == 0 else 7
        total = self.held[step]
        for i in range(first, 7 if step == 0 else 10):
            total = total + self.got[i]
        if step == 0:
            self.held[1] = total
        return total


BACK_STEPS = (
    (), (), ("a3", "b3", "o1"), ("e0",),
    ("u0", "o2"), ("p1", "d4"), ("e1", "p2"), ("u1", "o3", "a4"),
    ("q1",), ("p3", "b4", "v0"), ("q2",), ("p4", "o4"),
    ("r1", "v1"), ("k0", "w0", "q3"), (), ("r2", "w1", "k1"),
    ("l0",), ("r3",), ("l1",), ("q4",), ("r4",),
)


def backward_kernel(
    heads, devices,
    hidden, norm_h, coef_h, qkv_h, mem_h, gatt_h, gmid, lse, ublk, proj, wmat, vecs, vsum_a, usum, wq_h, p_out, gu_h, gd_h,
    gin, o_qkv, o_out, o_up, o_down, early, late, msum,
    norm_t, coef_t, qkv, mem, gatt, wq,
    gqkv, gmem, head_par, grows, dq_t, away, gm_buf, hid_buf, gin_buf,
    bufs, vsum, e_held, e_got, l_held, l_got, k_held, k_got, m_held, m_got, send, recv, local,
):
    place = Place()
    p = place
    tokens, width = hidden.shape
    seqs, _, length = proj.shape
    basis = wmat.shape[0]
    ff = o_up.shape[1]
    st = Started(send, recv)
    names = "abdopqr"
    red = {n: Reduce(place, st, n, i * Reduce.SLOTS, parts, bufs[i]) for i, (n, (_, _, parts)) in enumerate(zip(names, reduce_shapes(width, ff, devices)))}
    base = len(names) * Reduce.SLOTS
    sums = {"e": Everywhere(place, st, "e", base, e_held, e_got), "l": Everywhere(place, st, "l", base + Everywhere.SLOTS, l_held, l_got)}
    sums["k"] = Everywhere(place, st, "k", base + 5 * Everywhere.SLOTS, k_held, k_got)
    for i, n in enumerate("uvw"):
        sums[n] = Everywhere(place, st, n, base + (2 + i) * Everywhere.SLOTS, m_held.at[i], m_got.at[i])
    loads = []
    for i, (src, dst) in enumerate(((qkv_h, qkv), (mem_h, mem), (gatt_h, gatt), (norm_h, norm_t), (coef_h, coef_t), (wq_h, wq))):
        copy = pltpu.make_async_copy(src, dst, local.at[i])
        copy.start()
        loads.append(copy)
    grows[...] = jnp.zeros_like(grows)
    vsum[...] = jnp.zeros_like(vsum)
    e_held[0] = jnp.concatenate([vsum_a[...], usum[...]], axis=0)
    half = width // 2

    def side(c):
        return p_out.at[:, :, :, :, pl.ds(pl.multiple_of(c * half, 128), half)]

    own = [pltpu.make_async_copy(src, red[n].g, local.at[6 + i])
           for i, (n, src) in enumerate((("a", gu_h.at[0]), ("b", gu_h.at[1]), ("d", gd_h), ("o", side(p.c))))]
    for copy in own:
        copy.start()
    place.greet(place.layer())
    red["o"].core((side(1 - p.c), slice(None)))
    sums["e"].start(0)
    for copy in own:
        copy.wait()
    red["d"].send_along()
    red["a"].send_third(0)
    red["b"].send_third(1)
    pieces = 128
    outs = {
        "a": (o_up, lambda: [(k * half, k * width + p.c * half, half) for k in (0, 1)]),
        "b": (o_up, lambda: [(k * half, (2 + k) * width + p.c * half, half) for k in (0, 1)]),
        "d": (o_down, lambda: [(0, p.c * half, half)]),
        "o": (o_out, lambda: [(0, p.c * half, half)]),
    }
    for i, n in enumerate("pqr"):
        outs[n] = (o_qkv, lambda i=i: [(j * pieces, j * width + i * 2 * pieces + p.c * pieces, pieces) for j in range(3)])

    def perform(word):
        if word[0] in sums:
            total, step = sums[word[0]], int(word[1])
            value = total.add(step)
            if step == 0:
                total.start(1)
            else:
                if word[0] in "uvw":
                    n = value.shape[0]
                    msum["uvw".index(word[0]) * n:("uvw".index(word[0]) + 1) * n, :] = value
                else:
                    {"e": early, "l": late.at[0:2, :], "k": late.at[2:4, :]}[word[0]][...] = value
        else:
            r, step = red[word[0]], word[1]
            if step == "1":
                r.second()
            elif step == "2":
                r.third()
            elif step == "3":
                r.along()
            else:
                out, segments = outs[word[0]]
                r.last(out, segments())

    steps = iter(BACK_STEPS)

    def advance():
        for word in next(steps, ()):
            perform(word)

    for copy in loads[:3]:
        copy.wait()
    chunk = 2 * pieces
    m_held[...] = jnp.zeros_like(m_held)
    rows_of = [basis_rows(proj[s], heads, basis, head_par.at[s]) for s in range(seqs)]
    for i in range(3):
        for s in range(seqs):
            for k in range(2):
                def one(j, _):
                    backward_heads(s, j, 2 * i, heads, length, basis, width, qkv, mem, gatt, lse, head_par.at[s], grows, dq_t, gqkv, gmem)
                    return 0

                lax.fori_loop(2 * i + k, 2 * i + k + 1, one, 0)
                if k == 0:
                    advance()
            backward_finish(s, i * chunk, heads, rows_of[s], qkv, mem, ublk, grows, dq_t, wmat, gqkv, gmem, m_held.at[i, 0])
            if s < seqs - 1:
                advance()
        if i == 0:
            loads[3].wait()
            loads[4].wait()
        r = red["pqr"[i]]
        for j in range(3):
            c = j * width + i * chunk
            y = dot_nn(norm_t[...], gqkv[:, c:c + chunk])
            if j > 0:
                y = y + dot_nn(coef_t[...], gmem[:, (j - 1) * chunk:j * chunk])
            y = y.astype(BF).reshape(2, 4, 2, r.g.shape[3], chunk)
            low, high = y[..., :pieces], y[..., pieces:]
            keep, give = jnp.where(p.c == 0, low, high), jnp.where(p.c == 0, high, low)
            r.g[:, :, :, :, j * pieces:(j + 1) * pieces] = keep
            away[i, :, :, :, :, j * pieces:(j + 1) * pieces] = give
        r.core((away.at[i], slice(None)))
        sums["uvw"[i]].start(0)
        if i == 2:
            bias_sums(width, gqkv, k_held.at[0])
            sums["k"].start(0)
        advance()
    wflat = wq.reshape(width, 3 * width)
    loads[5].wait()
    blocks = tokens // 256

    def fetch(i):
        r = slice(i * 256, (i + 1) * 256)
        return (pltpu.make_async_copy(gmid.at[r, :], gm_buf.at[i % 2], local.at[16 + i % 2]),
                pltpu.make_async_copy(hidden.at[r, :], hid_buf.at[i % 2], local.at[18 + i % 2]))

    def emit(i):
        return pltpu.make_async_copy(gin_buf.at[i % 2], gin.at[i * 256:(i + 1) * 256, :], local.at[20 + i % 2])

    for i in (0, 1):
        for copy in fetch(i):
            copy.start()
    for i in range(blocks):
        for copy in fetch(i):
            copy.wait()
        if i >= 2:
            emit(i - 2).wait()
        backward_input(slice(i * 256, (i + 1) * 256), width, hid_buf[i % 2], gm_buf[i % 2], gqkv, wflat, vecs, gin_buf.at[i % 2], vsum)
        emit(i).start()
        if i + 2 < blocks:
            for copy in fetch(i + 2):
                copy.start()
        if i == blocks - 1:
            l_held[0] = vsum[...]
            sums["l"].start(0)
        advance()
    for _ in range(99):
        advance()
    for n in names:
        red[n].done()
    for i in (blocks - 2, blocks - 1):
        emit(i).wait()
    st.left()


def reduce_shapes(width, ff, devices):
    chip, chip_ff = 2 * width // devices, 2 * ff // devices
    h = width // 2
    more = (chip, h, {0: (0, chip, 0, 256), 1: (0, chip, 256, 128)})
    less = (chip, h, {0: (0, chip, 0, 128), 1: (0, chip, 128, 256)})
    return [(chip, width, {0: (0, chip, 0, width)}), (chip, width, {1: (0, chip, 0, width)}), (chip_ff, h, {}), more, less, more, less]


def backward_call(
    heads, devices, hidden, norm_t, coef_t, qkv, mem, gatt, gmid, lse, ublk, proj, wmat, vecs, vsum_a, usum, wq, p_out, g_up, g_down, ff,
):
    seqs, length, width = hidden.shape
    tokens = seqs * length
    brows = coef_t.shape[1]
    basis = brows // seqs
    vm = pl.BlockSpec(memory_space=pltpu.VMEM)
    anyw = pl.BlockSpec(memory_space=pl.ANY)
    shapes = (
        jax.ShapeDtypeStruct((tokens, width), BF),
        jax.ShapeDtypeStruct((width // devices, 3 * width), F32),
        jax.ShapeDtypeStruct((width // devices, width), F32),
        jax.ShapeDtypeStruct((width // devices, ff), F32),
        jax.ShapeDtypeStruct((ff // devices, width), F32),
        jax.ShapeDtypeStruct((16, width), F32),
        jax.ShapeDtypeStruct((4, width), F32),
        jax.ShapeDtypeStruct((24, basis), F32),
    )

    def buffers(i, shape):
        rows, cols, parts = shape
        none = pltpu.VMEM((8, 128), F32)
        whole = i > 2
        sizes = [parts.get(k, (0, 16, 0, 128)) for k in (0, 1)]
        (_, ra, _, ca), (_, rb, _, cb) = sizes
        return (
            pltpu.VMEM((4, rows, cols) if i == 2 else (2, 4, 2, rows, cols), BF),
            pltpu.VMEM((2, 4, 2, rows, cols), BF) if whole else none,
            (pltpu.VMEM((4, 2, ra, ca), BF), pltpu.VMEM((2, 4, rb, cb), BF)) if whole else (none, none),
            (pltpu.VMEM((4, ra, ca), BF), pltpu.VMEM((4, rb, cb), BF)),
            pltpu.VMEM((3, rows, cols), BF),
            pltpu.VMEM((rows, cols), F32),
        )

    table = reduce_shapes(width, ff, devices)
    slots = len(table) * Reduce.SLOTS + 6 * Everywhere.SLOTS
    return pl.pallas_call(
        lambda *refs: backward_kernel(heads, devices, *refs),
        out_shape=shapes,
        in_specs=[anyw] * 7 + [vm] * 7 + [anyw] * 4,
        out_specs=[anyw] + [vm] * 7,
        scratch_shapes=[pltpu.VMEM(a.shape, a.dtype) for a in (norm_t, coef_t, qkv, mem, gatt, wq)] + [
            pltpu.VMEM((tokens, 3 * width), BF),
            pltpu.VMEM((brows, 512), BF),
            pltpu.VMEM((seqs, heads, 8, length), F32),
            pltpu.VMEM((3, 16, length), F32),
            pltpu.VMEM((256, length), F32),
            pltpu.VMEM((3, 2, 4, 2, 2 * width // devices, 384), BF),
            pltpu.VMEM((2, 256, width), F32),
            pltpu.VMEM((2, 256, width), BF),
            pltpu.VMEM((2, 256, width), BF),
            [buffers(i, shape) for i, shape in enumerate(table)],
            pltpu.VMEM((2, width), F32),
            pltpu.VMEM((2, 16, width), F32),
            pltpu.VMEM((10, 16, width), F32),
            pltpu.VMEM((2, 2, width), F32),
            pltpu.VMEM((10, 2, width), F32),
            pltpu.VMEM((2, 2, width), F32),
            pltpu.VMEM((10, 2, width), F32),
            pltpu.VMEM((3, 2, 8, basis), F32),
            pltpu.VMEM((3, 10, 8, basis), F32),
            pltpu.SemaphoreType.DMA((slots,)),
            pltpu.SemaphoreType.DMA((slots,)),
            pltpu.SemaphoreType.DMA((22,)),
        ],
        compiler_params=pltpu.CompilerParams(vmem_limit_bytes=56 * 1024 * 1024, collective_id=1, has_side_effects=True),
        name="backward",
    )(hidden.reshape(tokens, width), norm_t, coef_t, qkv, mem, gatt, gmid, lse, ublk, proj, wmat, vecs, vsum_a, usum, wq, p_out, g_up, g_down)


def finish_call(heads, devices, ff, early, late, msum, whole):
    width = early.shape[1]
    basis = msum.shape[1]
    e, rows = width // devices, basis // devices
    group = 4
    vm = pl.BlockSpec(memory_space=pltpu.VMEM)
    anyw = pl.BlockSpec(memory_space=pl.ANY)
    n = len(whole)

    def kernel(*refs):
        early, late, msum = refs[:3]
        sources, results = refs[3:3 + n], refs[3 + n:3 + 2 * n]
        gain_a, shift_a, qv, out_b, gain_m, shift_m, up_b, down_b, mean, wide = refs[3 + 2 * n:-1]
        sem = refs[-1]
        copies = [pltpu.make_async_copy(a, b, sem.at[i]) for i, (a, b) in enumerate(zip(sources, results))]
        for copy in copies:
            copy.start()
        me = lax.axis_index("dp") * lax.axis_size("fsdp") + lax.axis_index("fsdp")

        def thirds(x):
            high = x.astype(BF)
            rest = x - high.astype(F32)
            middle = rest.astype(BF)
            return high, middle, (rest - middle.astype(F32)).astype(BF)

        def pick(x, start, size):
            at = (iota((x.shape[1], size), 0) == iota((x.shape[1], size), 1) + start).astype(F32).astype(BF)
            return sum(dot_nn(part, at) for part in thirds(x))

        def row_of(x, i):
            return jnp.sum(jnp.where(iota(x.shape, 0) == i, x, 0.0), axis=0, keepdims=True)

        some = pick(early[0:8, :], me * e, e)
        down_b[...], gain_m[...], shift_m[...], out_b[...] = (some[i:i + 1] for i in range(4))
        some = pick(late[...], me * e, e)
        gain_a[...], shift_a[...] = some[0:1], some[1:2]
        k = devices // 2
        qv[...] = pick(row_of(late[2:4, :], me // k), me % k * 2 * e, 2 * e)
        k = devices * width // ff
        up_b[...] = pick(row_of(early[8:16, :], me // k), me % k * (ff // devices), ff // devices)
        at = (iota((rows, basis), 1) == iota((rows, basis), 0) + me * rows).astype(F32).astype(BF)
        for out, first in ((mean, 0), (wide, group)):
            x = jnp.concatenate([msum[i + first:i + first + group, :] for i in range(0, 2 * heads, 2 * group)], axis=0)
            out[...] = sum(dot_nt(at, part) for part in thirds(x))
        for copy in copies:
            copy.wait()

    small = [(1, e), (1, e), (1, 2 * e), (1, e), (1, e), (1, e), (1, ff // devices), (1, e), (rows, heads), (rows, heads)]
    return pl.pallas_call(
        kernel,
        out_shape=[jax.ShapeDtypeStruct(a.shape, a.dtype) for a in whole] + [jax.ShapeDtypeStruct(s, F32) for s in small],
        in_specs=[vm] * 3 + [anyw] * n,
        out_specs=[anyw] * n + [vm] * len(small),
        scratch_shapes=[pltpu.SemaphoreType.DMA((n,))],
        name="finish",
    )(early, late, msum, *whole)


def gather(x):
    return lax.all_gather(x, AXES, axis=0, tiled=True)


def scatter(x):
    return lax.psum_scatter(x, AXES, scatter_dimension=0, tiled=True)


def shards_plain(
    hidden, grad_out, past_states, old_coeffs, fresh_flags, ridge_map,
    gain_attn, shift_attn, qkv_weight, qv_bias, out_weight, out_bias,
    gain_mlp, shift_mlp, up_weight, up_bias, down_weight, down_bias,
    mean_weight, width_weight,
):
    seqs, length, width = hidden.shape
    heads = mean_weight.shape[1]
    devices = lax.axis_size("dp") * lax.axis_size("fsdp")
    full_qkv, full_out, full_up, full_down = (gather(w) for w in (qkv_weight, out_weight, up_weight, down_weight))
    rows = jnp.zeros((mean_weight.shape[0], 128), BF)
    rows = rows.at[:, 0:heads].set(mean_weight).at[:, 16:16 + heads].set(width_weight)
    wmat = gather(rows)
    full_qv = gather(qv_bias)
    vecs = jnp.stack(
        [gather(gain_attn), gather(shift_attn), full_qv[:width], full_qv[width:],
         gather(out_bias), gather(gain_mlp), gather(shift_mlp), gather(down_bias)]).astype(F32)
    ubias = gather(up_bias).astype(F32).reshape(-1, width)
    ubias = jnp.concatenate([ubias, jnp.zeros((8 - ubias.shape[0], width), F32)], axis=0)

    norm_t, coef_t, qkv, mem, att, lse, ublk, proj = forward_plain_call(
        heads, fresh_flags, hidden, past_states, old_coeffs, ridge_map, wmat, vecs, full_qkv)
    output, gmid, gatt, dout, dup, ddown, vsum_a, usum = middle_call(
        att, hidden, grad_out, full_out, full_up, full_down, vecs, ubias)
    gin, dqkv, vsum_b, msum = backward_plain_call(
        heads, hidden, norm_t, coef_t, qkv, mem, gatt, gmid, lse, ublk, proj, wmat, vecs, full_qkv)

    up_sum = usum.reshape(-1)[:up_bias.shape[0] * devices]
    big = [scatter(a.astype(F32)) for a in (dqkv, dout, dup, ddown)]
    small = [
        scatter(a) for a in (
            vsum_b[2], vsum_b[3], jnp.concatenate([vsum_b[0], vsum_b[1]]), vsum_a[3], vsum_a[1], vsum_a[2],
            up_sum, vsum_a[0], msum[0:heads].T, msum[16:16 + heads].T)
    ]
    return (
        output.reshape(seqs, length, width), gin.reshape(seqs, length, width),
        small[0], small[1], big[0], small[2], big[1], small[3], small[4], small[5],
        big[2], small[6], big[3], small[7], small[8], small[9],
    )


def shards_block(
    hidden, grad_out, past_states, old_coeffs, fresh_flags, ridge_map,
    gain_attn, shift_attn, qkv_weight, qv_bias, out_weight, out_bias,
    gain_mlp, shift_mlp, up_weight, up_bias, down_weight, down_bias,
    mean_weight, width_weight,
):
    seqs, length, width = hidden.shape
    heads = mean_weight.shape[1]
    devices = 32
    ff = up_weight.shape[1]
    e = width // devices
    def put(v, row, col):
        v = v.reshape((1, -1)) if v.ndim == 1 else v
        return jnp.pad(v, ((row, 32 - row - v.shape[0]), (col, 128 - col - v.shape[1])))

    small = (
        put(mean_weight, 0, 0) + put(width_weight, 0, 16)
        + put(gain_attn, 16, 0) + put(shift_attn, 16, e) + put(out_bias, 16, 2 * e) + put(gain_mlp, 16, 3 * e)
        + put(shift_mlp, 17, 0) + put(down_bias, 17, e) + put(qv_bias, 17, 2 * e) + put(up_bias, 18, 0))

    norm_t, coef_t, qkv, mem, output, gmid, gatt, dout, g_up, g_down, wq, lse, ublk, proj, wmat, vecs, vsum_a, usum = forward_call(
        heads, devices, fresh_flags, hidden, past_states, old_coeffs, ridge_map, grad_out, small, qkv_weight, out_weight, up_weight, down_weight)
    gin, d_qkv, d_out, d_up, d_down, early, late, msum = backward_call(
        heads, devices, hidden, norm_t, coef_t, qkv, mem, gatt, gmid, lse, ublk, proj, wmat, vecs, vsum_a, usum, wq,
        dout.reshape(2, 4, 2, width // 16, width), g_up, g_down, ff)

    (output, gin, d_qkv, d_out, d_up, d_down, gain_a, shift_a, qv, out_b, gain_m, shift_m, up_b, down_b, mean, wide) = finish_call(
        heads, devices, ff, early, late, msum, (output, gin, d_qkv, d_out, d_up, d_down))
    flat = lambda v: v.reshape(v.shape[1])
    return (
        output.reshape(seqs, length, width), gin.reshape(seqs, length, width),
        flat(gain_a), flat(shift_a), d_qkv, flat(qv), d_out, flat(out_b), flat(gain_m), flat(shift_m),
        d_up, flat(up_b), d_down, flat(down_b), mean, wide,
    )


def solution(mesh):
    rows = P(AXES, None)
    cube = P(AXES, None, None)
    one = P(AXES)
    in_specs = (cube, cube, cube, cube, one, P(), one, one, rows, one, rows, one, one, one, rows, one, rows, one, rows, rows)
    out_specs = (cube, cube, one, one, rows, one, rows, one, one, one, rows, one, rows, one, rows, rows)
    body = shards_block if mesh.shape["dp"] == 2 and mesh.shape["fsdp"] == 16 else shards_plain
    return jax.shard_map(body, mesh=mesh, in_specs=in_specs, out_specs=out_specs, check_vma=False)
```

```python
import math

import jax
import jax.numpy as jnp
from jax import lax
from jax.experimental import pallas as pl
from jax.experimental.pallas import tpu as pltpu
from jax.sharding import PartitionSpec as P

EPS = 1e-05
LOG2E = 1.4426950408889634
BF = jnp.bfloat16
F32 = jnp.float32
AXES = ("dp", "fsdp")
VMEM_BYTES = 60 * 1024 * 1024


def dot_nn(a, b):
    return lax.dot_general(a, b, (((1,), (0,)), ((), ())), preferred_element_type=F32)


def dot_nt(a, b):
    return lax.dot_general(a, b, (((1,), (1,)), ((), ())), preferred_element_type=F32)


def dot_tn(a, b):
    return lax.dot_general(a, b, (((0,), (0,)), ((), ())), preferred_element_type=F32)


def split_high_low(x):
    high = x.astype(BF)
    return high, (x - high.astype(F32)).astype(BF)


def iota(shape, dim):
    return lax.broadcasted_iota(jnp.int32, shape, dim)


def head_masks(pair_lanes, head_dim):
    lane = iota((1, pair_lanes), 1)
    return [((lane // head_dim) == h).astype(F32).astype(BF) for h in range(pair_lanes // head_dim)]


def norm_parts(x):
    mean = jnp.mean(x, axis=-1, keepdims=True)
    centred = x - mean
    variance = jnp.mean(centred * centred, axis=-1, keepdims=True)
    inv = lax.rsqrt(variance + EPS)
    return centred * inv, inv


def norm_back(grad, unit, inv, gain):
    g = grad * gain
    return inv * (g - jnp.mean(g, axis=-1, keepdims=True) - unit * jnp.mean(g * unit, axis=-1, keepdims=True))


MESH = pl.DeviceIdType.MESH


class Place:
    def __init__(self):
        self.y = lax.axis_index("dp")
        f = lax.axis_index("fsdp")
        self.z, self.x, self.c = f // 4, (f // 2) % 2, f % 2

    def at(self, y=None, z=None, x=None, c=None):
        y, z, x, c = (b if a is None else a for a, b in ((y, self.y), (z, self.z), (x, self.x), (c, self.c)))
        return (y, z * 4 + x * 2 + c)

    def far_z(self, s):
        return (self.z + s) % 4

    def others(self):
        return [self.at(c=1 - self.c), self.at(x=1 - self.x), self.at(y=1 - self.y)] + [
            self.at(z=self.far_z(s)) for s in (1, 2, 3)]

    def layer(self):
        return [self.at(y=(self.y + d // 4) % 2, x=(self.x + d // 2) % 2, c=(self.c + d) % 2) for d in range(1, 8)] + [
            self.at(z=self.far_z(s)) for s in (1, 2, 3)]

    def greet(self, devices):
        barrier = pltpu.get_barrier_semaphore()
        for d in devices:
            pl.semaphore_signal(barrier, inc=1, device_id=d, device_id_type=MESH)
        pl.semaphore_wait(barrier, len(devices))


class Weight:
    def __init__(self, index, rows, half, parts):
        self.index, self.rows, self.half, self.parts = index, rows, half, parts

    def where(self, part, c=None):
        r0, rn, c0, cn = self.parts[part]
        if c is None:
            return pl.ds(r0, rn), pl.ds(c0, cn)
        return pl.ds(r0, rn), pl.ds(pl.multiple_of(c * self.half + c0, 128), cn)

    def columns(self, c):
        return pl.ds(pl.multiple_of(c * self.half, 128), self.half)


def split_columns(n):
    first = (n // 128 + 1) // 2 * 128
    return first


def weight_table(width, ff, devices):
    chip = 2 * width // devices
    chip_ff = 2 * ff // devices
    items = []
    for i, n in enumerate((3 * width, width, ff)):
        half = n // 2
        first = split_columns(half)
        items.append(Weight(i, chip, half, ((0, chip, 0, first), (0, chip, first, half - first))))
    half = width // 2
    items.append(Weight(3, chip_ff, half, ((0, chip_ff // 2, 0, half), (chip_ff // 2, chip_ff // 2, 0, half))))
    return items


def nested(conds, act):
    if not conds:
        act()
        return

    @pl.when(conds[0]())
    def _():
        nested(conds[1:], act)


class Started:
    def __init__(self, send, recv):
        self.send, self.recv, self.live = send, recv, {}

    def go(self, name, src, dst, slot, dev):
        copy = pltpu.make_async_remote_copy(
            src_ref=src, dst_ref=dst, send_sem=self.send.at[slot], recv_sem=self.recv.at[slot],
            device_id=dev, device_id_type=MESH)
        copy.start()
        self.live.setdefault(name, []).append(copy)

    def arrived(self, name):
        for copy in self.live[name]:
            copy.wait_recv()

    def left(self, name=None):
        for key in list(self.live) if name is None else [name]:
            for copy in self.live.pop(key):
                copy.wait_send()


class Gather:
    SLOTS = 2 * 23

    def __init__(self, place, send, recv, base, w, full):
        self.p, self.send, self.recv, self.base, self.w, self.full = place, send, recv, base, w, full
        self.begun = []

    def ref(self, part, y, z, x):
        if part is None:
            return self.full.at[y, z, x, :, self.w.columns(self.p.c)]
        r, c = self.w.where(part, self.p.c)
        return self.full.at[y, z, x, r, c]

    def go(self, src, dst, send, recv, dev, conds, like):
        pltpu.make_async_remote_copy(
            src_ref=src, dst_ref=dst, send_sem=self.send.at[self.base + send()], recv_sem=self.recv.at[self.base + recv],
            device_id=dev, device_id_type=MESH).start()
        self.begun.append((send, conds, like))

    def wait(self, ref, slot):
        pltpu.make_async_remote_copy(
            src_ref=ref, dst_ref=ref, send_sem=self.send.at[self.base], recv_sem=self.recv.at[self.base + slot],
            device_id=self.p.at(c=1 - self.p.c), device_id_type=MESH).wait_recv()

    def left(self):
        for send, conds, like in self.begun:
            def act():
                pltpu.make_async_remote_copy(
                    src_ref=like(), dst_ref=like(), send_sem=self.send.at[self.base + send()], recv_sem=self.recv.at[self.base],
                    device_id=self.p.at(c=1 - self.p.c), device_id_type=MESH).wait_send()

            nested(conds, act)

    def along(self, j, act):
        here = self.p.z
        for z, cond, toward in ((lambda: here - j, lambda: here >= j, 1), (lambda: here + j, lambda: here + j <= 3, -1)):
            nested((cond,), lambda: act(z, (cond,), toward))

    def pass_z(self, src, dst, z, toward, conds, like):
        p = self.p
        more = (lambda: p.z <= 2) if toward == 1 else (lambda: p.z >= 1)
        nested((more,), lambda: self.go(
            src, dst, lambda: z() + (0 if toward == 1 else 4), z(), p.at(z=p.z + toward), conds + (more,), like))

    def partner(self, part, step):
        p = self.p
        return p.at(x=1 - p.x) if (part + step) % 2 == 0 else p.at(y=1 - p.y)

    def behind(self, part):
        p = self.p
        return (p.y, 1 - p.x) if part == 0 else (1 - p.y, p.x)

    def own_z(self):
        return self.p.z

    def one(self, part):
        return self.ref(part, 0, 0, 0)

    def start(self, block):
        p = self.p
        for toward in (1, -1):
            self.pass_z(block, self.ref(None, p.y, p.z, p.x), self.own_z, toward, (), lambda: self.one(None))
        for part in (0, 1):
            self.onward(part, self.own_z, block.at[self.w.where(part)], ())

    def onward(self, part, z, src, conds):
        p = self.p
        dst = self.ref(part, p.y, z(), p.x)
        o = part * 23
        like = lambda: self.one(part)
        self.go(src, dst, lambda: o + 8 + z(), o + 8 + z(), self.partner(part, 0), conds, like)
        self.go(src, dst, lambda: o + 12 + z(), o + 12 + z(), self.partner(part, 1), conds, like)

    def on_z(self, j):
        def act(z, conds, toward):
            whole = self.ref(None, self.p.y, z(), self.p.x)
            self.wait(whole, z())
            self.pass_z(whole, whole, z, toward, conds, lambda: self.one(None))
            for part in (0, 1):
                self.onward(part, z, self.ref(part, self.p.y, z(), self.p.x), conds)

        self.along(j, act)

    def on_second(self, j):
        def act(z, conds, toward):
            for part in (0, 1):
                self.second_on(part, z, conds)

        if j == 0:
            act(self.own_z, (), 0)
        else:
            self.along(j, act)

    def second_on(self, part, z, conds):
        y, x = self.behind(part)
        ref = self.ref(part, y, z(), x)
        o = part * 23
        self.wait(ref, o + 8 + z())
        self.go(ref, ref, lambda: o + 16 + z(), o + 16 + z(), self.partner(part, 1), conds, lambda: self.one(part))

    def core(self, step):
        p = self.p
        for part in (0, 1):
            o = part * 23
            if step == 2:
                for z in range(4):
                    y, x = (1 - p.y, p.x) if part == 0 else (p.y, 1 - p.x)
                    self.wait(self.ref(part, y, z, x), o + 12 + z)
                    self.wait(self.ref(part, 1 - p.y, z, 1 - p.x), o + 16 + z)
            self.go_core(lambda part=part: self.of_step(part, step), o + 20 + step)

    def of_step(self, part, step):
        p = self.p
        if step == 0:
            y, x = p.y, p.x
        elif step == 1:
            y, x = self.behind(part)
        else:
            y, x = (1 - p.y, slice(None)) if part == 0 else (slice(None), 1 - p.x)
        return self.ref(part, y, slice(None), x)

    def go_core(self, make, slot):
        self.go(make(), make(), lambda: slot, slot, self.p.at(c=1 - self.p.c), (), make)

    def finish(self):
        p = self.p
        for part in (0, 1):
            r, c = self.w.where(part, 1 - p.c)
            for step in range(3):
                if step == 2:
                    ref = self.full.at[1 - p.y, :, :, r, c] if part == 0 else self.full.at[:, :, 1 - p.x, r, c]
                else:
                    y, x = (p.y, p.x) if step == 0 else self.behind(part)
                    ref = self.full.at[y, :, x, r, c]
                self.wait(ref, part * 23 + 20 + step)


class LateGather(Gather):
    def start(self, block):
        for part in (0, 1):
            self.onward(part, self.own_z, block.at[self.w.where(part)], ())

    def on_third(self):
        p = self.p
        for part in (0, 1):
            o = part * 23
            y, x = (1 - p.y, p.x) if part == 0 else (p.y, 1 - p.x)
            self.wait(self.ref(part, y, p.z, x), o + 12 + p.z)
            self.wait(self.ref(part, 1 - p.y, p.z, 1 - p.x), o + 16 + p.z)
        ref = self.layer(p.z)
        for toward in (1, -1):
            self.pass_z(ref, ref, self.own_z, toward, (), lambda: self.layer(0))

    def layer(self, z):
        return self.ref(None, slice(None), z, slice(None))

    def on_z(self, j):
        def act(z, conds, toward):
            ref = self.layer(z())
            self.wait(ref, z())
            self.pass_z(ref, ref, z, toward, conds, lambda: self.layer(0))

        self.along(j, act)

    def core(self):
        self.go_core(lambda: self.ref(None, slice(None), slice(None), slice(None)), 20)

    def finish(self):
        self.wait(self.full.at[:, :, :, :, self.w.columns(1 - self.p.c)], 20)


def middle_body(
    att, hidden, gout, wout, wup, wdown, vecs, ubias, vsum, usum,
    x_t, dout, mid, x, acc, gacc, act_s, slope_s, outs, local, sem, put_down, put_up, hook,
):
    output_h, gmid_h, gatt_h, dout_h = outs
    tokens, width = hidden.shape
    ff = wup.shape[1]
    block = 256
    blocks = tokens // block
    chunk = ubias.shape[1]
    chunks = ff // chunk
    out_bias, gain, shift, down_bias = (vecs[i:i + 1, :] for i in (4, 5, 6, 7))

    def enter(i, _):
        r = pl.ds(pl.multiple_of(i * block, block), block)
        m = hidden[r, :].astype(F32) + dot_nn(att[r, :], wout[...]) + out_bias
        mid[r, :] = m
        unit, _ = norm_parts(m)
        y = (unit * gain + shift).astype(BF)
        x[r, :] = y
        x_t[:, r] = y.T
        acc[r, :] = jnp.zeros((block, width), F32)
        gacc[r, :] = jnp.zeros((block, width), F32)
        hook("enter", i)
        return 0

    lax.fori_loop(0, blocks, enter, 0)
    hook("entered", 0)

    def chunk_of(i):
        return (i % 2) * 2 + i // 2

    def first(i):
        j = chunk_of(i)
        c = pl.ds(pl.multiple_of(j * chunk, chunk), chunk)
        slot = i % 2
        w_up = wup[:, c]
        bias = ubias[pl.ds(j, 1), :]
        for b in range(blocks):
            r = slice(b * block, (b + 1) * block)
            u = dot_nn(x[r, :], w_up) + bias
            u2 = u * u
            th = jnp.tanh(u * (0.7978845608028654 + 0.7978845608028654 * 0.044715 * u2))
            half_one = 0.5 + 0.5 * th
            act_s[slot, r, :] = (u * half_one).astype(BF)
            slope = half_one + (0.5 * u) * (1.0 - th * th) * (
                0.7978845608028654 + 3 * 0.7978845608028654 * 0.044715 * u2)
            slope_s[slot, r, :] = slope.astype(BF)
        for k in range(2):
            part = slice(k * chunk // 2, (k + 1) * chunk // 2)
            put_down(i, k, dot_tn(act_s[slot, :, part], gout[...]).astype(BF))
        hook("first", i)

    def second(i):
        j = chunk_of(i)
        c = pl.ds(pl.multiple_of(j * chunk, chunk), chunk)
        slot = i % 2
        w_up, w_down = wup[:, c], wdown[c, :]
        colsum = jnp.zeros((1, chunk), F32)
        for b in range(blocks):
            r = slice(b * block, (b + 1) * block)
            gu = (dot_nt(gout[r, :], w_down) * slope_s[slot, r, :].astype(F32)).astype(BF)
            colsum = colsum + jnp.sum(gu.astype(F32), axis=0, keepdims=True)
            slope_s[slot, r, :] = gu
            acc[r, :] += dot_nn(act_s[slot, r, :], w_down)
            gacc[r, :] += dot_nt(gu, w_up)
        usum[pl.ds(j, 1), :] = colsum
        hook("middle", i)
        for k in range(2):
            part = slice(k * width // 2, (k + 1) * width // 2)
            put_up(i, k, dot_nn(x_t[part, :], slope_s[slot]).astype(BF))
        hook("second", i)

    def ahead(i, _):
        first(i)
        return 0

    lax.fori_loop(0, 2, ahead, 0)
    hook("ready", 0)
    usum[...] = jnp.zeros_like(usum)

    def both(i, _):
        second(i)

        @pl.when(i + 2 < chunks)
        def _():
            first(i + 2)

        hook("both", i)
        return 0

    lax.fori_loop(0, chunks, both, 0)
    vsum[...] = jnp.zeros_like(vsum)

    def rows_out(i):
        r = pl.ds(pl.multiple_of(i * block, block), block)
        return (pltpu.make_async_copy(act_s.at[0, r, :], output_h.at[r, :], local.at[sem + 1 + 3 * i]),
                pltpu.make_async_copy(mid.at[r, :], gmid_h.at[r, :], local.at[sem + 2 + 3 * i]),
                pltpu.make_async_copy(act_s.at[1, r, :], gatt_h.at[r, :], local.at[sem + 3 + 3 * i]))

    def leave(i, _):
        r = pl.ds(pl.multiple_of(i * block, block), block)
        m = mid[r, :]
        act_s[0, r, :] = (m + acc[r, :] + down_bias).astype(BF)
        unit, inv = norm_parts(m)
        g = gacc[r, :]
        go = gout[r, :].astype(F32)
        gm = go + norm_back(g, unit, inv, gain)
        mid[r, :] = gm
        gp = gm.astype(BF)
        x[r, :] = gp
        act_s[1, r, :] = dot_nt(gp, wout[...]).astype(BF)
        for copy in rows_out(i):
            copy.start()
        vsum[0:1, :] += jnp.sum(go, axis=0, keepdims=True)
        vsum[1:2, :] += jnp.sum(g * unit, axis=0, keepdims=True)
        vsum[2:3, :] += jnp.sum(g, axis=0, keepdims=True)
        vsum[3:4, :] += jnp.sum(gp.astype(F32), axis=0, keepdims=True)
        hook("leave", i)
        return 0

    lax.fori_loop(0, blocks, leave, 0)
    for j in range(width // 256):
        c = slice(j * 256, (j + 1) * 256)
        dout[:, c] = dot_tn(att[...], x[:, c]).astype(BF)
    final = pltpu.make_async_copy(dout, dout_h, local.at[sem])
    final.start()
    hook("end", 0)
    for i in range(blocks):
        for copy in rows_out(i):
            copy.wait()
    final.wait()


def middle_scratch(tokens, width, chunk):
    return [
        pltpu.VMEM((tokens, width), F32),
        pltpu.VMEM((tokens, width), BF),
        pltpu.VMEM((tokens, width), F32),
        pltpu.VMEM((tokens, width), F32),
        pltpu.VMEM((2, tokens, chunk), BF),
        pltpu.VMEM((2, tokens, chunk), BF),
    ]


def middle_call(att, hidden, gout, wout, wup, wdown, vecs, ubias):
    tokens, width = att.shape
    ff = wup.shape[1]
    chunk = ubias.shape[1]
    vm = pl.BlockSpec(memory_space=pltpu.VMEM)
    anyw = pl.BlockSpec(memory_space=pl.ANY)
    shapes = (
        jax.ShapeDtypeStruct((tokens, width), BF),
        jax.ShapeDtypeStruct((tokens, width), F32),
        jax.ShapeDtypeStruct((tokens, width), BF),
        jax.ShapeDtypeStruct((width, width), BF),
        jax.ShapeDtypeStruct((width, ff), BF),
        jax.ShapeDtypeStruct((ff, width), BF),
        jax.ShapeDtypeStruct((8, width), F32),
        jax.ShapeDtypeStruct((8, chunk), F32),
    )

    def kernel(att, hidden, gout, wout, wup, wdown, vecs, ubias, o, gm, ga, do, du, dd, vsum, usum, *scratch):
        def place(i):
            return ((i % 2) * 2 + i // 2) * chunk

        def put_down(i, k, v):
            dd[pl.ds(pl.multiple_of(place(i) + k * chunk // 2, chunk // 2), chunk // 2), :] = v

        def put_up(i, k, v):
            du[k * width // 2:(k + 1) * width // 2, pl.ds(pl.multiple_of(place(i), chunk), chunk)] = v

        middle_body(att, hidden, gout, wout, wup, wdown, vecs, ubias, vsum, usum, *scratch[:-1], (o, gm, ga, do), scratch[-1], 0,
                    put_down, put_up, lambda where, i: None)

    return pl.pallas_call(
        kernel,
        out_shape=shapes,
        in_specs=[vm] * 8,
        out_specs=[anyw] * 4 + [vm] * 4,
        scratch_shapes=[pltpu.VMEM((width, tokens), BF), pltpu.VMEM((width, width), BF)] + middle_scratch(tokens, width, chunk) + [pltpu.SemaphoreType.DMA((1 + 3 * (tokens // 256),))],
        compiler_params=pltpu.CompilerParams(vmem_limit_bytes=58 * 1024 * 1024),
        name="middle",
    )(att, hidden.reshape(tokens, width), gout.reshape(tokens, width), wout, wup, wdown, vecs, ubias)


class EarlyReduce:
    SLOTS = 20

    def __init__(self, place, send, recv, g_d, g_u, away_d, away_u, r1_d, r1_u, r2_d, r2_y, r2_x, r3_d):
        self.p, self.send, self.recv = place, send, recv
        self.g_d, self.g_u, self.away_d, self.away_u = g_d, g_u, away_d, away_u
        self.r1_d, self.r1_u, self.r2_d, self.r2_y, self.r2_x, self.r3_d = r1_d, r1_u, r2_d, r2_y, r2_x, r3_d
        self.n = g_d.shape[-1]
        self.h = g_d.shape[-2] // 2

    def copy(self, src, dst, slot, dev):
        return pltpu.make_async_remote_copy(
            src_ref=src, dst_ref=dst, send_sem=self.send.at[slot], recv_sem=self.recv.at[slot], device_id=dev, device_id_type=MESH)

    def mate(self):
        return self.p.at(c=1 - self.p.c)

    def sides(self, v):
        low, high = v[..., :self.n], v[..., self.n:]
        return jnp.where(self.p.c == 0, low, high), jnp.where(self.p.c == 0, high, low)

    def down_core(self, i):
        return self.copy(self.away_d.at[i % 2], self.r1_d.at[i // 2, i % 2], i, self.mate())

    def put_down(self, i, k, v):
        if k == 0:
            @pl.when(i >= 2)
            def _():
                self.down_core(i - 2).wait_send()

        keep, give = self.sides(v.reshape(2, 2 * self.h, 2 * self.n))
        self.g_d[i // 2, i % 2, k] = keep
        self.away_d[i % 2, k] = give

    def down_second(self, t):
        p = self.p
        a, b = pl.ds(0, self.h), pl.ds(self.h, self.h)
        return (self.copy(self.g_d.at[t, 1 - p.y, :, :, a, :], self.r2_d.at[t, 0], 8 + 2 * t, p.at(y=1 - p.y)),
                self.copy(self.g_d.at[t, :, :, 1 - p.x, b, :], self.r2_d.at[t, 1], 9 + 2 * t, p.at(x=1 - p.x)))

    def down_third(self, t):
        p = self.p
        a, b = pl.ds(0, self.h), pl.ds(self.h, self.h)
        return (self.copy(self.g_d.at[t, p.y, :, 1 - p.x, a, :], self.r3_d.at[t, 0], 12 + 2 * t, p.at(x=1 - p.x)),
                self.copy(self.g_d.at[t, 1 - p.y, :, p.x, b, :], self.r3_d.at[t, 1], 13 + 2 * t, p.at(y=1 - p.y)))

    def down_add_core(self, t):
        for y in (0, 1):
            self.down_core(2 * t + y).wait_recv()

        def step(i, _):
            at = (t, i // 4, (i // 2) % 2, i % 2)
            self.g_d[at] = self.g_d[at] + self.r1_d[at]
            return 0

        lax.fori_loop(0, 8, step, 0)
        for copy in self.down_second(t):
            copy.start()

    def down_add_second(self, t):
        p, h = self.p, self.h
        for copy in self.down_second(t):
            copy.wait_recv()

        def step(i, _):
            u, v = i // 2, i % 2
            at, to = (t, p.y, u, v, slice(0, h)), (t, 0, u, v)
            self.g_d[at] = self.g_d[at] + self.r2_d[to]
            at, to = (t, u, v, p.x, slice(h, 2 * h)), (t, 1, u, v)
            self.g_d[at] = self.g_d[at] + self.r2_d[to]
            return 0

        lax.fori_loop(0, 4, step, 0)

    def down_add_third(self, t):
        p, h = self.p, self.h
        for copy in self.down_third(t):
            copy.wait_recv()
        for z in (0, 1):
            for part in (0, 1):
                rows = slice(part * h, (part + 1) * h)
                at = (t, p.y, z, p.x, rows)
                self.g_d[at] = self.g_d[at] + self.r3_d[t, part, z]

    def up_core(self, i):
        return self.copy(self.away_u.at[i % 2], self.r1_u.at[i], 4 + i, self.mate())

    def rows_u(self):
        return self.g_u.shape[-2]

    def put_up(self, i, k, v):
        if k == 0:
            @pl.when(i >= 2)
            def _():
                self.up_core(i - 2).wait_send()

        keep, give = self.sides(v)
        c = pl.ds(pl.multiple_of((i // 2) * self.n, 128), self.n)
        self.g_u[i % 2, k, :, :, :, c] = keep.reshape(4, 2, self.rows_u(), self.n)
        self.away_u[i % 2, k] = give.reshape(4, 2, self.rows_u(), self.n)

    def up_second(self, i):
        p = self.p
        t = i % 2
        c = pl.ds((i // 2) * self.n, self.n)
        if t == 0:
            return self.copy(self.g_u.at[0, 1 - p.y, :, :, :, c], self.r2_y.at[i // 2], 16 + i, p.at(y=1 - p.y))
        return self.copy(self.g_u.at[1, :, :, 1 - p.x, :, c], self.r2_x.at[i // 2], 16 + i, p.at(x=1 - p.x))

    def up_add_core(self, i):
        self.up_core(i).wait_recv()
        c = slice((i // 2) * self.n, (i // 2 + 1) * self.n)

        def step(b, _):
            at = (b // 8, (b // 2) % 4, b % 2)
            here = (i % 2,) + at + (slice(None), c)
            self.g_u[here] = self.g_u[here] + self.r1_u[(i,) + at]
            return 0

        lax.fori_loop(0, 16, step, 0)
        if i < 2:
            self.up_second(i).start()

    def up_add_second(self, i):
        p = self.p
        self.up_second(i).wait_recv()
        c = slice((i // 2) * self.n, (i // 2 + 1) * self.n)

        def step(b, _):
            if i % 2 == 0:
                here, got = (0, p.y, b // 2, b % 2, slice(None), c), self.r2_y[i // 2, b // 2, b % 2]
            else:
                here, got = (1, b // 4, b % 4, p.x, slice(None), c), self.r2_x[i // 2, b // 4, b % 4]
            self.g_u[here] = self.g_u[here] + got
            return 0

        lax.fori_loop(0, 8, step, 0)

    def left(self):
        for i in (2, 3):
            self.down_core(i).wait_send()
            self.up_core(i).wait_send()
        for t in (0, 1):
            for copy in self.down_second(t):
                copy.wait_send()
            self.up_second(t).wait_send()

    def resume(self):
        for copy in self.resumed():
            copy.start()

    def resumed(self):
        return [self.up_second(2), self.up_second(3), *self.down_third(0), *self.down_third(1)]


def forward_coeffs(s, flags, past, old, ridge, coeffs, coef_t):
    length, basis = past.shape[1], ridge.shape[0]
    samples = ridge.shape[1] - length
    brows = slice(s * basis, (s + 1) * basis)
    diff = (iota((samples, basis), 0) - iota((samples, basis), 1)).astype(F32)
    sampled = jnp.exp(-0.5 * diff * diff).astype(BF)
    keep = (1 - flags[s]).astype(F32)
    old_signal = (dot_nn(sampled, old[s]) * keep).astype(BF)
    co = (dot_nn(ridge[:, :samples], old_signal) + dot_nn(ridge[:, samples:], past[s])).astype(BF)
    coeffs[brows, :] = co
    coef_t[:, brows] = co.T


def forward_projections(s, half, heads, length, basis, hidden, vecs, wmat, wqkv, normed, norm_t, coeffs, qkv, mem, ublk, proj, head_par):
    width = hidden.shape[1]
    hd = width // heads
    rows = slice(s * length, (s + 1) * length)
    brows = slice(s * basis, (s + 1) * basis)
    step = width // 3
    if half == 0:
        unit, _ = norm_parts(hidden[rows, :].astype(F32))
        nrm = (unit * vecs[0:1, :] + vecs[1:2, :]).astype(BF)
        normed[...] = nrm
        norm_t[:, rows] = nrm.T
    for j in range(9) if half == 0 else ():
        cols = slice(j * step, (j + 1) * step)
        y = dot_nn(normed[...], wqkv[:, cols])
        if j < 3:
            y = y + vecs[2:3, cols]
        elif j >= 6:
            y = y + vecs[3:4, (j - 6) * step:(j - 5) * step]
        qkv[rows, cols] = y.astype(BF)
    if half == 0:
        return
    for j in range(6):
        cols = slice(j * step, (j + 1) * step)
        wcols = slice(width + j * step, width + (j + 1) * step)
        mem[brows, cols] = dot_nn(coeffs[brows, :], wqkv[:, wcols]).astype(BF)
    raw = dot_tn(wmat[...], mem[brows, 0:width])[0:32, :]
    own = (iota((32, width), 0) % 16) == (iota((32, width), 1) // hd)
    u = jnp.where(own, raw, 0.0) * (1.0 / math.sqrt(hd))
    ublk[s] = u
    u_hi, u_lo = split_high_low(u)
    q = qkv[rows, 0:width]
    pr = dot_nt(u_hi, q) + dot_nt(u_lo, q)
    proj[s] = pr
    basis_rows(pr, heads, basis, head_par)


def basis_rows(pr, heads, basis, head_par):
    centre = 1.0 / (1.0 + jnp.exp(-pr[0:16]))
    wide = pr[16:32]
    soft = jnp.maximum(wide, 0.0) + jnp.log(1.0 + jnp.exp(-jnp.abs(wide)))
    variance = (soft + 0.5) * 0.02
    inv_root = lax.rsqrt(variance)
    root = inv_root * math.sqrt(0.5 * LOG2E)
    shift_log = jnp.log(inv_root) * LOG2E - math.log2(basis)
    for h in range(heads):
        head_par[h, 0:1, :] = root[h:h + 1]
        head_par[h, 1:2, :] = centre[h:h + 1] * root[h:h + 1]
        head_par[h, 2:3, :] = shift_log[h:h + 1]
    return centre, wide, variance, root


def forward_heads(s, first, last, heads, length, basis, width, qkv, mem, att, lse, head_par, att_t):
    hd = width // heads
    half = length // 2
    rows = slice(s * length, (s + 1) * length)
    brows = slice(s * basis, (s + 1) * basis)
    masks = head_masks(2 * hd, hd)
    scale = LOG2E / math.sqrt(hd)

    def pair(p, _):
        c0 = pl.multiple_of(p * (2 * hd), 2 * hd)
        q = qkv[rows, pl.ds(c0, 2 * hd)]
        k = qkv[rows, pl.ds(pl.multiple_of(width + c0, 2 * hd), 2 * hd)]
        v_t = qkv[rows, pl.ds(pl.multiple_of(2 * width + c0, 2 * hd), 2 * hd)].T
        mv_t = mem[brows, pl.ds(pl.multiple_of(width + c0, 2 * hd), 2 * hd)].T
        cent = ((iota((basis, 1), 0).astype(F32) + 0.5) / basis)
        for h in range(2):
            head = p * 2 + h
            km = k * masks[h]
            lanes = slice(h * hd, (h + 1) * hd)
            for b in range(2):
                cols = slice(b * half, (b + 1) * half)
                depth = (b + 1) * half
                sc = dot_nt(km[:depth], q[cols]) * scale
                allowed = iota((depth, half), 0) <= iota((depth, half), 1) + b * half
                sc = jnp.where(allowed, sc, -1e30)
                top = jnp.max(sc, axis=0, keepdims=True)
                e = jnp.exp2(sc - top)
                total = jnp.sum(e, axis=0, keepdims=True)
                out = dot_nn(v_t[lanes, :depth], e.astype(BF)) / total
                lse[s, head, :, cols] = top + jnp.log(total) * LOG2E
                t = cent * head_par[head, 0:1, cols] - head_par[head, 1:2, cols]
                bas = jnp.exp2(head_par[head, 2:3, cols] - t * t).astype(BF)
                out = out + dot_nn(mv_t[lanes, :], bas)
                att_t[lanes, cols] = out
        att[rows, pl.ds(c0, 2 * hd)] = att_t[...].T.astype(BF)
        return 0

    lax.fori_loop(first, last, pair, 0)


def unpack_small(small, wmat, vecs, ubias, devices, width, ff):
    flat = small.reshape(devices * 32, 128)
    wmat[...] = small.reshape(devices, 32, 128)[:, 0:16, :].reshape(devices * 16, 128)
    every = flat[...]

    def spread(row, offset, each, n):
        pick = (iota((devices, devices * 32), 1) == iota((devices, devices * 32), 0) * 32 + row)
        mine = dot_nn(pick.astype(F32).astype(BF), every).astype(BF)
        place = iota((128, n), 0) == iota((128, n), 1) % each + offset
        wide = dot_nn(mine, place.astype(F32).astype(BF))
        own = iota((devices, n), 1) // each == iota((devices, n), 0)
        return jnp.sum(jnp.where(own, wide, 0.0), axis=0, keepdims=True)

    e = width // devices
    vecs[0:1, :] = spread(16, 0, e, width)
    vecs[1:2, :] = spread(16, e, e, width)
    both = spread(17, 2 * e, 2 * e, 2 * width)
    vecs[2:3, :] = both[:, :width]
    vecs[3:4, :] = both[:, width:]
    vecs[4:5, :] = spread(16, 2 * e, e, width)
    vecs[5:6, :] = spread(16, 3 * e, e, width)
    vecs[6:7, :] = spread(17, 0, e, width)
    vecs[7:8, :] = spread(17, e, e, width)
    up = spread(18, 0, ff // devices, ff)
    chunk = ubias.shape[1]
    ubias[...] = jnp.zeros_like(ubias)
    for j in range(ff // chunk):
        ubias[j:j + 1, :] = up[:, j * chunk:(j + 1) * chunk]


FIRST_STEPS = (
    "#0", "qz1", "qs0", "os0", "qz2", "qs1", "+0", "qz3", "ug", "own", "ot", "qc0", "#1", "qs2", "+1", "qs3", "qc1",
    "uz1", "us0", "oz1", "+2", "uz2", "us1", "oz2", "qc2",
)
LATER_STEPS = (
    ("uz3", "us2", "dg", "oz3", "oc"), ("us3", "uc0", "uc1"), ("dz1",), ("ds0",), ("dz2",), ("ds1",), ("dz3",), ("dc0",),
    (), ("ds2",), (), ("uc2",), ("ds3",), ("dc1",),
)


def forward_kernel(
    heads, devices,
    flags, hidden_h, past_h, old_h, ridge_h, gout_h, small, qkv_s, out_s, up_s, down_s,
    norm_h, coef_h, qkv_h, mem_h, output_h, gmid_h, gatt_h, dout_h, gu_h, gd_h, wq_h,
    lse, ublk, proj, wmat, vecs, vsum, usum,
    hidden, gout, att, wq, wo, wu, wd, ubias,
    wide_s, wide_r, block, block_d, sfull, early, send, recv, local, early_send, early_recv,
):
    place = Place()
    p = place
    tokens, width = hidden.shape
    seqs, length = past_h.shape[0], past_h.shape[1]
    basis = ridge_h.shape[0]
    ff = up_s.shape[1]
    t_qkv, t_out, t_up, t_down = weight_table(width, ff, devices)
    st = Started(send, recv)
    n = Gather.SLOTS
    g_qkv = Gather(place, send, recv, 0, t_qkv, wq)
    g_up = Gather(place, send, recv, n, t_up, wu)
    g_down = Gather(place, send, recv, 2 * n, t_down, wd)
    g_out = LateGather(place, send, recv, 3 * n, t_out, wo)
    base = 4 * n
    nh = wide_r.shape[1]
    blocks = {
        "q": block.at[:, 0:t_qkv.half], "o": block.at[:, t_qkv.half:t_qkv.half + t_out.half],
        "u": block.at[:, t_qkv.half + t_out.half:nh], "d": block_d}
    gather_of = {"q": g_qkv, "o": g_out, "u": g_up, "d": g_down}

    def pass_on(word):
        g, what, n = gather_of[word[0]], word[1], word[2:]
        if what == "g":
            g.start(blocks[word[0]])
        elif what == "z":
            g.on_z(int(n))
        elif what == "s":
            g.on_second(int(n))
        elif what == "t":
            g.on_third()
        elif what == "f":
            g.finish()
        elif n:
            g.core(int(n))
        else:
            g.core()

    stores = []

    def store(src, dst, rows=None):
        i = len(stores)

        def make():
            a, b = (src, dst) if rows is None else (src.at[rows, :], dst.at[rows, :])
            return pltpu.make_async_copy(a, b, local.at[9 + i])

        make().start()
        stores.append(make)

    def attention(norm_t, coef_t, qkv, mem, past, old, ridge, normed, coeffs, head_par, att_t):
        forward_attention(
            heads, devices, place, (flags, hidden_h, past_h, old_h, ridge_h, gout_h, small, qkv_s, out_s, up_s, down_s),
            (t_qkv, t_out, t_up, t_down), st, (g_qkv, g_up, g_down, g_out), base, store, blocks, pass_on,
            (norm_h, coef_h, qkv_h, mem_h, wq_h),
            lse, ublk, proj, wmat, vecs, hidden, gout, norm_t, coef_t, qkv, mem, att, wq, ubias,
            wide_s, wide_r, block, block_d, sfull, local,
            past, old, ridge, normed, coeffs, head_par, att_t)
        for make in stores:
            make().wait()

    pl.run_scoped(
        attention,
        pltpu.VMEM((width, tokens), BF),
        pltpu.VMEM((width, seqs * basis), BF),
        pltpu.VMEM((tokens, 3 * width), BF),
        pltpu.VMEM((seqs * basis, 2 * width), BF),
        pltpu.VMEM(past_h.shape, BF),
        pltpu.VMEM(old_h.shape, BF),
        pltpu.VMEM(ridge_h.shape, BF),
        pltpu.VMEM((length, width), BF),
        pltpu.VMEM((seqs * basis, width), BF),
        pltpu.VMEM((heads, 8, length), F32),
        pltpu.VMEM((2 * (width // heads), length), F32),
    )

    er = EarlyReduce(place, early_send, early_recv, *early)
    sem = 9 + 2 * seqs + 3

    def hook(where, i):
        def at(n, *acts):
            @pl.when(i == n)
            def _():
                for act, arg in acts:
                    act(arg)

        if where == "first":
            er.down_core(i).start()
        elif where == "entered":
            pass_on("uf")
        elif where == "ready":
            for word in ("dc2", "df"):
                pass_on(word)
        elif where == "second":
            er.up_core(i).start()
            at(0, (er.down_add_core, 0))
            at(2, (er.down_add_second, 0))
        elif where == "middle":
            at(2, (er.down_add_core, 1))
        elif where == "both":
            at(0, (er.up_add_core, 0))
            at(1, (er.up_add_core, 1))
        elif where == "leave":
            at(0, (er.up_add_core, 2), (er.up_add_core, 3))
            at(2, (er.up_add_second, 0), (er.up_add_second, 1))
        elif where == "end":
            er.down_add_second(1)

    wflat = wq.reshape(width, 3 * width)

    def feed_forward(*scratch):
        middle_body(
            att, hidden, gout, wo.reshape(width, width), wu.reshape(width, ff), wd.reshape(ff, width), vecs, ubias, vsum, usum,
            wflat.at[:, 0:tokens], wflat.at[:, tokens:tokens + width], *scratch, (output_h, gmid_h, gatt_h, dout_h), local, sem, er.put_down, er.put_up, hook)
        out = [pltpu.make_async_copy(er.g_u, gu_h, local.at[sem + 14]), pltpu.make_async_copy(er.g_d, gd_h, local.at[sem + 15])]
        for copy in out:
            copy.start()
        er.left()
        for g in (g_up, g_down, g_out):
            g.left()
        for copy in out:
            copy.wait()

    pl.run_scoped(feed_forward, *middle_scratch(tokens, width, ubias.shape[1]))


def forward_attention(
    heads, devices, place, inputs, table, st, gathers, base, store, blocks, pass_on, outs,
    lse, ublk, proj, wmat, vecs, hidden, gout, norm_t, coef_t, qkv, mem, att, wq, ubias,
    wide_s, wide_r, block, block_d, sfull, local,
    past, old, ridge, normed, coeffs, head_par, att_t,
):
    p = place
    flags, hidden_h, past_h, old_h, ridge_h, gout_h, small, qkv_s, out_s, up_s, down_s = inputs
    t_qkv, t_out, t_up, t_down = table
    g_qkv, g_up, g_down, g_out = gathers
    norm_h, coef_h, qkv_h, mem_h, wq_h = outs
    tokens, width = hidden.shape
    seqs, length = past.shape[0], past.shape[1]
    basis = ridge.shape[0]
    ff = up_s.shape[1]
    loads = []
    for i, (src, dst) in enumerate(((ridge_h, ridge), (old_h, old), (past_h, past), (hidden_h, hidden), (gout_h, gout))):
        copy = pltpu.make_async_copy(src, dst, local.at[i])
        copy.start()
        loads.append(copy)
    pos = 0
    for half in range(2):
        for ref, w in ((qkv_s, t_qkv), (out_s, t_out), (up_s, t_up)):
            wide_s[:, pos:pos + w.half] = ref[:, half * w.half:(half + 1) * w.half].astype(F32)
            pos += w.half
    nh = pos // 2
    sfull[p.y, p.z, p.x, p.c] = small[...]
    ed = down_s.shape[0]
    hd_cols = width // 2
    block_d[pl.ds(pl.multiple_of(p.c * ed, 16), ed), :] = down_s[:, pl.ds(pl.multiple_of(p.c * hd_cols, 128), hd_cols)]

    place.greet(place.others())
    mate = p.at(c=1 - p.c)
    there = pl.multiple_of((1 - p.c) * nh, 128)
    st.go("wide", wide_s.at[:, pl.ds(there, t_qkv.half)], wide_r.at[:, 0:t_qkv.half], base, mate)
    st.go("wide2", wide_s.at[:, pl.ds(pl.multiple_of(there + t_qkv.half, 128), nh - t_qkv.half)], wide_r.at[:, t_qkv.half:nh], base + 8, mate)
    ref = sfull.at[p.y, p.z, p.x, p.c]
    st.go("s0", ref, ref, base + 1, mate)
    st.go("down", down_s.at[:, pl.ds(pl.multiple_of((1 - p.c) * hd_cols, 128), hd_cols)],
          block_d.at[pl.ds(pl.multiple_of(p.c * ed, 16), ed), :], base + 2, mate)

    def make_block(c0, cn):
        mine = wide_s[:, pl.ds(pl.multiple_of(p.c * nh + c0, 128), cn)]
        other = wide_r[:, c0:c0 + cn]
        block[:, c0:c0 + cn] = jnp.concatenate(
            [jnp.where(p.c == 0, mine, other), jnp.where(p.c == 0, other, mine)], axis=0).astype(BF)

    b_qkv, b_out, b_up = blocks["q"], blocks["o"], blocks["u"]
    own = []

    def keep_own(g, src, i):
        copy = pltpu.make_async_copy(src, g.full.at[p.y, p.z, p.x, :, g.w.columns(p.c)], local.at[i])
        copy.start()
        own.append(copy)

    st.arrived("wide")
    make_block(0, t_qkv.half)
    g_qkv.start(b_qkv)
    st.arrived("s0")
    ref = sfull.at[p.y, p.z, p.x]
    for s in (1, 2, 3):
        st.go("sz", ref, ref, base + 2 + s, p.at(z=p.far_z(s)))
    st.arrived("wide2")
    make_block(t_qkv.half, nh - t_qkv.half)
    g_out.start(b_out)
    st.arrived("down")
    for i, (g, src) in enumerate(((g_qkv, b_qkv), (g_out, b_out), (g_up, b_up), (g_down, block_d))):
        keep_own(g, src, 5 + i)
    loads[0].wait()
    loads[1].wait()
    loads[2].wait()
    def small_step(i):
        if i == 0:
            st.arrived("sz")
            ref = sfull.at[p.y, :, p.x]
            st.go("sx", ref, ref, base + 6, p.at(x=1 - p.x))
        elif i == 1:
            st.arrived("sx")
            ref = sfull.at[p.y]
            st.go("sy", ref, ref, base + 7, p.at(y=1 - p.y))
        else:
            st.arrived("sy")
            unpack_small(sfull, wmat, vecs, ubias, devices, width, ff)

    def own_in_place():
        for copy in own:
            copy.wait()

    def perform(word):
        if word == "own":
            own_in_place()
        elif word[0] == "#":
            forward_coeffs(int(word[1]), flags, past, old, ridge, coeffs, coef_t)
        elif word[0] == "+":
            small_step(int(word[1]))
        else:
            pass_on(word)

    for word in FIRST_STEPS:
        perform(word)
    loads[3].wait()
    g_qkv.finish()
    wflat = wq.reshape(width, 3 * width)
    store(wq, wq_h)
    store(coef_t, coef_h)

    def project(s, half):
        forward_projections(s, half, heads, length, basis, hidden, vecs, wmat, wflat, normed, norm_t, coeffs, qkv, mem, ublk, proj, head_par)

    def attend(s, a, b):
        forward_heads(s, a, b, heads, length, basis, width, qkv, mem, att, lse, head_par, att_t)

    events = iter(LATER_STEPS)

    def step(count=1):
        for _ in range(count):
            for word in next(events, ()):
                perform(word)

    pairs = heads // 2
    for s in range(seqs):
        project(s, 0)
        step()
        project(s, 1)
        store(qkv, qkv_h, slice(s * length, (s + 1) * length))
        store(mem, mem_h, slice(s * basis, (s + 1) * basis))
        if s == seqs - 1:
            store(norm_t, norm_h)
        step()
        for a in range(pairs):
            attend(s, a, a + 1)
            step()
    step(99)
    g_out.finish()
    loads[4].wait()
    st.left()
    g_qkv.left()


def forward_call(heads, devices, flags, hidden, past, old, ridge, gout, small, qkv_s, out_s, up_s, down_s):
    seqs, length, width = hidden.shape
    basis = ridge.shape[0]
    tokens = seqs * length
    ff = up_s.shape[1]
    chip = 2 * width // devices
    chip_ff = 2 * ff // devices
    vm = pl.BlockSpec(memory_space=pltpu.VMEM)
    anyw = pl.BlockSpec(memory_space=pl.ANY)
    full = (2, 4, 2, chip, 3 * width)
    n = width // 2
    far = [
        ((width, tokens), BF), ((width, seqs * basis), BF), ((tokens, 3 * width), BF), ((seqs * basis, 2 * width), BF),
        ((tokens, width), BF), ((tokens, width), F32), ((tokens, width), BF),
        ((width, width), BF), ((2, 2, 4, 2, chip, 2 * n), BF), ((2, 2, 2, 2, chip_ff, n), BF), (full, BF)]
    near = [
        ((seqs, heads, 1, length), F32), ((seqs, 32, width), F32), ((seqs, 32, length), F32),
        ((basis, 128), BF), ((8, width), F32), ((8, width), F32), ((8, width), F32)]
    nh = (4 * width + ff) // 2
    slots = 4 * Gather.SLOTS + 9
    return pl.pallas_call(
        lambda *refs: forward_kernel(heads, devices, *refs),
        out_shape=tuple(jax.ShapeDtypeStruct(*m) for m in far + near),
        in_specs=[pl.BlockSpec(memory_space=pltpu.SMEM)] + [anyw] * 5 + [vm] * 5,
        out_specs=[anyw] * len(far) + [vm] * len(near),
        scratch_shapes=[
            pltpu.VMEM((tokens, width), BF),
            pltpu.VMEM((tokens, width), BF),
            pltpu.VMEM((tokens, width), BF),
            pltpu.VMEM(full, BF),
            pltpu.VMEM((2, 4, 2, chip, width), BF),
            pltpu.VMEM((2, 4, 2, chip, ff), BF),
            pltpu.VMEM((2, 4, 2, chip_ff, width), BF),
            pltpu.VMEM((8, width), F32),
            pltpu.VMEM((width // devices, 2 * nh), F32),
            pltpu.VMEM((width // devices, nh), F32),
            pltpu.VMEM((chip, nh), BF),
            pltpu.VMEM((chip_ff, width // 2), BF),
            pltpu.VMEM((2, 4, 2, 2, 32, 128), BF),
            [pltpu.VMEM(shape, BF) for shape in (
                (2, 2, 2, 2, chip_ff, n), (2, 2, 4, 2, chip, 2 * n), (2, 2, 2, chip_ff, n), (2, 2, 4, 2, chip, n),
                (2, 2, 2, 2, chip_ff, n), (4, 2, 4, 2, chip, n),
                (2, 2, 2, 2, chip_ff // 2, n), (2, 4, 2, chip, n), (2, 2, 4, chip, n), (8, 128))],
            pltpu.SemaphoreType.DMA((slots,)),
            pltpu.SemaphoreType.DMA((slots,)),
            pltpu.SemaphoreType.DMA((9 + 2 * seqs + 3 + 17,)),
            pltpu.SemaphoreType.DMA((EarlyReduce.SLOTS,)),
            pltpu.SemaphoreType.DMA((EarlyReduce.SLOTS,)),
        ],
        compiler_params=pltpu.CompilerParams(vmem_limit_bytes=61 * 1024 * 1024, collective_id=0, has_side_effects=True),
        name="forward",
    )(flags, hidden.reshape(tokens, width), past, old, ridge, gout.reshape(tokens, width), small, qkv_s, out_s, up_s, down_s)


def forward_plain_call(heads, flags, hidden, past, old, ridge, wmat, vecs, wqkv):
    seqs, length, width = hidden.shape
    basis = ridge.shape[0]
    tokens = seqs * length
    vm = pl.BlockSpec(memory_space=pltpu.VMEM)

    def kernel(
        flags, hidden, past, old, ridge, wmat, vecs, wqkv,
        norm_t, coef_t, qkv, mem, att, lse, ublk, proj, normed, coeffs, head_par, att_t,
    ):
        for s in range(seqs):
            forward_coeffs(s, flags, past, old, ridge, coeffs, coef_t)
            for half in (0, 1):
                forward_projections(s, half, heads, length, basis, hidden, vecs, wmat, wqkv, normed, norm_t, coeffs, qkv, mem, ublk, proj, head_par)
            forward_heads(s, 0, heads // 2, heads, length, basis, width, qkv, mem, att, lse, head_par, att_t)

    shapes = (
        jax.ShapeDtypeStruct((width, tokens), BF),
        jax.ShapeDtypeStruct((width, seqs * basis), BF),
        jax.ShapeDtypeStruct((tokens, 3 * width), BF),
        jax.ShapeDtypeStruct((seqs * basis, 2 * width), BF),
        jax.ShapeDtypeStruct((tokens, width), BF),
        jax.ShapeDtypeStruct((seqs, heads, 1, length), F32),
        jax.ShapeDtypeStruct((seqs, 32, width), F32),
        jax.ShapeDtypeStruct((seqs, 32, length), F32),
    )
    return pl.pallas_call(
        kernel,
        out_shape=shapes,
        in_specs=[pl.BlockSpec(memory_space=pltpu.SMEM)] + [vm] * 7,
        out_specs=[vm] * 8,
        scratch_shapes=[
            pltpu.VMEM((length, width), BF),
            pltpu.VMEM((seqs * basis, width), BF),
            pltpu.VMEM((heads, 8, length), F32),
            pltpu.VMEM((2 * (width // heads), length), F32),
        ],
        compiler_params=pltpu.CompilerParams(vmem_limit_bytes=VMEM_BYTES),
        name="forward_plain",
    )(flags, hidden.reshape(tokens, width), past, old, ridge, wmat, vecs, wqkv)


def backward_heads(s, p, first, heads, length, basis, width, qkv, mem, gatt, lse, head_par, grows, dq_t, gqkv, gmem):
    hd = width // heads
    half = length // 2
    rows = slice(s * length, (s + 1) * length)
    brows = slice(s * basis, (s + 1) * basis)
    masks = head_masks(2 * hd, hd)
    scale = LOG2E / math.sqrt(hd)
    c0 = pl.multiple_of(p * (2 * hd), 2 * hd)
    c1 = pl.multiple_of(width + c0, 2 * hd)
    c2 = pl.multiple_of(2 * width + c0, 2 * hd)
    here = pl.multiple_of((p - first) * (2 * hd), 2 * hd)
    wide = gmem.shape[1] // 2
    q = qkv[rows, pl.ds(c0, 2 * hd)]
    k = qkv[rows, pl.ds(c1, 2 * hd)]
    v = qkv[rows, pl.ds(c2, 2 * hd)]
    mv = mem[brows, pl.ds(c1, 2 * hd)]
    ga = gatt[rows, pl.ds(c0, 2 * hd)]
    k_t = k.T
    cent = ((iota((basis, 1), 0).astype(F32) + 0.5) / basis)
    dv = [0.0, 0.0]
    dk = [0.0, 0.0]
    dmv = 0.0
    for h in range(2):
        head = p * 2 + h
        km, vm, mvm, gam, qm = (a * masks[h] for a in (k, v, mv, ga, q))
        lanes = slice(h * hd, (h + 1) * hd)
        for b in range(2):
            cols = slice(b * half, (b + 1) * half)
            depth = (b + 1) * half
            sc = dot_nt(km[:depth], q[cols]) * scale
            pr = jnp.exp2(sc - lse[s, head, :, cols])
            allowed = iota((depth, half), 0) <= iota((depth, half), 1) + b * half
            pr = jnp.where(allowed, pr, 0.0)
            dp = dot_nt(vm[:depth], ga[cols])
            inner = jnp.sum(pr * dp, axis=0, keepdims=True)
            ds = (pr * (dp - inner)).astype(BF)
            pb = pr.astype(BF)
            dvb = dot_nn(pb, gam[cols])
            dkb = dot_nn(ds, qm[cols])
            dq_t[pl.ds(pl.multiple_of(here + h * hd, hd), hd), cols] = dot_nn(k_t[lanes, :depth], ds)
            for i in range(b + 1):
                part = slice(i * half, (i + 1) * half)
                dv[i] = dv[i] + dvb[part]
                dk[i] = dk[i] + dkb[part]
            t = cent * head_par[head, 0:1, cols] - head_par[head, 1:2, cols]
            bas = jnp.exp2(head_par[head, 2:3, cols] - t * t)
            e = dot_nt(mvm, ga[cols]) * bas
            et = e * t
            grows[0, pl.ds(head, 1), cols] = jnp.sum(e, axis=0, keepdims=True)
            grows[1, pl.ds(head, 1), cols] = jnp.sum(et, axis=0, keepdims=True)
            grows[2, pl.ds(head, 1), cols] = jnp.sum(et * t, axis=0, keepdims=True)
            dmv = dmv + dot_nn(bas.astype(BF), gam[cols])
    for i in range(2):
        out_rows = slice(s * length + i * half, s * length + (i + 1) * half)
        gqkv[out_rows, pl.ds(c1, 2 * hd)] = (dk[i] * (1.0 / math.sqrt(hd))).astype(BF)
        gqkv[out_rows, pl.ds(c2, 2 * hd)] = dv[i].astype(BF)
    gmem[brows, pl.ds(pl.multiple_of(wide + here, 2 * hd), 2 * hd)] = dmv.astype(BF)


def backward_finish(s, start, heads, rows_of, qkv, mem, ublk, grows, dq_t, wmat, gqkv, gmem, msum):
    centre, wide, variance, root = rows_of
    n, length = dq_t.shape
    width = ublk.shape[2]
    basis = wmat.shape[0]
    hd = width // heads
    rows = slice(s * length, (s + 1) * length)
    brows = slice(s * basis, (s + 1) * basis)
    cols = slice(start, start + n)
    inv_var = 1.0 / variance
    s0, s1, s2 = grows[0], grows[1], grows[2]
    to_centre = s1 * (inv_var / root) * centre * (1.0 - centre)
    wide_slope = 0.02 / (1.0 + jnp.exp(-wide))
    to_wide = (-0.5 * s0 * inv_var + s2 * (0.5 * inv_var * inv_var) / (root * root)) * wide_slope
    head = iota((16, length), 0)
    live = (head >= start // hd) & (head < (start + n) // hd)
    g = jnp.concatenate([jnp.where(live, to_centre, 0.0), jnp.where(live, to_wide, 0.0)], axis=0)
    g_hi, g_lo = split_high_low(g)
    u_hi, u_lo = split_high_low(ublk[s, :, cols])
    dqm = dot_tn(u_hi, g_hi) + dot_tn(u_hi, g_lo) + dot_tn(u_lo, g_hi)
    total = dq_t[...] * (1.0 / math.sqrt(hd)) + dqm
    gqkv[rows, cols] = total.T.astype(BF)
    q = qkv[rows, cols]
    own = (iota((32, n), 0) % 16) == (iota((32, n), 1) + start) // hd
    r = dot_nn(g_hi, q) + dot_nn(g_lo, q)
    r = jnp.where(own, r, 0.0) * (1.0 / math.sqrt(hd))
    r_hi, r_lo = split_high_low(r)
    w = wmat[...][:, 0:32]
    gmem[brows, 0:n] = (dot_nn(w, r_hi) + dot_nn(w, r_lo)).astype(BF)
    mk = mem[brows, cols]
    add = dot_nt(r_hi, mk) + dot_nt(r_lo, mk)
    if msum.shape[0] == 32:
        msum[...] += add
    else:
        some, at = n // hd, start // hd
        msum[...] += jnp.concatenate([add[at:at + some], add[16 + at:16 + at + some]], axis=0)


def backward_input(r, width, hid, gm, gqkv, wqkv, vecs, gin, vsum):
    g = dot_nt(gqkv[r, :], wqkv[...])
    unit, inv = norm_parts(hid.astype(F32))
    gin[...] = (gm + norm_back(g, unit, inv, vecs[0:1, :])).astype(BF)
    vsum[0:1, :] += jnp.sum(g * unit, axis=0, keepdims=True)
    vsum[1:2, :] += jnp.sum(g, axis=0, keepdims=True)


def bias_sums(width, gqkv, out):
    out[0:1, :] = jnp.sum(gqkv[:, 0:width].astype(F32), axis=0, keepdims=True)
    out[1:2, :] = jnp.sum(gqkv[:, 2 * width:3 * width].astype(F32), axis=0, keepdims=True)


def backward_plain_call(heads, hidden, norm_t, coef_t, qkv, mem, gatt, gmid, lse, ublk, proj, wmat, vecs, wqkv):
    seqs, length, width = hidden.shape
    tokens = seqs * length
    brows = coef_t.shape[1]
    basis = brows // seqs
    vm = pl.BlockSpec(memory_space=pltpu.VMEM)

    def kernel(
        hidden, norm_t, coef_t, qkv, mem, gatt, gmid, lse, ublk, proj, wmat, vecs, wqkv,
        gin, dqkv, vsum, msum, gqkv, gmem, head_par, grows, dq_t,
    ):
        vsum[...] = jnp.zeros_like(vsum)
        msum[...] = jnp.zeros_like(msum)
        grows[...] = jnp.zeros_like(grows)
        for s in range(seqs):
            rows_of = basis_rows(proj[s], heads, basis, head_par)

            def pair(p, _):
                backward_heads(s, p, 0, heads, length, basis, width, qkv, mem, gatt, lse, head_par, grows, dq_t, gqkv, gmem)
                return 0

            lax.fori_loop(0, heads // 2, pair, 0)
            backward_finish(s, 0, heads, rows_of, qkv, mem, ublk, grows, dq_t, wmat, gqkv, gmem, msum)
        step = width // 3
        for j in range(9):
            c = slice(j * step, (j + 1) * step)
            y = dot_nn(norm_t[...], gqkv[:, c])
            if j >= 3:
                y = y + dot_nn(coef_t[...], gmem[:, (j - 3) * step:(j - 2) * step])
            dqkv[:, c] = y.astype(BF)

        def last(i, _):
            r = pl.ds(pl.multiple_of(i * 256, 256), 256)
            backward_input(r, width, hidden[r, :], gmid[r, :], gqkv, wqkv, vecs, gin.at[r, :], vsum.at[2:4, :])
            return 0

        lax.fori_loop(0, tokens // 256, last, 0)
        bias_sums(width, gqkv, vsum)

    shapes = (
        jax.ShapeDtypeStruct((tokens, width), BF),
        jax.ShapeDtypeStruct((width, 3 * width), BF),
        jax.ShapeDtypeStruct((8, width), F32),
        jax.ShapeDtypeStruct((32, basis), F32),
    )
    return pl.pallas_call(
        kernel,
        out_shape=shapes,
        in_specs=[vm] * 13,
        out_specs=[vm] * 4,
        scratch_shapes=[
            pltpu.VMEM((tokens, 3 * width), BF),
            pltpu.VMEM((brows, 2 * width), BF),
            pltpu.VMEM((heads, 8, length), F32),
            pltpu.VMEM((3, 16, length), F32),
            pltpu.VMEM((width, length), F32),
        ],
        compiler_params=pltpu.CompilerParams(vmem_limit_bytes=VMEM_BYTES),
        name="backward_plain",
    )(hidden.reshape(tokens, width), norm_t, coef_t, qkv, mem, gatt, gmid, lse, ublk, proj, wmat, vecs, wqkv)


class Reduce:
    SLOTS = 13

    def __init__(self, place, started, name, base, parts, bufs):
        self.p, self.s, self.name, self.base, self.parts = place, started, name, base, parts
        self.g, self.r1, self.r2, self.r3, self.r4, self.f = bufs

    def where(self, part):
        r0, rn, c0, cn = self.parts[part]
        return pl.ds(r0, rn), pl.ds(c0, cn)

    def core(self, *pieces):
        for i, (src, rows) in enumerate(pieces):
            self.s.go((self.name, 1), src, self.r1.at[:, :, :, rows, :], self.base + i, self.p.at(c=1 - self.p.c))

    def second(self):
        p = self.p
        self.s.arrived((self.name, 1))

        def step(i, _):
            at = (i // 8, (i // 2) % 4, i % 2)
            self.g[at] = self.g[at] + self.r1[at]
            return 0

        lax.fori_loop(0, 16, step, 0)
        for part in (0, 1):
            r, c = self.where(part)
            if part == 0:
                self.s.go((self.name, 2), self.g.at[1 - p.y, :, :, r, c], self.r2[0], self.base + 2, p.at(y=1 - p.y))
            else:
                self.s.go((self.name, 2), self.g.at[:, :, 1 - p.x, r, c], self.r2[1], self.base + 3, p.at(x=1 - p.x))

    def third(self):
        p = self.p
        self.s.arrived((self.name, 2))
        r, c = self.where(0)
        r_b, c_b = self.where(1)

        def step(i, _):
            z, k = i // 2, i % 2
            self.g[p.y, z, k, r, c] = self.g[p.y, z, k, r, c] + self.r2[0][z, k]
            self.g[k, z, p.x, r_b, c_b] = self.g[k, z, p.x, r_b, c_b] + self.r2[1][k, z]
            return 0

        lax.fori_loop(0, 8, step, 0)
        for part in (0, 1):
            self.send_third(part)

    def send_third(self, part):
        p = self.p
        r, c = self.where(part)
        if part == 0:
            self.s.go((self.name, 3), self.g.at[p.y, :, 1 - p.x, r, c], self.r3[0], self.base + 4, p.at(x=1 - p.x))
        else:
            self.s.go((self.name, 3), self.g.at[1 - p.y, :, p.x, r, c], self.r3[1], self.base + 5, p.at(y=1 - p.y))

    def along(self):
        p = self.p
        self.s.arrived((self.name, 3))

        def step(z, _):
            for part in self.parts:
                r, c = self.where(part)
                self.g[p.y, z, p.x, r, c] = self.g[p.y, z, p.x, r, c] + self.r3[part][z]
            return 0

        lax.fori_loop(0, 4, step, 0)
        self.send_along()

    early = None

    def summand(self, z):
        p = self.p
        return self.g.at[p.y, z, p.x] if self.early is None else self.early.at[z // 2, p.y, z % 2, p.x]

    def send_along(self):
        p = self.p
        for s in (1, 2, 3):
            to = p.far_z(s)
            self.s.go((self.name, 4), self.summand(to), self.r4.at[s - 1], self.base + 5 + s, p.at(z=to))

    def last(self, out, segments):
        p = self.p
        self.s.arrived((self.name, 4))
        own = self.summand(p.z)[...].astype(F32)
        self.f[...] = (own + self.r4[0].astype(F32)) + (self.r4[1].astype(F32) + self.r4[2].astype(F32))
        n = self.f.shape[0] // 2
        theirs = pl.ds(pl.multiple_of((1 - p.c) * n, 8), n)
        mine = pl.ds(pl.multiple_of(p.c * n, 8), n)
        for i, (c0, to, cn) in enumerate(segments):
            there = out.at[:, pl.ds(pl.multiple_of(to, 128), cn)]
            self.s.go((self.name, 5), self.f.at[theirs, pl.ds(c0, cn)], there, self.base + 9 + i, p.at(c=1 - p.c))
            there[...] = self.f[mine, c0:c0 + cn]

    def done(self):
        self.s.arrived((self.name, 5))


class Everywhere:
    SLOTS = 10

    def __init__(self, place, started, name, slot, held, got):
        self.p, self.s, self.name, self.slot, self.held, self.got = place, started, name, slot, held, got

    def start(self, step):
        p = self.p
        if step == 0:
            for d in range(1, 8):
                to = p.at(y=(p.y + d // 4) % 2, x=(p.x + d // 2) % 2, c=(p.c + d) % 2)
                self.s.go((self.name, 0), self.held.at[0], self.got.at[d - 1], self.slot + d - 1, to)
        else:
            for s in (1, 2, 3):
                self.s.go((self.name, 1), self.held.at[1], self.got.at[6 + s], self.slot + 6 + s, p.at(z=p.far_z(s)))

    def add(self, step):
        self.s.arrived((self.name, step))
        first = 0 if step == 0 else 7
        total = self.held[step]
        for i in range(first, 7 if step == 0 else 10):
            total = total + self.got[i]
        if step == 0:
            self.held[1] = total
        return total


BACK_STEPS = (
    (), (), (), ("xx", "o1"),
    (), ("p1",), ("a3", "b3", "e0"), ("o2", "u0"),
    (), ("q1", "p2", "e1"), ("o3", "u1"), (),
    ("p3", "r1", "v0"), ("q2",), (), ("w0", "k0"),
    ("r2", "v1", "q3"), ("l0",), ("r3", "w1", "k1"), ("l1", "d4", "a4", "b4", "p4", "o4", "q4"), ("r4",),
)


def backward_kernel(
    heads, devices,
    hidden, norm_h, coef_h, qkv_h, mem_h, gatt_h, gmid, lse, ublk, proj, wmat, vecs, vsum_a, usum, wq_h, p_out, gu_h, gd_h,
    gin, o_qkv, o_out, o_up, o_down, early, late, msum,
    norm_t, coef_t, qkv, mem, gatt, wq,
    gqkv, gmem, head_par, grows, dq_t, away, gm_buf, hid_buf, gin_buf,
    bufs, vsum, e_held, e_got, l_held, l_got, k_held, k_got, m_held, m_got, early_bufs, send, recv, local, early_send, early_recv,
):
    place = Place()
    p = place
    tokens, width = hidden.shape
    seqs, _, length = proj.shape
    basis = wmat.shape[0]
    ff = o_up.shape[1]
    st = Started(send, recv)
    names = "abdopqr"
    red = {n: Reduce(place, st, n, i * Reduce.SLOTS, parts, bufs[i]) for i, (n, (_, _, parts)) in enumerate(zip(names, reduce_shapes(width, ff, devices)))}
    base = len(names) * Reduce.SLOTS
    sums = {"e": Everywhere(place, st, "e", base, e_held, e_got), "l": Everywhere(place, st, "l", base + Everywhere.SLOTS, l_held, l_got)}
    sums["k"] = Everywhere(place, st, "k", base + 5 * Everywhere.SLOTS, k_held, k_got)
    for i, n in enumerate("uvw"):
        sums[n] = Everywhere(place, st, n, base + (2 + i) * Everywhere.SLOTS, m_held.at[i], m_got.at[i])
    loads = []
    for i, (src, dst) in enumerate(((qkv_h, qkv), (mem_h, mem), (gatt_h, gatt), (norm_h, norm_t), (coef_h, coef_t), (wq_h, wq))):
        copy = pltpu.make_async_copy(src, dst, local.at[i])
        copy.start()
        loads.append(copy)
    grows[...] = jnp.zeros_like(grows)
    vsum[...] = jnp.zeros_like(vsum)
    e_held[0] = jnp.concatenate([vsum_a[0:4, :], usum[0:4, :]], axis=0)
    half = width // 2

    def side(c):
        return p_out.at[:, :, :, :, pl.ds(pl.multiple_of(c * half, 128), half)]

    er = EarlyReduce(place, early_send, early_recv, *early_bufs[:2], None, None, None, None, None, *early_bufs[2:])
    red["a"].g, red["b"].g, red["d"].early = er.g_u.at[0], er.g_u.at[1], er.g_d
    own = [pltpu.make_async_copy(src, dst, local.at[6 + i])
           for i, (src, dst) in enumerate(((gu_h, er.g_u), (gd_h, er.g_d), (side(p.c), red["o"].g)))]
    for copy in own:
        copy.start()
    place.greet(place.layer())
    red["o"].core((side(1 - p.c), slice(None)))
    sums["e"].start(0)
    for copy in own:
        copy.wait()
    er.resume()
    pieces = 128
    outs = {
        "a": (o_up, lambda: [(k * half, k * width + p.c * half, half) for k in (0, 1)]),
        "b": (o_up, lambda: [(k * half, (2 + k) * width + p.c * half, half) for k in (0, 1)]),
        "d": (o_down, lambda: [(0, p.c * half, half)]),
        "o": (o_out, lambda: [(0, p.c * half, half)]),
    }
    for i, n in enumerate("pqr"):
        outs[n] = (o_qkv, lambda i=i: [(j * pieces, j * width + i * 2 * pieces + p.c * pieces, pieces) for j in range(3)])

    def perform(word):
        if word[0] == "x":
            er.up_add_second(2)
            er.up_add_second(3)
            red["a"].send_third(0)
            red["b"].send_third(1)
            er.down_add_third(0)
            er.down_add_third(1)
            red["d"].send_along()
        elif word[0] in sums:
            total, step = sums[word[0]], int(word[1])
            value = total.add(step)
            if step == 0:
                total.start(1)
            else:
                if word[0] in "uvw":
                    n = value.shape[0]
                    msum["uvw".index(word[0]) * n:("uvw".index(word[0]) + 1) * n, :] = value
                else:
                    {"e": early, "l": late.at[0:2, :], "k": late.at[2:4, :]}[word[0]][...] = value
        else:
            r, step = red[word[0]], word[1]
            if step == "1":
                r.second()
            elif step == "2":
                r.third()
            elif step == "3":
                r.along()
            else:
                out, segments = outs[word[0]]
                r.last(out, segments())

    steps = iter(BACK_STEPS)

    def advance():
        for word in next(steps, ()):
            perform(word)

    for copy in loads[:3]:
        copy.wait()
    chunk = 2 * pieces
    m_held[...] = jnp.zeros_like(m_held)
    rows_of = [basis_rows(proj[s], heads, basis, head_par.at[s]) for s in range(seqs)]
    for i in range(3):
        for s in range(seqs):
            for k in range(2):
                def one(j, _):
                    backward_heads(s, j, 2 * i, heads, length, basis, width, qkv, mem, gatt, lse, head_par.at[s], grows, dq_t, gqkv, gmem)
                    return 0

                lax.fori_loop(2 * i + k, 2 * i + k + 1, one, 0)
                if k == 0:
                    advance()
            backward_finish(s, i * chunk, heads, rows_of[s], qkv, mem, ublk, grows, dq_t, wmat, gqkv, gmem, m_held.at[i, 0])
            if s < seqs - 1:
                advance()
        if i == 0:
            loads[3].wait()
            loads[4].wait()
        r = red["pqr"[i]]
        for j in range(3):
            c = j * width + i * chunk
            y = dot_nn(norm_t[...], gqkv[:, c:c + chunk])
            if j > 0:
                y = y + dot_nn(coef_t[...], gmem[:, (j - 1) * chunk:j * chunk])
            y = y.astype(BF).reshape(2, 4, 2, r.g.shape[3], chunk)
            low, high = y[..., :pieces], y[..., pieces:]
            keep, give = jnp.where(p.c == 0, low, high), jnp.where(p.c == 0, high, low)
            r.g[:, :, :, :, j * pieces:(j + 1) * pieces] = keep
            away[i, :, :, :, :, j * pieces:(j + 1) * pieces] = give
        r.core((away.at[i], slice(None)))
        sums["uvw"[i]].start(0)
        if i == 2:
            bias_sums(width, gqkv, k_held.at[0])
            sums["k"].start(0)
        advance()
    wflat = wq.reshape(width, 3 * width)
    loads[5].wait()
    blocks = tokens // 256

    def fetch(i):
        r = slice(i * 256, (i + 1) * 256)
        return (pltpu.make_async_copy(gmid.at[r, :], gm_buf.at[i % 2], local.at[16 + i % 2]),
                pltpu.make_async_copy(hidden.at[r, :], hid_buf.at[i % 2], local.at[18 + i % 2]))

    def emit(i):
        return pltpu.make_async_copy(gin_buf.at[i % 2], gin.at[i * 256:(i + 1) * 256, :], local.at[20 + i % 2])

    for i in (0, 1):
        for copy in fetch(i):
            copy.start()
    for i in range(blocks):
        for copy in fetch(i):
            copy.wait()
        if i >= 2:
            emit(i - 2).wait()
        backward_input(slice(i * 256, (i + 1) * 256), width, hid_buf[i % 2], gm_buf[i % 2], gqkv, wflat, vecs, gin_buf.at[i % 2], vsum)
        emit(i).start()
        if i + 2 < blocks:
            for copy in fetch(i + 2):
                copy.start()
        if i == blocks - 1:
            l_held[0] = vsum[...]
            sums["l"].start(0)
        advance()
    for _ in range(99):
        advance()
    for n in names:
        red[n].done()
    for i in (blocks - 2, blocks - 1):
        emit(i).wait()
    for copy in er.resumed():
        copy.wait_send()
    st.left()


def reduce_shapes(width, ff, devices):
    chip, chip_ff = 2 * width // devices, 2 * ff // devices
    h = width // 2
    more = (chip, h, {0: (0, chip, 0, 256), 1: (0, chip, 256, 128)})
    less = (chip, h, {0: (0, chip, 0, 128), 1: (0, chip, 128, 256)})
    return [(chip, width, {0: (0, chip, 0, width)}), (chip, width, {1: (0, chip, 0, width)}), (chip_ff, h, {}), more, less, more, less]


def backward_call(
    heads, devices, hidden, norm_t, coef_t, qkv, mem, gatt, gmid, lse, ublk, proj, wmat, vecs, vsum_a, usum, wq, p_out, g_up, g_down, ff,
):
    seqs, length, width = hidden.shape
    tokens = seqs * length
    brows = coef_t.shape[1]
    basis = brows // seqs
    vm = pl.BlockSpec(memory_space=pltpu.VMEM)
    anyw = pl.BlockSpec(memory_space=pl.ANY)
    shapes = (
        jax.ShapeDtypeStruct((tokens, width), BF),
        jax.ShapeDtypeStruct((width // devices, 3 * width), F32),
        jax.ShapeDtypeStruct((width // devices, width), F32),
        jax.ShapeDtypeStruct((width // devices, ff), F32),
        jax.ShapeDtypeStruct((ff // devices, width), F32),
        jax.ShapeDtypeStruct((8, width), F32),
        jax.ShapeDtypeStruct((4, width), F32),
        jax.ShapeDtypeStruct((24, basis), F32),
    )

    def buffers(i, shape):
        rows, cols, parts = shape
        none = pltpu.VMEM((8, 128), F32)
        whole = i > 2
        sizes = [parts.get(k, (0, 16, 0, 128)) for k in (0, 1)]
        (_, ra, _, ca), (_, rb, _, cb) = sizes
        return (
            none if i < 3 else pltpu.VMEM((2, 4, 2, rows, cols), BF),
            pltpu.VMEM((2, 4, 2, rows, cols), BF) if whole else none,
            (pltpu.VMEM((4, 2, ra, ca), BF), pltpu.VMEM((2, 4, rb, cb), BF)) if whole else (none, none),
            (pltpu.VMEM((4, ra, ca), BF), pltpu.VMEM((4, rb, cb), BF)),
            pltpu.VMEM((3, rows, cols), BF),
            pltpu.VMEM((rows, cols), F32),
        )

    chip, chip_ff = 2 * width // devices, 2 * ff // devices
    table = reduce_shapes(width, ff, devices)
    slots = len(table) * Reduce.SLOTS + 6 * Everywhere.SLOTS
    return pl.pallas_call(
        lambda *refs: backward_kernel(heads, devices, *refs),
        out_shape=shapes,
        in_specs=[anyw] * 7 + [vm] * 7 + [anyw] * 4,
        out_specs=[anyw] + [vm] * 7,
        scratch_shapes=[pltpu.VMEM(a.shape, a.dtype) for a in (norm_t, coef_t, qkv, mem, gatt, wq)] + [
            pltpu.VMEM((tokens, 3 * width), BF),
            pltpu.VMEM((brows, 512), BF),
            pltpu.VMEM((seqs, heads, 8, length), F32),
            pltpu.VMEM((3, 16, length), F32),
            pltpu.VMEM((256, length), F32),
            pltpu.VMEM((3, 2, 4, 2, 2 * width // devices, 384), BF),
            pltpu.VMEM((2, 256, width), F32),
            pltpu.VMEM((2, 256, width), BF),
            pltpu.VMEM((2, 256, width), BF),
            [buffers(i, shape) for i, shape in enumerate(table)],
            pltpu.VMEM((2, width), F32),
            pltpu.VMEM((2, 8, width), F32),
            pltpu.VMEM((10, 8, width), F32),
            pltpu.VMEM((2, 2, width), F32),
            pltpu.VMEM((10, 2, width), F32),
            pltpu.VMEM((2, 2, width), F32),
            pltpu.VMEM((10, 2, width), F32),
            pltpu.VMEM((3, 2, 8, basis), F32),
            pltpu.VMEM((3, 10, 8, basis), F32),
            [pltpu.VMEM(shape, BF) for shape in (
                g_down.shape, g_up.shape, (2, 4, 2, chip, width // 2), (2, 2, 4, chip, width // 2), (2, 2, 2, chip_ff // 2, width // 2))],
            pltpu.SemaphoreType.DMA((slots,)),
            pltpu.SemaphoreType.DMA((slots,)),
            pltpu.SemaphoreType.DMA((22,)),
            pltpu.SemaphoreType.DMA((EarlyReduce.SLOTS,)),
            pltpu.SemaphoreType.DMA((EarlyReduce.SLOTS,)),
        ],
        compiler_params=pltpu.CompilerParams(vmem_limit_bytes=56 * 1024 * 1024, collective_id=1, has_side_effects=True),
        name="backward",
    )(hidden.reshape(tokens, width), norm_t, coef_t, qkv, mem, gatt, gmid, lse, ublk, proj, wmat, vecs, vsum_a, usum, wq, p_out, g_up, g_down)


def finish_call(heads, devices, ff, early, late, msum, whole):
    width = early.shape[1]
    basis = msum.shape[1]
    e, rows = width // devices, basis // devices
    group = 4
    vm = pl.BlockSpec(memory_space=pltpu.VMEM)
    anyw = pl.BlockSpec(memory_space=pl.ANY)
    n = len(whole)

    def kernel(*refs):
        early, late, msum = refs[:3]
        sources, results = refs[3:3 + n], refs[3 + n:3 + 2 * n]
        gain_a, shift_a, qv, out_b, gain_m, shift_m, up_b, down_b, mean, wide = refs[3 + 2 * n:-1]
        sem = refs[-1]
        copies = [pltpu.make_async_copy(a, b, sem.at[i]) for i, (a, b) in enumerate(zip(sources, results))]
        for copy in copies:
            copy.start()
        me = lax.axis_index("dp") * lax.axis_size("fsdp") + lax.axis_index("fsdp")

        def thirds(x):
            high = x.astype(BF)
            rest = x - high.astype(F32)
            middle = rest.astype(BF)
            return high, middle, (rest - middle.astype(F32)).astype(BF)

        def pick(x, start, size):
            at = (iota((x.shape[1], size), 0) == iota((x.shape[1], size), 1) + start).astype(F32).astype(BF)
            return sum(dot_nn(part, at) for part in thirds(x))

        def row_of(x, i):
            return jnp.sum(jnp.where(iota(x.shape, 0) == i, x, 0.0), axis=0, keepdims=True)

        some = pick(early[...], me * e, e)
        down_b[...], gain_m[...], shift_m[...], out_b[...] = (some[i:i + 1] for i in range(4))
        some = pick(late[...], me * e, e)
        gain_a[...], shift_a[...] = some[0:1], some[1:2]
        k = devices // 2
        qv[...] = pick(row_of(late[2:4, :], me // k), me % k * 2 * e, 2 * e)
        k = devices * width // ff
        up_b[...] = pick(row_of(early[4:8, :], me // k), me % k * (ff // devices), ff // devices)
        at = (iota((rows, basis), 1) == iota((rows, basis), 0) + me * rows).astype(F32).astype(BF)
        for out, first in ((mean, 0), (wide, group)):
            x = jnp.concatenate([msum[i + first:i + first + group, :] for i in range(0, 2 * heads, 2 * group)], axis=0)
            out[...] = sum(dot_nt(at, part) for part in thirds(x))
        for copy in copies:
            copy.wait()

    small = [(1, e), (1, e), (1, 2 * e), (1, e), (1, e), (1, e), (1, ff // devices), (1, e), (rows, heads), (rows, heads)]
    return pl.pallas_call(
        kernel,
        out_shape=[jax.ShapeDtypeStruct(a.shape, a.dtype) for a in whole] + [jax.ShapeDtypeStruct(s, F32) for s in small],
        in_specs=[vm] * (3 + n),
        out_specs=[anyw] * n + [vm] * len(small),
        scratch_shapes=[pltpu.SemaphoreType.DMA((n,))],
        name="finish",
    )(early, late, msum, *whole)


def gather(x):
    return lax.all_gather(x, AXES, axis=0, tiled=True)


def scatter(x):
    return lax.psum_scatter(x, AXES, scatter_dimension=0, tiled=True)


def shards_plain(
    hidden, grad_out, past_states, old_coeffs, fresh_flags, ridge_map,
    gain_attn, shift_attn, qkv_weight, qv_bias, out_weight, out_bias,
    gain_mlp, shift_mlp, up_weight, up_bias, down_weight, down_bias,
    mean_weight, width_weight,
):
    seqs, length, width = hidden.shape
    heads = mean_weight.shape[1]
    devices = lax.axis_size("dp") * lax.axis_size("fsdp")
    full_qkv, full_out, full_up, full_down = (gather(w) for w in (qkv_weight, out_weight, up_weight, down_weight))
    rows = jnp.zeros((mean_weight.shape[0], 128), BF)
    rows = rows.at[:, 0:heads].set(mean_weight).at[:, 16:16 + heads].set(width_weight)
    wmat = gather(rows)
    full_qv = gather(qv_bias)
    vecs = jnp.stack(
        [gather(gain_attn), gather(shift_attn), full_qv[:width], full_qv[width:],
         gather(out_bias), gather(gain_mlp), gather(shift_mlp), gather(down_bias)]).astype(F32)
    ubias = gather(up_bias).astype(F32).reshape(-1, width)
    ubias = jnp.concatenate([ubias, jnp.zeros((8 - ubias.shape[0], width), F32)], axis=0)

    norm_t, coef_t, qkv, mem, att, lse, ublk, proj = forward_plain_call(
        heads, fresh_flags, hidden, past_states, old_coeffs, ridge_map, wmat, vecs, full_qkv)
    output, gmid, gatt, dout, dup, ddown, vsum_a, usum = middle_call(
        att, hidden, grad_out, full_out, full_up, full_down, vecs, ubias)
    gin, dqkv, vsum_b, msum = backward_plain_call(
        heads, hidden, norm_t, coef_t, qkv, mem, gatt, gmid, lse, ublk, proj, wmat, vecs, full_qkv)

    up_sum = usum.reshape(-1)[:up_bias.shape[0] * devices]
    big = [scatter(a.astype(F32)) for a in (dqkv, dout, dup, ddown)]
    small = [
        scatter(a) for a in (
            vsum_b[2], vsum_b[3], jnp.concatenate([vsum_b[0], vsum_b[1]]), vsum_a[3], vsum_a[1], vsum_a[2],
            up_sum, vsum_a[0], msum[0:heads].T, msum[16:16 + heads].T)
    ]
    return (
        output.reshape(seqs, length, width), gin.reshape(seqs, length, width),
        small[0], small[1], big[0], small[2], big[1], small[3], small[4], small[5],
        big[2], small[6], big[3], small[7], small[8], small[9],
    )


def shards_block(
    hidden, grad_out, past_states, old_coeffs, fresh_flags, ridge_map,
    gain_attn, shift_attn, qkv_weight, qv_bias, out_weight, out_bias,
    gain_mlp, shift_mlp, up_weight, up_bias, down_weight, down_bias,
    mean_weight, width_weight,
):
    seqs, length, width = hidden.shape
    heads = mean_weight.shape[1]
    devices = 32
    ff = up_weight.shape[1]
    e = width // devices
    def put(v, row, col):
        v = v.reshape((1, -1)) if v.ndim == 1 else v
        return jnp.pad(v, ((row, 32 - row - v.shape[0]), (col, 128 - col - v.shape[1])))

    small = (
        put(mean_weight, 0, 0) + put(width_weight, 0, 16)
        + put(gain_attn, 16, 0) + put(shift_attn, 16, e) + put(out_bias, 16, 2 * e) + put(gain_mlp, 16, 3 * e)
        + put(shift_mlp, 17, 0) + put(down_bias, 17, e) + put(qv_bias, 17, 2 * e) + put(up_bias, 18, 0))

    norm_t, coef_t, qkv, mem, output, gmid, gatt, dout, g_up, g_down, wq, lse, ublk, proj, wmat, vecs, vsum_a, usum = forward_call(
        heads, devices, fresh_flags, hidden, past_states, old_coeffs, ridge_map, grad_out, small, qkv_weight, out_weight, up_weight, down_weight)
    gin, d_qkv, d_out, d_up, d_down, early, late, msum = backward_call(
        heads, devices, hidden, norm_t, coef_t, qkv, mem, gatt, gmid, lse, ublk, proj, wmat, vecs, vsum_a, usum, wq,
        dout.reshape(2, 4, 2, width // 16, width), g_up, g_down, ff)

    (output, gin, d_qkv, d_out, d_up, d_down, gain_a, shift_a, qv, out_b, gain_m, shift_m, up_b, down_b, mean, wide) = finish_call(
        heads, devices, ff, early, late, msum, (output, gin, d_qkv, d_out, d_up, d_down))
    flat = lambda v: v.reshape(v.shape[1])
    return (
        output.reshape(seqs, length, width), gin.reshape(seqs, length, width),
        flat(gain_a), flat(shift_a), d_qkv, flat(qv), d_out, flat(out_b), flat(gain_m), flat(shift_m),
        d_up, flat(up_b), d_down, flat(down_b), mean, wide,
    )


def solution(mesh):
    rows = P(AXES, None)
    cube = P(AXES, None, None)
    one = P(AXES)
    in_specs = (cube, cube, cube, cube, one, P(), one, one, rows, one, rows, one, one, one, rows, one, rows, one, rows, rows)
    out_specs = (cube, cube, one, one, rows, one, rows, one, one, one, rows, one, rows, one, rows, rows)
    body = shards_block if mesh.shape["dp"] == 2 and mesh.shape["fsdp"] == 16 else shards_plain
    return jax.shard_map(body, mesh=mesh, in_specs=in_specs, out_specs=out_specs, check_vma=False)
```

```python
import math

import jax
import jax.numpy as jnp
from jax import lax
from jax.experimental import pallas as pl
from jax.experimental.pallas import tpu as pltpu
from jax.sharding import PartitionSpec as P

EPS = 1e-05
LOG2E = 1.4426950408889634
BF = jnp.bfloat16
F32 = jnp.float32
AXES = ("dp", "fsdp")
VMEM_BYTES = 60 * 1024 * 1024


def dot_nn(a, b):
    return lax.dot_general(a, b, (((1,), (0,)), ((), ())), preferred_element_type=F32)


def dot_nt(a, b):
    return lax.dot_general(a, b, (((1,), (1,)), ((), ())), preferred_element_type=F32)


def dot_tn(a, b):
    return lax.dot_general(a, b, (((0,), (0,)), ((), ())), preferred_element_type=F32)


def split_high_low(x):
    high = x.astype(BF)
    return high, (x - high.astype(F32)).astype(BF)


def iota(shape, dim):
    return lax.broadcasted_iota(jnp.int32, shape, dim)


def head_masks(pair_lanes, head_dim):
    lane = iota((1, pair_lanes), 1)
    return [((lane // head_dim) == h).astype(F32).astype(BF) for h in range(pair_lanes // head_dim)]


def norm_parts(x):
    mean = jnp.mean(x, axis=-1, keepdims=True)
    centred = x - mean
    variance = jnp.mean(centred * centred, axis=-1, keepdims=True)
    inv = lax.rsqrt(variance + EPS)
    return centred * inv, inv


def norm_back(grad, unit, inv, gain):
    g = grad * gain
    return inv * (g - jnp.mean(g, axis=-1, keepdims=True) - unit * jnp.mean(g * unit, axis=-1, keepdims=True))


MESH = pl.DeviceIdType.MESH


class Place:
    def __init__(self):
        self.y = lax.axis_index("dp")
        f = lax.axis_index("fsdp")
        self.z, self.x, self.c = f // 4, (f // 2) % 2, f % 2

    def at(self, y=None, z=None, x=None, c=None):
        y, z, x, c = (b if a is None else a for a, b in ((y, self.y), (z, self.z), (x, self.x), (c, self.c)))
        return (y, z * 4 + x * 2 + c)

    def far_z(self, s):
        return (self.z + s) % 4

    def others(self):
        return [self.at(c=1 - self.c), self.at(x=1 - self.x), self.at(y=1 - self.y)] + [
            self.at(z=self.far_z(s)) for s in (1, 2, 3)]

    def layer(self):
        return self.others() + [self.at(y=1 - self.y, x=1 - self.x)]

    def hello(self, devices):
        barrier = pltpu.get_barrier_semaphore()
        for d in devices:
            pl.semaphore_signal(barrier, inc=1, device_id=d, device_id_type=MESH)

    def wait_hello(self, devices):
        pl.semaphore_wait(pltpu.get_barrier_semaphore(), len(devices))


class Weight:
    def __init__(self, index, rows, half, parts):
        self.index, self.rows, self.half, self.parts = index, rows, half, parts

    def where(self, part, c=None):
        r0, rn, c0, cn = self.parts[part]
        if c is None:
            return pl.ds(r0, rn), pl.ds(c0, cn)
        return pl.ds(r0, rn), pl.ds(pl.multiple_of(c * self.half + c0, 128), cn)

    def columns(self, c):
        return pl.ds(pl.multiple_of(c * self.half, 128), self.half)


def split_columns(n):
    first = (n // 128 + 1) // 2 * 128
    return first


def weight_table(width, ff, devices):
    chip = 2 * width // devices
    chip_ff = 2 * ff // devices
    items = []
    for i, n in enumerate((3 * width, width, ff)):
        half = n // 2
        first = split_columns(half)
        items.append(Weight(i, chip, half, ((0, chip, 0, first), (0, chip, first, half - first))))
    half = width // 2
    items.append(Weight(3, chip_ff, half, ((0, chip_ff // 2, 0, half), (chip_ff // 2, chip_ff // 2, 0, half))))
    return items


def nested(conds, act):
    if not conds:
        act()
        return

    @pl.when(conds[0]())
    def _():
        nested(conds[1:], act)


class Started:
    def __init__(self, send, recv):
        self.send, self.recv, self.live = send, recv, {}

    def go(self, name, src, dst, slot, dev):
        copy = pltpu.make_async_remote_copy(
            src_ref=src, dst_ref=dst, send_sem=self.send.at[slot], recv_sem=self.recv.at[slot],
            device_id=dev, device_id_type=MESH)
        copy.start()
        self.live.setdefault(name, []).append(copy)

    def arrived(self, name):
        for copy in self.live[name]:
            copy.wait_recv()

    def left(self, name=None):
        for key in list(self.live) if name is None else [name]:
            for copy in self.live.pop(key):
                copy.wait_send()


class Gather:
    SLOTS = 2 * 23

    def __init__(self, place, send, recv, base, w, full):
        self.p, self.send, self.recv, self.base, self.w, self.full = place, send, recv, base, w, full
        self.begun = []

    def ref(self, part, y, z, x):
        if part is None:
            return self.full.at[y, z, x, :, self.w.columns(self.p.c)]
        r, c = self.w.where(part, self.p.c)
        return self.full.at[y, z, x, r, c]

    def go(self, src, dst, send, recv, dev, conds, like):
        pltpu.make_async_remote_copy(
            src_ref=src, dst_ref=dst, send_sem=self.send.at[self.base + send()], recv_sem=self.recv.at[self.base + recv],
            device_id=dev, device_id_type=MESH).start()
        self.begun.append((send, conds, like))

    def wait(self, ref, slot):
        pltpu.make_async_remote_copy(
            src_ref=ref, dst_ref=ref, send_sem=self.send.at[self.base], recv_sem=self.recv.at[self.base + slot],
            device_id=self.p.at(c=1 - self.p.c), device_id_type=MESH).wait_recv()

    def left(self):
        for send, conds, like in self.begun:
            def act():
                pltpu.make_async_remote_copy(
                    src_ref=like(), dst_ref=like(), send_sem=self.send.at[self.base + send()], recv_sem=self.recv.at[self.base],
                    device_id=self.p.at(c=1 - self.p.c), device_id_type=MESH).wait_send()

            nested(conds, act)

    def along(self, j, act):
        here = self.p.z
        for z, cond, toward in ((lambda: here - j, lambda: here >= j, 1), (lambda: here + j, lambda: here + j <= 3, -1)):
            nested((cond,), lambda: act(z, (cond,), toward))

    def pass_z(self, src, dst, z, toward, conds, like):
        p = self.p
        more = (lambda: p.z <= 2) if toward == 1 else (lambda: p.z >= 1)
        nested((more,), lambda: self.go(
            src, dst, lambda: z() + (0 if toward == 1 else 4), z(), p.at(z=p.z + toward), conds + (more,), like))

    def partner(self, part, step):
        p = self.p
        return p.at(x=1 - p.x) if (part + step) % 2 == 0 else p.at(y=1 - p.y)

    def behind(self, part):
        p = self.p
        return (p.y, 1 - p.x) if part == 0 else (1 - p.y, p.x)

    def own_z(self):
        return self.p.z

    def one(self, part):
        return self.ref(part, 0, 0, 0)

    def start(self, block):
        p = self.p
        for toward in (1, -1):
            self.pass_z(block, self.ref(None, p.y, p.z, p.x), self.own_z, toward, (), lambda: self.one(None))
        for part in (0, 1):
            self.onward(part, self.own_z, block.at[self.w.where(part)], ())

    def onward(self, part, z, src, conds):
        p = self.p
        dst = self.ref(part, p.y, z(), p.x)
        o = part * 23
        like = lambda: self.one(part)
        self.go(src, dst, lambda: o + 8 + z(), o + 8 + z(), self.partner(part, 0), conds, like)
        self.go(src, dst, lambda: o + 12 + z(), o + 12 + z(), self.partner(part, 1), conds, like)

    def on_z(self, j):
        def act(z, conds, toward):
            whole = self.ref(None, self.p.y, z(), self.p.x)
            self.wait(whole, z())
            self.pass_z(whole, whole, z, toward, conds, lambda: self.one(None))
            for part in (0, 1):
                self.onward(part, z, self.ref(part, self.p.y, z(), self.p.x), conds)

        self.along(j, act)

    def on_second(self, j):
        def act(z, conds, toward):
            for part in (0, 1):
                self.second_on(part, z, conds)

        if j == 0:
            act(self.own_z, (), 0)
        else:
            self.along(j, act)

    def second_on(self, part, z, conds):
        y, x = self.behind(part)
        ref = self.ref(part, y, z(), x)
        o = part * 23
        self.wait(ref, o + 8 + z())
        self.go(ref, ref, lambda: o + 16 + z(), o + 16 + z(), self.partner(part, 1), conds, lambda: self.one(part))

    def core(self, step):
        p = self.p
        for part in (0, 1):
            o = part * 23
            if step == 2:
                for z in range(4):
                    y, x = (1 - p.y, p.x) if part == 0 else (p.y, 1 - p.x)
                    self.wait(self.ref(part, y, z, x), o + 12 + z)
                    self.wait(self.ref(part, 1 - p.y, z, 1 - p.x), o + 16 + z)
            self.go_core(lambda part=part: self.of_step(part, step), o + 20 + step)

    def of_step(self, part, step):
        p = self.p
        if step == 0:
            y, x = p.y, p.x
        elif step == 1:
            y, x = self.behind(part)
        else:
            y, x = (1 - p.y, slice(None)) if part == 0 else (slice(None), 1 - p.x)
        return self.ref(part, y, slice(None), x)

    def go_core(self, make, slot):
        self.go(make(), make(), lambda: slot, slot, self.p.at(c=1 - self.p.c), (), make)

    def finish(self):
        p = self.p
        for part in (0, 1):
            r, c = self.w.where(part, 1 - p.c)
            for step in range(3):
                if step == 2:
                    ref = self.full.at[1 - p.y, :, :, r, c] if part == 0 else self.full.at[:, :, 1 - p.x, r, c]
                else:
                    y, x = (p.y, p.x) if step == 0 else self.behind(part)
                    ref = self.full.at[y, :, x, r, c]
                self.wait(ref, part * 23 + 20 + step)


class LateGather(Gather):
    def start(self, block):
        for part in (0, 1):
            self.onward(part, self.own_z, block.at[self.w.where(part)], ())

    def on_third(self):
        p = self.p
        for part in (0, 1):
            o = part * 23
            y, x = (1 - p.y, p.x) if part == 0 else (p.y, 1 - p.x)
            self.wait(self.ref(part, y, p.z, x), o + 12 + p.z)
            self.wait(self.ref(part, 1 - p.y, p.z, 1 - p.x), o + 16 + p.z)
        ref = self.layer(p.z)
        for toward in (1, -1):
            self.pass_z(ref, ref, self.own_z, toward, (), lambda: self.layer(0))

    def layer(self, z):
        return self.ref(None, slice(None), z, slice(None))

    def on_z(self, j):
        def act(z, conds, toward):
            ref = self.layer(z())
            self.wait(ref, z())
            self.pass_z(ref, ref, z, toward, conds, lambda: self.layer(0))

        self.along(j, act)

    def core(self):
        self.go_core(lambda: self.ref(None, slice(None), slice(None), slice(None)), 20)

    def finish(self):
        self.wait(self.full.at[:, :, :, :, self.w.columns(1 - self.p.c)], 20)


def middle_body(
    att, hidden, gout, wout, wup, wdown, vecs, ubias, vsum, usum,
    x_t, dout, mid, x, acc, gacc, act_s, slope_s, outs, local, sem, put_down, put_up, hook,
):
    output_h, gmid_h, gatt_h, dout_h = outs
    tokens, width = hidden.shape
    ff = wup.shape[1]
    block = 256
    blocks = tokens // block
    chunk = ubias.shape[1]
    chunks = ff // chunk
    out_bias, gain, shift, down_bias = (vecs[i:i + 1, :] for i in (4, 5, 6, 7))

    def enter(i, _):
        r = pl.ds(pl.multiple_of(i * block, block), block)
        m = hidden[r, :].astype(F32) + dot_nn(att[r, :], wout[...]) + out_bias
        mid[r, :] = m
        unit, _ = norm_parts(m)
        y = (unit * gain + shift).astype(BF)
        x[r, :] = y
        x_t[:, r] = y.T
        acc[r, :] = jnp.zeros((block, width), F32)
        gacc[r, :] = jnp.zeros((block, width), F32)
        hook("enter", i)
        return 0

    lax.fori_loop(0, blocks, enter, 0)
    hook("entered", 0)

    def chunk_of(i):
        return (i % 2) * 2 + i // 2

    def first(i):
        j = chunk_of(i)
        c = pl.ds(pl.multiple_of(j * chunk, chunk), chunk)
        slot = i % 2
        w_up = wup[:, c]
        bias = ubias[pl.ds(j, 1), :]
        for b in range(blocks):
            r = slice(b * block, (b + 1) * block)
            u = dot_nn(x[r, :], w_up) + bias
            u2 = u * u
            th = jnp.tanh(u * (0.7978845608028654 + 0.7978845608028654 * 0.044715 * u2))
            half_one = 0.5 + 0.5 * th
            act_s[slot, r, :] = (u * half_one).astype(BF)
            slope = half_one + (0.5 * u) * (1.0 - th * th) * (
                0.7978845608028654 + 3 * 0.7978845608028654 * 0.044715 * u2)
            slope_s[slot, r, :] = slope.astype(BF)
        for k in range(2):
            part = slice(k * chunk // 2, (k + 1) * chunk // 2)
            put_down(i, k, dot_tn(act_s[slot, :, part], gout[...]).astype(BF))
        hook("first", i)

    def second(i):
        j = chunk_of(i)
        c = pl.ds(pl.multiple_of(j * chunk, chunk), chunk)
        slot = i % 2
        w_up, w_down = wup[:, c], wdown[c, :]
        colsum = jnp.zeros((1, chunk), F32)
        for b in range(blocks):
            r = slice(b * block, (b + 1) * block)
            gu = (dot_nt(gout[r, :], w_down) * slope_s[slot, r, :].astype(F32)).astype(BF)
            colsum = colsum + jnp.sum(gu.astype(F32), axis=0, keepdims=True)
            slope_s[slot, r, :] = gu
            acc[r, :] += dot_nn(act_s[slot, r, :], w_down)
            gacc[r, :] += dot_nt(gu, w_up)
        usum[pl.ds(j, 1), :] = colsum
        hook("middle", i)
        for k in range(2):
            part = slice(k * width // 2, (k + 1) * width // 2)
            put_up(i, k, dot_nn(x_t[part, :], slope_s[slot]).astype(BF))
        hook("second", i)

    def ahead(i, _):
        first(i)
        return 0

    lax.fori_loop(0, 2, ahead, 0)
    hook("ready", 0)
    usum[...] = jnp.zeros_like(usum)

    def both(i, _):
        second(i)

        @pl.when(i + 2 < chunks)
        def _():
            first(i + 2)

        hook("both", i)
        return 0

    lax.fori_loop(0, chunks, both, 0)
    vsum[...] = jnp.zeros_like(vsum)

    def rows_out(i):
        r = pl.ds(pl.multiple_of(i * block, block), block)
        return (pltpu.make_async_copy(act_s.at[0, r, :], output_h.at[r, :], local.at[sem + 1 + 3 * i]),
                pltpu.make_async_copy(mid.at[r, :], gmid_h.at[r, :], local.at[sem + 2 + 3 * i]),
                pltpu.make_async_copy(act_s.at[1, r, :], gatt_h.at[r, :], local.at[sem + 3 + 3 * i]))

    def leave(i, _):
        r = pl.ds(pl.multiple_of(i * block, block), block)
        m = mid[r, :]
        act_s[0, r, :] = (m + acc[r, :] + down_bias).astype(BF)
        unit, inv = norm_parts(m)
        g = gacc[r, :]
        go = gout[r, :].astype(F32)
        gm = go + norm_back(g, unit, inv, gain)
        mid[r, :] = gm
        gp = gm.astype(BF)
        x[r, :] = gp
        act_s[1, r, :] = dot_nt(gp, wout[...]).astype(BF)
        for copy in rows_out(i):
            copy.start()
        vsum[0:1, :] += jnp.sum(go, axis=0, keepdims=True)
        vsum[1:2, :] += jnp.sum(g * unit, axis=0, keepdims=True)
        vsum[2:3, :] += jnp.sum(g, axis=0, keepdims=True)
        vsum[3:4, :] += jnp.sum(gp.astype(F32), axis=0, keepdims=True)
        hook("leave", i)
        return 0

    lax.fori_loop(0, blocks, leave, 0)
    for j in range(width // 256):
        c = slice(j * 256, (j + 1) * 256)
        dout[:, c] = dot_tn(att[...], x[:, c]).astype(BF)
    final = pltpu.make_async_copy(dout, dout_h, local.at[sem])
    final.start()
    hook("end", 0)
    for i in range(blocks):
        for copy in rows_out(i):
            copy.wait()
    final.wait()


def middle_scratch(tokens, width, chunk):
    return [
        pltpu.VMEM((tokens, width), F32),
        pltpu.VMEM((tokens, width), BF),
        pltpu.VMEM((tokens, width), F32),
        pltpu.VMEM((tokens, width), F32),
        pltpu.VMEM((2, tokens, chunk), BF),
        pltpu.VMEM((2, tokens, chunk), BF),
    ]


def middle_call(att, hidden, gout, wout, wup, wdown, vecs, ubias):
    tokens, width = att.shape
    ff = wup.shape[1]
    chunk = ubias.shape[1]
    vm = pl.BlockSpec(memory_space=pltpu.VMEM)
    anyw = pl.BlockSpec(memory_space=pl.ANY)
    shapes = (
        jax.ShapeDtypeStruct((tokens, width), BF),
        jax.ShapeDtypeStruct((tokens, width), F32),
        jax.ShapeDtypeStruct((tokens, width), BF),
        jax.ShapeDtypeStruct((width, width), BF),
        jax.ShapeDtypeStruct((width, ff), BF),
        jax.ShapeDtypeStruct((ff, width), BF),
        jax.ShapeDtypeStruct((8, width), F32),
        jax.ShapeDtypeStruct((8, chunk), F32),
    )

    def kernel(att, hidden, gout, wout, wup, wdown, vecs, ubias, o, gm, ga, do, du, dd, vsum, usum, *scratch):
        def place(i):
            return ((i % 2) * 2 + i // 2) * chunk

        def put_down(i, k, v):
            dd[pl.ds(pl.multiple_of(place(i) + k * chunk // 2, chunk // 2), chunk // 2), :] = v

        def put_up(i, k, v):
            du[k * width // 2:(k + 1) * width // 2, pl.ds(pl.multiple_of(place(i), chunk), chunk)] = v

        middle_body(att, hidden, gout, wout, wup, wdown, vecs, ubias, vsum, usum, *scratch[:-1], (o, gm, ga, do), scratch[-1], 0,
                    put_down, put_up, lambda where, i: None)

    return pl.pallas_call(
        kernel,
        out_shape=shapes,
        in_specs=[vm] * 8,
        out_specs=[anyw] * 4 + [vm] * 4,
        scratch_shapes=[pltpu.VMEM((width, tokens), BF), pltpu.VMEM((width, width), BF)] + middle_scratch(tokens, width, chunk) + [pltpu.SemaphoreType.DMA((1 + 3 * (tokens // 256),))],
        compiler_params=pltpu.CompilerParams(vmem_limit_bytes=58 * 1024 * 1024),
        name="middle",
    )(att, hidden.reshape(tokens, width), gout.reshape(tokens, width), wout, wup, wdown, vecs, ubias)


class EarlyReduce:
    SLOTS = 20

    def __init__(self, place, send, recv, g_d, g_u, away_d, away_u, r1_d, r1_u, r2_d, r2_y, r2_x, r3_d):
        self.p, self.send, self.recv = place, send, recv
        self.g_d, self.g_u, self.away_d, self.away_u = g_d, g_u, away_d, away_u
        self.r1_d, self.r1_u, self.r2_d, self.r2_y, self.r2_x, self.r3_d = r1_d, r1_u, r2_d, r2_y, r2_x, r3_d
        self.n = g_d.shape[-1]
        self.h = g_d.shape[-2] // 2

    def copy(self, src, dst, slot, dev):
        return pltpu.make_async_remote_copy(
            src_ref=src, dst_ref=dst, send_sem=self.send.at[slot], recv_sem=self.recv.at[slot], device_id=dev, device_id_type=MESH)

    def mate(self):
        return self.p.at(c=1 - self.p.c)

    def sides(self, v):
        low, high = v[..., :self.n], v[..., self.n:]
        return jnp.where(self.p.c == 0, low, high), jnp.where(self.p.c == 0, high, low)

    def down_core(self, i):
        return self.copy(self.away_d.at[i % 2], self.r1_d.at[i // 2, i % 2], i, self.mate())

    def put_down(self, i, k, v):
        if k == 0:
            @pl.when(i >= 2)
            def _():
                self.down_core(i - 2).wait_send()

        keep, give = self.sides(v.reshape(2, 2 * self.h, 2 * self.n))
        self.g_d[i // 2, i % 2, k] = keep
        self.away_d[i % 2, k] = give

    def down_second(self, t):
        p = self.p
        a, b = pl.ds(0, self.h), pl.ds(self.h, self.h)
        return (self.copy(self.g_d.at[t, 1 - p.y, :, :, a, :], self.r2_d.at[t, 0], 8 + 2 * t, p.at(y=1 - p.y)),
                self.copy(self.g_d.at[t, :, :, 1 - p.x, b, :], self.r2_d.at[t, 1], 9 + 2 * t, p.at(x=1 - p.x)))

    def down_third(self, t):
        p = self.p
        a, b = pl.ds(0, self.h), pl.ds(self.h, self.h)
        return (self.copy(self.g_d.at[t, p.y, :, 1 - p.x, a, :], self.r3_d.at[t, 0], 12 + 2 * t, p.at(x=1 - p.x)),
                self.copy(self.g_d.at[t, 1 - p.y, :, p.x, b, :], self.r3_d.at[t, 1], 13 + 2 * t, p.at(y=1 - p.y)))

    def down_add_core(self, t):
        for y in (0, 1):
            self.down_core(2 * t + y).wait_recv()

        def step(i, _):
            at = (t, i // 4, (i // 2) % 2, i % 2)
            self.g_d[at] = self.g_d[at] + self.r1_d[at]
            return 0

        lax.fori_loop(0, 8, step, 0)
        for copy in self.down_second(t):
            copy.start()

    def down_add_second(self, t):
        p, h = self.p, self.h
        for copy in self.down_second(t):
            copy.wait_recv()

        def step(i, _):
            u, v = i // 2, i % 2
            at, to = (t, p.y, u, v, slice(0, h)), (t, 0, u, v)
            self.g_d[at] = self.g_d[at] + self.r2_d[to]
            at, to = (t, u, v, p.x, slice(h, 2 * h)), (t, 1, u, v)
            self.g_d[at] = self.g_d[at] + self.r2_d[to]
            return 0

        lax.fori_loop(0, 4, step, 0)

    def down_add_third(self, t):
        p, h = self.p, self.h
        for copy in self.down_third(t):
            copy.wait_recv()
        for z in (0, 1):
            for part in (0, 1):
                rows = slice(part * h, (part + 1) * h)
                at = (t, p.y, z, p.x, rows)
                self.g_d[at] = self.g_d[at] + self.r3_d[t, part, z]

    def up_core(self, i):
        return self.copy(self.away_u.at[i % 2], self.r1_u.at[i], 4 + i, self.mate())

    def rows_u(self):
        return self.g_u.shape[-2]

    def put_up(self, i, k, v):
        if k == 0:
            @pl.when(i >= 2)
            def _():
                self.up_core(i - 2).wait_send()

        keep, give = self.sides(v)
        c = pl.ds(pl.multiple_of((i // 2) * self.n, 128), self.n)
        self.g_u[i % 2, k, :, :, :, c] = keep.reshape(4, 2, self.rows_u(), self.n)
        self.away_u[i % 2, k] = give.reshape(4, 2, self.rows_u(), self.n)

    def up_second(self, i):
        p = self.p
        t = i % 2
        c = pl.ds((i // 2) * self.n, self.n)
        if t == 0:
            return self.copy(self.g_u.at[0, 1 - p.y, :, :, :, c], self.r2_y.at[i // 2], 16 + i, p.at(y=1 - p.y))
        return self.copy(self.g_u.at[1, :, :, 1 - p.x, :, c], self.r2_x.at[i // 2], 16 + i, p.at(x=1 - p.x))

    def up_add_core(self, i):
        self.up_core(i).wait_recv()
        c = slice((i // 2) * self.n, (i // 2 + 1) * self.n)

        def step(b, _):
            at = (b // 8, (b // 2) % 4, b % 2)
            here = (i % 2,) + at + (slice(None), c)
            self.g_u[here] = self.g_u[here] + self.r1_u[(i,) + at]
            return 0

        lax.fori_loop(0, 16, step, 0)
        if i < 2:
            self.up_second(i).start()

    def up_add_second(self, i):
        p = self.p
        self.up_second(i).wait_recv()
        c = slice((i // 2) * self.n, (i // 2 + 1) * self.n)

        def step(b, _):
            if i % 2 == 0:
                here, got = (0, p.y, b // 2, b % 2, slice(None), c), self.r2_y[i // 2, b // 2, b % 2]
            else:
                here, got = (1, b // 4, b % 4, p.x, slice(None), c), self.r2_x[i // 2, b // 4, b % 4]
            self.g_u[here] = self.g_u[here] + got
            return 0

        lax.fori_loop(0, 8, step, 0)

    def left(self):
        for i in (2, 3):
            self.down_core(i).wait_send()
            self.up_core(i).wait_send()
        for t in (0, 1):
            for copy in self.down_second(t):
                copy.wait_send()
            self.up_second(t).wait_send()

    def resume(self):
        for copy in self.resumed():
            copy.start()

    def resumed(self):
        return [self.up_second(2), self.up_second(3), *self.down_third(0), *self.down_third(1)]


def forward_coeffs(s, flags, past, old, ridge, coeffs, coef_t):
    length, basis = past.shape[1], ridge.shape[0]
    samples = ridge.shape[1] - length
    brows = slice(s * basis, (s + 1) * basis)
    diff = (iota((samples, basis), 0) - iota((samples, basis), 1)).astype(F32)
    sampled = jnp.exp(-0.5 * diff * diff).astype(BF)
    keep = (1 - flags[s]).astype(F32)
    old_signal = (dot_nn(sampled, old[s]) * keep).astype(BF)
    co = (dot_nn(ridge[:, :samples], old_signal) + dot_nn(ridge[:, samples:], past[s])).astype(BF)
    coeffs[brows, :] = co
    coef_t[:, brows] = co.T


def forward_projections(s, half, heads, length, basis, hidden, vecs, wmat, wqkv, normed, norm_t, coeffs, qkv, mem, ublk, proj, head_par):
    width = hidden.shape[1]
    hd = width // heads
    rows = slice(s * length, (s + 1) * length)
    brows = slice(s * basis, (s + 1) * basis)
    step = width // 3
    if half == 0:
        unit, _ = norm_parts(hidden[rows, :].astype(F32))
        nrm = (unit * vecs[0:1, :] + vecs[1:2, :]).astype(BF)
        normed[...] = nrm
        norm_t[:, rows] = nrm.T
    for j in range(9) if half == 0 else ():
        cols = slice(j * step, (j + 1) * step)
        y = dot_nn(normed[...], wqkv[:, cols])
        if j < 3:
            y = y + vecs[2:3, cols]
        elif j >= 6:
            y = y + vecs[3:4, (j - 6) * step:(j - 5) * step]
        qkv[rows, cols] = y.astype(BF)
    if half == 0:
        return
    for j in range(6):
        cols = slice(j * step, (j + 1) * step)
        wcols = slice(width + j * step, width + (j + 1) * step)
        mem[brows, cols] = dot_nn(coeffs[brows, :], wqkv[:, wcols]).astype(BF)
    raw = dot_tn(wmat[...], mem[brows, 0:width])[0:32, :]
    own = (iota((32, width), 0) % 16) == (iota((32, width), 1) // hd)
    u = jnp.where(own, raw, 0.0) * (1.0 / math.sqrt(hd))
    ublk[s] = u
    u_hi, u_lo = split_high_low(u)
    q = qkv[rows, 0:width]
    pr = dot_nt(u_hi, q) + dot_nt(u_lo, q)
    proj[s] = pr
    basis_rows(pr, heads, basis, head_par)


def basis_rows(pr, heads, basis, head_par):
    centre = 1.0 / (1.0 + jnp.exp(-pr[0:16]))
    wide = pr[16:32]
    soft = jnp.maximum(wide, 0.0) + jnp.log(1.0 + jnp.exp(-jnp.abs(wide)))
    variance = (soft + 0.5) * 0.02
    inv_root = lax.rsqrt(variance)
    root = inv_root * math.sqrt(0.5 * LOG2E)
    shift_log = jnp.log(inv_root) * LOG2E - math.log2(basis)
    for h in range(heads):
        head_par[h, 0:1, :] = root[h:h + 1]
        head_par[h, 1:2, :] = centre[h:h + 1] * root[h:h + 1]
        head_par[h, 2:3, :] = shift_log[h:h + 1]
    return centre, wide, variance, root


def causal(scores, allowed):
    n = allowed.shape[0]
    last = jnp.where(allowed, scores[-n:], -1e30)
    return last if scores.shape[0] == n else jnp.concatenate([scores[:-n], last], axis=0)


def forward_heads(s, first, last, heads, length, basis, width, qkv, mem, att, lse, head_par, att_t):
    hd = width // heads
    half = length // 2
    rows = slice(s * length, (s + 1) * length)
    brows = slice(s * basis, (s + 1) * basis)
    masks = head_masks(2 * hd, hd)
    scale = LOG2E / math.sqrt(hd)

    def pair(p, _):
        c0 = pl.multiple_of(p * (2 * hd), 2 * hd)
        q = qkv[rows, pl.ds(c0, 2 * hd)]
        k = qkv[rows, pl.ds(pl.multiple_of(width + c0, 2 * hd), 2 * hd)]
        v_t = qkv[rows, pl.ds(pl.multiple_of(2 * width + c0, 2 * hd), 2 * hd)].T
        mv_t = mem[brows, pl.ds(pl.multiple_of(width + c0, 2 * hd), 2 * hd)].T
        cent = ((iota((basis, 1), 0).astype(F32) + 0.5) / basis)
        allowed = iota((half, half), 0) <= iota((half, half), 1)
        for h in range(2):
            head = p * 2 + h
            km = k * masks[h]
            lanes = slice(h * hd, (h + 1) * hd)
            for b in range(2):
                cols = slice(b * half, (b + 1) * half)
                depth = (b + 1) * half
                sc = causal(dot_nt(km[:depth], q[cols]) * scale, allowed)
                top = jnp.max(sc, axis=0, keepdims=True)
                e = jnp.exp2(sc - top)
                total = jnp.sum(e, axis=0, keepdims=True)
                out = dot_nn(v_t[lanes, :depth], e.astype(BF)) / total
                lse[s, head, :, cols] = top + jnp.log(total) * LOG2E
                t = cent * head_par[head, 0:1, cols] - head_par[head, 1:2, cols]
                bas = jnp.exp2(head_par[head, 2:3, cols] - t * t).astype(BF)
                out = out + dot_nn(mv_t[lanes, :], bas)
                att_t[lanes, cols] = out
        att[rows, pl.ds(c0, 2 * hd)] = att_t[...].T.astype(BF)
        return 0

    lax.fori_loop(first, last, pair, 0)


def unpack_small(small, wmat, vecs, ubias, devices, width, ff):
    flat = small.reshape(devices * 32, 128)
    wmat[...] = small.reshape(devices, 32, 128)[:, 0:16, :].reshape(devices * 16, 128)
    every = flat[...]

    def spread(row, offset, each, n):
        pick = (iota((devices, devices * 32), 1) == iota((devices, devices * 32), 0) * 32 + row)
        mine = dot_nn(pick.astype(F32).astype(BF), every).astype(BF)
        place = iota((128, n), 0) == iota((128, n), 1) % each + offset
        wide = dot_nn(mine, place.astype(F32).astype(BF))
        own = iota((devices, n), 1) // each == iota((devices, n), 0)
        return jnp.sum(jnp.where(own, wide, 0.0), axis=0, keepdims=True)

    e = width // devices
    vecs[0:1, :] = spread(16, 0, e, width)
    vecs[1:2, :] = spread(16, e, e, width)
    both = spread(17, 2 * e, 2 * e, 2 * width)
    vecs[2:3, :] = both[:, :width]
    vecs[3:4, :] = both[:, width:]
    vecs[4:5, :] = spread(16, 2 * e, e, width)
    vecs[5:6, :] = spread(16, 3 * e, e, width)
    vecs[6:7, :] = spread(17, 0, e, width)
    vecs[7:8, :] = spread(17, e, e, width)
    up = spread(18, 0, ff // devices, ff)
    chunk = ubias.shape[1]
    ubias[...] = jnp.zeros_like(ubias)
    for j in range(ff // chunk):
        ubias[j:j + 1, :] = up[:, j * chunk:(j + 1) * chunk]


FIRST_STEPS = (
    "#0", "qz1", "qs0", "os0", "qz2", "qs1", "+0", "qz3", "ug", "own", "ot", "qc0", "#1", "qs2", "+1", "qs3", "qc1",
    "uz1", "us0", "oz1", "+2", "uz2", "us1", "oz2", "qc2",
)
LATER_STEPS = (
    ("uz3", "us2", "dg", "oz3", "oc"), ("us3", "uc0", "uc1"), ("dz1",), ("ds0",), ("dz2",), ("ds1",), ("dz3",), ("dc0",),
    (), ("ds2",), (), ("uc2",), ("ds3",), ("dc1",),
)


def forward_kernel(
    heads, devices,
    flags, hidden_h, past_h, old_h, ridge_h, gout_h, small, qkv_s, out_s, up_s, down_s,
    norm_h, coef_h, qkv_h, mem_h, output_h, gmid_h, gatt_h, dout_h, gu_h, gd_h, wq_h,
    lse, ublk, proj, wmat, vecs, vsum, usum,
    hidden, gout, att, wq, wo, wu, wd, ubias,
    wide_s, wide_r, block, block_d, sfull, early, send, recv, local, early_send, early_recv,
):
    place = Place()
    p = place
    tokens, width = hidden.shape
    seqs, length = past_h.shape[0], past_h.shape[1]
    basis = ridge_h.shape[0]
    ff = up_s.shape[1]
    t_qkv, t_out, t_up, t_down = weight_table(width, ff, devices)
    st = Started(send, recv)
    n = Gather.SLOTS
    g_qkv = Gather(place, send, recv, 0, t_qkv, wq)
    g_up = Gather(place, send, recv, n, t_up, wu)
    g_down = Gather(place, send, recv, 2 * n, t_down, wd)
    g_out = LateGather(place, send, recv, 3 * n, t_out, wo)
    base = 4 * n
    nh = wide_r.shape[1]
    blocks = {
        "q": block.at[:, 0:t_qkv.half], "o": block.at[:, t_qkv.half:t_qkv.half + t_out.half],
        "u": block.at[:, t_qkv.half + t_out.half:nh], "d": block_d}
    gather_of = {"q": g_qkv, "o": g_out, "u": g_up, "d": g_down}

    def pass_on(word):
        g, what, n = gather_of[word[0]], word[1], word[2:]
        if what == "g":
            g.start(blocks[word[0]])
        elif what == "z":
            g.on_z(int(n))
        elif what == "s":
            g.on_second(int(n))
        elif what == "t":
            g.on_third()
        elif what == "f":
            g.finish()
        elif n:
            g.core(int(n))
        else:
            g.core()

    stores = []

    def store(src, dst, rows=None):
        i = len(stores)

        def make():
            a, b = (src, dst) if rows is None else (src.at[rows, :], dst.at[rows, :])
            return pltpu.make_async_copy(a, b, local.at[9 + i])

        make().start()
        stores.append(make)

    def attention(norm_t, coef_t, qkv, mem, past, old, ridge, normed, coeffs, head_par, att_t):
        forward_attention(
            heads, devices, place, (flags, hidden_h, past_h, old_h, ridge_h, gout_h, small, qkv_s, out_s, up_s, down_s),
            (t_qkv, t_out, t_up, t_down), st, (g_qkv, g_up, g_down, g_out), base, store, blocks, pass_on,
            (norm_h, coef_h, qkv_h, mem_h, wq_h),
            lse, ublk, proj, wmat, vecs, hidden, gout, norm_t, coef_t, qkv, mem, att, wq, ubias,
            wide_s, wide_r, block, block_d, sfull, local,
            past, old, ridge, normed, coeffs, head_par, att_t)
        for make in stores:
            make().wait()

    pl.run_scoped(
        attention,
        pltpu.VMEM((width, tokens), BF),
        pltpu.VMEM((width, seqs * basis), BF),
        pltpu.VMEM((tokens, 3 * width), BF),
        pltpu.VMEM((seqs * basis, 2 * width), BF),
        pltpu.VMEM(past_h.shape, BF),
        pltpu.VMEM(old_h.shape, BF),
        pltpu.VMEM(ridge_h.shape, BF),
        pltpu.VMEM((length, width), BF),
        pltpu.VMEM((seqs * basis, width), BF),
        pltpu.VMEM((heads, 8, length), F32),
        pltpu.VMEM((2 * (width // heads), length), F32),
    )

    er = EarlyReduce(place, early_send, early_recv, *early)
    sem = 9 + 2 * seqs + 3

    def hook(where, i):
        def at(n, *acts):
            @pl.when(i == n)
            def _():
                for act, arg in acts:
                    act(arg)

        if where == "first":
            er.down_core(i).start()
        elif where == "entered":
            pass_on("uf")
        elif where == "ready":
            for word in ("dc2", "df"):
                pass_on(word)
        elif where == "second":
            er.up_core(i).start()
            at(0, (er.down_add_core, 0))
            at(2, (er.down_add_second, 0))
        elif where == "middle":
            at(2, (er.down_add_core, 1))
        elif where == "both":
            at(0, (er.up_add_core, 0))
            at(1, (er.up_add_core, 1))
        elif where == "leave":
            at(0, (er.up_add_core, 2), (er.up_add_core, 3))
            at(2, (er.up_add_second, 0), (er.up_add_second, 1))
        elif where == "end":
            er.down_add_second(1)

    wflat = wq.reshape(width, 3 * width)

    def feed_forward(*scratch):
        middle_body(
            att, hidden, gout, wo.reshape(width, width), wu.reshape(width, ff), wd.reshape(ff, width), vecs, ubias, vsum, usum,
            wflat.at[:, 0:tokens], wflat.at[:, tokens:tokens + width], *scratch, (output_h, gmid_h, gatt_h, dout_h), local, sem, er.put_down, er.put_up, hook)
        out = [pltpu.make_async_copy(er.g_u, gu_h, local.at[sem + 14]), pltpu.make_async_copy(er.g_d, gd_h, local.at[sem + 15])]
        for copy in out:
            copy.start()
        er.left()
        for g in (g_up, g_down, g_out):
            g.left()
        for copy in out:
            copy.wait()

    pl.run_scoped(feed_forward, *middle_scratch(tokens, width, ubias.shape[1]))


def forward_attention(
    heads, devices, place, inputs, table, st, gathers, base, store, blocks, pass_on, outs,
    lse, ublk, proj, wmat, vecs, hidden, gout, norm_t, coef_t, qkv, mem, att, wq, ubias,
    wide_s, wide_r, block, block_d, sfull, local,
    past, old, ridge, normed, coeffs, head_par, att_t,
):
    p = place
    flags, hidden_h, past_h, old_h, ridge_h, gout_h, small, qkv_s, out_s, up_s, down_s = inputs
    t_qkv, t_out, t_up, t_down = table
    g_qkv, g_up, g_down, g_out = gathers
    norm_h, coef_h, qkv_h, mem_h, wq_h = outs
    tokens, width = hidden.shape
    seqs, length = past.shape[0], past.shape[1]
    basis = ridge.shape[0]
    ff = up_s.shape[1]
    place.hello(place.others())
    loads = []
    for i, (src, dst) in enumerate(((ridge_h, ridge), (old_h, old), (past_h, past), (hidden_h, hidden), (gout_h, gout))):
        copy = pltpu.make_async_copy(src, dst, local.at[i])
        copy.start()
        loads.append(copy)
    pos = 0
    for half in range(2):
        for ref, w in ((qkv_s, t_qkv), (out_s, t_out), (up_s, t_up)):
            wide_s[:, pos:pos + w.half] = ref[:, half * w.half:(half + 1) * w.half].astype(F32)
            pos += w.half
    nh = pos // 2
    sfull[p.y, p.z, p.x, p.c] = small[...]
    ed = down_s.shape[0]
    hd_cols = width // 2
    block_d[pl.ds(pl.multiple_of(p.c * ed, 16), ed), :] = down_s[:, pl.ds(pl.multiple_of(p.c * hd_cols, 128), hd_cols)]

    place.wait_hello(place.others())
    mate = p.at(c=1 - p.c)
    there = pl.multiple_of((1 - p.c) * nh, 128)
    st.go("wide", wide_s.at[:, pl.ds(there, t_qkv.half)], wide_r.at[:, 0:t_qkv.half], base, mate)
    st.go("wide2", wide_s.at[:, pl.ds(pl.multiple_of(there + t_qkv.half, 128), nh - t_qkv.half)], wide_r.at[:, t_qkv.half:nh], base + 8, mate)
    ref = sfull.at[p.y, p.z, p.x, p.c]
    st.go("s0", ref, ref, base + 1, mate)
    st.go("down", down_s.at[:, pl.ds(pl.multiple_of((1 - p.c) * hd_cols, 128), hd_cols)],
          block_d.at[pl.ds(pl.multiple_of(p.c * ed, 16), ed), :], base + 2, mate)

    def make_block(c0, cn):
        mine = wide_s[:, pl.ds(pl.multiple_of(p.c * nh + c0, 128), cn)]
        other = wide_r[:, c0:c0 + cn]
        block[:, c0:c0 + cn] = jnp.concatenate(
            [jnp.where(p.c == 0, mine, other), jnp.where(p.c == 0, other, mine)], axis=0).astype(BF)

    b_qkv, b_out, b_up = blocks["q"], blocks["o"], blocks["u"]
    own = []

    def keep_own(g, src, i):
        copy = pltpu.make_async_copy(src, g.full.at[p.y, p.z, p.x, :, g.w.columns(p.c)], local.at[i])
        copy.start()
        own.append(copy)

    st.arrived("wide")
    make_block(0, t_qkv.half)
    g_qkv.start(b_qkv)
    st.arrived("s0")
    ref = sfull.at[p.y, p.z, p.x]
    for s in (1, 2, 3):
        st.go("sz", ref, ref, base + 2 + s, p.at(z=p.far_z(s)))
    st.arrived("wide2")
    make_block(t_qkv.half, nh - t_qkv.half)
    g_out.start(b_out)
    st.arrived("down")
    for i, (g, src) in enumerate(((g_qkv, b_qkv), (g_out, b_out), (g_up, b_up), (g_down, block_d))):
        keep_own(g, src, 5 + i)
    loads[0].wait()
    loads[1].wait()
    loads[2].wait()
    def small_step(i):
        if i == 0:
            st.arrived("sz")
            ref = sfull.at[p.y, :, p.x]
            st.go("sx", ref, ref, base + 6, p.at(x=1 - p.x))
        elif i == 1:
            st.arrived("sx")
            ref = sfull.at[p.y]
            st.go("sy", ref, ref, base + 7, p.at(y=1 - p.y))
        else:
            st.arrived("sy")
            unpack_small(sfull, wmat, vecs, ubias, devices, width, ff)

    def own_in_place():
        for copy in own:
            copy.wait()

    def perform(word):
        if word == "own":
            own_in_place()
        elif word[0] == "#":
            forward_coeffs(int(word[1]), flags, past, old, ridge, coeffs, coef_t)
        elif word[0] == "+":
            small_step(int(word[1]))
        else:
            pass_on(word)

    for word in FIRST_STEPS:
        perform(word)
    loads[3].wait()
    g_qkv.finish()
    wflat = wq.reshape(width, 3 * width)
    store(wq, wq_h)
    store(coef_t, coef_h)

    def project(s, half):
        forward_projections(s, half, heads, length, basis, hidden, vecs, wmat, wflat, normed, norm_t, coeffs, qkv, mem, ublk, proj, head_par)

    def attend(s, a, b):
        forward_heads(s, a, b, heads, length, basis, width, qkv, mem, att, lse, head_par, att_t)

    events = iter(LATER_STEPS)

    def step(count=1):
        for _ in range(count):
            for word in next(events, ()):
                perform(word)

    pairs = heads // 2
    for s in range(seqs):
        project(s, 0)
        step()
        project(s, 1)
        store(qkv, qkv_h, slice(s * length, (s + 1) * length))
        store(mem, mem_h, slice(s * basis, (s + 1) * basis))
        if s == seqs - 1:
            store(norm_t, norm_h)
        step()
        for a in range(pairs):
            attend(s, a, a + 1)
            step()
    step(99)
    g_out.finish()
    loads[4].wait()
    st.left()
    g_qkv.left()


def forward_call(heads, devices, flags, hidden, past, old, ridge, gout, small, qkv_s, out_s, up_s, down_s):
    seqs, length, width = hidden.shape
    basis = ridge.shape[0]
    tokens = seqs * length
    ff = up_s.shape[1]
    chip = 2 * width // devices
    chip_ff = 2 * ff // devices
    vm = pl.BlockSpec(memory_space=pltpu.VMEM)
    anyw = pl.BlockSpec(memory_space=pl.ANY)
    full = (2, 4, 2, chip, 3 * width)
    n = width // 2
    far = [
        ((width, tokens), BF), ((width, seqs * basis), BF), ((tokens, 3 * width), BF), ((seqs * basis, 2 * width), BF),
        ((tokens, width), BF), ((tokens, width), F32), ((tokens, width), BF),
        ((width, width), BF), ((2, 2, 4, 2, chip, 2 * n), BF), ((2, 2, 2, 2, chip_ff, n), BF), (full, BF)]
    near = [
        ((seqs, heads, 1, length), F32), ((seqs, 32, width), F32), ((seqs, 32, length), F32),
        ((basis, 128), BF), ((8, width), F32), ((8, width), F32), ((8, width), F32)]
    nh = (4 * width + ff) // 2
    slots = 4 * Gather.SLOTS + 9
    return pl.pallas_call(
        lambda *refs: forward_kernel(heads, devices, *refs),
        out_shape=tuple(jax.ShapeDtypeStruct(*m) for m in far + near),
        in_specs=[pl.BlockSpec(memory_space=pltpu.SMEM)] + [anyw] * 5 + [vm] * 5,
        out_specs=[anyw] * len(far) + [vm] * len(near),
        scratch_shapes=[
            pltpu.VMEM((tokens, width), BF),
            pltpu.VMEM((tokens, width), BF),
            pltpu.VMEM((tokens, width), BF),
            pltpu.VMEM(full, BF),
            pltpu.VMEM((2, 4, 2, chip, width), BF),
            pltpu.VMEM((2, 4, 2, chip, ff), BF),
            pltpu.VMEM((2, 4, 2, chip_ff, width), BF),
            pltpu.VMEM((8, width), F32),
            pltpu.VMEM((width // devices, 2 * nh), F32),
            pltpu.VMEM((width // devices, nh), F32),
            pltpu.VMEM((chip, nh), BF),
            pltpu.VMEM((chip_ff, width // 2), BF),
            pltpu.VMEM((2, 4, 2, 2, 32, 128), BF),
            [pltpu.VMEM(shape, BF) for shape in (
                (2, 2, 2, 2, chip_ff, n), (2, 2, 4, 2, chip, 2 * n), (2, 2, 2, chip_ff, n), (2, 2, 4, 2, chip, n),
                (2, 2, 2, 2, chip_ff, n), (4, 2, 4, 2, chip, n),
                (2, 2, 2, 2, chip_ff // 2, n), (2, 4, 2, chip, n), (2, 2, 4, chip, n), (8, 128))],
            pltpu.SemaphoreType.DMA((slots,)),
            pltpu.SemaphoreType.DMA((slots,)),
            pltpu.SemaphoreType.DMA((9 + 2 * seqs + 3 + 17,)),
            pltpu.SemaphoreType.DMA((EarlyReduce.SLOTS,)),
            pltpu.SemaphoreType.DMA((EarlyReduce.SLOTS,)),
        ],
        compiler_params=pltpu.CompilerParams(vmem_limit_bytes=61 * 1024 * 1024, collective_id=0, has_side_effects=True),
        name="forward",
    )(flags, hidden.reshape(tokens, width), past, old, ridge, gout.reshape(tokens, width), small, qkv_s, out_s, up_s, down_s)


def forward_plain_call(heads, flags, hidden, past, old, ridge, wmat, vecs, wqkv):
    seqs, length, width = hidden.shape
    basis = ridge.shape[0]
    tokens = seqs * length
    vm = pl.BlockSpec(memory_space=pltpu.VMEM)

    def kernel(
        flags, hidden, past, old, ridge, wmat, vecs, wqkv,
        norm_t, coef_t, qkv, mem, att, lse, ublk, proj, normed, coeffs, head_par, att_t,
    ):
        for s in range(seqs):
            forward_coeffs(s, flags, past, old, ridge, coeffs, coef_t)
            for half in (0, 1):
                forward_projections(s, half, heads, length, basis, hidden, vecs, wmat, wqkv, normed, norm_t, coeffs, qkv, mem, ublk, proj, head_par)
            forward_heads(s, 0, heads // 2, heads, length, basis, width, qkv, mem, att, lse, head_par, att_t)

    shapes = (
        jax.ShapeDtypeStruct((width, tokens), BF),
        jax.ShapeDtypeStruct((width, seqs * basis), BF),
        jax.ShapeDtypeStruct((tokens, 3 * width), BF),
        jax.ShapeDtypeStruct((seqs * basis, 2 * width), BF),
        jax.ShapeDtypeStruct((tokens, width), BF),
        jax.ShapeDtypeStruct((seqs, heads, 1, length), F32),
        jax.ShapeDtypeStruct((seqs, 32, width), F32),
        jax.ShapeDtypeStruct((seqs, 32, length), F32),
    )
    return pl.pallas_call(
        kernel,
        out_shape=shapes,
        in_specs=[pl.BlockSpec(memory_space=pltpu.SMEM)] + [vm] * 7,
        out_specs=[vm] * 8,
        scratch_shapes=[
            pltpu.VMEM((length, width), BF),
            pltpu.VMEM((seqs * basis, width), BF),
            pltpu.VMEM((heads, 8, length), F32),
            pltpu.VMEM((2 * (width // heads), length), F32),
        ],
        compiler_params=pltpu.CompilerParams(vmem_limit_bytes=VMEM_BYTES),
        name="forward_plain",
    )(flags, hidden.reshape(tokens, width), past, old, ridge, wmat, vecs, wqkv)


def backward_heads(s, p, first, heads, length, basis, width, qkv, mem, gatt, lse, head_par, grows, dq_t, gqkv, gmem):
    hd = width // heads
    half = length // 2
    rows = slice(s * length, (s + 1) * length)
    brows = slice(s * basis, (s + 1) * basis)
    masks = head_masks(2 * hd, hd)
    scale = LOG2E / math.sqrt(hd)
    c0 = pl.multiple_of(p * (2 * hd), 2 * hd)
    c1 = pl.multiple_of(width + c0, 2 * hd)
    c2 = pl.multiple_of(2 * width + c0, 2 * hd)
    here = pl.multiple_of((p - first) * (2 * hd), 2 * hd)
    wide = gmem.shape[1] // 2
    q = qkv[rows, pl.ds(c0, 2 * hd)]
    k = qkv[rows, pl.ds(c1, 2 * hd)]
    v = qkv[rows, pl.ds(c2, 2 * hd)]
    mv = mem[brows, pl.ds(c1, 2 * hd)]
    ga = gatt[rows, pl.ds(c0, 2 * hd)]
    k_t = k.T
    cent = ((iota((basis, 1), 0).astype(F32) + 0.5) / basis)
    allowed = iota((half, half), 0) <= iota((half, half), 1)
    dv = [0.0, 0.0]
    dk = [0.0, 0.0]
    dmv = 0.0
    for h in range(2):
        head = p * 2 + h
        km, vm, mvm, gam, qm = (a * masks[h] for a in (k, v, mv, ga, q))
        lanes = slice(h * hd, (h + 1) * hd)
        for b in range(2):
            cols = slice(b * half, (b + 1) * half)
            depth = (b + 1) * half
            sc = dot_nt(km[:depth], q[cols]) * scale - lse[s, head, :, cols]
            pr = jnp.exp2(causal(sc, allowed))
            dp = dot_nt(vm[:depth], ga[cols])
            inner = jnp.sum(pr * dp, axis=0, keepdims=True)
            ds = (pr * (dp - inner)).astype(BF)
            pb = pr.astype(BF)
            dvb = dot_nn(pb, gam[cols])
            dkb = dot_nn(ds, qm[cols])
            dq_t[pl.ds(pl.multiple_of(here + h * hd, hd), hd), cols] = dot_nn(k_t[lanes, :depth], ds)
            for i in range(b + 1):
                part = slice(i * half, (i + 1) * half)
                dv[i] = dv[i] + dvb[part]
                dk[i] = dk[i] + dkb[part]
            t = cent * head_par[head, 0:1, cols] - head_par[head, 1:2, cols]
            bas = jnp.exp2(head_par[head, 2:3, cols] - t * t)
            e = dot_nt(mvm, ga[cols]) * bas
            et = e * t
            grows[0, pl.ds(head, 1), cols] = jnp.sum(e, axis=0, keepdims=True)
            grows[1, pl.ds(head, 1), cols] = jnp.sum(et, axis=0, keepdims=True)
            grows[2, pl.ds(head, 1), cols] = jnp.sum(et * t, axis=0, keepdims=True)
            dmv = dmv + dot_nn(bas.astype(BF), gam[cols])
    for i in range(2):
        out_rows = slice(s * length + i * half, s * length + (i + 1) * half)
        gqkv[out_rows, pl.ds(c1, 2 * hd)] = (dk[i] * (1.0 / math.sqrt(hd))).astype(BF)
        gqkv[out_rows, pl.ds(c2, 2 * hd)] = dv[i].astype(BF)
    gmem[brows, pl.ds(pl.multiple_of(wide + here, 2 * hd), 2 * hd)] = dmv.astype(BF)


def backward_finish(s, start, heads, rows_of, qkv, mem, ublk, grows, dq_t, wmat, gqkv, gmem, msum):
    centre, wide, variance, root = rows_of
    n, length = dq_t.shape
    width = ublk.shape[2]
    basis = wmat.shape[0]
    hd = width // heads
    rows = slice(s * length, (s + 1) * length)
    brows = slice(s * basis, (s + 1) * basis)
    cols = slice(start, start + n)
    inv_var = 1.0 / variance
    s0, s1, s2 = grows[0], grows[1], grows[2]
    to_centre = s1 * (inv_var / root) * centre * (1.0 - centre)
    wide_slope = 0.02 / (1.0 + jnp.exp(-wide))
    to_wide = (-0.5 * s0 * inv_var + s2 * (0.5 * inv_var * inv_var) / (root * root)) * wide_slope
    head = iota((16, length), 0)
    live = (head >= start // hd) & (head < (start + n) // hd)
    g = jnp.concatenate([jnp.where(live, to_centre, 0.0), jnp.where(live, to_wide, 0.0)], axis=0)
    g_hi, g_lo = split_high_low(g)
    u_hi, u_lo = split_high_low(ublk[s, :, cols])
    dqm = dot_tn(u_hi, g_hi) + dot_tn(u_hi, g_lo) + dot_tn(u_lo, g_hi)
    total = dq_t[...] * (1.0 / math.sqrt(hd)) + dqm
    gqkv[rows, cols] = total.T.astype(BF)
    q = qkv[rows, cols]
    own = (iota((32, n), 0) % 16) == (iota((32, n), 1) + start) // hd
    r = dot_nn(g_hi, q) + dot_nn(g_lo, q)
    r = jnp.where(own, r, 0.0) * (1.0 / math.sqrt(hd))
    r_hi, r_lo = split_high_low(r)
    w = wmat[...][:, 0:32]
    gmem[brows, 0:n] = (dot_nn(w, r_hi) + dot_nn(w, r_lo)).astype(BF)
    mk = mem[brows, cols]
    add = dot_nt(r_hi, mk) + dot_nt(r_lo, mk)
    if msum.shape[0] == 32:
        msum[...] += add
    else:
        some, at = n // hd, start // hd
        msum[...] += jnp.concatenate([add[at:at + some], add[16 + at:16 + at + some]], axis=0)


def backward_input(r, width, hid, gm, gqkv, wqkv, vecs, gin, vsum):
    g = dot_nt(gqkv[r, :], wqkv[...])
    unit, inv = norm_parts(hid.astype(F32))
    gin[...] = (gm + norm_back(g, unit, inv, vecs[0:1, :])).astype(BF)
    vsum[0:1, :] += jnp.sum(g * unit, axis=0, keepdims=True)
    vsum[1:2, :] += jnp.sum(g, axis=0, keepdims=True)


def bias_sums(width, gqkv, out):
    out[0:1, :] = jnp.sum(gqkv[:, 0:width].astype(F32), axis=0, keepdims=True)
    out[1:2, :] = jnp.sum(gqkv[:, 2 * width:3 * width].astype(F32), axis=0, keepdims=True)


def backward_plain_call(heads, hidden, norm_t, coef_t, qkv, mem, gatt, gmid, lse, ublk, proj, wmat, vecs, wqkv):
    seqs, length, width = hidden.shape
    tokens = seqs * length
    brows = coef_t.shape[1]
    basis = brows // seqs
    vm = pl.BlockSpec(memory_space=pltpu.VMEM)

    def kernel(
        hidden, norm_t, coef_t, qkv, mem, gatt, gmid, lse, ublk, proj, wmat, vecs, wqkv,
        gin, dqkv, vsum, msum, gqkv, gmem, head_par, grows, dq_t,
    ):
        vsum[...] = jnp.zeros_like(vsum)
        msum[...] = jnp.zeros_like(msum)
        grows[...] = jnp.zeros_like(grows)
        for s in range(seqs):
            rows_of = basis_rows(proj[s], heads, basis, head_par)

            def pair(p, _):
                backward_heads(s, p, 0, heads, length, basis, width, qkv, mem, gatt, lse, head_par, grows, dq_t, gqkv, gmem)
                return 0

            lax.fori_loop(0, heads // 2, pair, 0)
            backward_finish(s, 0, heads, rows_of, qkv, mem, ublk, grows, dq_t, wmat, gqkv, gmem, msum)
        step = width // 3
        for j in range(9):
            c = slice(j * step, (j + 1) * step)
            y = dot_nn(norm_t[...], gqkv[:, c])
            if j >= 3:
                y = y + dot_nn(coef_t[...], gmem[:, (j - 3) * step:(j - 2) * step])
            dqkv[:, c] = y.astype(BF)

        def last(i, _):
            r = pl.ds(pl.multiple_of(i * 256, 256), 256)
            backward_input(r, width, hidden[r, :], gmid[r, :], gqkv, wqkv, vecs, gin.at[r, :], vsum.at[2:4, :])
            return 0

        lax.fori_loop(0, tokens // 256, last, 0)
        bias_sums(width, gqkv, vsum)

    shapes = (
        jax.ShapeDtypeStruct((tokens, width), BF),
        jax.ShapeDtypeStruct((width, 3 * width), BF),
        jax.ShapeDtypeStruct((8, width), F32),
        jax.ShapeDtypeStruct((32, basis), F32),
    )
    return pl.pallas_call(
        kernel,
        out_shape=shapes,
        in_specs=[vm] * 13,
        out_specs=[vm] * 4,
        scratch_shapes=[
            pltpu.VMEM((tokens, 3 * width), BF),
            pltpu.VMEM((brows, 2 * width), BF),
            pltpu.VMEM((heads, 8, length), F32),
            pltpu.VMEM((3, 16, length), F32),
            pltpu.VMEM((width, length), F32),
        ],
        compiler_params=pltpu.CompilerParams(vmem_limit_bytes=VMEM_BYTES),
        name="backward_plain",
    )(hidden.reshape(tokens, width), norm_t, coef_t, qkv, mem, gatt, gmid, lse, ublk, proj, wmat, vecs, wqkv)


class Reduce:
    SLOTS = 13

    def __init__(self, place, started, name, base, parts, bufs):
        self.p, self.s, self.name, self.base, self.parts = place, started, name, base, parts
        self.g, self.r1, self.r2, self.r3, self.r4, self.f = bufs

    def where(self, part):
        r0, rn, c0, cn = self.parts[part]
        return pl.ds(r0, rn), pl.ds(c0, cn)

    def core(self, *pieces):
        for i, (src, rows) in enumerate(pieces):
            self.s.go((self.name, 1), src, self.r1.at[:, :, :, rows, :], self.base + i, self.p.at(c=1 - self.p.c))

    def second(self):
        p = self.p
        self.s.arrived((self.name, 1))

        def step(i, _):
            at = (i // 8, (i // 2) % 4, i % 2)
            self.g[at] = self.g[at] + self.r1[at]
            return 0

        lax.fori_loop(0, 16, step, 0)
        for part in (0, 1):
            r, c = self.where(part)
            if part == 0:
                self.s.go((self.name, 2), self.g.at[1 - p.y, :, :, r, c], self.r2[0], self.base + 2, p.at(y=1 - p.y))
            else:
                self.s.go((self.name, 2), self.g.at[:, :, 1 - p.x, r, c], self.r2[1], self.base + 3, p.at(x=1 - p.x))

    def third(self):
        p = self.p
        self.s.arrived((self.name, 2))
        r, c = self.where(0)
        r_b, c_b = self.where(1)

        def step(i, _):
            z, k = i // 2, i % 2
            self.g[p.y, z, k, r, c] = self.g[p.y, z, k, r, c] + self.r2[0][z, k]
            self.g[k, z, p.x, r_b, c_b] = self.g[k, z, p.x, r_b, c_b] + self.r2[1][k, z]
            return 0

        lax.fori_loop(0, 8, step, 0)
        for part in (0, 1):
            self.send_third(part)

    def send_third(self, part):
        p = self.p
        r, c = self.where(part)
        if part == 0:
            self.s.go((self.name, 3), self.g.at[p.y, :, 1 - p.x, r, c], self.r3[0], self.base + 4, p.at(x=1 - p.x))
        else:
            self.s.go((self.name, 3), self.g.at[1 - p.y, :, p.x, r, c], self.r3[1], self.base + 5, p.at(y=1 - p.y))

    def along(self):
        p = self.p
        self.s.arrived((self.name, 3))

        def step(z, _):
            for part in self.parts:
                r, c = self.where(part)
                self.g[p.y, z, p.x, r, c] = self.g[p.y, z, p.x, r, c] + self.r3[part][z]
            return 0

        lax.fori_loop(0, 4, step, 0)
        self.send_along()

    early = None

    def summand(self, z):
        p = self.p
        return self.g.at[p.y, z, p.x] if self.early is None else self.early.at[z // 2, p.y, z % 2, p.x]

    def send_along(self):
        p = self.p
        for s in (1, 2, 3):
            to = p.far_z(s)
            self.s.go((self.name, 4), self.summand(to), self.r4.at[s - 1], self.base + 5 + s, p.at(z=to))

    def last(self, out, segments):
        p = self.p
        self.s.arrived((self.name, 4))
        own = self.summand(p.z)[...].astype(F32)
        self.f[...] = (own + self.r4[0].astype(F32)) + (self.r4[1].astype(F32) + self.r4[2].astype(F32))
        n = self.f.shape[0] // 2
        theirs = pl.ds(pl.multiple_of((1 - p.c) * n, 8), n)
        mine = pl.ds(pl.multiple_of(p.c * n, 8), n)
        for i, (c0, to, cn) in enumerate(segments):
            there = out.at[:, pl.ds(pl.multiple_of(to, 128), cn)]
            self.s.go((self.name, 5), self.f.at[theirs, pl.ds(c0, cn)], there, self.base + 9 + i, p.at(c=1 - p.c))
            there[...] = self.f[mine, c0:c0 + cn]

    def done(self):
        self.s.arrived((self.name, 5))


class Everywhere:
    SLOTS = 8

    def __init__(self, place, started, name, slot, held, got):
        self.p, self.s, self.name, self.slot, self.held, self.got = place, started, name, slot, held, got
        n = held.shape[-1] // 2
        self.half = pl.ds(pl.multiple_of(place.c * n, 128), n)

    def start(self, step):
        p, name, half = self.p, (self.name, step), self.half
        if step == 0:
            self.s.go(name, self.held.at[0], self.got.at[0], self.slot, p.at(c=1 - p.c))
        elif step == 1:
            for d in (1, 2, 3):
                to = p.at(y=(p.y + d // 2) % 2, x=(p.x + d) % 2)
                self.s.go(name, self.held.at[1, :, half], self.got.at[d, :, half], self.slot + d, to)
        elif step == 2:
            for s in (1, 2, 3):
                self.s.go(name, self.held.at[2, :, half], self.got.at[3 + s, :, half], self.slot + 3 + s, p.at(z=p.far_z(s)))
        else:
            ref = self.held.at[3, :, half]
            self.s.go(name, ref, ref, self.slot + 7, p.at(c=1 - p.c))

    def add(self, step):
        self.s.arrived((self.name, step))
        half = self.half
        if step == 0:
            self.held[1] = self.held[0] + self.got[0]
        elif step < 3:
            i = 1 if step == 1 else 4
            self.held[step + 1, :, half] = (self.held[step, :, half] + self.got[i, :, half]) + (
                self.got[i + 1, :, half] + self.got[i + 2, :, half])
        else:
            return self.held[3]
        self.start(step + 1)
        return None


BACK_STEPS = (
    (), (), (), (),
    ("xx", "o1"), ("p1",), ("a3", "b3"), ("o2",),
    ("q1",), ("p2",), ("o3",), ("p3", "q2"),
    ("r1",), ("q3",), ("w0", "k0"), ("r2", "w1", "k1"),
    ("l0",), ("r3", "l1", "w2", "k2"), ("l2", "w3", "k3", "d4", "a4", "b4", "p4", "o4", "q4"), ("l3", "r4"),
)


def backward_kernel(
    heads, devices,
    hidden, norm_h, coef_h, qkv_h, mem_h, gatt_h, gmid, lse, ublk, proj, wmat, vecs, vsum_a, usum, wq_h, p_out, gu_h, gd_h,
    gin, o_qkv, o_out, o_up, o_down, early, late, msum,
    norm_t, coef_t, qkv, mem, gatt, wq,
    gqkv, gmem, head_par, grows, dq_t, away, gm_buf, hid_buf, gin_buf,
    bufs, vsum, k_held, k_got, l_held, l_got, m_held, m_got, early_bufs, send, recv, local, early_send, early_recv,
):
    place = Place()
    p = place
    tokens, width = hidden.shape
    seqs, _, length = proj.shape
    basis = wmat.shape[0]
    ff = o_up.shape[1]
    st = Started(send, recv)
    names = "abdopqr"
    red = {n: Reduce(place, st, n, i * Reduce.SLOTS, parts, bufs[i]) for i, (n, (_, _, parts)) in enumerate(zip(names, reduce_shapes(width, ff, devices)))}
    base = len(names) * Reduce.SLOTS
    sums = {n: Everywhere(place, st, n, base + i * Everywhere.SLOTS, held, got)
            for i, (n, held, got) in enumerate((("k", k_held, k_got), ("w", m_held, m_got), ("l", l_held, l_got)))}
    loads = []
    for i, (src, dst) in enumerate(((qkv_h, qkv), (mem_h, mem), (gatt_h, gatt), (norm_h, norm_t), (coef_h, coef_t), (wq_h, wq))):
        copy = pltpu.make_async_copy(src, dst, local.at[i])
        copy.start()
        loads.append(copy)
    grows[...] = jnp.zeros_like(grows)
    vsum[...] = jnp.zeros_like(vsum)
    k_held[0] = jnp.concatenate([vsum_a[0:4, :], usum[0:4, :], jnp.zeros((8, width), F32)], axis=0)
    half = width // 2

    def side(c):
        return p_out.at[:, :, :, :, pl.ds(pl.multiple_of(c * half, 128), half)]

    er = EarlyReduce(place, early_send, early_recv, *early_bufs[:2], None, None, None, None, None, *early_bufs[2:])
    red["a"].g, red["b"].g, red["d"].early = er.g_u.at[0], er.g_u.at[1], er.g_d
    own = [pltpu.make_async_copy(src, dst, local.at[6 + i])
           for i, (src, dst) in enumerate(((gu_h, er.g_u), (gd_h, er.g_d), (side(p.c), red["o"].g)))]
    for copy in own:
        copy.start()
    place.hello(place.layer())

    def begin():
        place.wait_hello(place.layer())
        red["o"].core((side(1 - p.c), slice(None)))
        for copy in own:
            copy.wait()
        er.resume()
    pieces = 128
    outs = {
        "a": (o_up, lambda: [(k * half, k * width + p.c * half, half) for k in (0, 1)]),
        "b": (o_up, lambda: [(k * half, (2 + k) * width + p.c * half, half) for k in (0, 1)]),
        "d": (o_down, lambda: [(0, p.c * half, half)]),
        "o": (o_out, lambda: [(0, p.c * half, half)]),
    }
    for i, n in enumerate("pqr"):
        outs[n] = (o_qkv, lambda i=i: [(j * pieces, j * width + i * 2 * pieces + p.c * pieces, pieces) for j in range(3)])

    def perform(word):
        if word[0] == "x":
            er.up_add_second(2)
            er.up_add_second(3)
            red["a"].send_third(0)
            red["b"].send_third(1)
            er.down_add_third(0)
            er.down_add_third(1)
            red["d"].send_along()
        elif word[0] in sums:
            total, step = sums[word[0]], int(word[1])
            value = total.add(step)
            if step == 3:
                if word[0] == "w":
                    msum[...] = value
                elif word[0] == "l":
                    late[0:2, :] = value
                else:
                    early[...] = value[0:8]
                    late[2:4, :] = value[8:10]
        else:
            r, step = red[word[0]], word[1]
            if step == "1":
                r.second()
            elif step == "2":
                r.third()
            elif step == "3":
                r.along()
            else:
                out, segments = outs[word[0]]
                r.last(out, segments())

    steps = iter(BACK_STEPS)

    def advance():
        for word in next(steps, ()):
            perform(word)

    for copy in loads[:3]:
        copy.wait()
    chunk = 2 * pieces
    m_held[...] = jnp.zeros_like(m_held)
    rows_of = [basis_rows(proj[s], heads, basis, head_par.at[s]) for s in range(seqs)]
    for i in range(3):
        for s in range(seqs):
            for k in range(2):
                def one(j, _):
                    backward_heads(s, j, 2 * i, heads, length, basis, width, qkv, mem, gatt, lse, head_par.at[s], grows, dq_t, gqkv, gmem)
                    return 0

                lax.fori_loop(2 * i + k, 2 * i + k + 1, one, 0)
                if i + s + k == 0:
                    begin()
                if k == 0:
                    advance()
            backward_finish(s, i * chunk, heads, rows_of[s], qkv, mem, ublk, grows, dq_t, wmat, gqkv, gmem, m_held.at[0, 8 * i:8 * i + 8, :])
            if s < seqs - 1:
                advance()
        if i == 0:
            loads[3].wait()
            loads[4].wait()
        r = red["pqr"[i]]
        for j in range(3):
            c = j * width + i * chunk
            y = dot_nn(norm_t[...], gqkv[:, c:c + chunk])
            if j > 0:
                y = y + dot_nn(coef_t[...], gmem[:, (j - 1) * chunk:j * chunk])
            y = y.astype(BF).reshape(2, 4, 2, r.g.shape[3], chunk)
            low, high = y[..., :pieces], y[..., pieces:]
            keep, give = jnp.where(p.c == 0, low, high), jnp.where(p.c == 0, high, low)
            r.g[:, :, :, :, j * pieces:(j + 1) * pieces] = keep
            away[i, :, :, :, :, j * pieces:(j + 1) * pieces] = give
        r.core((away.at[i], slice(None)))
        if i == 2:
            sums["w"].start(0)
            bias_sums(width, gqkv, k_held.at[0, 8:10, :])
            sums["k"].start(0)
        advance()
    wflat = wq.reshape(width, 3 * width)
    loads[5].wait()
    blocks = tokens // 256

    def fetch(i):
        r = slice(i * 256, (i + 1) * 256)
        return (pltpu.make_async_copy(gmid.at[r, :], gm_buf.at[i % 2], local.at[16 + i % 2]),
                pltpu.make_async_copy(hidden.at[r, :], hid_buf.at[i % 2], local.at[18 + i % 2]))

    def emit(i):
        return pltpu.make_async_copy(gin_buf.at[i % 2], gin.at[i * 256:(i + 1) * 256, :], local.at[20 + i % 2])

    for i in (0, 1):
        for copy in fetch(i):
            copy.start()
    for i in range(blocks):
        for copy in fetch(i):
            copy.wait()
        if i >= 2:
            emit(i - 2).wait()
        backward_input(slice(i * 256, (i + 1) * 256), width, hid_buf[i % 2], gm_buf[i % 2], gqkv, wflat, vecs, gin_buf.at[i % 2], vsum)
        emit(i).start()
        if i + 2 < blocks:
            for copy in fetch(i + 2):
                copy.start()
        if i == blocks - 1:
            l_held[0] = vsum[...]
            sums["l"].start(0)
        advance()
    for _ in range(99):
        advance()
    for n in names:
        red[n].done()
    for i in (blocks - 2, blocks - 1):
        emit(i).wait()
    for copy in er.resumed():
        copy.wait_send()
    st.left()


def reduce_shapes(width, ff, devices):
    chip, chip_ff = 2 * width // devices, 2 * ff // devices
    h = width // 2
    more = (chip, h, {0: (0, chip, 0, 256), 1: (0, chip, 256, 128)})
    less = (chip, h, {0: (0, chip, 0, 128), 1: (0, chip, 128, 256)})
    return [(chip, width, {0: (0, chip, 0, width)}), (chip, width, {1: (0, chip, 0, width)}), (chip_ff, h, {}), more, less, more, less]


def backward_call(
    heads, devices, hidden, norm_t, coef_t, qkv, mem, gatt, gmid, lse, ublk, proj, wmat, vecs, vsum_a, usum, wq, p_out, g_up, g_down, ff,
):
    seqs, length, width = hidden.shape
    tokens = seqs * length
    brows = coef_t.shape[1]
    basis = brows // seqs
    vm = pl.BlockSpec(memory_space=pltpu.VMEM)
    anyw = pl.BlockSpec(memory_space=pl.ANY)
    shapes = (
        jax.ShapeDtypeStruct((tokens, width), BF),
        jax.ShapeDtypeStruct((width // devices, 3 * width), F32),
        jax.ShapeDtypeStruct((width // devices, width), F32),
        jax.ShapeDtypeStruct((width // devices, ff), F32),
        jax.ShapeDtypeStruct((ff // devices, width), F32),
        jax.ShapeDtypeStruct((8, width), F32),
        jax.ShapeDtypeStruct((4, width), F32),
        jax.ShapeDtypeStruct((24, basis), F32),
    )

    def buffers(i, shape):
        rows, cols, parts = shape
        none = pltpu.VMEM((8, 128), F32)
        whole = i > 2
        sizes = [parts.get(k, (0, 16, 0, 128)) for k in (0, 1)]
        (_, ra, _, ca), (_, rb, _, cb) = sizes
        return (
            none if i < 3 else pltpu.VMEM((2, 4, 2, rows, cols), BF),
            pltpu.VMEM((2, 4, 2, rows, cols), BF) if whole else none,
            (pltpu.VMEM((4, 2, ra, ca), BF), pltpu.VMEM((2, 4, rb, cb), BF)) if whole else (none, none),
            (pltpu.VMEM((4, ra, ca), BF), pltpu.VMEM((4, rb, cb), BF)),
            pltpu.VMEM((3, rows, cols), BF),
            pltpu.VMEM((rows, cols), F32),
        )

    chip, chip_ff = 2 * width // devices, 2 * ff // devices
    table = reduce_shapes(width, ff, devices)
    slots = len(table) * Reduce.SLOTS + 3 * Everywhere.SLOTS
    return pl.pallas_call(
        lambda *refs: backward_kernel(heads, devices, *refs),
        out_shape=shapes,
        in_specs=[anyw] * 7 + [vm] * 7 + [anyw] * 4,
        out_specs=[anyw] + [vm] * 7,
        scratch_shapes=[pltpu.VMEM(a.shape, a.dtype) for a in (norm_t, coef_t, qkv, mem, gatt, wq)] + [
            pltpu.VMEM((tokens, 3 * width), BF),
            pltpu.VMEM((brows, 512), BF),
            pltpu.VMEM((seqs, heads, 8, length), F32),
            pltpu.VMEM((3, 16, length), F32),
            pltpu.VMEM((256, length), F32),
            pltpu.VMEM((3, 2, 4, 2, 2 * width // devices, 384), BF),
            pltpu.VMEM((2, 256, width), F32),
            pltpu.VMEM((2, 256, width), BF),
            pltpu.VMEM((2, 256, width), BF),
            [buffers(i, shape) for i, shape in enumerate(table)],
            pltpu.VMEM((2, width), F32),
            pltpu.VMEM((4, 16, width), F32),
            pltpu.VMEM((7, 16, width), F32),
            pltpu.VMEM((4, 2, width), F32),
            pltpu.VMEM((7, 2, width), F32),
            pltpu.VMEM((4, 24, basis), F32),
            pltpu.VMEM((7, 24, basis), F32),
            [pltpu.VMEM(shape, BF) for shape in (
                g_down.shape, g_up.shape, (2, 4, 2, chip, width // 2), (2, 2, 4, chip, width // 2), (2, 2, 2, chip_ff // 2, width // 2))],
            pltpu.SemaphoreType.DMA((slots,)),
            pltpu.SemaphoreType.DMA((slots,)),
            pltpu.SemaphoreType.DMA((22,)),
            pltpu.SemaphoreType.DMA((EarlyReduce.SLOTS,)),
            pltpu.SemaphoreType.DMA((EarlyReduce.SLOTS,)),
        ],
        compiler_params=pltpu.CompilerParams(vmem_limit_bytes=56 * 1024 * 1024, collective_id=1, has_side_effects=True),
        name="backward",
    )(hidden.reshape(tokens, width), norm_t, coef_t, qkv, mem, gatt, gmid, lse, ublk, proj, wmat, vecs, vsum_a, usum, wq, p_out, g_up, g_down)


def finish_call(heads, devices, ff, early, late, msum, whole):
    width = early.shape[1]
    basis = msum.shape[1]
    e, rows = width // devices, basis // devices
    group = 4
    vm = pl.BlockSpec(memory_space=pltpu.VMEM)
    anyw = pl.BlockSpec(memory_space=pl.ANY)
    n = len(whole)

    def kernel(*refs):
        early, late, msum = refs[:3]
        sources, results = refs[3:3 + n], refs[3 + n:3 + 2 * n]
        gain_a, shift_a, qv, out_b, gain_m, shift_m, up_b, down_b, mean, wide = refs[3 + 2 * n:-1]
        sem = refs[-1]
        copies = [pltpu.make_async_copy(a, b, sem.at[i]) for i, (a, b) in enumerate(zip(sources, results))]
        for copy in copies:
            copy.start()
        me = lax.axis_index("dp") * lax.axis_size("fsdp") + lax.axis_index("fsdp")

        def thirds(x):
            high = x.astype(BF)
            rest = x - high.astype(F32)
            middle = rest.astype(BF)
            return high, middle, (rest - middle.astype(F32)).astype(BF)

        def pick(x, start, size):
            at = (iota((x.shape[1], size), 0) == iota((x.shape[1], size), 1) + start).astype(F32).astype(BF)
            return sum(dot_nn(part, at) for part in thirds(x))

        def row_of(x, i):
            return jnp.sum(jnp.where(iota(x.shape, 0) == i, x, 0.0), axis=0, keepdims=True)

        some = pick(early[...], me * e, e)
        down_b[...], gain_m[...], shift_m[...], out_b[...] = (some[i:i + 1] for i in range(4))
        some = pick(late[...], me * e, e)
        gain_a[...], shift_a[...] = some[0:1], some[1:2]
        k = devices // 2
        qv[...] = pick(row_of(late[2:4, :], me // k), me % k * 2 * e, 2 * e)
        k = devices * width // ff
        up_b[...] = pick(row_of(early[4:8, :], me // k), me % k * (ff // devices), ff // devices)
        at = (iota((rows, basis), 1) == iota((rows, basis), 0) + me * rows).astype(F32).astype(BF)
        for out, first in ((mean, 0), (wide, group)):
            x = jnp.concatenate([msum[i + first:i + first + group, :] for i in range(0, 2 * heads, 2 * group)], axis=0)
            out[...] = sum(dot_nt(at, part) for part in thirds(x))
        for copy in copies:
            copy.wait()

    small = [(1, e), (1, e), (1, 2 * e), (1, e), (1, e), (1, e), (1, ff // devices), (1, e), (rows, heads), (rows, heads)]
    return pl.pallas_call(
        kernel,
        out_shape=[jax.ShapeDtypeStruct(a.shape, a.dtype) for a in whole] + [jax.ShapeDtypeStruct(s, F32) for s in small],
        in_specs=[vm] * (3 + n),
        out_specs=[anyw] * n + [vm] * len(small),
        scratch_shapes=[pltpu.SemaphoreType.DMA((n,))],
        name="finish",
    )(early, late, msum, *whole)


def gather(x):
    return lax.all_gather(x, AXES, axis=0, tiled=True)


def scatter(x):
    return lax.psum_scatter(x, AXES, scatter_dimension=0, tiled=True)


def shards_plain(
    hidden, grad_out, past_states, old_coeffs, fresh_flags, ridge_map,
    gain_attn, shift_attn, qkv_weight, qv_bias, out_weight, out_bias,
    gain_mlp, shift_mlp, up_weight, up_bias, down_weight, down_bias,
    mean_weight, width_weight,
):
    seqs, length, width = hidden.shape
    heads = mean_weight.shape[1]
    devices = lax.axis_size("dp") * lax.axis_size("fsdp")
    full_qkv, full_out, full_up, full_down = (gather(w) for w in (qkv_weight, out_weight, up_weight, down_weight))
    rows = jnp.zeros((mean_weight.shape[0], 128), BF)
    rows = rows.at[:, 0:heads].set(mean_weight).at[:, 16:16 + heads].set(width_weight)
    wmat = gather(rows)
    full_qv = gather(qv_bias)
    vecs = jnp.stack(
        [gather(gain_attn), gather(shift_attn), full_qv[:width], full_qv[width:],
         gather(out_bias), gather(gain_mlp), gather(shift_mlp), gather(down_bias)]).astype(F32)
    ubias = gather(up_bias).astype(F32).reshape(-1, width)
    ubias = jnp.concatenate([ubias, jnp.zeros((8 - ubias.shape[0], width), F32)], axis=0)

    norm_t, coef_t, qkv, mem, att, lse, ublk, proj = forward_plain_call(
        heads, fresh_flags, hidden, past_states, old_coeffs, ridge_map, wmat, vecs, full_qkv)
    output, gmid, gatt, dout, dup, ddown, vsum_a, usum = middle_call(
        att, hidden, grad_out, full_out, full_up, full_down, vecs, ubias)
    gin, dqkv, vsum_b, msum = backward_plain_call(
        heads, hidden, norm_t, coef_t, qkv, mem, gatt, gmid, lse, ublk, proj, wmat, vecs, full_qkv)

    up_sum = usum.reshape(-1)[:up_bias.shape[0] * devices]
    big = [scatter(a.astype(F32)) for a in (dqkv, dout, dup, ddown)]
    small = [
        scatter(a) for a in (
            vsum_b[2], vsum_b[3], jnp.concatenate([vsum_b[0], vsum_b[1]]), vsum_a[3], vsum_a[1], vsum_a[2],
            up_sum, vsum_a[0], msum[0:heads].T, msum[16:16 + heads].T)
    ]
    return (
        output.reshape(seqs, length, width), gin.reshape(seqs, length, width),
        small[0], small[1], big[0], small[2], big[1], small[3], small[4], small[5],
        big[2], small[6], big[3], small[7], small[8], small[9],
    )


def shards_block(
    hidden, grad_out, past_states, old_coeffs, fresh_flags, ridge_map,
    gain_attn, shift_attn, qkv_weight, qv_bias, out_weight, out_bias,
    gain_mlp, shift_mlp, up_weight, up_bias, down_weight, down_bias,
    mean_weight, width_weight,
):
    seqs, length, width = hidden.shape
    heads = mean_weight.shape[1]
    devices = 32
    ff = up_weight.shape[1]
    e = width // devices
    def put(v, row, col):
        v = v.reshape((1, -1)) if v.ndim == 1 else v
        return jnp.pad(v, ((row, 32 - row - v.shape[0]), (col, 128 - col - v.shape[1])))

    small = (
        put(mean_weight, 0, 0) + put(width_weight, 0, 16)
        + put(gain_attn, 16, 0) + put(shift_attn, 16, e) + put(out_bias, 16, 2 * e) + put(gain_mlp, 16, 3 * e)
        + put(shift_mlp, 17, 0) + put(down_bias, 17, e) + put(qv_bias, 17, 2 * e) + put(up_bias, 18, 0))

    norm_t, coef_t, qkv, mem, output, gmid, gatt, dout, g_up, g_down, wq, lse, ublk, proj, wmat, vecs, vsum_a, usum = forward_call(
        heads, devices, fresh_flags, hidden, past_states, old_coeffs, ridge_map, grad_out, small, qkv_weight, out_weight, up_weight, down_weight)
    gin, d_qkv, d_out, d_up, d_down, early, late, msum = backward_call(
        heads, devices, hidden, norm_t, coef_t, qkv, mem, gatt, gmid, lse, ublk, proj, wmat, vecs, vsum_a, usum, wq,
        dout.reshape(2, 4, 2, width // 16, width), g_up, g_down, ff)

    (output, gin, d_qkv, d_out, d_up, d_down, gain_a, shift_a, qv, out_b, gain_m, shift_m, up_b, down_b, mean, wide) = finish_call(
        heads, devices, ff, early, late, msum, (output, gin, d_qkv, d_out, d_up, d_down))
    flat = lambda v: v.reshape(v.shape[1])
    return (
        output.reshape(seqs, length, width), gin.reshape(seqs, length, width),
        flat(gain_a), flat(shift_a), d_qkv, flat(qv), d_out, flat(out_b), flat(gain_m), flat(shift_m),
        d_up, flat(up_b), d_down, flat(down_b), mean, wide,
    )


def solution(mesh):
    rows = P(AXES, None)
    cube = P(AXES, None, None)
    one = P(AXES)
    in_specs = (cube, cube, cube, cube, one, P(), one, one, rows, one, rows, one, one, one, rows, one, rows, one, rows, rows)
    out_specs = (cube, cube, one, one, rows, one, rows, one, one, one, rows, one, rows, one, rows, rows)
    body = shards_block if mesh.shape["dp"] == 2 and mesh.shape["fsdp"] == 16 else shards_plain
    return jax.shard_map(body, mesh=mesh, in_specs=in_specs, out_specs=out_specs, check_vma=False)
```

```python
import math

import jax
import jax.numpy as jnp
from jax import lax
from jax.experimental import pallas as pl
from jax.experimental.pallas import tpu as pltpu
from jax.sharding import PartitionSpec as P

EPS = 1e-05
LOG2E = 1.4426950408889634
BF = jnp.bfloat16
F32 = jnp.float32
AXES = ("dp", "fsdp")
VMEM_BYTES = 60 * 1024 * 1024


def dot_nn(a, b):
    return lax.dot_general(a, b, (((1,), (0,)), ((), ())), preferred_element_type=F32)


def dot_nt(a, b):
    return lax.dot_general(a, b, (((1,), (1,)), ((), ())), preferred_element_type=F32)


def dot_tn(a, b):
    return lax.dot_general(a, b, (((0,), (0,)), ((), ())), preferred_element_type=F32)


def split_high_low(x):
    high = x.astype(BF)
    return high, (x - high.astype(F32)).astype(BF)


def iota(shape, dim):
    return lax.broadcasted_iota(jnp.int32, shape, dim)


def head_masks(pair_lanes, head_dim):
    lane = iota((1, pair_lanes), 1)
    return [((lane // head_dim) == h).astype(F32).astype(BF) for h in range(pair_lanes // head_dim)]


def norm_parts(x):
    mean = jnp.mean(x, axis=-1, keepdims=True)
    centred = x - mean
    variance = jnp.mean(centred * centred, axis=-1, keepdims=True)
    inv = lax.rsqrt(variance + EPS)
    return centred * inv, inv


def norm_back(grad, unit, inv, gain):
    g = grad * gain
    return inv * (g - jnp.mean(g, axis=-1, keepdims=True) - unit * jnp.mean(g * unit, axis=-1, keepdims=True))


MESH = pl.DeviceIdType.MESH


class Place:
    def __init__(self):
        self.y = lax.axis_index("dp")
        f = lax.axis_index("fsdp")
        self.z, self.x, self.c = f // 4, (f // 2) % 2, f % 2

    def at(self, y=None, z=None, x=None, c=None):
        y, z, x, c = (b if a is None else a for a, b in ((y, self.y), (z, self.z), (x, self.x), (c, self.c)))
        return (y, z * 4 + x * 2 + c)

    def far_z(self, s):
        return (self.z + s) % 4

    def others(self):
        return [self.at(c=1 - self.c), self.at(x=1 - self.x), self.at(y=1 - self.y)] + [
            self.at(z=self.far_z(s)) for s in (1, 2, 3)]

    def layer(self):
        return self.others() + [self.at(y=1 - self.y, x=1 - self.x)]

    def hello(self, devices):
        barrier = pltpu.get_barrier_semaphore()
        for d in devices:
            pl.semaphore_signal(barrier, inc=1, device_id=d, device_id_type=MESH)

    def wait_hello(self, devices):
        pl.semaphore_wait(pltpu.get_barrier_semaphore(), len(devices))


class Weight:
    def __init__(self, index, rows, half, parts):
        self.index, self.rows, self.half, self.parts = index, rows, half, parts

    def where(self, part, c=None):
        r0, rn, c0, cn = self.parts[part]
        if c is None:
            return pl.ds(r0, rn), pl.ds(c0, cn)
        return pl.ds(r0, rn), pl.ds(pl.multiple_of(c * self.half + c0, 128), cn)

    def columns(self, c):
        return pl.ds(pl.multiple_of(c * self.half, 128), self.half)


def split_columns(n):
    first = (n // 128 + 1) // 2 * 128
    return first


def weight_table(width, ff, devices):
    chip = 2 * width // devices
    chip_ff = 2 * ff // devices
    items = []
    for i, n in enumerate((3 * width, width, ff)):
        half = n // 2
        first = split_columns(half)
        items.append(Weight(i, chip, half, ((0, chip, 0, first), (0, chip, first, half - first))))
    half = width // 2
    items.append(Weight(3, chip_ff, half, ((0, chip_ff // 2, 0, half), (chip_ff // 2, chip_ff // 2, 0, half))))
    return items


def nested(conds, act):
    if not conds:
        act()
        return

    @pl.when(conds[0]())
    def _():
        nested(conds[1:], act)


class Started:
    def __init__(self, send, recv):
        self.send, self.recv, self.live = send, recv, {}

    def go(self, name, src, dst, slot, dev):
        copy = pltpu.make_async_remote_copy(
            src_ref=src, dst_ref=dst, send_sem=self.send.at[slot], recv_sem=self.recv.at[slot],
            device_id=dev, device_id_type=MESH)
        copy.start()
        self.live.setdefault(name, []).append(copy)

    def arrived(self, name):
        for copy in self.live[name]:
            copy.wait_recv()

    def left(self, name=None):
        for key in list(self.live) if name is None else [name]:
            for copy in self.live.pop(key):
                copy.wait_send()


class Gather:
    SLOTS = 2 * 23

    def __init__(self, place, send, recv, base, w, full):
        self.p, self.send, self.recv, self.base, self.w, self.full = place, send, recv, base, w, full
        self.begun = []

    def ref(self, part, y, z, x):
        if part is None:
            return self.full.at[y, z, x, :, self.w.columns(self.p.c)]
        r, c = self.w.where(part, self.p.c)
        return self.full.at[y, z, x, r, c]

    def go(self, src, dst, send, recv, dev, conds, like):
        pltpu.make_async_remote_copy(
            src_ref=src, dst_ref=dst, send_sem=self.send.at[self.base + send()], recv_sem=self.recv.at[self.base + recv],
            device_id=dev, device_id_type=MESH).start()
        self.begun.append((send, conds, like))

    def wait(self, ref, slot):
        pltpu.make_async_remote_copy(
            src_ref=ref, dst_ref=ref, send_sem=self.send.at[self.base], recv_sem=self.recv.at[self.base + slot],
            device_id=self.p.at(c=1 - self.p.c), device_id_type=MESH).wait_recv()

    def left(self):
        for send, conds, like in self.begun:
            def act():
                pltpu.make_async_remote_copy(
                    src_ref=like(), dst_ref=like(), send_sem=self.send.at[self.base + send()], recv_sem=self.recv.at[self.base],
                    device_id=self.p.at(c=1 - self.p.c), device_id_type=MESH).wait_send()

            nested(conds, act)

    def along(self, j, act):
        here = self.p.z
        for z, cond, toward in ((lambda: here - j, lambda: here >= j, 1), (lambda: here + j, lambda: here + j <= 3, -1)):
            nested((cond,), lambda: act(z, (cond,), toward))

    def pass_z(self, src, dst, z, toward, conds, like):
        p = self.p
        more = (lambda: p.z <= 2) if toward == 1 else (lambda: p.z >= 1)
        nested((more,), lambda: self.go(
            src, dst, lambda: z() + (0 if toward == 1 else 4), z(), p.at(z=p.z + toward), conds + (more,), like))

    def partner(self, part, step):
        p = self.p
        return p.at(x=1 - p.x) if (part + step) % 2 == 0 else p.at(y=1 - p.y)

    def behind(self, part):
        p = self.p
        return (p.y, 1 - p.x) if part == 0 else (1 - p.y, p.x)

    def own_z(self):
        return self.p.z

    def one(self, part):
        return self.ref(part, 0, 0, 0)

    def start(self, block):
        p = self.p
        for toward in (1, -1):
            self.pass_z(block, self.ref(None, p.y, p.z, p.x), self.own_z, toward, (), lambda: self.one(None))
        for part in (0, 1):
            self.onward(part, self.own_z, block.at[self.w.where(part)], ())

    def onward(self, part, z, src, conds):
        p = self.p
        dst = self.ref(part, p.y, z(), p.x)
        o = part * 23
        like = lambda: self.one(part)
        self.go(src, dst, lambda: o + 8 + z(), o + 8 + z(), self.partner(part, 0), conds, like)
        self.go(src, dst, lambda: o + 12 + z(), o + 12 + z(), self.partner(part, 1), conds, like)

    def on_z(self, j):
        def act(z, conds, toward):
            whole = self.ref(None, self.p.y, z(), self.p.x)
            self.wait(whole, z())
            self.pass_z(whole, whole, z, toward, conds, lambda: self.one(None))
            for part in (0, 1):
                self.onward(part, z, self.ref(part, self.p.y, z(), self.p.x), conds)

        self.along(j, act)

    def on_second(self, j):
        def act(z, conds, toward):
            for part in (0, 1):
                self.second_on(part, z, conds)

        if j == 0:
            act(self.own_z, (), 0)
        else:
            self.along(j, act)

    def second_on(self, part, z, conds):
        y, x = self.behind(part)
        ref = self.ref(part, y, z(), x)
        o = part * 23
        self.wait(ref, o + 8 + z())
        self.go(ref, ref, lambda: o + 16 + z(), o + 16 + z(), self.partner(part, 1), conds, lambda: self.one(part))

    def core(self, step):
        p = self.p
        for part in (0, 1):
            o = part * 23
            if step == 2:
                for z in range(4):
                    y, x = (1 - p.y, p.x) if part == 0 else (p.y, 1 - p.x)
                    self.wait(self.ref(part, y, z, x), o + 12 + z)
                    self.wait(self.ref(part, 1 - p.y, z, 1 - p.x), o + 16 + z)
            self.go_core(lambda part=part: self.of_step(part, step), o + 20 + step)

    def of_step(self, part, step):
        p = self.p
        if step == 0:
            y, x = p.y, p.x
        elif step == 1:
            y, x = self.behind(part)
        else:
            y, x = (1 - p.y, slice(None)) if part == 0 else (slice(None), 1 - p.x)
        return self.ref(part, y, slice(None), x)

    def go_core(self, make, slot):
        self.go(make(), make(), lambda: slot, slot, self.p.at(c=1 - self.p.c), (), make)

    def finish(self):
        p = self.p
        for part in (0, 1):
            r, c = self.w.where(part, 1 - p.c)
            for step in range(3):
                if step == 2:
                    ref = self.full.at[1 - p.y, :, :, r, c] if part == 0 else self.full.at[:, :, 1 - p.x, r, c]
                else:
                    y, x = (p.y, p.x) if step == 0 else self.behind(part)
                    ref = self.full.at[y, :, x, r, c]
                self.wait(ref, part * 23 + 20 + step)


class LateGather(Gather):
    def start(self, block):
        for part in (0, 1):
            self.onward(part, self.own_z, block.at[self.w.where(part)], ())

    def on_third(self):
        p = self.p
        for part in (0, 1):
            o = part * 23
            y, x = (1 - p.y, p.x) if part == 0 else (p.y, 1 - p.x)
            self.wait(self.ref(part, y, p.z, x), o + 12 + p.z)
            self.wait(self.ref(part, 1 - p.y, p.z, 1 - p.x), o + 16 + p.z)
        ref = self.layer(p.z)
        for toward in (1, -1):
            self.pass_z(ref, ref, self.own_z, toward, (), lambda: self.layer(0))

    def layer(self, z):
        return self.ref(None, slice(None), z, slice(None))

    def on_z(self, j):
        def act(z, conds, toward):
            ref = self.layer(z())
            self.wait(ref, z())
            self.pass_z(ref, ref, z, toward, conds, lambda: self.layer(0))

        self.along(j, act)

    def core(self):
        self.go_core(lambda: self.ref(None, slice(None), slice(None), slice(None)), 20)

    def finish(self):
        self.wait(self.full.at[:, :, :, :, self.w.columns(1 - self.p.c)], 20)


def middle_body(
    att, hidden, gout, wout, wup, wdown, vecs, ubias, vsum, usum,
    x_t, dout, mid, x, acc, gacc, act_s, slope_s, outs, local, sem, put_down, put_up, hook,
):
    output_h, gmid_h, gatt_h, dout_h = outs
    tokens, width = hidden.shape
    ff = wup.shape[1]
    block = 256
    blocks = tokens // block
    chunk = ubias.shape[1]
    chunks = ff // chunk
    out_bias, gain, shift, down_bias = (vecs[i:i + 1, :] for i in (4, 5, 6, 7))

    def enter(i, _):
        r = pl.ds(pl.multiple_of(i * block, block), block)
        m = hidden[r, :].astype(F32) + dot_nn(att[r, :], wout[...]) + out_bias
        mid[r, :] = m
        unit, _ = norm_parts(m)
        y = (unit * gain + shift).astype(BF)
        x[r, :] = y
        x_t[:, r] = y.T
        acc[r, :] = jnp.zeros((block, width), F32)
        gacc[r, :] = jnp.zeros((block, width), F32)
        hook("enter", i)
        return 0

    lax.fori_loop(0, blocks, enter, 0)
    hook("entered", 0)

    def chunk_of(i):
        return (i % 2) * 2 + i // 2

    def first(i):
        j = chunk_of(i)
        c = pl.ds(pl.multiple_of(j * chunk, chunk), chunk)
        slot = i % 2
        w_up = wup[:, c]
        bias = ubias[pl.ds(j, 1), :]
        for b in range(blocks):
            r = slice(b * block, (b + 1) * block)
            u = dot_nn(x[r, :], w_up) + bias
            u2 = u * u
            th = jnp.tanh(u * (0.7978845608028654 + 0.7978845608028654 * 0.044715 * u2))
            half_one = 0.5 + 0.5 * th
            act_s[slot, r, :] = (u * half_one).astype(BF)
            slope = half_one + (0.5 * u) * (1.0 - th * th) * (
                0.7978845608028654 + 3 * 0.7978845608028654 * 0.044715 * u2)
            slope_s[slot, r, :] = slope.astype(BF)
        for k in range(2):
            part = slice(k * chunk // 2, (k + 1) * chunk // 2)
            put_down(i, k, dot_tn(act_s[slot, :, part], gout[...]).astype(BF))
        hook("first", i)

    def second(i):
        j = chunk_of(i)
        c = pl.ds(pl.multiple_of(j * chunk, chunk), chunk)
        slot = i % 2
        w_up, w_down = wup[:, c], wdown[c, :]
        colsum = jnp.zeros((1, chunk), F32)
        for b in range(blocks):
            r = slice(b * block, (b + 1) * block)
            gu = (dot_nt(gout[r, :], w_down) * slope_s[slot, r, :].astype(F32)).astype(BF)
            colsum = colsum + jnp.sum(gu.astype(F32), axis=0, keepdims=True)
            slope_s[slot, r, :] = gu
            acc[r, :] += dot_nn(act_s[slot, r, :], w_down)
            gacc[r, :] += dot_nt(gu, w_up)
        usum[pl.ds(j, 1), :] = colsum
        hook("middle", i)
        for k in range(2):
            part = slice(k * width // 2, (k + 1) * width // 2)
            put_up(i, k, dot_nn(x_t[part, :], slope_s[slot]).astype(BF))
        hook("second", i)

    def ahead(i, _):
        first(i)
        return 0

    lax.fori_loop(0, 2, ahead, 0)
    hook("ready", 0)
    usum[...] = jnp.zeros_like(usum)

    def both(i, _):
        second(i)

        @pl.when(i + 2 < chunks)
        def _():
            first(i + 2)

        hook("both", i)
        return 0

    lax.fori_loop(0, chunks, both, 0)
    vsum[...] = jnp.zeros_like(vsum)

    def rows_out(i):
        r = pl.ds(pl.multiple_of(i * block, block), block)
        return (pltpu.make_async_copy(act_s.at[0, r, :], output_h.at[r, :], local.at[sem + 1 + 3 * i]),
                pltpu.make_async_copy(mid.at[r, :], gmid_h.at[r, :], local.at[sem + 2 + 3 * i]),
                pltpu.make_async_copy(act_s.at[1, r, :], gatt_h.at[r, :], local.at[sem + 3 + 3 * i]))

    def leave(i, _):
        r = pl.ds(pl.multiple_of(i * block, block), block)
        m = mid[r, :]
        act_s[0, r, :] = (m + acc[r, :] + down_bias).astype(BF)
        unit, inv = norm_parts(m)
        g = gacc[r, :]
        go = gout[r, :].astype(F32)
        gm = go + norm_back(g, unit, inv, gain)
        mid[r, :] = gm
        gp = gm.astype(BF)
        x[r, :] = gp
        act_s[1, r, :] = dot_nt(gp, wout[...]).astype(BF)
        for copy in rows_out(i):
            copy.start()
        vsum[0:1, :] += jnp.sum(go, axis=0, keepdims=True)
        vsum[1:2, :] += jnp.sum(g * unit, axis=0, keepdims=True)
        vsum[2:3, :] += jnp.sum(g, axis=0, keepdims=True)
        vsum[3:4, :] += jnp.sum(gp.astype(F32), axis=0, keepdims=True)
        hook("leave", i)
        return 0

    lax.fori_loop(0, blocks, leave, 0)
    for j in range(width // 256):
        c = slice(j * 256, (j + 1) * 256)
        dout[:, c] = dot_tn(att[...], x[:, c]).astype(BF)
    final = pltpu.make_async_copy(dout, dout_h, local.at[sem])
    final.start()
    hook("end", 0)
    for i in range(blocks):
        for copy in rows_out(i):
            copy.wait()
    final.wait()


def middle_scratch(tokens, width, chunk):
    return [
        pltpu.VMEM((tokens, width), F32),
        pltpu.VMEM((tokens, width), BF),
        pltpu.VMEM((tokens, width), F32),
        pltpu.VMEM((tokens, width), F32),
        pltpu.VMEM((2, tokens, chunk), BF),
        pltpu.VMEM((2, tokens, chunk), BF),
    ]


def middle_call(att, hidden, gout, wout, wup, wdown, vecs, ubias):
    tokens, width = att.shape
    ff = wup.shape[1]
    chunk = ubias.shape[1]
    vm = pl.BlockSpec(memory_space=pltpu.VMEM)
    anyw = pl.BlockSpec(memory_space=pl.ANY)
    shapes = (
        jax.ShapeDtypeStruct((tokens, width), BF),
        jax.ShapeDtypeStruct((tokens, width), F32),
        jax.ShapeDtypeStruct((tokens, width), BF),
        jax.ShapeDtypeStruct((width, width), BF),
        jax.ShapeDtypeStruct((width, ff), BF),
        jax.ShapeDtypeStruct((ff, width), BF),
        jax.ShapeDtypeStruct((8, width), F32),
        jax.ShapeDtypeStruct((8, chunk), F32),
    )

    def kernel(att, hidden, gout, wout, wup, wdown, vecs, ubias, o, gm, ga, do, du, dd, vsum, usum, *scratch):
        def place(i):
            return ((i % 2) * 2 + i // 2) * chunk

        def put_down(i, k, v):
            dd[pl.ds(pl.multiple_of(place(i) + k * chunk // 2, chunk // 2), chunk // 2), :] = v

        def put_up(i, k, v):
            du[k * width // 2:(k + 1) * width // 2, pl.ds(pl.multiple_of(place(i), chunk), chunk)] = v

        middle_body(att, hidden, gout, wout, wup, wdown, vecs, ubias, vsum, usum, *scratch[:-1], (o, gm, ga, do), scratch[-1], 0,
                    put_down, put_up, lambda where, i: None)

    return pl.pallas_call(
        kernel,
        out_shape=shapes,
        in_specs=[vm] * 8,
        out_specs=[anyw] * 4 + [vm] * 4,
        scratch_shapes=[pltpu.VMEM((width, tokens), BF), pltpu.VMEM((width, width), BF)] + middle_scratch(tokens, width, chunk) + [pltpu.SemaphoreType.DMA((1 + 3 * (tokens // 256),))],
        compiler_params=pltpu.CompilerParams(vmem_limit_bytes=58 * 1024 * 1024),
        name="middle",
    )(att, hidden.reshape(tokens, width), gout.reshape(tokens, width), wout, wup, wdown, vecs, ubias)


class EarlyReduce:
    SLOTS = 20

    def __init__(self, place, send, recv, g_d, g_u, away_d, away_u, r1_d, r1_u, r2_d, r2_y, r2_x, r3_d):
        self.p, self.send, self.recv = place, send, recv
        self.g_d, self.g_u, self.away_d, self.away_u = g_d, g_u, away_d, away_u
        self.r1_d, self.r1_u, self.r2_d, self.r2_y, self.r2_x, self.r3_d = r1_d, r1_u, r2_d, r2_y, r2_x, r3_d
        self.n = g_d.shape[-1]
        self.h = g_d.shape[-2] // 2

    def copy(self, src, dst, slot, dev):
        return pltpu.make_async_remote_copy(
            src_ref=src, dst_ref=dst, send_sem=self.send.at[slot], recv_sem=self.recv.at[slot], device_id=dev, device_id_type=MESH)

    def mate(self):
        return self.p.at(c=1 - self.p.c)

    def sides(self, v):
        low, high = v[..., :self.n], v[..., self.n:]
        return jnp.where(self.p.c == 0, low, high), jnp.where(self.p.c == 0, high, low)

    def down_core(self, i):
        return self.copy(self.away_d.at[i % 2], self.r1_d.at[i // 2, i % 2], i, self.mate())

    def put_down(self, i, k, v):
        if k == 0:
            @pl.when(i >= 2)
            def _():
                self.down_core(i - 2).wait_send()

        keep, give = self.sides(v.reshape(2, 2 * self.h, 2 * self.n))
        self.g_d[i // 2, i % 2, k] = keep
        self.away_d[i % 2, k] = give

    def down_second(self, t):
        p = self.p
        a, b = pl.ds(0, self.h), pl.ds(self.h, self.h)
        return (self.copy(self.g_d.at[t, 1 - p.y, :, :, a, :], self.r2_d.at[t, 0], 8 + 2 * t, p.at(y=1 - p.y)),
                self.copy(self.g_d.at[t, :, :, 1 - p.x, b, :], self.r2_d.at[t, 1], 9 + 2 * t, p.at(x=1 - p.x)))

    def down_third(self, t):
        p = self.p
        a, b = pl.ds(0, self.h), pl.ds(self.h, self.h)
        return (self.copy(self.g_d.at[t, p.y, :, 1 - p.x, a, :], self.r3_d.at[t, 0], 12 + 2 * t, p.at(x=1 - p.x)),
                self.copy(self.g_d.at[t, 1 - p.y, :, p.x, b, :], self.r3_d.at[t, 1], 13 + 2 * t, p.at(y=1 - p.y)))

    def down_add_core(self, t):
        for y in (0, 1):
            self.down_core(2 * t + y).wait_recv()

        def step(i, _):
            at = (t, i // 4, (i // 2) % 2, i % 2)
            self.g_d[at] = self.g_d[at] + self.r1_d[at]
            return 0

        lax.fori_loop(0, 8, step, 0)
        for copy in self.down_second(t):
            copy.start()

    def down_add_second(self, t):
        p, h = self.p, self.h
        for copy in self.down_second(t):
            copy.wait_recv()

        def step(i, _):
            u, v = i // 2, i % 2
            at, to = (t, p.y, u, v, slice(0, h)), (t, 0, u, v)
            self.g_d[at] = self.g_d[at] + self.r2_d[to]
            at, to = (t, u, v, p.x, slice(h, 2 * h)), (t, 1, u, v)
            self.g_d[at] = self.g_d[at] + self.r2_d[to]
            return 0

        lax.fori_loop(0, 4, step, 0)

    def down_add_third(self, t):
        p, h = self.p, self.h
        for copy in self.down_third(t):
            copy.wait_recv()
        for z in (0, 1):
            for part in (0, 1):
                rows = slice(part * h, (part + 1) * h)
                at = (t, p.y, z, p.x, rows)
                self.g_d[at] = self.g_d[at] + self.r3_d[t, part, z]

    def up_core(self, i):
        return self.copy(self.away_u.at[i % 2], self.r1_u.at[i], 4 + i, self.mate())

    def rows_u(self):
        return self.g_u.shape[-2]

    def put_up(self, i, k, v):
        if k == 0:
            @pl.when(i >= 2)
            def _():
                self.up_core(i - 2).wait_send()

        keep, give = self.sides(v)
        c = pl.ds(pl.multiple_of((i // 2) * self.n, 128), self.n)
        self.g_u[i % 2, k, :, :, :, c] = keep.reshape(4, 2, self.rows_u(), self.n)
        self.away_u[i % 2, k] = give.reshape(4, 2, self.rows_u(), self.n)

    def up_second(self, i):
        p = self.p
        t = i % 2
        c = pl.ds((i // 2) * self.n, self.n)
        if t == 0:
            return self.copy(self.g_u.at[0, 1 - p.y, :, :, :, c], self.r2_y.at[i // 2], 16 + i, p.at(y=1 - p.y))
        return self.copy(self.g_u.at[1, :, :, 1 - p.x, :, c], self.r2_x.at[i // 2], 16 + i, p.at(x=1 - p.x))

    def up_add_core(self, i):
        self.up_core(i).wait_recv()
        c = slice((i // 2) * self.n, (i // 2 + 1) * self.n)

        def step(b, _):
            at = (b // 8, (b // 2) % 4, b % 2)
            here = (i % 2,) + at + (slice(None), c)
            self.g_u[here] = self.g_u[here] + self.r1_u[(i,) + at]
            return 0

        lax.fori_loop(0, 16, step, 0)
        if i < 2:
            self.up_second(i).start()

    def up_add_second(self, i):
        p = self.p
        self.up_second(i).wait_recv()
        c = slice((i // 2) * self.n, (i // 2 + 1) * self.n)

        def step(b, _):
            if i % 2 == 0:
                here, got = (0, p.y, b // 2, b % 2, slice(None), c), self.r2_y[i // 2, b // 2, b % 2]
            else:
                here, got = (1, b // 4, b % 4, p.x, slice(None), c), self.r2_x[i // 2, b // 4, b % 4]
            self.g_u[here] = self.g_u[here] + got
            return 0

        lax.fori_loop(0, 8, step, 0)

    def left(self):
        for i in (2, 3):
            self.down_core(i).wait_send()
            self.up_core(i).wait_send()
        for t in (0, 1):
            for copy in self.down_second(t):
                copy.wait_send()
            self.up_second(t).wait_send()

    def resume(self):
        for copy in self.resumed():
            copy.start()

    def resumed(self):
        return [self.up_second(2), self.up_second(3), *self.down_third(0), *self.down_third(1)]


def forward_coeffs(s, flags, past, old, ridge, coeffs, coef_t):
    length, basis = past.shape[1], ridge.shape[0]
    samples = ridge.shape[1] - length
    brows = slice(s * basis, (s + 1) * basis)
    diff = (iota((samples, basis), 0) - iota((samples, basis), 1)).astype(F32)
    sampled = jnp.exp(-0.5 * diff * diff).astype(BF)
    keep = (1 - flags[s]).astype(F32)
    old_signal = (dot_nn(sampled, old[s]) * keep).astype(BF)
    co = (dot_nn(ridge[:, :samples], old_signal) + dot_nn(ridge[:, samples:], past[s])).astype(BF)
    coeffs[brows, :] = co
    coef_t[:, brows] = co.T


def forward_projections(s, half, heads, length, basis, hidden, vecs, wmat, wqkv, normed, norm_t, coeffs, qkv, mem, ublk, proj, head_par):
    width = hidden.shape[1]
    hd = width // heads
    rows = slice(s * length, (s + 1) * length)
    brows = slice(s * basis, (s + 1) * basis)
    step = width // 3
    if half == 0:
        unit, _ = norm_parts(hidden[rows, :].astype(F32))
        nrm = (unit * vecs[0:1, :] + vecs[1:2, :]).astype(BF)
        normed[...] = nrm
        norm_t[:, rows] = nrm.T
    for j in range(9) if half == 0 else ():
        cols = slice(j * step, (j + 1) * step)
        y = dot_nn(normed[...], wqkv[:, cols])
        if j < 3:
            y = y + vecs[2:3, cols]
        elif j >= 6:
            y = y + vecs[3:4, (j - 6) * step:(j - 5) * step]
        qkv[rows, cols] = y.astype(BF)
    if half == 0:
        return
    for j in range(6):
        cols = slice(j * step, (j + 1) * step)
        wcols = slice(width + j * step, width + (j + 1) * step)
        mem[brows, cols] = dot_nn(coeffs[brows, :], wqkv[:, wcols]).astype(BF)
    raw = dot_tn(wmat[...], mem[brows, 0:width])[0:32, :]
    own = (iota((32, width), 0) % 16) == (iota((32, width), 1) // hd)
    u = jnp.where(own, raw, 0.0) * (1.0 / math.sqrt(hd))
    ublk[s] = u
    u_hi, u_lo = split_high_low(u)
    q = qkv[rows, 0:width]
    pr = dot_nt(u_hi, q) + dot_nt(u_lo, q)
    proj[s] = pr
    basis_rows(pr, heads, basis, head_par)


def basis_rows(pr, heads, basis, head_par):
    centre = 1.0 / (1.0 + jnp.exp(-pr[0:16]))
    wide = pr[16:32]
    soft = jnp.maximum(wide, 0.0) + jnp.log(1.0 + jnp.exp(-jnp.abs(wide)))
    variance = (soft + 0.5) * 0.02
    inv_root = lax.rsqrt(variance)
    root = inv_root * math.sqrt(0.5 * LOG2E)
    shift_log = jnp.log(inv_root) * LOG2E - math.log2(basis)
    for h in range(heads):
        head_par[h, 0:1, :] = root[h:h + 1]
        head_par[h, 1:2, :] = centre[h:h + 1] * root[h:h + 1]
        head_par[h, 2:3, :] = shift_log[h:h + 1]
    return centre, wide, variance, root


def causal(scores, allowed):
    n = allowed.shape[0]
    last = jnp.where(allowed, scores[-n:], -1e30)
    return last if scores.shape[0] == n else jnp.concatenate([scores[:-n], last], axis=0)


def forward_heads(s, first, last, heads, length, basis, width, qkv, mem, att, lse, head_par, att_t):
    hd = width // heads
    half = length // 2
    rows = slice(s * length, (s + 1) * length)
    brows = slice(s * basis, (s + 1) * basis)
    masks = head_masks(2 * hd, hd)
    scale = LOG2E / math.sqrt(hd)

    def pair(p, _):
        c0 = pl.multiple_of(p * (2 * hd), 2 * hd)
        q = qkv[rows, pl.ds(c0, 2 * hd)]
        k = qkv[rows, pl.ds(pl.multiple_of(width + c0, 2 * hd), 2 * hd)]
        v_t = qkv[rows, pl.ds(pl.multiple_of(2 * width + c0, 2 * hd), 2 * hd)].T
        mv_t = mem[brows, pl.ds(pl.multiple_of(width + c0, 2 * hd), 2 * hd)].T
        cent = ((iota((basis, 1), 0).astype(F32) + 0.5) / basis)
        allowed = iota((half, half), 0) <= iota((half, half), 1)
        for h in range(2):
            head = p * 2 + h
            km = k * masks[h]
            lanes = slice(h * hd, (h + 1) * hd)
            for b in range(2):
                cols = slice(b * half, (b + 1) * half)
                depth = (b + 1) * half
                sc = causal(dot_nt(km[:depth], q[cols]) * scale, allowed)
                top = jnp.max(sc, axis=0, keepdims=True)
                e = jnp.exp2(sc - top)
                total = jnp.sum(e, axis=0, keepdims=True)
                out = dot_nn(v_t[lanes, :depth], e.astype(BF)) / total
                lse[s, head, :, cols] = top + jnp.log(total) * LOG2E
                t = cent * head_par[head, 0:1, cols] - head_par[head, 1:2, cols]
                bas = jnp.exp2(head_par[head, 2:3, cols] - t * t).astype(BF)
                out = out + dot_nn(mv_t[lanes, :], bas)
                att_t[lanes, cols] = out
        att[rows, pl.ds(c0, 2 * hd)] = att_t[...].T.astype(BF)
        return 0

    lax.fori_loop(first, last, pair, 0)


def unpack_small(small, wmat, vecs, ubias, devices, width, ff):
    flat = small.reshape(devices * 32, 128)
    wmat[...] = small.reshape(devices, 32, 128)[:, 0:16, :].reshape(devices * 16, 128)
    every = flat[...]

    def spread(row, offset, each, n):
        pick = (iota((devices, devices * 32), 1) == iota((devices, devices * 32), 0) * 32 + row)
        mine = dot_nn(pick.astype(F32).astype(BF), every).astype(BF)
        place = iota((128, n), 0) == iota((128, n), 1) % each + offset
        wide = dot_nn(mine, place.astype(F32).astype(BF))
        own = iota((devices, n), 1) // each == iota((devices, n), 0)
        return jnp.sum(jnp.where(own, wide, 0.0), axis=0, keepdims=True)

    e = width // devices
    vecs[0:1, :] = spread(16, 0, e, width)
    vecs[1:2, :] = spread(16, e, e, width)
    both = spread(17, 2 * e, 2 * e, 2 * width)
    vecs[2:3, :] = both[:, :width]
    vecs[3:4, :] = both[:, width:]
    vecs[4:5, :] = spread(16, 2 * e, e, width)
    vecs[5:6, :] = spread(16, 3 * e, e, width)
    vecs[6:7, :] = spread(17, 0, e, width)
    vecs[7:8, :] = spread(17, e, e, width)
    up = spread(18, 0, ff // devices, ff)
    chunk = ubias.shape[1]
    ubias[...] = jnp.zeros_like(ubias)
    for j in range(ff // chunk):
        ubias[j:j + 1, :] = up[:, j * chunk:(j + 1) * chunk]


FIRST_STEPS = (
    "#0", "qz1", "qs0", "os0", "qz2", "qs1", "+0", "qz3", "ug", "own", "ot", "qc0", "#1", "qs2", "+1", "qs3", "qc1",
    "uz1", "us0", "oz1", "+2", "uz2", "us1", "oz2", "qc2",
)
LATER_STEPS = (
    ("uz3", "us2", "dg", "oz3", "oc"), ("us3", "uc0", "uc1"), ("dz1",), ("ds0",), ("dz2",), ("ds1",), ("dz3",), ("dc0",),
    (), ("ds2",), (), ("uc2",), ("ds3",), ("dc1",),
)


def forward_kernel(
    heads, devices,
    flags, hidden_h, past_h, old_h, ridge_h, gout_h, small, qkv_s, out_s, up_s, down_s,
    norm_h, coef_h, qkv_h, mem_h, output_h, gmid_h, gatt_h, dout_h, gu_h, gd_h, wq_h,
    lse, ublk, proj, wmat, vecs, vsum, usum,
    hidden, gout, att, wq, wo, wu, wd, ubias,
    wide_s, wide_r, block, block_d, sfull, early, send, recv, local, early_send, early_recv,
):
    place = Place()
    p = place
    tokens, width = hidden.shape
    seqs, length = past_h.shape[0], past_h.shape[1]
    basis = ridge_h.shape[0]
    ff = up_s.shape[1]
    t_qkv, t_out, t_up, t_down = weight_table(width, ff, devices)
    st = Started(send, recv)
    n = Gather.SLOTS
    g_qkv = Gather(place, send, recv, 0, t_qkv, wq)
    g_up = Gather(place, send, recv, n, t_up, wu)
    g_down = Gather(place, send, recv, 2 * n, t_down, wd)
    g_out = LateGather(place, send, recv, 3 * n, t_out, wo)
    base = 4 * n
    nh = wide_r.shape[1]
    blocks = {
        "q": block.at[:, 0:t_qkv.half], "o": block.at[:, t_qkv.half:t_qkv.half + t_out.half],
        "u": block.at[:, t_qkv.half + t_out.half:nh], "d": block_d}
    gather_of = {"q": g_qkv, "o": g_out, "u": g_up, "d": g_down}

    def pass_on(word):
        g, what, n = gather_of[word[0]], word[1], word[2:]
        if what == "g":
            g.start(blocks[word[0]])
        elif what == "z":
            g.on_z(int(n))
        elif what == "s":
            g.on_second(int(n))
        elif what == "t":
            g.on_third()
        elif what == "f":
            g.finish()
        elif n:
            g.core(int(n))
        else:
            g.core()

    stores = []

    def store(src, dst, rows=None):
        i = len(stores)

        def make():
            a, b = (src, dst) if rows is None else (src.at[rows, :], dst.at[rows, :])
            return pltpu.make_async_copy(a, b, local.at[9 + i])

        make().start()
        stores.append(make)

    def attention(norm_t, coef_t, qkv, mem, past, old, ridge, normed, coeffs, head_par, att_t):
        forward_attention(
            heads, devices, place, (flags, hidden_h, past_h, old_h, ridge_h, gout_h, small, qkv_s, out_s, up_s, down_s),
            (t_qkv, t_out, t_up, t_down), st, (g_qkv, g_up, g_down, g_out), base, store, blocks, pass_on,
            (norm_h, coef_h, qkv_h, mem_h, wq_h),
            lse, ublk, proj, wmat, vecs, hidden, gout, norm_t, coef_t, qkv, mem, att, wq, ubias,
            wide_s, wide_r, block, block_d, sfull, local,
            past, old, ridge, normed, coeffs, head_par, att_t)
        for make in stores:
            make().wait()

    pl.run_scoped(
        attention,
        pltpu.VMEM((width, tokens), BF),
        pltpu.VMEM((width, seqs * basis), BF),
        pltpu.VMEM((tokens, 3 * width), BF),
        pltpu.VMEM((seqs * basis, 2 * width), BF),
        pltpu.VMEM(past_h.shape, BF),
        pltpu.VMEM(old_h.shape, BF),
        pltpu.VMEM(ridge_h.shape, BF),
        pltpu.VMEM((length, width), BF),
        pltpu.VMEM((seqs * basis, width), BF),
        pltpu.VMEM((heads, 8, length), F32),
        pltpu.VMEM((2 * (width // heads), length), F32),
    )

    er = EarlyReduce(place, early_send, early_recv, *early)
    sem = 9 + 2 * seqs + 3

    def hook(where, i):
        def at(n, *acts):
            @pl.when(i == n)
            def _():
                for act, arg in acts:
                    act(arg)

        if where == "first":
            er.down_core(i).start()
        elif where == "entered":
            pass_on("uf")
        elif where == "ready":
            for word in ("dc2", "df"):
                pass_on(word)
        elif where == "second":
            er.up_core(i).start()
            at(1, (er.down_add_core, 0))
            at(3, (er.down_add_second, 0))
        elif where == "middle":
            at(2, (er.down_add_core, 1))
        elif where == "both":
            at(0, (er.up_add_core, 0))
            at(1, (er.up_add_core, 1))
        elif where == "leave":
            at(1, (er.up_add_core, 2), (er.up_add_core, 3))
            at(3, (er.up_add_second, 0), (er.up_add_second, 1))
        elif where == "end":
            er.down_add_second(1)

    wflat = wq.reshape(width, 3 * width)

    def feed_forward(*scratch):
        middle_body(
            att, hidden, gout, wo.reshape(width, width), wu.reshape(width, ff), wd.reshape(ff, width), vecs, ubias, vsum, usum,
            wflat.at[:, 0:tokens], wflat.at[:, tokens:tokens + width], *scratch, (output_h, gmid_h, gatt_h, dout_h), local, sem, er.put_down, er.put_up, hook)
        out = [pltpu.make_async_copy(er.g_u, gu_h, local.at[sem + 14]), pltpu.make_async_copy(er.g_d, gd_h, local.at[sem + 15])]
        for copy in out:
            copy.start()
        er.left()
        for g in (g_up, g_down, g_out):
            g.left()
        for copy in out:
            copy.wait()

    pl.run_scoped(feed_forward, *middle_scratch(tokens, width, ubias.shape[1]))


def forward_attention(
    heads, devices, place, inputs, table, st, gathers, base, store, blocks, pass_on, outs,
    lse, ublk, proj, wmat, vecs, hidden, gout, norm_t, coef_t, qkv, mem, att, wq, ubias,
    wide_s, wide_r, block, block_d, sfull, local,
    past, old, ridge, normed, coeffs, head_par, att_t,
):
    p = place
    flags, hidden_h, past_h, old_h, ridge_h, gout_h, small, qkv_s, out_s, up_s, down_s = inputs
    t_qkv, t_out, t_up, t_down = table
    g_qkv, g_up, g_down, g_out = gathers
    norm_h, coef_h, qkv_h, mem_h, wq_h = outs
    tokens, width = hidden.shape
    seqs, length = past.shape[0], past.shape[1]
    basis = ridge.shape[0]
    ff = up_s.shape[1]
    place.hello(place.others())
    loads = []
    for i, (src, dst) in enumerate(((ridge_h, ridge), (old_h, old), (past_h, past), (hidden_h, hidden), (gout_h, gout))):
        copy = pltpu.make_async_copy(src, dst, local.at[i])
        copy.start()
        loads.append(copy)
    pos = 0
    for half in range(2):
        for ref, w in ((qkv_s, t_qkv), (out_s, t_out), (up_s, t_up)):
            wide_s[:, pos:pos + w.half] = ref[:, half * w.half:(half + 1) * w.half].astype(F32)
            pos += w.half
    nh = pos // 2
    sfull[p.y, p.z, p.x, p.c] = small[...]
    ed = down_s.shape[0]
    hd_cols = width // 2
    block_d[pl.ds(pl.multiple_of(p.c * ed, 16), ed), :] = down_s[:, pl.ds(pl.multiple_of(p.c * hd_cols, 128), hd_cols)]

    place.wait_hello(place.others())
    mate = p.at(c=1 - p.c)
    there = pl.multiple_of((1 - p.c) * nh, 128)
    st.go("wide", wide_s.at[:, pl.ds(there, t_qkv.half)], wide_r.at[:, 0:t_qkv.half], base, mate)
    st.go("wide2", wide_s.at[:, pl.ds(pl.multiple_of(there + t_qkv.half, 128), nh - t_qkv.half)], wide_r.at[:, t_qkv.half:nh], base + 8, mate)
    ref = sfull.at[p.y, p.z, p.x, p.c]
    st.go("s0", ref, ref, base + 1, mate)
    st.go("down", down_s.at[:, pl.ds(pl.multiple_of((1 - p.c) * hd_cols, 128), hd_cols)],
          block_d.at[pl.ds(pl.multiple_of(p.c * ed, 16), ed), :], base + 2, mate)

    def make_block(c0, cn):
        mine = wide_s[:, pl.ds(pl.multiple_of(p.c * nh + c0, 128), cn)]
        other = wide_r[:, c0:c0 + cn]
        block[:, c0:c0 + cn] = jnp.concatenate(
            [jnp.where(p.c == 0, mine, other), jnp.where(p.c == 0, other, mine)], axis=0).astype(BF)

    b_qkv, b_out, b_up = blocks["q"], blocks["o"], blocks["u"]
    own = []

    def keep_own(g, src, i):
        copy = pltpu.make_async_copy(src, g.full.at[p.y, p.z, p.x, :, g.w.columns(p.c)], local.at[i])
        copy.start()
        own.append(copy)

    st.arrived("wide")
    make_block(0, t_qkv.half)
    g_qkv.start(b_qkv)
    st.arrived("s0")
    ref = sfull.at[p.y, p.z, p.x]
    for s in (1, 2, 3):
        st.go("sz", ref, ref, base + 2 + s, p.at(z=p.far_z(s)))
    st.arrived("wide2")
    make_block(t_qkv.half, nh - t_qkv.half)
    g_out.start(b_out)
    st.arrived("down")
    for i, (g, src) in enumerate(((g_qkv, b_qkv), (g_out, b_out), (g_up, b_up), (g_down, block_d))):
        keep_own(g, src, 5 + i)
    loads[0].wait()
    loads[1].wait()
    loads[2].wait()
    def small_step(i):
        if i == 0:
            st.arrived("sz")
            ref = sfull.at[p.y, :, p.x]
            st.go("sx", ref, ref, base + 6, p.at(x=1 - p.x))
        elif i == 1:
            st.arrived("sx")
            ref = sfull.at[p.y]
            st.go("sy", ref, ref, base + 7, p.at(y=1 - p.y))
        else:
            st.arrived("sy")
            unpack_small(sfull, wmat, vecs, ubias, devices, width, ff)

    def own_in_place():
        for copy in own:
            copy.wait()

    def perform(word):
        if word == "own":
            own_in_place()
        elif word[0] == "#":
            forward_coeffs(int(word[1]), flags, past, old, ridge, coeffs, coef_t)
        elif word[0] == "+":
            small_step(int(word[1]))
        else:
            pass_on(word)

    for word in FIRST_STEPS:
        perform(word)
    loads[3].wait()
    g_qkv.finish()
    wflat = wq.reshape(width, 3 * width)
    store(wq, wq_h)
    store(coef_t, coef_h)

    def project(s, half):
        forward_projections(s, half, heads, length, basis, hidden, vecs, wmat, wflat, normed, norm_t, coeffs, qkv, mem, ublk, proj, head_par)

    def attend(s, a, b):
        forward_heads(s, a, b, heads, length, basis, width, qkv, mem, att, lse, head_par, att_t)

    events = iter(LATER_STEPS)

    def step(count=1):
        for _ in range(count):
            for word in next(events, ()):
                perform(word)

    pairs = heads // 2
    for s in range(seqs):
        project(s, 0)
        step()
        project(s, 1)
        store(qkv, qkv_h, slice(s * length, (s + 1) * length))
        store(mem, mem_h, slice(s * basis, (s + 1) * basis))
        if s == seqs - 1:
            store(norm_t, norm_h)
        step()
        for a in range(pairs):
            attend(s, a, a + 1)
            step()
    step(99)
    g_out.finish()
    loads[4].wait()
    st.left()
    g_qkv.left()


def forward_call(heads, devices, flags, hidden, past, old, ridge, gout, small, qkv_s, out_s, up_s, down_s):
    seqs, length, width = hidden.shape
    basis = ridge.shape[0]
    tokens = seqs * length
    ff = up_s.shape[1]
    chip = 2 * width // devices
    chip_ff = 2 * ff // devices
    vm = pl.BlockSpec(memory_space=pltpu.VMEM)
    anyw = pl.BlockSpec(memory_space=pl.ANY)
    full = (2, 4, 2, chip, 3 * width)
    n = width // 2
    far = [
        ((width, tokens), BF), ((width, seqs * basis), BF), ((tokens, 3 * width), BF), ((seqs * basis, 2 * width), BF),
        ((tokens, width), BF), ((tokens, width), F32), ((tokens, width), BF),
        ((width, width), BF), ((2, 2, 4, 2, chip, 2 * n), BF), ((2, 2, 2, 2, chip_ff, n), BF), (full, BF)]
    near = [
        ((seqs, heads, 1, length), F32), ((seqs, 32, width), F32), ((seqs, 32, length), F32),
        ((basis, 128), BF), ((8, width), F32), ((8, width), F32), ((8, width), F32)]
    nh = (4 * width + ff) // 2
    slots = 4 * Gather.SLOTS + 9
    return pl.pallas_call(
        lambda *refs: forward_kernel(heads, devices, *refs),
        out_shape=tuple(jax.ShapeDtypeStruct(*m) for m in far + near),
        in_specs=[pl.BlockSpec(memory_space=pltpu.SMEM)] + [anyw] * 5 + [vm] * 5,
        out_specs=[anyw] * len(far) + [vm] * len(near),
        scratch_shapes=[
            pltpu.VMEM((tokens, width), BF),
            pltpu.VMEM((tokens, width), BF),
            pltpu.VMEM((tokens, width), BF),
            pltpu.VMEM(full, BF),
            pltpu.VMEM((2, 4, 2, chip, width), BF),
            pltpu.VMEM((2, 4, 2, chip, ff), BF),
            pltpu.VMEM((2, 4, 2, chip_ff, width), BF),
            pltpu.VMEM((8, width), F32),
            pltpu.VMEM((width // devices, 2 * nh), F32),
            pltpu.VMEM((width // devices, nh), F32),
            pltpu.VMEM((chip, nh), BF),
            pltpu.VMEM((chip_ff, width // 2), BF),
            pltpu.VMEM((2, 4, 2, 2, 32, 128), BF),
            [pltpu.VMEM(shape, BF) for shape in (
                (2, 2, 2, 2, chip_ff, n), (2, 2, 4, 2, chip, 2 * n), (2, 2, 2, chip_ff, n), (2, 2, 4, 2, chip, n),
                (2, 2, 2, 2, chip_ff, n), (4, 2, 4, 2, chip, n),
                (2, 2, 2, 2, chip_ff // 2, n), (2, 4, 2, chip, n), (2, 2, 4, chip, n), (8, 128))],
            pltpu.SemaphoreType.DMA((slots,)),
            pltpu.SemaphoreType.DMA((slots,)),
            pltpu.SemaphoreType.DMA((9 + 2 * seqs + 3 + 17,)),
            pltpu.SemaphoreType.DMA((EarlyReduce.SLOTS,)),
            pltpu.SemaphoreType.DMA((EarlyReduce.SLOTS,)),
        ],
        compiler_params=pltpu.CompilerParams(vmem_limit_bytes=61 * 1024 * 1024, collective_id=0, has_side_effects=True),
        name="forward",
    )(flags, hidden.reshape(tokens, width), past, old, ridge, gout.reshape(tokens, width), small, qkv_s, out_s, up_s, down_s)


def forward_plain_call(heads, flags, hidden, past, old, ridge, wmat, vecs, wqkv):
    seqs, length, width = hidden.shape
    basis = ridge.shape[0]
    tokens = seqs * length
    vm = pl.BlockSpec(memory_space=pltpu.VMEM)

    def kernel(
        flags, hidden, past, old, ridge, wmat, vecs, wqkv,
        norm_t, coef_t, qkv, mem, att, lse, ublk, proj, normed, coeffs, head_par, att_t,
    ):
        for s in range(seqs):
            forward_coeffs(s, flags, past, old, ridge, coeffs, coef_t)
            for half in (0, 1):
                forward_projections(s, half, heads, length, basis, hidden, vecs, wmat, wqkv, normed, norm_t, coeffs, qkv, mem, ublk, proj, head_par)
            forward_heads(s, 0, heads // 2, heads, length, basis, width, qkv, mem, att, lse, head_par, att_t)

    shapes = (
        jax.ShapeDtypeStruct((width, tokens), BF),
        jax.ShapeDtypeStruct((width, seqs * basis), BF),
        jax.ShapeDtypeStruct((tokens, 3 * width), BF),
        jax.ShapeDtypeStruct((seqs * basis, 2 * width), BF),
        jax.ShapeDtypeStruct((tokens, width), BF),
        jax.ShapeDtypeStruct((seqs, heads, 1, length), F32),
        jax.ShapeDtypeStruct((seqs, 32, width), F32),
        jax.ShapeDtypeStruct((seqs, 32, length), F32),
    )
    return pl.pallas_call(
        kernel,
        out_shape=shapes,
        in_specs=[pl.BlockSpec(memory_space=pltpu.SMEM)] + [vm] * 7,
        out_specs=[vm] * 8,
        scratch_shapes=[
            pltpu.VMEM((length, width), BF),
            pltpu.VMEM((seqs * basis, width), BF),
            pltpu.VMEM((heads, 8, length), F32),
            pltpu.VMEM((2 * (width // heads), length), F32),
        ],
        compiler_params=pltpu.CompilerParams(vmem_limit_bytes=VMEM_BYTES),
        name="forward_plain",
    )(flags, hidden.reshape(tokens, width), past, old, ridge, wmat, vecs, wqkv)


def backward_heads(s, p, first, heads, length, basis, width, qkv, mem, gatt, lse, head_par, grows, dq_t, gqkv, gmem):
    hd = width // heads
    half = length // 2
    rows = slice(s * length, (s + 1) * length)
    brows = slice(s * basis, (s + 1) * basis)
    masks = head_masks(2 * hd, hd)
    scale = LOG2E / math.sqrt(hd)
    c0 = pl.multiple_of(p * (2 * hd), 2 * hd)
    c1 = pl.multiple_of(width + c0, 2 * hd)
    c2 = pl.multiple_of(2 * width + c0, 2 * hd)
    here = pl.multiple_of((p - first) * (2 * hd), 2 * hd)
    wide = gmem.shape[1] // 2
    q = qkv[rows, pl.ds(c0, 2 * hd)]
    k = qkv[rows, pl.ds(c1, 2 * hd)]
    v = qkv[rows, pl.ds(c2, 2 * hd)]
    mv = mem[brows, pl.ds(c1, 2 * hd)]
    ga = gatt[rows, pl.ds(c0, 2 * hd)]
    k_t = k.T
    cent = ((iota((basis, 1), 0).astype(F32) + 0.5) / basis)
    allowed = iota((half, half), 0) <= iota((half, half), 1)
    dv = [0.0, 0.0]
    dk = [0.0, 0.0]
    dmv = 0.0
    for h in range(2):
        head = p * 2 + h
        km, vm, mvm, gam, qm = (a * masks[h] for a in (k, v, mv, ga, q))
        lanes = slice(h * hd, (h + 1) * hd)
        for b in range(2):
            cols = slice(b * half, (b + 1) * half)
            depth = (b + 1) * half
            sc = dot_nt(km[:depth], q[cols]) * scale - lse[s, head, :, cols]
            pr = jnp.exp2(causal(sc, allowed))
            dp = dot_nt(vm[:depth], ga[cols])
            inner = jnp.sum(pr * dp, axis=0, keepdims=True)
            ds = (pr * (dp - inner)).astype(BF)
            pb = pr.astype(BF)
            dvb = dot_nn(pb, gam[cols])
            dkb = dot_nn(ds, qm[cols])
            dq_t[pl.ds(pl.multiple_of(here + h * hd, hd), hd), cols] = dot_nn(k_t[lanes, :depth], ds)
            for i in range(b + 1):
                part = slice(i * half, (i + 1) * half)
                dv[i] = dv[i] + dvb[part]
                dk[i] = dk[i] + dkb[part]
            t = cent * head_par[head, 0:1, cols] - head_par[head, 1:2, cols]
            bas = jnp.exp2(head_par[head, 2:3, cols] - t * t)
            e = dot_nt(mvm, ga[cols]) * bas
            et = e * t
            grows[0, pl.ds(head, 1), cols] = jnp.sum(e, axis=0, keepdims=True)
            grows[1, pl.ds(head, 1), cols] = jnp.sum(et, axis=0, keepdims=True)
            grows[2, pl.ds(head, 1), cols] = jnp.sum(et * t, axis=0, keepdims=True)
            dmv = dmv + dot_nn(bas.astype(BF), gam[cols])
    for i in range(2):
        out_rows = slice(s * length + i * half, s * length + (i + 1) * half)
        gqkv[out_rows, pl.ds(c1, 2 * hd)] = (dk[i] * (1.0 / math.sqrt(hd))).astype(BF)
        gqkv[out_rows, pl.ds(c2, 2 * hd)] = dv[i].astype(BF)
    gmem[brows, pl.ds(pl.multiple_of(wide + here, 2 * hd), 2 * hd)] = dmv.astype(BF)


def backward_finish(s, start, heads, rows_of, qkv, mem, ublk, grows, dq_t, wmat, gqkv, gmem, msum):
    centre, wide, variance, root = rows_of
    n, length = dq_t.shape
    width = ublk.shape[2]
    basis = wmat.shape[0]
    hd = width // heads
    rows = slice(s * length, (s + 1) * length)
    brows = slice(s * basis, (s + 1) * basis)
    cols = slice(start, start + n)
    inv_var = 1.0 / variance
    s0, s1, s2 = grows[0], grows[1], grows[2]
    to_centre = s1 * (inv_var / root) * centre * (1.0 - centre)
    wide_slope = 0.02 / (1.0 + jnp.exp(-wide))
    to_wide = (-0.5 * s0 * inv_var + s2 * (0.5 * inv_var * inv_var) / (root * root)) * wide_slope
    head = iota((16, length), 0)
    live = (head >= start // hd) & (head < (start + n) // hd)
    g = jnp.concatenate([jnp.where(live, to_centre, 0.0), jnp.where(live, to_wide, 0.0)], axis=0)
    g_hi, g_lo = split_high_low(g)
    u_hi, u_lo = split_high_low(ublk[s, :, cols])
    dqm = dot_tn(u_hi, g_hi) + dot_tn(u_hi, g_lo) + dot_tn(u_lo, g_hi)
    total = dq_t[...] * (1.0 / math.sqrt(hd)) + dqm
    gqkv[rows, cols] = total.T.astype(BF)
    q = qkv[rows, cols]
    own = (iota((32, n), 0) % 16) == (iota((32, n), 1) + start) // hd
    r = dot_nn(g_hi, q) + dot_nn(g_lo, q)
    r = jnp.where(own, r, 0.0) * (1.0 / math.sqrt(hd))
    r_hi, r_lo = split_high_low(r)
    w = wmat[...][:, 0:32]
    gmem[brows, 0:n] = (dot_nn(w, r_hi) + dot_nn(w, r_lo)).astype(BF)
    mk = mem[brows, cols]
    add = dot_nt(r_hi, mk) + dot_nt(r_lo, mk)
    if msum.shape[0] == 32:
        msum[...] += add
    else:
        some, at = n // hd, start // hd
        msum[...] += jnp.concatenate([add[at:at + some], add[16 + at:16 + at + some]], axis=0)


def backward_input(r, width, hid, gm, gqkv, wqkv, vecs, gin, vsum):
    g = dot_nt(gqkv[r, :], wqkv[...])
    unit, inv = norm_parts(hid.astype(F32))
    gin[...] = (gm + norm_back(g, unit, inv, vecs[0:1, :])).astype(BF)
    vsum[0:1, :] += jnp.sum(g * unit, axis=0, keepdims=True)
    vsum[1:2, :] += jnp.sum(g, axis=0, keepdims=True)


def bias_sums(width, gqkv, out):
    out[0:1, :] = jnp.sum(gqkv[:, 0:width].astype(F32), axis=0, keepdims=True)
    out[1:2, :] = jnp.sum(gqkv[:, 2 * width:3 * width].astype(F32), axis=0, keepdims=True)


def backward_plain_call(heads, hidden, norm_t, coef_t, qkv, mem, gatt, gmid, lse, ublk, proj, wmat, vecs, wqkv):
    seqs, length, width = hidden.shape
    tokens = seqs * length
    brows = coef_t.shape[1]
    basis = brows // seqs
    vm = pl.BlockSpec(memory_space=pltpu.VMEM)

    def kernel(
        hidden, norm_t, coef_t, qkv, mem, gatt, gmid, lse, ublk, proj, wmat, vecs, wqkv,
        gin, dqkv, vsum, msum, gqkv, gmem, head_par, grows, dq_t,
    ):
        vsum[...] = jnp.zeros_like(vsum)
        msum[...] = jnp.zeros_like(msum)
        grows[...] = jnp.zeros_like(grows)
        for s in range(seqs):
            rows_of = basis_rows(proj[s], heads, basis, head_par)

            def pair(p, _):
                backward_heads(s, p, 0, heads, length, basis, width, qkv, mem, gatt, lse, head_par, grows, dq_t, gqkv, gmem)
                return 0

            lax.fori_loop(0, heads // 2, pair, 0)
            backward_finish(s, 0, heads, rows_of, qkv, mem, ublk, grows, dq_t, wmat, gqkv, gmem, msum)
        step = width // 3
        for j in range(9):
            c = slice(j * step, (j + 1) * step)
            y = dot_nn(norm_t[...], gqkv[:, c])
            if j >= 3:
                y = y + dot_nn(coef_t[...], gmem[:, (j - 3) * step:(j - 2) * step])
            dqkv[:, c] = y.astype(BF)

        def last(i, _):
            r = pl.ds(pl.multiple_of(i * 256, 256), 256)
            backward_input(r, width, hidden[r, :], gmid[r, :], gqkv, wqkv, vecs, gin.at[r, :], vsum.at[2:4, :])
            return 0

        lax.fori_loop(0, tokens // 256, last, 0)
        bias_sums(width, gqkv, vsum)

    shapes = (
        jax.ShapeDtypeStruct((tokens, width), BF),
        jax.ShapeDtypeStruct((width, 3 * width), BF),
        jax.ShapeDtypeStruct((8, width), F32),
        jax.ShapeDtypeStruct((32, basis), F32),
    )
    return pl.pallas_call(
        kernel,
        out_shape=shapes,
        in_specs=[vm] * 13,
        out_specs=[vm] * 4,
        scratch_shapes=[
            pltpu.VMEM((tokens, 3 * width), BF),
            pltpu.VMEM((brows, 2 * width), BF),
            pltpu.VMEM((heads, 8, length), F32),
            pltpu.VMEM((3, 16, length), F32),
            pltpu.VMEM((width, length), F32),
        ],
        compiler_params=pltpu.CompilerParams(vmem_limit_bytes=VMEM_BYTES),
        name="backward_plain",
    )(hidden.reshape(tokens, width), norm_t, coef_t, qkv, mem, gatt, gmid, lse, ublk, proj, wmat, vecs, wqkv)


class Reduce:
    SLOTS = 13

    def __init__(self, place, started, name, base, parts, bufs):
        self.p, self.s, self.name, self.base, self.parts = place, started, name, base, parts
        self.g, self.r1, self.r2, self.r3, self.r4, self.f = bufs

    def where(self, part):
        r0, rn, c0, cn = self.parts[part]
        return pl.ds(r0, rn), pl.ds(c0, cn)

    def core(self, *pieces):
        for i, (src, rows) in enumerate(pieces):
            self.s.go((self.name, 1), src, self.r1.at[:, :, :, rows, :], self.base + i, self.p.at(c=1 - self.p.c))

    def second(self):
        p = self.p
        self.s.arrived((self.name, 1))

        def step(i, _):
            at = (i // 8, (i // 2) % 4, i % 2)
            self.g[at] = self.g[at] + self.r1[at]
            return 0

        lax.fori_loop(0, 16, step, 0)
        for part in (0, 1):
            r, c = self.where(part)
            if part == 0:
                self.s.go((self.name, 2), self.g.at[1 - p.y, :, :, r, c], self.r2[0], self.base + 2, p.at(y=1 - p.y))
            else:
                self.s.go((self.name, 2), self.g.at[:, :, 1 - p.x, r, c], self.r2[1], self.base + 3, p.at(x=1 - p.x))

    def third(self):
        p = self.p
        self.s.arrived((self.name, 2))
        r, c = self.where(0)
        r_b, c_b = self.where(1)

        def step(i, _):
            z, k = i // 2, i % 2
            self.g[p.y, z, k, r, c] = self.g[p.y, z, k, r, c] + self.r2[0][z, k]
            self.g[k, z, p.x, r_b, c_b] = self.g[k, z, p.x, r_b, c_b] + self.r2[1][k, z]
            return 0

        lax.fori_loop(0, 8, step, 0)
        for part in (0, 1):
            self.send_third(part)

    def send_third(self, part):
        p = self.p
        r, c = self.where(part)
        if part == 0:
            self.s.go((self.name, 3), self.g.at[p.y, :, 1 - p.x, r, c], self.r3[0], self.base + 4, p.at(x=1 - p.x))
        else:
            self.s.go((self.name, 3), self.g.at[1 - p.y, :, p.x, r, c], self.r3[1], self.base + 5, p.at(y=1 - p.y))

    def along(self):
        p = self.p
        self.s.arrived((self.name, 3))

        def step(z, _):
            for part in self.parts:
                r, c = self.where(part)
                self.g[p.y, z, p.x, r, c] = self.g[p.y, z, p.x, r, c] + self.r3[part][z]
            return 0

        lax.fori_loop(0, 4, step, 0)
        self.send_along()

    early = None

    def summand(self, z):
        p = self.p
        return self.g.at[p.y, z, p.x] if self.early is None else self.early.at[z // 2, p.y, z % 2, p.x]

    def send_along(self):
        p = self.p
        for s in (1, 2, 3):
            to = p.far_z(s)
            self.s.go((self.name, 4), self.summand(to), self.r4.at[s - 1], self.base + 5 + s, p.at(z=to))

    def last(self, out, segments):
        p = self.p
        self.s.arrived((self.name, 4))
        own = self.summand(p.z)[...].astype(F32)
        self.f[...] = (own + self.r4[0].astype(F32)) + (self.r4[1].astype(F32) + self.r4[2].astype(F32))
        n = self.f.shape[0] // 2
        theirs = pl.ds(pl.multiple_of((1 - p.c) * n, 8), n)
        mine = pl.ds(pl.multiple_of(p.c * n, 8), n)
        for i, (c0, to, cn) in enumerate(segments):
            there = out.at[:, pl.ds(pl.multiple_of(to, 128), cn)]
            self.s.go((self.name, 5), self.f.at[theirs, pl.ds(c0, cn)], there, self.base + 9 + i, p.at(c=1 - p.c))
            there[...] = self.f[mine, c0:c0 + cn]

    def done(self):
        self.s.arrived((self.name, 5))


class Everywhere:
    SLOTS = 8

    def __init__(self, place, started, name, slot, held, got):
        self.p, self.s, self.name, self.slot, self.held, self.got = place, started, name, slot, held, got
        n = held.shape[-1] // 2
        self.half = pl.ds(pl.multiple_of(place.c * n, 128), n)

    def start(self, step):
        p, name, half = self.p, (self.name, step), self.half
        if step == 0:
            self.s.go(name, self.held.at[0], self.got.at[0], self.slot, p.at(c=1 - p.c))
        elif step == 1:
            for d in (1, 2, 3):
                to = p.at(y=(p.y + d // 2) % 2, x=(p.x + d) % 2)
                self.s.go(name, self.held.at[1, :, half], self.got.at[d, :, half], self.slot + d, to)
        elif step == 2:
            for s in (1, 2, 3):
                self.s.go(name, self.held.at[2, :, half], self.got.at[3 + s, :, half], self.slot + 3 + s, p.at(z=p.far_z(s)))
        else:
            ref = self.held.at[3, :, half]
            self.s.go(name, ref, ref, self.slot + 7, p.at(c=1 - p.c))

    def add(self, step):
        self.s.arrived((self.name, step))
        half = self.half
        if step == 0:
            self.held[1] = self.held[0] + self.got[0]
        elif step < 3:
            i = 1 if step == 1 else 4
            self.held[step + 1, :, half] = (self.held[step, :, half] + self.got[i, :, half]) + (
                self.got[i + 1, :, half] + self.got[i + 2, :, half])
        else:
            return self.held[3]
        self.start(step + 1)
        return None


BACK_STEPS = (
    (), (), (), (), (),
    ("xx", "o1"), ("p1",), ("a3", "b3"), ("o2", "q1"),
    ("p2",), ("o3", "q2"), ("p3",),
    ("r1",), ("q3",), ("w0", "k0"), ("r2", "w1", "k1"),
    ("l0",), ("r3", "l1", "w2", "k2"), ("l2", "w3", "k3", "d4", "a4", "b4", "p4", "o4", "q4"), ("l3", "r4"),
)


def backward_kernel(
    heads, devices,
    hidden, norm_h, coef_h, qkv_h, mem_h, gatt_h, gmid, lse, ublk, proj, wmat, vecs, vsum_a, usum, wq_h, p_out, gu_h, gd_h,
    gin, o_qkv, o_out, o_up, o_down, early, late, msum,
    norm_t, coef_t, qkv, mem, gatt, wq,
    gqkv, gmem, head_par, grows, dq_t, away, gm_buf, hid_buf, gin_buf,
    bufs, vsum, k_held, k_got, l_held, l_got, m_held, m_got, early_bufs, send, recv, local, early_send, early_recv,
):
    place = Place()
    p = place
    tokens, width = hidden.shape
    seqs, _, length = proj.shape
    basis = wmat.shape[0]
    ff = o_up.shape[1]
    st = Started(send, recv)
    names = "abdopqr"
    red = {n: Reduce(place, st, n, i * Reduce.SLOTS, parts, bufs[i]) for i, (n, (_, _, parts)) in enumerate(zip(names, reduce_shapes(width, ff, devices)))}
    base = len(names) * Reduce.SLOTS
    sums = {n: Everywhere(place, st, n, base + i * Everywhere.SLOTS, held, got)
            for i, (n, held, got) in enumerate((("k", k_held, k_got), ("w", m_held, m_got), ("l", l_held, l_got)))}
    loads = []
    for i, (src, dst) in enumerate(((qkv_h, qkv), (mem_h, mem), (gatt_h, gatt), (norm_h, norm_t), (coef_h, coef_t), (wq_h, wq))):
        copy = pltpu.make_async_copy(src, dst, local.at[i])
        copy.start()
        loads.append(copy)
    grows[...] = jnp.zeros_like(grows)
    vsum[...] = jnp.zeros_like(vsum)
    k_held[0] = jnp.concatenate([vsum_a[0:4, :], usum[0:4, :], jnp.zeros((8, width), F32)], axis=0)
    half = width // 2

    def side(c):
        return p_out.at[:, :, :, :, pl.ds(pl.multiple_of(c * half, 128), half)]

    er = EarlyReduce(place, early_send, early_recv, *early_bufs[:2], None, None, None, None, None, *early_bufs[2:])
    red["a"].g, red["b"].g, red["d"].early = er.g_u.at[0], er.g_u.at[1], er.g_d
    own = [pltpu.make_async_copy(src, dst, local.at[6 + i])
           for i, (src, dst) in enumerate(((gu_h, er.g_u), (gd_h, er.g_d), (side(p.c), red["o"].g)))]
    for copy in own:
        copy.start()
    place.hello(place.layer())

    def begin():
        place.wait_hello(place.layer())
        red["o"].core((side(1 - p.c), slice(None)))
        for copy in own:
            copy.wait()
        er.resume()
    pieces = 128
    outs = {
        "a": (o_up, lambda: [(k * half, k * width + p.c * half, half) for k in (0, 1)]),
        "b": (o_up, lambda: [(k * half, (2 + k) * width + p.c * half, half) for k in (0, 1)]),
        "d": (o_down, lambda: [(0, p.c * half, half)]),
        "o": (o_out, lambda: [(0, p.c * half, half)]),
    }
    for i, n in enumerate("pqr"):
        outs[n] = (o_qkv, lambda i=i: [(j * pieces, j * width + i * 2 * pieces + p.c * pieces, pieces) for j in range(3)])

    def perform(word):
        if word[0] == "x":
            er.up_add_second(2)
            er.up_add_second(3)
            red["a"].send_third(0)
            red["b"].send_third(1)
            er.down_add_third(0)
            er.down_add_third(1)
            red["d"].send_along()
        elif word[0] in sums:
            total, step = sums[word[0]], int(word[1])
            value = total.add(step)
            if step == 3:
                if word[0] == "w":
                    msum[...] = value
                elif word[0] == "l":
                    late[0:2, :] = value
                else:
                    early[...] = value[0:8]
                    late[2:4, :] = value[8:10]
        else:
            r, step = red[word[0]], word[1]
            if step == "1":
                r.second()
            elif step == "2":
                r.third()
            elif step == "3":
                r.along()
            else:
                out, segments = outs[word[0]]
                r.last(out, segments())

    steps = iter(BACK_STEPS)

    def advance():
        for word in next(steps, ()):
            perform(word)

    for copy in loads[:3]:
        copy.wait()
    chunk = 2 * pieces
    m_held[...] = jnp.zeros_like(m_held)
    rows_of = [basis_rows(proj[s], heads, basis, head_par.at[s]) for s in range(seqs)]
    for i in range(3):
        for s in range(seqs):
            for k in range(2):
                def one(j, _):
                    backward_heads(s, j, 2 * i, heads, length, basis, width, qkv, mem, gatt, lse, head_par.at[s], grows, dq_t, gqkv, gmem)
                    return 0

                lax.fori_loop(2 * i + k, 2 * i + k + 1, one, 0)
                if i + s + k == 0:
                    begin()
                if k == 0:
                    advance()
            backward_finish(s, i * chunk, heads, rows_of[s], qkv, mem, ublk, grows, dq_t, wmat, gqkv, gmem, m_held.at[0, 8 * i:8 * i + 8, :])
            if s < seqs - 1:
                advance()
        if i == 0:
            loads[3].wait()
            loads[4].wait()
        r = red["pqr"[i]]
        for j in range(3):
            c = j * width + i * chunk
            y = dot_nn(norm_t[...], gqkv[:, c:c + chunk])
            if j > 0:
                y = y + dot_nn(coef_t[...], gmem[:, (j - 1) * chunk:j * chunk])
            y = y.astype(BF).reshape(2, 4, 2, r.g.shape[3], chunk)
            low, high = y[..., :pieces], y[..., pieces:]
            keep, give = jnp.where(p.c == 0, low, high), jnp.where(p.c == 0, high, low)
            r.g[:, :, :, :, j * pieces:(j + 1) * pieces] = keep
            away[i, :, :, :, :, j * pieces:(j + 1) * pieces] = give
        r.core((away.at[i], slice(None)))
        if i == 2:
            sums["w"].start(0)
            bias_sums(width, gqkv, k_held.at[0, 8:10, :])
            sums["k"].start(0)
        advance()
    wflat = wq.reshape(width, 3 * width)
    loads[5].wait()
    blocks = tokens // 256

    def fetch(i):
        r = slice(i * 256, (i + 1) * 256)
        return (pltpu.make_async_copy(gmid.at[r, :], gm_buf.at[i % 2], local.at[16 + i % 2]),
                pltpu.make_async_copy(hidden.at[r, :], hid_buf.at[i % 2], local.at[18 + i % 2]))

    def emit(i):
        return pltpu.make_async_copy(gin_buf.at[i % 2], gin.at[i * 256:(i + 1) * 256, :], local.at[20 + i % 2])

    for i in (0, 1):
        for copy in fetch(i):
            copy.start()
    for i in range(blocks):
        for copy in fetch(i):
            copy.wait()
        if i >= 2:
            emit(i - 2).wait()
        backward_input(slice(i * 256, (i + 1) * 256), width, hid_buf[i % 2], gm_buf[i % 2], gqkv, wflat, vecs, gin_buf.at[i % 2], vsum)
        emit(i).start()
        if i + 2 < blocks:
            for copy in fetch(i + 2):
                copy.start()
        if i == blocks - 1:
            l_held[0] = vsum[...]
            sums["l"].start(0)
        advance()
    for _ in range(99):
        advance()
    for n in names:
        red[n].done()
    for i in (blocks - 2, blocks - 1):
        emit(i).wait()
    for copy in er.resumed():
        copy.wait_send()
    st.left()


def reduce_shapes(width, ff, devices):
    chip, chip_ff = 2 * width // devices, 2 * ff // devices
    h = width // 2
    more = (chip, h, {0: (0, chip, 0, 256), 1: (0, chip, 256, 128)})
    less = (chip, h, {0: (0, chip, 0, 128), 1: (0, chip, 128, 256)})
    return [(chip, width, {0: (0, chip, 0, width)}), (chip, width, {1: (0, chip, 0, width)}), (chip_ff, h, {}), more, less, more, less]


def backward_call(
    heads, devices, hidden, norm_t, coef_t, qkv, mem, gatt, gmid, lse, ublk, proj, wmat, vecs, vsum_a, usum, wq, p_out, g_up, g_down, ff,
):
    seqs, length, width = hidden.shape
    tokens = seqs * length
    brows = coef_t.shape[1]
    basis = brows // seqs
    vm = pl.BlockSpec(memory_space=pltpu.VMEM)
    anyw = pl.BlockSpec(memory_space=pl.ANY)
    shapes = (
        jax.ShapeDtypeStruct((tokens, width), BF),
        jax.ShapeDtypeStruct((width // devices, 3 * width), F32),
        jax.ShapeDtypeStruct((width // devices, width), F32),
        jax.ShapeDtypeStruct((width // devices, ff), F32),
        jax.ShapeDtypeStruct((ff // devices, width), F32),
        jax.ShapeDtypeStruct((8, width), F32),
        jax.ShapeDtypeStruct((4, width), F32),
        jax.ShapeDtypeStruct((24, basis), F32),
    )

    def buffers(i, shape):
        rows, cols, parts = shape
        none = pltpu.VMEM((8, 128), F32)
        whole = i > 2
        sizes = [parts.get(k, (0, 16, 0, 128)) for k in (0, 1)]
        (_, ra, _, ca), (_, rb, _, cb) = sizes
        return (
            none if i < 3 else pltpu.VMEM((2, 4, 2, rows, cols), BF),
            pltpu.VMEM((2, 4, 2, rows, cols), BF) if whole else none,
            (pltpu.VMEM((4, 2, ra, ca), BF), pltpu.VMEM((2, 4, rb, cb), BF)) if whole else (none, none),
            (pltpu.VMEM((4, ra, ca), BF), pltpu.VMEM((4, rb, cb), BF)),
            pltpu.VMEM((3, rows, cols), BF),
            pltpu.VMEM((rows, cols), F32),
        )

    chip, chip_ff = 2 * width // devices, 2 * ff // devices
    table = reduce_shapes(width, ff, devices)
    slots = len(table) * Reduce.SLOTS + 3 * Everywhere.SLOTS
    return pl.pallas_call(
        lambda *refs: backward_kernel(heads, devices, *refs),
        out_shape=shapes,
        in_specs=[anyw] * 7 + [vm] * 7 + [anyw] * 4,
        out_specs=[anyw] + [vm] * 7,
        scratch_shapes=[pltpu.VMEM(a.shape, a.dtype) for a in (norm_t, coef_t, qkv, mem, gatt, wq)] + [
            pltpu.VMEM((tokens, 3 * width), BF),
            pltpu.VMEM((brows, 512), BF),
            pltpu.VMEM((seqs, heads, 8, length), F32),
            pltpu.VMEM((3, 16, length), F32),
            pltpu.VMEM((256, length), F32),
            pltpu.VMEM((3, 2, 4, 2, 2 * width // devices, 384), BF),
            pltpu.VMEM((2, 256, width), F32),
            pltpu.VMEM((2, 256, width), BF),
            pltpu.VMEM((2, 256, width), BF),
            [buffers(i, shape) for i, shape in enumerate(table)],
            pltpu.VMEM((2, width), F32),
            pltpu.VMEM((4, 16, width), F32),
            pltpu.VMEM((7, 16, width), F32),
            pltpu.VMEM((4, 2, width), F32),
            pltpu.VMEM((7, 2, width), F32),
            pltpu.VMEM((4, 24, basis), F32),
            pltpu.VMEM((7, 24, basis), F32),
            [pltpu.VMEM(shape, BF) for shape in (
                g_down.shape, g_up.shape, (2, 4, 2, chip, width // 2), (2, 2, 4, chip, width // 2), (2, 2, 2, chip_ff // 2, width // 2))],
            pltpu.SemaphoreType.DMA((slots,)),
            pltpu.SemaphoreType.DMA((slots,)),
            pltpu.SemaphoreType.DMA((22,)),
            pltpu.SemaphoreType.DMA((EarlyReduce.SLOTS,)),
            pltpu.SemaphoreType.DMA((EarlyReduce.SLOTS,)),
        ],
        compiler_params=pltpu.CompilerParams(vmem_limit_bytes=56 * 1024 * 1024, collective_id=1, has_side_effects=True),
        name="backward",
    )(hidden.reshape(tokens, width), norm_t, coef_t, qkv, mem, gatt, gmid, lse, ublk, proj, wmat, vecs, vsum_a, usum, wq, p_out, g_up, g_down)


def finish_call(heads, devices, ff, early, late, msum, whole):
    width = early.shape[1]
    basis = msum.shape[1]
    e, rows = width // devices, basis // devices
    group = 4
    vm = pl.BlockSpec(memory_space=pltpu.VMEM)
    anyw = pl.BlockSpec(memory_space=pl.ANY)
    n = len(whole)

    def kernel(*refs):
        early, late, msum = refs[:3]
        sources, results = refs[3:3 + n], refs[3 + n:3 + 2 * n]
        gain_a, shift_a, qv, out_b, gain_m, shift_m, up_b, down_b, mean, wide = refs[3 + 2 * n:-1 - n]
        held, sem = refs[-1 - n:-1], refs[-1]
        taken = [pltpu.make_async_copy(a, b, sem.at[i]) for i, (a, b) in enumerate(zip(sources, held))]
        copies = [pltpu.make_async_copy(a, b, sem.at[n + i]) for i, (a, b) in enumerate(zip(held, results))]
        for copy in taken:
            copy.start()
        me = lax.axis_index("dp") * lax.axis_size("fsdp") + lax.axis_index("fsdp")

        def thirds(x):
            high = x.astype(BF)
            rest = x - high.astype(F32)
            middle = rest.astype(BF)
            return high, middle, (rest - middle.astype(F32)).astype(BF)

        def pick(x, start, size):
            at = (iota((x.shape[1], size), 0) == iota((x.shape[1], size), 1) + start).astype(F32).astype(BF)
            return sum(dot_nn(part, at) for part in thirds(x))

        def row_of(x, i):
            return jnp.sum(jnp.where(iota(x.shape, 0) == i, x, 0.0), axis=0, keepdims=True)

        for take, copy in zip(taken, copies):
            take.wait()
            copy.start()
        some = pick(early[...], me * e, e)
        down_b[...], gain_m[...], shift_m[...], out_b[...] = (some[i:i + 1] for i in range(4))
        some = pick(late[...], me * e, e)
        gain_a[...], shift_a[...] = some[0:1], some[1:2]
        k = devices // 2
        qv[...] = pick(row_of(late[2:4, :], me // k), me % k * 2 * e, 2 * e)
        k = devices * width // ff
        up_b[...] = pick(row_of(early[4:8, :], me // k), me % k * (ff // devices), ff // devices)
        at = (iota((rows, basis), 1) == iota((rows, basis), 0) + me * rows).astype(F32).astype(BF)
        for out, first in ((mean, 0), (wide, group)):
            x = jnp.concatenate([msum[i + first:i + first + group, :] for i in range(0, 2 * heads, 2 * group)], axis=0)
            out[...] = sum(dot_nt(at, part) for part in thirds(x))
        for copy in copies:
            copy.wait()

    small = [(1, e), (1, e), (1, 2 * e), (1, e), (1, e), (1, e), (1, ff // devices), (1, e), (rows, heads), (rows, heads)]
    return pl.pallas_call(
        kernel,
        out_shape=[jax.ShapeDtypeStruct(a.shape, a.dtype) for a in whole] + [jax.ShapeDtypeStruct(s, F32) for s in small],
        in_specs=[vm] * 3 + [anyw] * n,
        out_specs=[anyw] * n + [vm] * len(small),
        scratch_shapes=[pltpu.VMEM(a.shape, a.dtype) for a in whole] + [pltpu.SemaphoreType.DMA((2 * n,))],
        name="finish",
    )(early, late, msum, *whole)


def gather(x):
    return lax.all_gather(x, AXES, axis=0, tiled=True)


def scatter(x):
    return lax.psum_scatter(x, AXES, scatter_dimension=0, tiled=True)


def shards_plain(
    hidden, grad_out, past_states, old_coeffs, fresh_flags, ridge_map,
    gain_attn, shift_attn, qkv_weight, qv_bias, out_weight, out_bias,
    gain_mlp, shift_mlp, up_weight, up_bias, down_weight, down_bias,
    mean_weight, width_weight,
):
    seqs, length, width = hidden.shape
    heads = mean_weight.shape[1]
    devices = lax.axis_size("dp") * lax.axis_size("fsdp")
    full_qkv, full_out, full_up, full_down = (gather(w) for w in (qkv_weight, out_weight, up_weight, down_weight))
    rows = jnp.zeros((mean_weight.shape[0], 128), BF)
    rows = rows.at[:, 0:heads].set(mean_weight).at[:, 16:16 + heads].set(width_weight)
    wmat = gather(rows)
    full_qv = gather(qv_bias)
    vecs = jnp.stack(
        [gather(gain_attn), gather(shift_attn), full_qv[:width], full_qv[width:],
         gather(out_bias), gather(gain_mlp), gather(shift_mlp), gather(down_bias)]).astype(F32)
    ubias = gather(up_bias).astype(F32).reshape(-1, width)
    ubias = jnp.concatenate([ubias, jnp.zeros((8 - ubias.shape[0], width), F32)], axis=0)

    norm_t, coef_t, qkv, mem, att, lse, ublk, proj = forward_plain_call(
        heads, fresh_flags, hidden, past_states, old_coeffs, ridge_map, wmat, vecs, full_qkv)
    output, gmid, gatt, dout, dup, ddown, vsum_a, usum = middle_call(
        att, hidden, grad_out, full_out, full_up, full_down, vecs, ubias)
    gin, dqkv, vsum_b, msum = backward_plain_call(
        heads, hidden, norm_t, coef_t, qkv, mem, gatt, gmid, lse, ublk, proj, wmat, vecs, full_qkv)

    up_sum = usum.reshape(-1)[:up_bias.shape[0] * devices]
    big = [scatter(a.astype(F32)) for a in (dqkv, dout, dup, ddown)]
    small = [
        scatter(a) for a in (
            vsum_b[2], vsum_b[3], jnp.concatenate([vsum_b[0], vsum_b[1]]), vsum_a[3], vsum_a[1], vsum_a[2],
            up_sum, vsum_a[0], msum[0:heads].T, msum[16:16 + heads].T)
    ]
    return (
        output.reshape(seqs, length, width), gin.reshape(seqs, length, width),
        small[0], small[1], big[0], small[2], big[1], small[3], small[4], small[5],
        big[2], small[6], big[3], small[7], small[8], small[9],
    )


def shards_block(
    hidden, grad_out, past_states, old_coeffs, fresh_flags, ridge_map,
    gain_attn, shift_attn, qkv_weight, qv_bias, out_weight, out_bias,
    gain_mlp, shift_mlp, up_weight, up_bias, down_weight, down_bias,
    mean_weight, width_weight,
):
    seqs, length, width = hidden.shape
    heads = mean_weight.shape[1]
    devices = 32
    ff = up_weight.shape[1]
    e = width // devices
    def put(v, row, col):
        v = v.reshape((1, -1)) if v.ndim == 1 else v
        return jnp.pad(v, ((row, 32 - row - v.shape[0]), (col, 128 - col - v.shape[1])))

    small = (
        put(mean_weight, 0, 0) + put(width_weight, 0, 16)
        + put(gain_attn, 16, 0) + put(shift_attn, 16, e) + put(out_bias, 16, 2 * e) + put(gain_mlp, 16, 3 * e)
        + put(shift_mlp, 17, 0) + put(down_bias, 17, e) + put(qv_bias, 17, 2 * e) + put(up_bias, 18, 0))

    norm_t, coef_t, qkv, mem, output, gmid, gatt, dout, g_up, g_down, wq, lse, ublk, proj, wmat, vecs, vsum_a, usum = forward_call(
        heads, devices, fresh_flags, hidden, past_states, old_coeffs, ridge_map, grad_out, small, qkv_weight, out_weight, up_weight, down_weight)
    gin, d_qkv, d_out, d_up, d_down, early, late, msum = backward_call(
        heads, devices, hidden, norm_t, coef_t, qkv, mem, gatt, gmid, lse, ublk, proj, wmat, vecs, vsum_a, usum, wq,
        dout.reshape(2, 4, 2, width // 16, width), g_up, g_down, ff)

    (output, gin, d_qkv, d_out, d_up, d_down, gain_a, shift_a, qv, out_b, gain_m, shift_m, up_b, down_b, mean, wide) = finish_call(
        heads, devices, ff, early, late, msum, (output, gin, d_qkv, d_out, d_up, d_down))
    flat = lambda v: v.reshape(v.shape[1])
    return (
        output.reshape(seqs, length, width), gin.reshape(seqs, length, width),
        flat(gain_a), flat(shift_a), d_qkv, flat(qv), d_out, flat(out_b), flat(gain_m), flat(shift_m),
        d_up, flat(up_b), d_down, flat(down_b), mean, wide,
    )


def solution(mesh):
    rows = P(AXES, None)
    cube = P(AXES, None, None)
    one = P(AXES)
    in_specs = (cube, cube, cube, cube, one, P(), one, one, rows, one, rows, one, one, one, rows, one, rows, one, rows, rows)
    out_specs = (cube, cube, one, one, rows, one, rows, one, one, one, rows, one, rows, one, rows, rows)
    body = shards_block if mesh.shape["dp"] == 2 and mesh.shape["fsdp"] == 16 else shards_plain
    return jax.shard_map(body, mesh=mesh, in_specs=in_specs, out_specs=out_specs, check_vma=False)
```

```python
import math

import jax
import jax.numpy as jnp
from jax import lax
from jax.experimental import pallas as pl
from jax.experimental.pallas import tpu as pltpu
from jax.sharding import PartitionSpec as P

EPS = 1e-05
LOG2E = 1.4426950408889634
BF = jnp.bfloat16
F32 = jnp.float32
AXES = ("dp", "fsdp")
VMEM_BYTES = 60 * 1024 * 1024


def dot_nn(a, b):
    return lax.dot_general(a, b, (((1,), (0,)), ((), ())), preferred_element_type=F32)


def dot_nt(a, b):
    return lax.dot_general(a, b, (((1,), (1,)), ((), ())), preferred_element_type=F32)


def dot_tn(a, b):
    return lax.dot_general(a, b, (((0,), (0,)), ((), ())), preferred_element_type=F32)


def split_high_low(x):
    high = x.astype(BF)
    return high, (x - high.astype(F32)).astype(BF)


def iota(shape, dim):
    return lax.broadcasted_iota(jnp.int32, shape, dim)


def head_masks(pair_lanes, head_dim):
    lane = iota((1, pair_lanes), 1)
    return [((lane // head_dim) == h).astype(F32).astype(BF) for h in range(pair_lanes // head_dim)]


def norm_parts(x):
    mean = jnp.mean(x, axis=-1, keepdims=True)
    centred = x - mean
    variance = jnp.mean(centred * centred, axis=-1, keepdims=True)
    inv = lax.rsqrt(variance + EPS)
    return centred * inv, inv


def norm_back(grad, unit, inv, gain):
    g = grad * gain
    return inv * (g - jnp.mean(g, axis=-1, keepdims=True) - unit * jnp.mean(g * unit, axis=-1, keepdims=True))


MESH = pl.DeviceIdType.MESH


class Place:
    def __init__(self):
        self.y = lax.axis_index("dp")
        f = lax.axis_index("fsdp")
        self.z, self.x, self.c = f // 4, (f // 2) % 2, f % 2

    def at(self, y=None, z=None, x=None, c=None):
        y, z, x, c = (b if a is None else a for a, b in ((y, self.y), (z, self.z), (x, self.x), (c, self.c)))
        return (y, z * 4 + x * 2 + c)

    def far_z(self, s):
        return (self.z + s) % 4

    def others(self):
        return [self.at(c=1 - self.c), self.at(x=1 - self.x), self.at(y=1 - self.y)] + [
            self.at(z=self.far_z(s)) for s in (1, 2, 3)]

    def layer(self):
        return self.others() + [self.at(y=1 - self.y, x=1 - self.x)]

    def hello(self, devices):
        barrier = pltpu.get_barrier_semaphore()
        for d in devices:
            pl.semaphore_signal(barrier, inc=1, device_id=d, device_id_type=MESH)

    def wait_hello(self, devices):
        pl.semaphore_wait(pltpu.get_barrier_semaphore(), len(devices))


class Weight:
    def __init__(self, index, rows, half, parts):
        self.index, self.rows, self.half, self.parts = index, rows, half, parts

    def where(self, part, c=None):
        r0, rn, c0, cn = self.parts[part]
        if c is None:
            return pl.ds(r0, rn), pl.ds(c0, cn)
        return pl.ds(r0, rn), pl.ds(pl.multiple_of(c * self.half + c0, 128), cn)

    def columns(self, c):
        return pl.ds(pl.multiple_of(c * self.half, 128), self.half)


def split_columns(n):
    first = (n // 128 + 1) // 2 * 128
    return first


def weight_table(width, ff, devices):
    chip = 2 * width // devices
    chip_ff = 2 * ff // devices
    items = []
    for i, n in enumerate((3 * width, width, ff)):
        half = n // 2
        first = split_columns(half)
        items.append(Weight(i, chip, half, ((0, chip, 0, first), (0, chip, first, half - first))))
    half = width // 2
    items.append(Weight(3, chip_ff, half, ((0, chip_ff // 2, 0, half), (chip_ff // 2, chip_ff // 2, 0, half))))
    return items


def nested(conds, act):
    if not conds:
        act()
        return

    @pl.when(conds[0]())
    def _():
        nested(conds[1:], act)


class Started:
    def __init__(self, send, recv):
        self.send, self.recv, self.live = send, recv, {}

    def go(self, name, src, dst, slot, dev):
        copy = pltpu.make_async_remote_copy(
            src_ref=src, dst_ref=dst, send_sem=self.send.at[slot], recv_sem=self.recv.at[slot],
            device_id=dev, device_id_type=MESH)
        copy.start()
        self.live.setdefault(name, []).append(copy)

    def arrived(self, name):
        for copy in self.live[name]:
            copy.wait_recv()

    def left(self, name=None):
        for key in list(self.live) if name is None else [name]:
            for copy in self.live.pop(key):
                copy.wait_send()


class Gather:
    SLOTS = 2 * 23

    def __init__(self, place, send, recv, base, w, full):
        self.p, self.send, self.recv, self.base, self.w, self.full = place, send, recv, base, w, full
        self.begun = []

    def ref(self, part, y, z, x):
        if part is None:
            return self.full.at[y, z, x, :, self.w.columns(self.p.c)]
        r, c = self.w.where(part, self.p.c)
        return self.full.at[y, z, x, r, c]

    def go(self, src, dst, send, recv, dev, conds, like):
        pltpu.make_async_remote_copy(
            src_ref=src, dst_ref=dst, send_sem=self.send.at[self.base + send()], recv_sem=self.recv.at[self.base + recv],
            device_id=dev, device_id_type=MESH).start()
        self.begun.append((send, conds, like))

    def wait(self, ref, slot):
        pltpu.make_async_remote_copy(
            src_ref=ref, dst_ref=ref, send_sem=self.send.at[self.base], recv_sem=self.recv.at[self.base + slot],
            device_id=self.p.at(c=1 - self.p.c), device_id_type=MESH).wait_recv()

    def left(self):
        for send, conds, like in self.begun:
            def act():
                pltpu.make_async_remote_copy(
                    src_ref=like(), dst_ref=like(), send_sem=self.send.at[self.base + send()], recv_sem=self.recv.at[self.base],
                    device_id=self.p.at(c=1 - self.p.c), device_id_type=MESH).wait_send()

            nested(conds, act)

    def along(self, j, act):
        here = self.p.z
        for z, cond, toward in ((lambda: here - j, lambda: here >= j, 1), (lambda: here + j, lambda: here + j <= 3, -1)):
            nested((cond,), lambda: act(z, (cond,), toward))

    def pass_z(self, src, dst, z, toward, conds, like):
        p = self.p
        more = (lambda: p.z <= 2) if toward == 1 else (lambda: p.z >= 1)
        nested((more,), lambda: self.go(
            src, dst, lambda: z() + (0 if toward == 1 else 4), z(), p.at(z=p.z + toward), conds + (more,), like))

    def partner(self, part, step):
        p = self.p
        return p.at(x=1 - p.x) if (part + step) % 2 == 0 else p.at(y=1 - p.y)

    def behind(self, part):
        p = self.p
        return (p.y, 1 - p.x) if part == 0 else (1 - p.y, p.x)

    def own_z(self):
        return self.p.z

    def one(self, part):
        return self.ref(part, 0, 0, 0)

    def start(self, block):
        p = self.p
        for toward in (1, -1):
            self.pass_z(block, self.ref(None, p.y, p.z, p.x), self.own_z, toward, (), lambda: self.one(None))
        for part in (0, 1):
            self.onward(part, self.own_z, block.at[self.w.where(part)], ())

    def onward(self, part, z, src, conds):
        p = self.p
        dst = self.ref(part, p.y, z(), p.x)
        o = part * 23
        like = lambda: self.one(part)
        self.go(src, dst, lambda: o + 8 + z(), o + 8 + z(), self.partner(part, 0), conds, like)
        self.go(src, dst, lambda: o + 12 + z(), o + 12 + z(), self.partner(part, 1), conds, like)

    def on_z(self, j):
        def act(z, conds, toward):
            whole = self.ref(None, self.p.y, z(), self.p.x)
            self.wait(whole, z())
            self.pass_z(whole, whole, z, toward, conds, lambda: self.one(None))
            for part in (0, 1):
                self.onward(part, z, self.ref(part, self.p.y, z(), self.p.x), conds)

        self.along(j, act)

    def on_second(self, j):
        def act(z, conds, toward):
            for part in (0, 1):
                self.second_on(part, z, conds)

        if j == 0:
            act(self.own_z, (), 0)
        else:
            self.along(j, act)

    def second_on(self, part, z, conds):
        y, x = self.behind(part)
        ref = self.ref(part, y, z(), x)
        o = part * 23
        self.wait(ref, o + 8 + z())
        self.go(ref, ref, lambda: o + 16 + z(), o + 16 + z(), self.partner(part, 1), conds, lambda: self.one(part))

    def core(self, step):
        p = self.p
        for part in (0, 1):
            o = part * 23
            if step == 2:
                for z in range(4):
                    y, x = (1 - p.y, p.x) if part == 0 else (p.y, 1 - p.x)
                    self.wait(self.ref(part, y, z, x), o + 12 + z)
                    self.wait(self.ref(part, 1 - p.y, z, 1 - p.x), o + 16 + z)
            self.go_core(lambda part=part: self.of_step(part, step), o + 20 + step)

    def of_step(self, part, step):
        p = self.p
        if step == 0:
            y, x = p.y, p.x
        elif step == 1:
            y, x = self.behind(part)
        else:
            y, x = (1 - p.y, slice(None)) if part == 0 else (slice(None), 1 - p.x)
        return self.ref(part, y, slice(None), x)

    def go_core(self, make, slot):
        self.go(make(), make(), lambda: slot, slot, self.p.at(c=1 - self.p.c), (), make)

    def finish(self):
        p = self.p
        for part in (0, 1):
            r, c = self.w.where(part, 1 - p.c)
            for step in range(3):
                if step == 2:
                    ref = self.full.at[1 - p.y, :, :, r, c] if part == 0 else self.full.at[:, :, 1 - p.x, r, c]
                else:
                    y, x = (p.y, p.x) if step == 0 else self.behind(part)
                    ref = self.full.at[y, :, x, r, c]
                self.wait(ref, part * 23 + 20 + step)


class LateGather(Gather):
    def start(self, block):
        for part in (0, 1):
            self.onward(part, self.own_z, block.at[self.w.where(part)], ())

    def on_third(self):
        p = self.p
        for part in (0, 1):
            o = part * 23
            y, x = (1 - p.y, p.x) if part == 0 else (p.y, 1 - p.x)
            self.wait(self.ref(part, y, p.z, x), o + 12 + p.z)
            self.wait(self.ref(part, 1 - p.y, p.z, 1 - p.x), o + 16 + p.z)
        ref = self.layer(p.z)
        for toward in (1, -1):
            self.pass_z(ref, ref, self.own_z, toward, (), lambda: self.layer(0))

    def layer(self, z):
        return self.ref(None, slice(None), z, slice(None))

    def on_z(self, j):
        def act(z, conds, toward):
            ref = self.layer(z())
            self.wait(ref, z())
            self.pass_z(ref, ref, z, toward, conds, lambda: self.layer(0))

        self.along(j, act)

    def core(self):
        self.go_core(lambda: self.ref(None, slice(None), slice(None), slice(None)), 20)

    def finish(self):
        self.wait(self.full.at[:, :, :, :, self.w.columns(1 - self.p.c)], 20)


def middle_body(
    att, hidden, gout, wout, wup, wdown, vecs, ubias, vsum, usum,
    x_t, dout, mid, x, acc, gacc, act_s, slope_s, outs, local, sem, put_down, put_up, hook,
):
    output_h, gmid_h, gatt_h, dout_h = outs
    tokens, width = hidden.shape
    ff = wup.shape[1]
    block = 256
    blocks = tokens // block
    chunk = ubias.shape[1]
    chunks = ff // chunk
    out_bias, gain, shift, down_bias = (vecs[i:i + 1, :] for i in (4, 5, 6, 7))

    def enter(i, _):
        r = pl.ds(pl.multiple_of(i * block, block), block)
        m = hidden[r, :].astype(F32) + dot_nn(att[r, :], wout[...]) + out_bias
        mid[r, :] = m
        unit, _ = norm_parts(m)
        y = (unit * gain + shift).astype(BF)
        x[r, :] = y
        x_t[:, r] = y.T
        acc[r, :] = jnp.zeros((block, width), F32)
        gacc[r, :] = jnp.zeros((block, width), F32)
        hook("enter", i)
        return 0

    lax.fori_loop(0, blocks, enter, 0)
    hook("entered", 0)

    def chunk_of(i):
        return (i % 2) * 2 + i // 2

    def first(i):
        j = chunk_of(i)
        c = pl.ds(pl.multiple_of(j * chunk, chunk), chunk)
        slot = i % 2
        w_up = wup[:, c]
        bias = ubias[pl.ds(j, 1), :]
        for b in range(blocks):
            r = slice(b * block, (b + 1) * block)
            u = dot_nn(x[r, :], w_up) + bias
            u2 = u * u
            th = jnp.tanh(u * (0.7978845608028654 + 0.7978845608028654 * 0.044715 * u2))
            half_one = 0.5 + 0.5 * th
            act_s[slot, r, :] = (u * half_one).astype(BF)
            slope = half_one + (0.5 * u) * (1.0 - th * th) * (
                0.7978845608028654 + 3 * 0.7978845608028654 * 0.044715 * u2)
            slope_s[slot, r, :] = slope.astype(BF)
        for k in range(2):
            part = slice(k * chunk // 2, (k + 1) * chunk // 2)
            put_down(i, k, dot_tn(act_s[slot, :, part], gout[...]).astype(BF))
        hook("first", i)

    def second(i):
        j = chunk_of(i)
        c = pl.ds(pl.multiple_of(j * chunk, chunk), chunk)
        slot = i % 2
        w_up, w_down = wup[:, c], wdown[c, :]
        colsum = jnp.zeros((1, chunk), F32)
        for b in range(blocks):
            r = slice(b * block, (b + 1) * block)
            gu = (dot_nt(gout[r, :], w_down) * slope_s[slot, r, :].astype(F32)).astype(BF)
            colsum = colsum + jnp.sum(gu.astype(F32), axis=0, keepdims=True)
            slope_s[slot, r, :] = gu
            acc[r, :] += dot_nn(act_s[slot, r, :], w_down)
            gacc[r, :] += dot_nt(gu, w_up)
        usum[pl.ds(j, 1), :] = colsum
        hook("middle", i)
        for k in range(2):
            part = slice(k * width // 2, (k + 1) * width // 2)
            put_up(i, k, dot_nn(x_t[part, :], slope_s[slot]).astype(BF))
        hook("second", i)

    def ahead(i, _):
        first(i)
        return 0

    lax.fori_loop(0, 2, ahead, 0)
    hook("ready", 0)
    usum[...] = jnp.zeros_like(usum)

    def both(i, _):
        second(i)

        @pl.when(i + 2 < chunks)
        def _():
            first(i + 2)

        hook("both", i)
        return 0

    lax.fori_loop(0, chunks, both, 0)
    vsum[...] = jnp.zeros_like(vsum)

    def rows_out(i):
        r = pl.ds(pl.multiple_of(i * block, block), block)
        return (pltpu.make_async_copy(act_s.at[0, r, :], output_h.at[r, :], local.at[sem + 1 + 3 * i]),
                pltpu.make_async_copy(mid.at[r, :], gmid_h.at[r, :], local.at[sem + 2 + 3 * i]),
                pltpu.make_async_copy(act_s.at[1, r, :], gatt_h.at[r, :], local.at[sem + 3 + 3 * i]))

    def leave(i, _):
        r = pl.ds(pl.multiple_of(i * block, block), block)
        m = mid[r, :]
        act_s[0, r, :] = (m + acc[r, :] + down_bias).astype(BF)
        unit, inv = norm_parts(m)
        g = gacc[r, :]
        go = gout[r, :].astype(F32)
        gm = go + norm_back(g, unit, inv, gain)
        mid[r, :] = gm
        gp = gm.astype(BF)
        x[r, :] = gp
        act_s[1, r, :] = dot_nt(gp, wout[...]).astype(BF)
        for copy in rows_out(i):
            copy.start()
        vsum[0:1, :] += jnp.sum(go, axis=0, keepdims=True)
        vsum[1:2, :] += jnp.sum(g * unit, axis=0, keepdims=True)
        vsum[2:3, :] += jnp.sum(g, axis=0, keepdims=True)
        vsum[3:4, :] += jnp.sum(gp.astype(F32), axis=0, keepdims=True)
        hook("leave", i)
        return 0

    lax.fori_loop(0, blocks, leave, 0)
    for j in range(width // 256):
        c = slice(j * 256, (j + 1) * 256)
        dout[:, c] = dot_tn(att[...], x[:, c]).astype(BF)
    final = pltpu.make_async_copy(dout, dout_h, local.at[sem])
    final.start()
    hook("end", 0)
    for i in range(blocks):
        for copy in rows_out(i):
            copy.wait()
    final.wait()


def middle_scratch(tokens, width, chunk):
    return [
        pltpu.VMEM((tokens, width), F32),
        pltpu.VMEM((tokens, width), BF),
        pltpu.VMEM((tokens, width), F32),
        pltpu.VMEM((tokens, width), F32),
        pltpu.VMEM((2, tokens, chunk), BF),
        pltpu.VMEM((2, tokens, chunk), BF),
    ]


def middle_call(att, hidden, gout, wout, wup, wdown, vecs, ubias):
    tokens, width = att.shape
    ff = wup.shape[1]
    chunk = ubias.shape[1]
    vm = pl.BlockSpec(memory_space=pltpu.VMEM)
    anyw = pl.BlockSpec(memory_space=pl.ANY)
    shapes = (
        jax.ShapeDtypeStruct((tokens, width), BF),
        jax.ShapeDtypeStruct((tokens, width), F32),
        jax.ShapeDtypeStruct((tokens, width), BF),
        jax.ShapeDtypeStruct((width, width), BF),
        jax.ShapeDtypeStruct((width, ff), BF),
        jax.ShapeDtypeStruct((ff, width), BF),
        jax.ShapeDtypeStruct((8, width), F32),
        jax.ShapeDtypeStruct((8, chunk), F32),
    )

    def kernel(att, hidden, gout, wout, wup, wdown, vecs, ubias, o, gm, ga, do, du, dd, vsum, usum, *scratch):
        def place(i):
            return ((i % 2) * 2 + i // 2) * chunk

        def put_down(i, k, v):
            dd[pl.ds(pl.multiple_of(place(i) + k * chunk // 2, chunk // 2), chunk // 2), :] = v

        def put_up(i, k, v):
            du[k * width // 2:(k + 1) * width // 2, pl.ds(pl.multiple_of(place(i), chunk), chunk)] = v

        middle_body(att, hidden, gout, wout, wup, wdown, vecs, ubias, vsum, usum, *scratch[:-1], (o, gm, ga, do), scratch[-1], 0,
                    put_down, put_up, lambda where, i: None)

    return pl.pallas_call(
        kernel,
        out_shape=shapes,
        in_specs=[vm] * 8,
        out_specs=[anyw] * 4 + [vm] * 4,
        scratch_shapes=[pltpu.VMEM((width, tokens), BF), pltpu.VMEM((width, width), BF)] + middle_scratch(tokens, width, chunk) + [pltpu.SemaphoreType.DMA((1 + 3 * (tokens // 256),))],
        compiler_params=pltpu.CompilerParams(vmem_limit_bytes=58 * 1024 * 1024),
        name="middle",
    )(att, hidden.reshape(tokens, width), gout.reshape(tokens, width), wout, wup, wdown, vecs, ubias)


class EarlyReduce:
    SLOTS = 20

    def __init__(self, place, send, recv, g_d, g_u, away_d, away_u, r1_d, r1_u, r2_d, r2_y, r2_x, r3_d):
        self.p, self.send, self.recv = place, send, recv
        self.g_d, self.g_u, self.away_d, self.away_u = g_d, g_u, away_d, away_u
        self.r1_d, self.r1_u, self.r2_d, self.r2_y, self.r2_x, self.r3_d = r1_d, r1_u, r2_d, r2_y, r2_x, r3_d
        self.n = g_d.shape[-1]
        self.h = g_d.shape[-2] // 2

    def copy(self, src, dst, slot, dev):
        return pltpu.make_async_remote_copy(
            src_ref=src, dst_ref=dst, send_sem=self.send.at[slot], recv_sem=self.recv.at[slot], device_id=dev, device_id_type=MESH)

    def mate(self):
        return self.p.at(c=1 - self.p.c)

    def sides(self, v):
        low, high = v[..., :self.n], v[..., self.n:]
        return jnp.where(self.p.c == 0, low, high), jnp.where(self.p.c == 0, high, low)

    def down_core(self, i):
        return self.copy(self.away_d.at[i % 2], self.r1_d.at[i // 2, i % 2], i, self.mate())

    def put_down(self, i, k, v):
        if k == 0:
            @pl.when(i >= 2)
            def _():
                self.down_core(i - 2).wait_send()

        keep, give = self.sides(v.reshape(2, 2 * self.h, 2 * self.n))
        self.g_d[i // 2, i % 2, k] = keep
        self.away_d[i % 2, k] = give

    def down_second(self, t):
        p = self.p
        a, b = pl.ds(0, self.h), pl.ds(self.h, self.h)
        return (self.copy(self.g_d.at[t, 1 - p.y, :, :, a, :], self.r2_d.at[t, 0], 8 + 2 * t, p.at(y=1 - p.y)),
                self.copy(self.g_d.at[t, :, :, 1 - p.x, b, :], self.r2_d.at[t, 1], 9 + 2 * t, p.at(x=1 - p.x)))

    def down_third(self, t):
        p = self.p
        a, b = pl.ds(0, self.h), pl.ds(self.h, self.h)
        return (self.copy(self.g_d.at[t, p.y, :, 1 - p.x, a, :], self.r3_d.at[t, 0], 12 + 2 * t, p.at(x=1 - p.x)),
                self.copy(self.g_d.at[t, 1 - p.y, :, p.x, b, :], self.r3_d.at[t, 1], 13 + 2 * t, p.at(y=1 - p.y)))

    def down_add_core(self, t):
        for y in (0, 1):
            self.down_core(2 * t + y).wait_recv()

        def step(i, _):
            at = (t, i // 4, (i // 2) % 2, i % 2)
            self.g_d[at] = self.g_d[at] + self.r1_d[at]
            return 0

        lax.fori_loop(0, 8, step, 0)
        for copy in self.down_second(t):
            copy.start()

    def down_add_second(self, t):
        p, h = self.p, self.h
        for copy in self.down_second(t):
            copy.wait_recv()

        def step(i, _):
            u, v = i // 2, i % 2
            at, to = (t, p.y, u, v, slice(0, h)), (t, 0, u, v)
            self.g_d[at] = self.g_d[at] + self.r2_d[to]
            at, to = (t, u, v, p.x, slice(h, 2 * h)), (t, 1, u, v)
            self.g_d[at] = self.g_d[at] + self.r2_d[to]
            return 0

        lax.fori_loop(0, 4, step, 0)

    def down_add_third(self, t):
        p, h = self.p, self.h
        for copy in self.down_third(t):
            copy.wait_recv()
        for z in (0, 1):
            for part in (0, 1):
                rows = slice(part * h, (part + 1) * h)
                at = (t, p.y, z, p.x, rows)
                self.g_d[at] = self.g_d[at] + self.r3_d[t, part, z]

    def up_core(self, i):
        return self.copy(self.away_u.at[i % 2], self.r1_u.at[i], 4 + i, self.mate())

    def rows_u(self):
        return self.g_u.shape[-2]

    def put_up(self, i, k, v):
        if k == 0:
            @pl.when(i >= 2)
            def _():
                self.up_core(i - 2).wait_send()

        keep, give = self.sides(v)
        c = pl.ds(pl.multiple_of((i // 2) * self.n, 128), self.n)
        self.g_u[i % 2, k, :, :, :, c] = keep.reshape(4, 2, self.rows_u(), self.n)
        self.away_u[i % 2, k] = give.reshape(4, 2, self.rows_u(), self.n)

    def up_second(self, i):
        p = self.p
        t = i % 2
        c = pl.ds((i // 2) * self.n, self.n)
        if t == 0:
            return self.copy(self.g_u.at[0, 1 - p.y, :, :, :, c], self.r2_y.at[i // 2], 16 + i, p.at(y=1 - p.y))
        return self.copy(self.g_u.at[1, :, :, 1 - p.x, :, c], self.r2_x.at[i // 2], 16 + i, p.at(x=1 - p.x))

    def up_add_core(self, i):
        self.up_core(i).wait_recv()
        c = slice((i // 2) * self.n, (i // 2 + 1) * self.n)

        def step(b, _):
            at = (b // 8, (b // 2) % 4, b % 2)
            here = (i % 2,) + at + (slice(None), c)
            self.g_u[here] = self.g_u[here] + self.r1_u[(i,) + at]
            return 0

        lax.fori_loop(0, 16, step, 0)
        if i < 2:
            self.up_second(i).start()

    def up_add_second(self, i):
        p = self.p
        self.up_second(i).wait_recv()
        c = slice((i // 2) * self.n, (i // 2 + 1) * self.n)

        def step(b, _):
            if i % 2 == 0:
                here, got = (0, p.y, b // 2, b % 2, slice(None), c), self.r2_y[i // 2, b // 2, b % 2]
            else:
                here, got = (1, b // 4, b % 4, p.x, slice(None), c), self.r2_x[i // 2, b // 4, b % 4]
            self.g_u[here] = self.g_u[here] + got
            return 0

        lax.fori_loop(0, 8, step, 0)

    def left(self):
        for i in (2, 3):
            self.down_core(i).wait_send()
            self.up_core(i).wait_send()
        for t in (0, 1):
            for copy in self.down_second(t):
                copy.wait_send()
            self.up_second(t).wait_send()

    def resume(self):
        for copy in self.resumed():
            copy.start()

    def resumed(self):
        return [self.up_second(2), self.up_second(3), *self.down_third(0), *self.down_third(1)]


def forward_coeffs(s, flags, past, old, ridge, coeffs, coef_t):
    length, basis = past.shape[1], ridge.shape[0]
    samples = ridge.shape[1] - length
    brows = slice(s * basis, (s + 1) * basis)
    diff = (iota((samples, basis), 0) - iota((samples, basis), 1)).astype(F32)
    sampled = jnp.exp(-0.5 * diff * diff).astype(BF)
    keep = (1 - flags[s]).astype(F32)
    old_signal = (dot_nn(sampled, old[s]) * keep).astype(BF)
    co = (dot_nn(ridge[:, :samples], old_signal) + dot_nn(ridge[:, samples:], past[s])).astype(BF)
    coeffs[brows, :] = co
    coef_t[:, brows] = co.T


def forward_projections(s, half, heads, length, basis, hidden, vecs, wmat, wqkv, normed, norm_t, coeffs, qkv, mem, ublk, proj, head_par):
    width = hidden.shape[1]
    hd = width // heads
    rows = slice(s * length, (s + 1) * length)
    brows = slice(s * basis, (s + 1) * basis)
    step = width // 3
    if half == 0:
        unit, _ = norm_parts(hidden[rows, :].astype(F32))
        nrm = (unit * vecs[0:1, :] + vecs[1:2, :]).astype(BF)
        normed[...] = nrm
        norm_t[:, rows] = nrm.T
    for j in range(9) if half == 0 else ():
        cols = slice(j * step, (j + 1) * step)
        y = dot_nn(normed[...], wqkv[:, cols])
        if j < 3:
            y = y + vecs[2:3, cols]
        elif j >= 6:
            y = y + vecs[3:4, (j - 6) * step:(j - 5) * step]
        qkv[rows, cols] = y.astype(BF)
    if half == 0:
        return
    for j in range(6):
        cols = slice(j * step, (j + 1) * step)
        wcols = slice(width + j * step, width + (j + 1) * step)
        mem[brows, cols] = dot_nn(coeffs[brows, :], wqkv[:, wcols]).astype(BF)
    raw = dot_tn(wmat[...], mem[brows, 0:width])[0:32, :]
    own = (iota((32, width), 0) % 16) == (iota((32, width), 1) // hd)
    u = jnp.where(own, raw, 0.0) * (1.0 / math.sqrt(hd))
    ublk[s] = u
    u_hi, u_lo = split_high_low(u)
    q = qkv[rows, 0:width]
    pr = dot_nt(u_hi, q) + dot_nt(u_lo, q)
    proj[s] = pr
    basis_rows(pr, heads, basis, head_par)


def basis_rows(pr, heads, basis, head_par):
    centre = 1.0 / (1.0 + jnp.exp(-pr[0:16]))
    wide = pr[16:32]
    soft = jnp.maximum(wide, 0.0) + jnp.log(1.0 + jnp.exp(-jnp.abs(wide)))
    variance = (soft + 0.5) * 0.02
    inv_root = lax.rsqrt(variance)
    root = inv_root * math.sqrt(0.5 * LOG2E)
    shift_log = jnp.log(inv_root) * LOG2E - math.log2(basis)
    for h in range(heads):
        head_par[h, 0:1, :] = root[h:h + 1]
        head_par[h, 1:2, :] = centre[h:h + 1] * root[h:h + 1]
        head_par[h, 2:3, :] = shift_log[h:h + 1]
    return centre, wide, variance, root


def causal(scores, allowed):
    n = allowed.shape[0]
    last = jnp.where(allowed, scores[-n:], -1e30)
    return last if scores.shape[0] == n else jnp.concatenate([scores[:-n], last], axis=0)


def forward_heads(s, first, last, heads, length, basis, width, qkv, mem, att, lse, head_par, att_t):
    hd = width // heads
    half = length // 2
    rows = slice(s * length, (s + 1) * length)
    brows = slice(s * basis, (s + 1) * basis)
    masks = head_masks(2 * hd, hd)
    scale = LOG2E / math.sqrt(hd)

    def pair(p, _):
        c0 = pl.multiple_of(p * (2 * hd), 2 * hd)
        q = qkv[rows, pl.ds(c0, 2 * hd)]
        k = qkv[rows, pl.ds(pl.multiple_of(width + c0, 2 * hd), 2 * hd)]
        v_t = qkv[rows, pl.ds(pl.multiple_of(2 * width + c0, 2 * hd), 2 * hd)].T
        mv_t = mem[brows, pl.ds(pl.multiple_of(width + c0, 2 * hd), 2 * hd)].T
        cent = ((iota((basis, 1), 0).astype(F32) + 0.5) / basis)
        allowed = iota((half, half), 0) <= iota((half, half), 1)
        for h in range(2):
            head = p * 2 + h
            km = k * masks[h]
            lanes = slice(h * hd, (h + 1) * hd)
            for b in range(2):
                cols = slice(b * half, (b + 1) * half)
                depth = (b + 1) * half
                sc = causal(dot_nt(km[:depth], q[cols]) * scale, allowed)
                top = jnp.max(sc, axis=0, keepdims=True)
                e = jnp.exp2(sc - top)
                total = jnp.sum(e, axis=0, keepdims=True)
                out = dot_nn(v_t[lanes, :depth], e.astype(BF)) / total
                lse[s, head, :, cols] = top + jnp.log(total) * LOG2E
                t = cent * head_par[head, 0:1, cols] - head_par[head, 1:2, cols]
                bas = jnp.exp2(head_par[head, 2:3, cols] - t * t).astype(BF)
                out = out + dot_nn(mv_t[lanes, :], bas)
                att_t[lanes, cols] = out
        att[rows, pl.ds(c0, 2 * hd)] = att_t[...].T.astype(BF)
        return 0

    lax.fori_loop(first, last, pair, 0)


def unpack_small(small, wmat, vecs, ubias, devices, width, ff):
    flat = small.reshape(devices * 32, 128)
    wmat[...] = small.reshape(devices, 32, 128)[:, 0:16, :].reshape(devices * 16, 128)
    every = flat[...]

    def spread(row, offset, each, n):
        pick = (iota((devices, devices * 32), 1) == iota((devices, devices * 32), 0) * 32 + row)
        mine = dot_nn(pick.astype(F32).astype(BF), every).astype(BF)
        place = iota((128, n), 0) == iota((128, n), 1) % each + offset
        wide = dot_nn(mine, place.astype(F32).astype(BF))
        own = iota((devices, n), 1) // each == iota((devices, n), 0)
        return jnp.sum(jnp.where(own, wide, 0.0), axis=0, keepdims=True)

    e = width // devices
    vecs[0:1, :] = spread(16, 0, e, width)
    vecs[1:2, :] = spread(16, e, e, width)
    both = spread(17, 2 * e, 2 * e, 2 * width)
    vecs[2:3, :] = both[:, :width]
    vecs[3:4, :] = both[:, width:]
    vecs[4:5, :] = spread(16, 2 * e, e, width)
    vecs[5:6, :] = spread(16, 3 * e, e, width)
    vecs[6:7, :] = spread(17, 0, e, width)
    vecs[7:8, :] = spread(17, e, e, width)
    up = spread(18, 0, ff // devices, ff)
    chunk = ubias.shape[1]
    ubias[...] = jnp.zeros_like(ubias)
    for j in range(ff // chunk):
        ubias[j:j + 1, :] = up[:, j * chunk:(j + 1) * chunk]


FIRST_STEPS = (
    "#0", "qz1", "qs0", "os0", "qz2", "qs1", "+0", "qz3", "ug", "own", "ot", "qc0", "#1", "qs2", "+1", "qs3", "qc1",
    "uz1", "us0", "oz1", "+2", "uz2", "us1", "oz2", "qc2",
)
LATER_STEPS = (
    ("uz3", "us2", "dg", "oz3", "oc"), ("us3", "uc0", "uc1"), ("dz1",), ("ds0",), ("dz2",), ("ds1",), ("dz3",), ("dc0",),
    (), ("ds2",), (), ("uc2",), ("ds3",), ("dc1",),
)


def forward_kernel(
    heads, devices,
    flags, hidden_h, past_h, old_h, ridge_h, gout_h, small, qkv_s, out_s, up_s, down_s,
    norm_h, coef_h, qkv_h, mem_h, output_h, gmid_h, gatt_h, dout_h, gu_h, gd_h, wq_h,
    lse, ublk, proj, wmat, vecs, vsum, usum,
    hidden, gout, att, wq, wo, wu, wd, ubias,
    wide_s, wide_r, block, block_d, sfull, early, send, recv, local, early_send, early_recv,
):
    place = Place()
    p = place
    tokens, width = hidden.shape
    seqs, length = past_h.shape[0], past_h.shape[1]
    basis = ridge_h.shape[0]
    ff = up_s.shape[1]
    t_qkv, t_out, t_up, t_down = weight_table(width, ff, devices)
    st = Started(send, recv)
    n = Gather.SLOTS
    g_qkv = Gather(place, send, recv, 0, t_qkv, wq)
    g_up = Gather(place, send, recv, n, t_up, wu)
    g_down = Gather(place, send, recv, 2 * n, t_down, wd)
    g_out = LateGather(place, send, recv, 3 * n, t_out, wo)
    base = 4 * n
    nh = wide_r.shape[1]
    blocks = {
        "q": block.at[:, 0:t_qkv.half], "o": block.at[:, t_qkv.half:t_qkv.half + t_out.half],
        "u": block.at[:, t_qkv.half + t_out.half:nh], "d": block_d}
    gather_of = {"q": g_qkv, "o": g_out, "u": g_up, "d": g_down}

    def pass_on(word):
        g, what, n = gather_of[word[0]], word[1], word[2:]
        if what == "g":
            g.start(blocks[word[0]])
        elif what == "z":
            g.on_z(int(n))
        elif what == "s":
            g.on_second(int(n))
        elif what == "t":
            g.on_third()
        elif what == "f":
            g.finish()
        elif n:
            g.core(int(n))
        else:
            g.core()

    stores = []

    def store(src, dst, rows=None):
        i = len(stores)

        def make():
            a, b = (src, dst) if rows is None else (src.at[rows, :], dst.at[rows, :])
            return pltpu.make_async_copy(a, b, local.at[9 + i])

        make().start()
        stores.append(make)

    def attention(norm_t, coef_t, qkv, mem, past, old, ridge, normed, coeffs, head_par, att_t):
        forward_attention(
            heads, devices, place, (flags, hidden_h, past_h, old_h, ridge_h, gout_h, small, qkv_s, out_s, up_s, down_s),
            (t_qkv, t_out, t_up, t_down), st, (g_qkv, g_up, g_down, g_out), base, store, blocks, pass_on,
            (norm_h, coef_h, qkv_h, mem_h, wq_h),
            lse, ublk, proj, wmat, vecs, hidden, gout, norm_t, coef_t, qkv, mem, att, wq, ubias,
            wide_s, wide_r, block, block_d, sfull, local,
            past, old, ridge, normed, coeffs, head_par, att_t)
        for make in stores:
            make().wait()

    pl.run_scoped(
        attention,
        pltpu.VMEM((width, tokens), BF),
        pltpu.VMEM((width, seqs * basis), BF),
        pltpu.VMEM((tokens, 3 * width), BF),
        pltpu.VMEM((seqs * basis, 2 * width), BF),
        pltpu.VMEM(past_h.shape, BF),
        pltpu.VMEM(old_h.shape, BF),
        pltpu.VMEM(ridge_h.shape, BF),
        pltpu.VMEM((length, width), BF),
        pltpu.VMEM((seqs * basis, width), BF),
        pltpu.VMEM((heads, 8, length), F32),
        pltpu.VMEM((2 * (width // heads), length), F32),
    )

    er = EarlyReduce(place, early_send, early_recv, *early)
    sem = 9 + 2 * seqs + 3

    def hook(where, i):
        def at(n, *acts):
            @pl.when(i == n)
            def _():
                for act, arg in acts:
                    act(arg)

        if where == "first":
            er.down_core(i).start()
        elif where == "entered":
            pass_on("uf")
        elif where == "ready":
            for word in ("dc2", "df"):
                pass_on(word)
        elif where == "second":
            er.up_core(i).start()
            at(1, (er.down_add_core, 0))
            at(3, (er.down_add_second, 0))
        elif where == "middle":
            at(2, (er.down_add_core, 1))
        elif where == "both":
            at(0, (er.up_add_core, 0))
            at(1, (er.up_add_core, 1))
        elif where == "leave":
            at(1, (er.up_add_core, 2), (er.up_add_core, 3))
            at(3, (er.up_add_second, 0), (er.up_add_second, 1))
        elif where == "end":
            er.down_add_second(1)

    wflat = wq.reshape(width, 3 * width)

    def feed_forward(*scratch):
        middle_body(
            att, hidden, gout, wo.reshape(width, width), wu.reshape(width, ff), wd.reshape(ff, width), vecs, ubias, vsum, usum,
            wflat.at[:, 0:tokens], wflat.at[:, tokens:tokens + width], *scratch, (output_h, gmid_h, gatt_h, dout_h), local, sem, er.put_down, er.put_up, hook)
        out = [pltpu.make_async_copy(er.g_u, gu_h, local.at[sem + 14]), pltpu.make_async_copy(er.g_d, gd_h, local.at[sem + 15])]
        for copy in out:
            copy.start()
        er.left()
        for g in (g_up, g_down, g_out):
            g.left()
        for copy in out:
            copy.wait()

    pl.run_scoped(feed_forward, *middle_scratch(tokens, width, ubias.shape[1]))


def forward_attention(
    heads, devices, place, inputs, table, st, gathers, base, store, blocks, pass_on, outs,
    lse, ublk, proj, wmat, vecs, hidden, gout, norm_t, coef_t, qkv, mem, att, wq, ubias,
    wide_s, wide_r, block, block_d, sfull, local,
    past, old, ridge, normed, coeffs, head_par, att_t,
):
    p = place
    flags, hidden_h, past_h, old_h, ridge_h, gout_h, small, qkv_s, out_s, up_s, down_s = inputs
    t_qkv, t_out, t_up, t_down = table
    g_qkv, g_up, g_down, g_out = gathers
    norm_h, coef_h, qkv_h, mem_h, wq_h = outs
    tokens, width = hidden.shape
    seqs, length = past.shape[0], past.shape[1]
    basis = ridge.shape[0]
    ff = up_s.shape[1]
    place.hello(place.others())
    loads = []
    for i, (src, dst) in enumerate(((ridge_h, ridge), (old_h, old), (past_h, past), (hidden_h, hidden), (gout_h, gout))):
        copy = pltpu.make_async_copy(src, dst, local.at[i])
        copy.start()
        loads.append(copy)
    pos = 0
    for half in range(2):
        for ref, w in ((qkv_s, t_qkv), (out_s, t_out), (up_s, t_up)):
            wide_s[:, pos:pos + w.half] = ref[:, half * w.half:(half + 1) * w.half].astype(F32)
            pos += w.half
    nh = pos // 2
    sfull[p.y, p.z, p.x, p.c] = small[...]
    ed = down_s.shape[0]
    hd_cols = width // 2
    block_d[pl.ds(pl.multiple_of(p.c * ed, 16), ed), :] = down_s[:, pl.ds(pl.multiple_of(p.c * hd_cols, 128), hd_cols)]

    place.wait_hello(place.others())
    mate = p.at(c=1 - p.c)
    there = pl.multiple_of((1 - p.c) * nh, 128)
    st.go("wide", wide_s.at[:, pl.ds(there, t_qkv.half)], wide_r.at[:, 0:t_qkv.half], base, mate)
    st.go("wide2", wide_s.at[:, pl.ds(pl.multiple_of(there + t_qkv.half, 128), nh - t_qkv.half)], wide_r.at[:, t_qkv.half:nh], base + 8, mate)
    ref = sfull.at[p.y, p.z, p.x, p.c]
    st.go("s0", ref, ref, base + 1, mate)
    st.go("down", down_s.at[:, pl.ds(pl.multiple_of((1 - p.c) * hd_cols, 128), hd_cols)],
          block_d.at[pl.ds(pl.multiple_of(p.c * ed, 16), ed), :], base + 2, mate)

    def make_block(c0, cn):
        mine = wide_s[:, pl.ds(pl.multiple_of(p.c * nh + c0, 128), cn)]
        other = wide_r[:, c0:c0 + cn]
        block[:, c0:c0 + cn] = jnp.concatenate(
            [jnp.where(p.c == 0, mine, other), jnp.where(p.c == 0, other, mine)], axis=0).astype(BF)

    b_qkv, b_out, b_up = blocks["q"], blocks["o"], blocks["u"]
    own = []

    def keep_own(g, src, i):
        copy = pltpu.make_async_copy(src, g.full.at[p.y, p.z, p.x, :, g.w.columns(p.c)], local.at[i])
        copy.start()
        own.append(copy)

    st.arrived("wide")
    make_block(0, t_qkv.half)
    g_qkv.start(b_qkv)
    st.arrived("s0")
    ref = sfull.at[p.y, p.z, p.x]
    for s in (1, 2, 3):
        st.go("sz", ref, ref, base + 2 + s, p.at(z=p.far_z(s)))
    st.arrived("wide2")
    make_block(t_qkv.half, nh - t_qkv.half)
    g_out.start(b_out)
    st.arrived("down")
    for i, (g, src) in enumerate(((g_qkv, b_qkv), (g_out, b_out), (g_up, b_up), (g_down, block_d))):
        keep_own(g, src, 5 + i)
    loads[0].wait()
    loads[1].wait()
    loads[2].wait()
    def small_step(i):
        if i == 0:
            st.arrived("sz")
            ref = sfull.at[p.y, :, p.x]
            st.go("sx", ref, ref, base + 6, p.at(x=1 - p.x))
        elif i == 1:
            st.arrived("sx")
            ref = sfull.at[p.y]
            st.go("sy", ref, ref, base + 7, p.at(y=1 - p.y))
        else:
            st.arrived("sy")
            unpack_small(sfull, wmat, vecs, ubias, devices, width, ff)

    def own_in_place():
        for copy in own:
            copy.wait()

    def perform(word):
        if word == "own":
            own_in_place()
        elif word[0] == "#":
            forward_coeffs(int(word[1]), flags, past, old, ridge, coeffs, coef_t)
        elif word[0] == "+":
            small_step(int(word[1]))
        else:
            pass_on(word)

    for word in FIRST_STEPS:
        perform(word)
    loads[3].wait()
    g_qkv.finish()
    wflat = wq.reshape(width, 3 * width)
    store(wq, wq_h)
    store(coef_t, coef_h)

    def project(s, half):
        forward_projections(s, half, heads, length, basis, hidden, vecs, wmat, wflat, normed, norm_t, coeffs, qkv, mem, ublk, proj, head_par)

    def attend(s, a, b):
        forward_heads(s, a, b, heads, length, basis, width, qkv, mem, att, lse, head_par, att_t)

    events = iter(LATER_STEPS)

    def step(count=1):
        for _ in range(count):
            for word in next(events, ()):
                perform(word)

    pairs = heads // 2
    for s in range(seqs):
        project(s, 0)
        step()
        project(s, 1)
        store(qkv, qkv_h, slice(s * length, (s + 1) * length))
        store(mem, mem_h, slice(s * basis, (s + 1) * basis))
        if s == seqs - 1:
            store(norm_t, norm_h)
        step()
        for a in range(pairs):
            attend(s, a, a + 1)
            step()
    step(99)
    g_out.finish()
    loads[4].wait()
    st.left()
    g_qkv.left()


def forward_call(heads, devices, flags, hidden, past, old, ridge, gout, small, qkv_s, out_s, up_s, down_s):
    seqs, length, width = hidden.shape
    basis = ridge.shape[0]
    tokens = seqs * length
    ff = up_s.shape[1]
    chip = 2 * width // devices
    chip_ff = 2 * ff // devices
    vm = pl.BlockSpec(memory_space=pltpu.VMEM)
    anyw = pl.BlockSpec(memory_space=pl.ANY)
    full = (2, 4, 2, chip, 3 * width)
    n = width // 2
    far = [
        ((width, tokens), BF), ((width, seqs * basis), BF), ((tokens, 3 * width), BF), ((seqs * basis, 2 * width), BF),
        ((tokens, width), BF), ((tokens, width), F32), ((tokens, width), BF),
        ((width, width), BF), ((2, 2, 4, 2, chip, 2 * n), BF), ((2, 2, 2, 2, chip_ff, n), BF), (full, BF)]
    near = [
        ((seqs, heads, 1, length), F32), ((seqs, 32, width), F32), ((seqs, 32, length), F32),
        ((basis, 128), BF), ((8, width), F32), ((8, width), F32), ((8, width), F32)]
    nh = (4 * width + ff) // 2
    slots = 4 * Gather.SLOTS + 9
    return pl.pallas_call(
        lambda *refs: forward_kernel(heads, devices, *refs),
        out_shape=tuple(jax.ShapeDtypeStruct(*m) for m in far + near),
        in_specs=[pl.BlockSpec(memory_space=pltpu.SMEM)] + [anyw] * 5 + [vm] * 5,
        out_specs=[anyw] * len(far) + [vm] * len(near),
        scratch_shapes=[
            pltpu.VMEM((tokens, width), BF),
            pltpu.VMEM((tokens, width), BF),
            pltpu.VMEM((tokens, width), BF),
            pltpu.VMEM(full, BF),
            pltpu.VMEM((2, 4, 2, chip, width), BF),
            pltpu.VMEM((2, 4, 2, chip, ff), BF),
            pltpu.VMEM((2, 4, 2, chip_ff, width), BF),
            pltpu.VMEM((8, width), F32),
            pltpu.VMEM((width // devices, 2 * nh), F32),
            pltpu.VMEM((width // devices, nh), F32),
            pltpu.VMEM((chip, nh), BF),
            pltpu.VMEM((chip_ff, width // 2), BF),
            pltpu.VMEM((2, 4, 2, 2, 32, 128), BF),
            [pltpu.VMEM(shape, BF) for shape in (
                (2, 2, 2, 2, chip_ff, n), (2, 2, 4, 2, chip, 2 * n), (2, 2, 2, chip_ff, n), (2, 2, 4, 2, chip, n),
                (2, 2, 2, 2, chip_ff, n), (4, 2, 4, 2, chip, n),
                (2, 2, 2, 2, chip_ff // 2, n), (2, 4, 2, chip, n), (2, 2, 4, chip, n), (8, 128))],
            pltpu.SemaphoreType.DMA((slots,)),
            pltpu.SemaphoreType.DMA((slots,)),
            pltpu.SemaphoreType.DMA((9 + 2 * seqs + 3 + 17,)),
            pltpu.SemaphoreType.DMA((EarlyReduce.SLOTS,)),
            pltpu.SemaphoreType.DMA((EarlyReduce.SLOTS,)),
        ],
        compiler_params=pltpu.CompilerParams(vmem_limit_bytes=61 * 1024 * 1024, collective_id=0, has_side_effects=True),
        name="forward",
    )(flags, hidden.reshape(tokens, width), past, old, ridge, gout.reshape(tokens, width), small, qkv_s, out_s, up_s, down_s)


def forward_plain_call(heads, flags, hidden, past, old, ridge, wmat, vecs, wqkv):
    seqs, length, width = hidden.shape
    basis = ridge.shape[0]
    tokens = seqs * length
    vm = pl.BlockSpec(memory_space=pltpu.VMEM)

    def kernel(
        flags, hidden, past, old, ridge, wmat, vecs, wqkv,
        norm_t, coef_t, qkv, mem, att, lse, ublk, proj, normed, coeffs, head_par, att_t,
    ):
        for s in range(seqs):
            forward_coeffs(s, flags, past, old, ridge, coeffs, coef_t)
            for half in (0, 1):
                forward_projections(s, half, heads, length, basis, hidden, vecs, wmat, wqkv, normed, norm_t, coeffs, qkv, mem, ublk, proj, head_par)
            forward_heads(s, 0, heads // 2, heads, length, basis, width, qkv, mem, att, lse, head_par, att_t)

    shapes = (
        jax.ShapeDtypeStruct((width, tokens), BF),
        jax.ShapeDtypeStruct((width, seqs * basis), BF),
        jax.ShapeDtypeStruct((tokens, 3 * width), BF),
        jax.ShapeDtypeStruct((seqs * basis, 2 * width), BF),
        jax.ShapeDtypeStruct((tokens, width), BF),
        jax.ShapeDtypeStruct((seqs, heads, 1, length), F32),
        jax.ShapeDtypeStruct((seqs, 32, width), F32),
        jax.ShapeDtypeStruct((seqs, 32, length), F32),
    )
    return pl.pallas_call(
        kernel,
        out_shape=shapes,
        in_specs=[pl.BlockSpec(memory_space=pltpu.SMEM)] + [vm] * 7,
        out_specs=[vm] * 8,
        scratch_shapes=[
            pltpu.VMEM((length, width), BF),
            pltpu.VMEM((seqs * basis, width), BF),
            pltpu.VMEM((heads, 8, length), F32),
            pltpu.VMEM((2 * (width // heads), length), F32),
        ],
        compiler_params=pltpu.CompilerParams(vmem_limit_bytes=VMEM_BYTES),
        name="forward_plain",
    )(flags, hidden.reshape(tokens, width), past, old, ridge, wmat, vecs, wqkv)


def backward_heads(s, p, first, heads, length, basis, width, qkv, mem, gatt, lse, head_par, grows, dq_t, gqkv, gmem):
    hd = width // heads
    half = length // 2
    rows = slice(s * length, (s + 1) * length)
    brows = slice(s * basis, (s + 1) * basis)
    masks = head_masks(2 * hd, hd)
    scale = LOG2E / math.sqrt(hd)
    c0 = pl.multiple_of(p * (2 * hd), 2 * hd)
    c1 = pl.multiple_of(width + c0, 2 * hd)
    c2 = pl.multiple_of(2 * width + c0, 2 * hd)
    here = pl.multiple_of((p - first) * (2 * hd), 2 * hd)
    wide = gmem.shape[1] // 2
    q = qkv[rows, pl.ds(c0, 2 * hd)]
    k = qkv[rows, pl.ds(c1, 2 * hd)]
    v = qkv[rows, pl.ds(c2, 2 * hd)]
    mv = mem[brows, pl.ds(c1, 2 * hd)]
    ga = gatt[rows, pl.ds(c0, 2 * hd)]
    k_t = k.T
    cent = ((iota((basis, 1), 0).astype(F32) + 0.5) / basis)
    allowed = iota((half, half), 0) <= iota((half, half), 1)
    dv = [0.0, 0.0]
    dk = [0.0, 0.0]
    dmv = 0.0
    for h in range(2):
        head = p * 2 + h
        km, vm, mvm, gam, qm = (a * masks[h] for a in (k, v, mv, ga, q))
        lanes = slice(h * hd, (h + 1) * hd)
        for b in range(2):
            cols = slice(b * half, (b + 1) * half)
            depth = (b + 1) * half
            sc = dot_nt(km[:depth], q[cols]) * scale - lse[s, head, :, cols]
            pr = jnp.exp2(causal(sc, allowed))
            dp = dot_nt(vm[:depth], ga[cols])
            inner = jnp.sum(pr * dp, axis=0, keepdims=True)
            ds = (pr * (dp - inner)).astype(BF)
            pb = pr.astype(BF)
            dvb = dot_nn(pb, gam[cols])
            dkb = dot_nn(ds, qm[cols])
            dq_t[pl.ds(pl.multiple_of(here + h * hd, hd), hd), cols] = dot_nn(k_t[lanes, :depth], ds)
            for i in range(b + 1):
                part = slice(i * half, (i + 1) * half)
                dv[i] = dv[i] + dvb[part]
                dk[i] = dk[i] + dkb[part]
            t = cent * head_par[head, 0:1, cols] - head_par[head, 1:2, cols]
            bas = jnp.exp2(head_par[head, 2:3, cols] - t * t)
            e = dot_nt(mvm, ga[cols]) * bas
            et = e * t
            grows[0, pl.ds(head, 1), cols] = jnp.sum(e, axis=0, keepdims=True)
            grows[1, pl.ds(head, 1), cols] = jnp.sum(et, axis=0, keepdims=True)
            grows[2, pl.ds(head, 1), cols] = jnp.sum(et * t, axis=0, keepdims=True)
            dmv = dmv + dot_nn(bas.astype(BF), gam[cols])
    for i in range(2):
        out_rows = slice(s * length + i * half, s * length + (i + 1) * half)
        gqkv[out_rows, pl.ds(c1, 2 * hd)] = (dk[i] * (1.0 / math.sqrt(hd))).astype(BF)
        gqkv[out_rows, pl.ds(c2, 2 * hd)] = dv[i].astype(BF)
    gmem[brows, pl.ds(pl.multiple_of(wide + here, 2 * hd), 2 * hd)] = dmv.astype(BF)


def backward_finish(s, start, heads, rows_of, qkv, mem, ublk, grows, dq_t, wmat, gqkv, gmem, msum):
    centre, wide, variance, root = rows_of
    n, length = dq_t.shape
    width = ublk.shape[2]
    basis = wmat.shape[0]
    hd = width // heads
    rows = slice(s * length, (s + 1) * length)
    brows = slice(s * basis, (s + 1) * basis)
    cols = slice(start, start + n)
    inv_var = 1.0 / variance
    s0, s1, s2 = grows[0], grows[1], grows[2]
    to_centre = s1 * (inv_var / root) * centre * (1.0 - centre)
    wide_slope = 0.02 / (1.0 + jnp.exp(-wide))
    to_wide = (-0.5 * s0 * inv_var + s2 * (0.5 * inv_var * inv_var) / (root * root)) * wide_slope
    head = iota((16, length), 0)
    live = (head >= start // hd) & (head < (start + n) // hd)
    g = jnp.concatenate([jnp.where(live, to_centre, 0.0), jnp.where(live, to_wide, 0.0)], axis=0)
    g_hi, g_lo = split_high_low(g)
    u_hi, u_lo = split_high_low(ublk[s, :, cols])
    dqm = dot_tn(u_hi, g_hi) + dot_tn(u_hi, g_lo) + dot_tn(u_lo, g_hi)
    total = dq_t[...] * (1.0 / math.sqrt(hd)) + dqm
    gqkv[rows, cols] = total.T.astype(BF)
    q = qkv[rows, cols]
    own = (iota((32, n), 0) % 16) == (iota((32, n), 1) + start) // hd
    r = dot_nn(g_hi, q) + dot_nn(g_lo, q)
    r = jnp.where(own, r, 0.0) * (1.0 / math.sqrt(hd))
    r_hi, r_lo = split_high_low(r)
    w = wmat[...][:, 0:32]
    gmem[brows, 0:n] = (dot_nn(w, r_hi) + dot_nn(w, r_lo)).astype(BF)
    mk = mem[brows, cols]
    add = dot_nt(r_hi, mk) + dot_nt(r_lo, mk)
    if msum.shape[0] == 32:
        msum[...] += add
    else:
        some, at = n // hd, start // hd
        msum[...] += jnp.concatenate([add[at:at + some], add[16 + at:16 + at + some]], axis=0)


def backward_input(r, width, hid, gm, gqkv, wqkv, vecs, gin, vsum):
    g = dot_nt(gqkv[r, :], wqkv[...])
    unit, inv = norm_parts(hid.astype(F32))
    gin[...] = (gm + norm_back(g, unit, inv, vecs[0:1, :])).astype(BF)
    vsum[0:1, :] += jnp.sum(g * unit, axis=0, keepdims=True)
    vsum[1:2, :] += jnp.sum(g, axis=0, keepdims=True)


def bias_sums(width, gqkv, out):
    out[0:1, :] = jnp.sum(gqkv[:, 0:width].astype(F32), axis=0, keepdims=True)
    out[1:2, :] = jnp.sum(gqkv[:, 2 * width:3 * width].astype(F32), axis=0, keepdims=True)


def backward_plain_call(heads, hidden, norm_t, coef_t, qkv, mem, gatt, gmid, lse, ublk, proj, wmat, vecs, wqkv):
    seqs, length, width = hidden.shape
    tokens = seqs * length
    brows = coef_t.shape[1]
    basis = brows // seqs
    vm = pl.BlockSpec(memory_space=pltpu.VMEM)

    def kernel(
        hidden, norm_t, coef_t, qkv, mem, gatt, gmid, lse, ublk, proj, wmat, vecs, wqkv,
        gin, dqkv, vsum, msum, gqkv, gmem, head_par, grows, dq_t,
    ):
        vsum[...] = jnp.zeros_like(vsum)
        msum[...] = jnp.zeros_like(msum)
        grows[...] = jnp.zeros_like(grows)
        for s in range(seqs):
            rows_of = basis_rows(proj[s], heads, basis, head_par)

            def pair(p, _):
                backward_heads(s, p, 0, heads, length, basis, width, qkv, mem, gatt, lse, head_par, grows, dq_t, gqkv, gmem)
                return 0

            lax.fori_loop(0, heads // 2, pair, 0)
            backward_finish(s, 0, heads, rows_of, qkv, mem, ublk, grows, dq_t, wmat, gqkv, gmem, msum)
        step = width // 3
        for j in range(9):
            c = slice(j * step, (j + 1) * step)
            y = dot_nn(norm_t[...], gqkv[:, c])
            if j >= 3:
                y = y + dot_nn(coef_t[...], gmem[:, (j - 3) * step:(j - 2) * step])
            dqkv[:, c] = y.astype(BF)

        def last(i, _):
            r = pl.ds(pl.multiple_of(i * 256, 256), 256)
            backward_input(r, width, hidden[r, :], gmid[r, :], gqkv, wqkv, vecs, gin.at[r, :], vsum.at[2:4, :])
            return 0

        lax.fori_loop(0, tokens // 256, last, 0)
        bias_sums(width, gqkv, vsum)

    shapes = (
        jax.ShapeDtypeStruct((tokens, width), BF),
        jax.ShapeDtypeStruct((width, 3 * width), BF),
        jax.ShapeDtypeStruct((8, width), F32),
        jax.ShapeDtypeStruct((32, basis), F32),
    )
    return pl.pallas_call(
        kernel,
        out_shape=shapes,
        in_specs=[vm] * 13,
        out_specs=[vm] * 4,
        scratch_shapes=[
            pltpu.VMEM((tokens, 3 * width), BF),
            pltpu.VMEM((brows, 2 * width), BF),
            pltpu.VMEM((heads, 8, length), F32),
            pltpu.VMEM((3, 16, length), F32),
            pltpu.VMEM((width, length), F32),
        ],
        compiler_params=pltpu.CompilerParams(vmem_limit_bytes=VMEM_BYTES),
        name="backward_plain",
    )(hidden.reshape(tokens, width), norm_t, coef_t, qkv, mem, gatt, gmid, lse, ublk, proj, wmat, vecs, wqkv)


class Reduce:
    SLOTS = 13

    def __init__(self, place, started, name, base, parts, bufs):
        self.p, self.s, self.name, self.base, self.parts = place, started, name, base, parts
        self.g, self.r1, self.r2, self.r3, self.r4, self.f = bufs

    def where(self, part):
        r0, rn, c0, cn = self.parts[part]
        return pl.ds(r0, rn), pl.ds(c0, cn)

    def core(self, *pieces):
        for i, (src, rows) in enumerate(pieces):
            self.s.go((self.name, 1), src, self.r1.at[:, :, :, rows, :], self.base + i, self.p.at(c=1 - self.p.c))

    def core_columns(self, i, src, cols):
        self.s.go((self.name, 1), src, self.r1.at[:, :, :, :, cols], self.base + (0, 1, 12)[i], self.p.at(c=1 - self.p.c))

    def second(self):
        p = self.p
        self.s.arrived((self.name, 1))

        def step(i, _):
            at = (i // 8, (i // 2) % 4, i % 2)
            self.g[at] = self.g[at] + self.r1[at]
            return 0

        lax.fori_loop(0, 16, step, 0)
        for part in (0, 1):
            r, c = self.where(part)
            if part == 0:
                self.s.go((self.name, 2), self.g.at[1 - p.y, :, :, r, c], self.r2[0], self.base + 2, p.at(y=1 - p.y))
            else:
                self.s.go((self.name, 2), self.g.at[:, :, 1 - p.x, r, c], self.r2[1], self.base + 3, p.at(x=1 - p.x))

    def third(self):
        p = self.p
        self.s.arrived((self.name, 2))
        r, c = self.where(0)
        r_b, c_b = self.where(1)

        def step(i, _):
            z, k = i // 2, i % 2
            self.g[p.y, z, k, r, c] = self.g[p.y, z, k, r, c] + self.r2[0][z, k]
            self.g[k, z, p.x, r_b, c_b] = self.g[k, z, p.x, r_b, c_b] + self.r2[1][k, z]
            return 0

        lax.fori_loop(0, 8, step, 0)
        for part in (0, 1):
            self.send_third(part)

    def send_third(self, part):
        p = self.p
        r, c = self.where(part)
        if part == 0:
            self.s.go((self.name, 3), self.g.at[p.y, :, 1 - p.x, r, c], self.r3[0], self.base + 4, p.at(x=1 - p.x))
        else:
            self.s.go((self.name, 3), self.g.at[1 - p.y, :, p.x, r, c], self.r3[1], self.base + 5, p.at(y=1 - p.y))

    def along(self):
        p = self.p
        self.s.arrived((self.name, 3))

        def step(z, _):
            for part in self.parts:
                r, c = self.where(part)
                self.g[p.y, z, p.x, r, c] = self.g[p.y, z, p.x, r, c] + self.r3[part][z]
            return 0

        lax.fori_loop(0, 4, step, 0)
        self.send_along()

    early = None

    def summand(self, z):
        p = self.p
        return self.g.at[p.y, z, p.x] if self.early is None else self.early.at[z // 2, p.y, z % 2, p.x]

    def send_along(self):
        p = self.p
        for s in (1, 2, 3):
            to = p.far_z(s)
            self.s.go((self.name, 4), self.summand(to), self.r4.at[s - 1], self.base + 5 + s, p.at(z=to))

    def last(self, out, segments):
        p = self.p
        self.s.arrived((self.name, 4))
        own = self.summand(p.z)[...].astype(F32)
        self.f[...] = (own + self.r4[0].astype(F32)) + (self.r4[1].astype(F32) + self.r4[2].astype(F32))
        n = self.f.shape[0] // 2
        theirs = pl.ds(pl.multiple_of((1 - p.c) * n, 8), n)
        mine = pl.ds(pl.multiple_of(p.c * n, 8), n)
        for i, (c0, to, cn) in enumerate(segments):
            there = out.at[:, pl.ds(pl.multiple_of(to, 128), cn)]
            self.s.go((self.name, 5), self.f.at[theirs, pl.ds(c0, cn)], there, self.base + 9 + i, p.at(c=1 - p.c))
            there[...] = self.f[mine, c0:c0 + cn]

    def done(self):
        self.s.arrived((self.name, 5))


class Everywhere:
    SLOTS = 8

    def __init__(self, place, started, name, slot, held, got):
        self.p, self.s, self.name, self.slot, self.held, self.got = place, started, name, slot, held, got
        n = held.shape[-1] // 2
        self.half = pl.ds(pl.multiple_of(place.c * n, 128), n)

    def start(self, step):
        p, name, half = self.p, (self.name, step), self.half
        if step == 0:
            self.s.go(name, self.held.at[0], self.got.at[0], self.slot, p.at(c=1 - p.c))
        elif step == 1:
            for d in (1, 2, 3):
                to = p.at(y=(p.y + d // 2) % 2, x=(p.x + d) % 2)
                self.s.go(name, self.held.at[1, :, half], self.got.at[d, :, half], self.slot + d, to)
        elif step == 2:
            for s in (1, 2, 3):
                self.s.go(name, self.held.at[2, :, half], self.got.at[3 + s, :, half], self.slot + 3 + s, p.at(z=p.far_z(s)))
        else:
            ref = self.held.at[3, :, half]
            self.s.go(name, ref, ref, self.slot + 7, p.at(c=1 - p.c))

    def add(self, step):
        self.s.arrived((self.name, step))
        half = self.half
        if step == 0:
            self.held[1] = self.held[0] + self.got[0]
        elif step < 3:
            i = 1 if step == 1 else 4
            self.held[step + 1, :, half] = (self.held[step, :, half] + self.got[i, :, half]) + (
                self.got[i + 1, :, half] + self.got[i + 2, :, half])
        else:
            return self.held[3]
        self.start(step + 1)
        return None


BACK_STEPS = (
    (), (), (), (), (),
    ("xx", "o1"), ("p1",), ("a3", "b3"), ("o2", "q1"),
    ("p2",), ("o3", "q2"), ("p3",),
    ("r1",), ("q3",), ("w0", "k0"), ("r2", "w1", "k1"),
    ("l0",), ("r3", "l1", "w2", "k2"), ("l2", "w3", "k3", "d4", "a4", "b4", "p4", "o4", "q4"), ("l3", "r4"),
)


def backward_kernel(
    heads, devices,
    hidden, norm_h, coef_h, qkv_h, mem_h, gatt_h, gmid, lse, ublk, proj, wmat, vecs, vsum_a, usum, wq_h, p_out, gu_h, gd_h,
    gin, o_qkv, o_out, o_up, o_down, early, late, msum,
    norm_t, coef_t, qkv, mem, gatt, wq,
    gqkv, gmem, head_par, grows, dq_t, away, gm_buf, hid_buf, gin_buf,
    bufs, vsum, k_held, k_got, l_held, l_got, m_held, m_got, early_bufs, send, recv, local, early_send, early_recv,
):
    place = Place()
    p = place
    tokens, width = hidden.shape
    seqs, _, length = proj.shape
    basis = wmat.shape[0]
    ff = o_up.shape[1]
    st = Started(send, recv)
    names = "abdopqr"
    red = {n: Reduce(place, st, n, i * Reduce.SLOTS, parts, bufs[i]) for i, (n, (_, _, parts)) in enumerate(zip(names, reduce_shapes(width, ff, devices)))}
    base = len(names) * Reduce.SLOTS
    sums = {n: Everywhere(place, st, n, base + i * Everywhere.SLOTS, held, got)
            for i, (n, held, got) in enumerate((("k", k_held, k_got), ("w", m_held, m_got), ("l", l_held, l_got)))}
    loads = []
    for i, (src, dst) in enumerate(((qkv_h, qkv), (mem_h, mem), (gatt_h, gatt), (norm_h, norm_t), (coef_h, coef_t), (wq_h, wq))):
        copy = pltpu.make_async_copy(src, dst, local.at[i])
        copy.start()
        loads.append(copy)
    grows[...] = jnp.zeros_like(grows)
    vsum[...] = jnp.zeros_like(vsum)
    k_held[0] = jnp.concatenate([vsum_a[0:4, :], usum[0:4, :], jnp.zeros((8, width), F32)], axis=0)
    half = width // 2

    def side(c):
        return p_out.at[:, :, :, :, pl.ds(pl.multiple_of(c * half, 128), half)]

    er = EarlyReduce(place, early_send, early_recv, *early_bufs[:2], None, None, None, None, None, *early_bufs[2:])
    red["a"].g, red["b"].g, red["d"].early = er.g_u.at[0], er.g_u.at[1], er.g_d
    own = [pltpu.make_async_copy(src, dst, local.at[6 + i])
           for i, (src, dst) in enumerate(((gu_h, er.g_u), (gd_h, er.g_d), (side(p.c), red["o"].g)))]
    for copy in own:
        copy.start()
    place.hello(place.layer())

    def begin():
        place.wait_hello(place.layer())
        red["o"].core((side(1 - p.c), slice(None)))
        for copy in own:
            copy.wait()
        er.resume()
    pieces = 128
    outs = {
        "a": (o_up, lambda: [(k * half, k * width + p.c * half, half) for k in (0, 1)]),
        "b": (o_up, lambda: [(k * half, (2 + k) * width + p.c * half, half) for k in (0, 1)]),
        "d": (o_down, lambda: [(0, p.c * half, half)]),
        "o": (o_out, lambda: [(0, p.c * half, half)]),
    }
    for i, n in enumerate("pqr"):
        outs[n] = (o_qkv, lambda i=i: [(j * pieces, j * width + i * 2 * pieces + p.c * pieces, pieces) for j in range(3)])

    def perform(word):
        if word[0] == "x":
            er.up_add_second(2)
            er.up_add_second(3)
            red["a"].send_third(0)
            red["b"].send_third(1)
            er.down_add_third(0)
            er.down_add_third(1)
            red["d"].send_along()
        elif word[0] in sums:
            total, step = sums[word[0]], int(word[1])
            value = total.add(step)
            if step == 3:
                if word[0] == "w":
                    msum[...] = value
                elif word[0] == "l":
                    late[0:2, :] = value
                else:
                    early[...] = value[0:8]
                    late[2:4, :] = value[8:10]
        else:
            r, step = red[word[0]], word[1]
            if step == "1":
                r.second()
            elif step == "2":
                r.third()
            elif step == "3":
                r.along()
            else:
                out, segments = outs[word[0]]
                r.last(out, segments())

    steps = iter(BACK_STEPS)

    def advance():
        for word in next(steps, ()):
            perform(word)

    for copy in loads[:3]:
        copy.wait()
    chunk = 2 * pieces
    m_held[...] = jnp.zeros_like(m_held)
    rows_of = [basis_rows(proj[s], heads, basis, head_par.at[s]) for s in range(seqs)]
    for i in range(3):
        for s in range(seqs):
            for k in range(2):
                def one(j, _):
                    backward_heads(s, j, 2 * i, heads, length, basis, width, qkv, mem, gatt, lse, head_par.at[s], grows, dq_t, gqkv, gmem)
                    return 0

                lax.fori_loop(2 * i + k, 2 * i + k + 1, one, 0)
                if i + s + k == 0:
                    begin()
                if k == 0:
                    advance()
            backward_finish(s, i * chunk, heads, rows_of[s], qkv, mem, ublk, grows, dq_t, wmat, gqkv, gmem, m_held.at[0, 8 * i:8 * i + 8, :])
            if s < seqs - 1:
                advance()
        if i == 0:
            loads[3].wait()
            loads[4].wait()
        r = red["pqr"[i]]
        for j in range(3):
            c = j * width + i * chunk
            y = dot_nn(norm_t[...], gqkv[:, c:c + chunk])
            if j > 0:
                y = y + dot_nn(coef_t[...], gmem[:, (j - 1) * chunk:j * chunk])
            y = y.astype(BF).reshape(2, 4, 2, r.g.shape[3], chunk)
            low, high = y[..., :pieces], y[..., pieces:]
            keep, give = jnp.where(p.c == 0, low, high), jnp.where(p.c == 0, high, low)
            r.g[:, :, :, :, j * pieces:(j + 1) * pieces] = keep
            part = slice(j * pieces, (j + 1) * pieces)
            away[i, :, :, :, :, part] = give
            r.core_columns(j, away.at[i, :, :, :, :, part], part)
        if i == 2:
            sums["w"].start(0)
            bias_sums(width, gqkv, k_held.at[0, 8:10, :])
            sums["k"].start(0)
        advance()
    wflat = wq.reshape(width, 3 * width)
    loads[5].wait()
    blocks = tokens // 256

    def fetch(i):
        r = slice(i * 256, (i + 1) * 256)
        return (pltpu.make_async_copy(gmid.at[r, :], gm_buf.at[i % 2], local.at[16 + i % 2]),
                pltpu.make_async_copy(hidden.at[r, :], hid_buf.at[i % 2], local.at[18 + i % 2]))

    def emit(i):
        return pltpu.make_async_copy(gin_buf.at[i % 2], gin.at[i * 256:(i + 1) * 256, :], local.at[20 + i % 2])

    for i in (0, 1):
        for copy in fetch(i):
            copy.start()
    for i in range(blocks):
        for copy in fetch(i):
            copy.wait()
        if i >= 2:
            emit(i - 2).wait()
        backward_input(slice(i * 256, (i + 1) * 256), width, hid_buf[i % 2], gm_buf[i % 2], gqkv, wflat, vecs, gin_buf.at[i % 2], vsum)
        emit(i).start()
        if i + 2 < blocks:
            for copy in fetch(i + 2):
                copy.start()
        if i == blocks - 1:
            l_held[0] = vsum[...]
            sums["l"].start(0)
        advance()
    for _ in range(99):
        advance()
    for n in names:
        red[n].done()
    for i in (blocks - 2, blocks - 1):
        emit(i).wait()
    for copy in er.resumed():
        copy.wait_send()
    st.left()


def reduce_shapes(width, ff, devices):
    chip, chip_ff = 2 * width // devices, 2 * ff // devices
    h = width // 2
    more = (chip, h, {0: (0, chip, 0, 256), 1: (0, chip, 256, 128)})
    less = (chip, h, {0: (0, chip, 0, 128), 1: (0, chip, 128, 256)})
    return [(chip, width, {0: (0, chip, 0, width)}), (chip, width, {1: (0, chip, 0, width)}), (chip_ff, h, {}), more, less, more, less]


def backward_call(
    heads, devices, hidden, norm_t, coef_t, qkv, mem, gatt, gmid, lse, ublk, proj, wmat, vecs, vsum_a, usum, wq, p_out, g_up, g_down, ff,
):
    seqs, length, width = hidden.shape
    tokens = seqs * length
    brows = coef_t.shape[1]
    basis = brows // seqs
    vm = pl.BlockSpec(memory_space=pltpu.VMEM)
    anyw = pl.BlockSpec(memory_space=pl.ANY)
    shapes = (
        jax.ShapeDtypeStruct((tokens, width), BF),
        jax.ShapeDtypeStruct((width // devices, 3 * width), F32),
        jax.ShapeDtypeStruct((width // devices, width), F32),
        jax.ShapeDtypeStruct((width // devices, ff), F32),
        jax.ShapeDtypeStruct((ff // devices, width), F32),
        jax.ShapeDtypeStruct((8, width), F32),
        jax.ShapeDtypeStruct((4, width), F32),
        jax.ShapeDtypeStruct((24, basis), F32),
    )

    def buffers(i, shape):
        rows, cols, parts = shape
        none = pltpu.VMEM((8, 128), F32)
        whole = i > 2
        sizes = [parts.get(k, (0, 16, 0, 128)) for k in (0, 1)]
        (_, ra, _, ca), (_, rb, _, cb) = sizes
        return (
            none if i < 3 else pltpu.VMEM((2, 4, 2, rows, cols), BF),
            pltpu.VMEM((2, 4, 2, rows, cols), BF) if whole else none,
            (pltpu.VMEM((4, 2, ra, ca), BF), pltpu.VMEM((2, 4, rb, cb), BF)) if whole else (none, none),
            (pltpu.VMEM((4, ra, ca), BF), pltpu.VMEM((4, rb, cb), BF)),
            pltpu.VMEM((3, rows, cols), BF),
            pltpu.VMEM((rows, cols), F32),
        )

    chip, chip_ff = 2 * width // devices, 2 * ff // devices
    table = reduce_shapes(width, ff, devices)
    slots = len(table) * Reduce.SLOTS + 3 * Everywhere.SLOTS
    return pl.pallas_call(
        lambda *refs: backward_kernel(heads, devices, *refs),
        out_shape=shapes,
        in_specs=[anyw] * 7 + [vm] * 7 + [anyw] * 4,
        out_specs=[anyw] + [vm] * 7,
        scratch_shapes=[pltpu.VMEM(a.shape, a.dtype) for a in (norm_t, coef_t, qkv, mem, gatt, wq)] + [
            pltpu.VMEM((tokens, 3 * width), BF),
            pltpu.VMEM((brows, 512), BF),
            pltpu.VMEM((seqs, heads, 8, length), F32),
            pltpu.VMEM((3, 16, length), F32),
            pltpu.VMEM((256, length), F32),
            pltpu.VMEM((3, 2, 4, 2, 2 * width // devices, 384), BF),
            pltpu.VMEM((2, 256, width), F32),
            pltpu.VMEM((2, 256, width), BF),
            pltpu.VMEM((2, 256, width), BF),
            [buffers(i, shape) for i, shape in enumerate(table)],
            pltpu.VMEM((2, width), F32),
            pltpu.VMEM((4, 16, width), F32),
            pltpu.VMEM((7, 16, width), F32),
            pltpu.VMEM((4, 2, width), F32),
            pltpu.VMEM((7, 2, width), F32),
            pltpu.VMEM((4, 24, basis), F32),
            pltpu.VMEM((7, 24, basis), F32),
            [pltpu.VMEM(shape, BF) for shape in (
                g_down.shape, g_up.shape, (2, 4, 2, chip, width // 2), (2, 2, 4, chip, width // 2), (2, 2, 2, chip_ff // 2, width // 2))],
            pltpu.SemaphoreType.DMA((slots,)),
            pltpu.SemaphoreType.DMA((slots,)),
            pltpu.SemaphoreType.DMA((22,)),
            pltpu.SemaphoreType.DMA((EarlyReduce.SLOTS,)),
            pltpu.SemaphoreType.DMA((EarlyReduce.SLOTS,)),
        ],
        compiler_params=pltpu.CompilerParams(vmem_limit_bytes=56 * 1024 * 1024, collective_id=1, has_side_effects=True),
        name="backward",
    )(hidden.reshape(tokens, width), norm_t, coef_t, qkv, mem, gatt, gmid, lse, ublk, proj, wmat, vecs, vsum_a, usum, wq, p_out, g_up, g_down)


def finish_call(heads, devices, ff, early, late, msum, whole):
    width = early.shape[1]
    basis = msum.shape[1]
    e, rows = width // devices, basis // devices
    group = 4
    vm = pl.BlockSpec(memory_space=pltpu.VMEM)
    anyw = pl.BlockSpec(memory_space=pl.ANY)
    n = len(whole)

    def kernel(*refs):
        early, late, msum = refs[:3]
        sources, results = refs[3:3 + n], refs[3 + n:3 + 2 * n]
        gain_a, shift_a, qv, out_b, gain_m, shift_m, up_b, down_b, mean, wide = refs[3 + 2 * n:-1 - n]
        held, sem = refs[-1 - n:-1], refs[-1]
        taken = [pltpu.make_async_copy(a, b, sem.at[i]) for i, (a, b) in enumerate(zip(sources, held))]
        copies = [pltpu.make_async_copy(a, b, sem.at[n + i]) for i, (a, b) in enumerate(zip(held, results))]
        for copy in taken:
            copy.start()
        me = lax.axis_index("dp") * lax.axis_size("fsdp") + lax.axis_index("fsdp")

        def thirds(x):
            high = x.astype(BF)
            rest = x - high.astype(F32)
            middle = rest.astype(BF)
            return high, middle, (rest - middle.astype(F32)).astype(BF)

        def pick(x, start, size):
            at = (iota((x.shape[1], size), 0) == iota((x.shape[1], size), 1) + start).astype(F32).astype(BF)
            return sum(dot_nn(part, at) for part in thirds(x))

        def row_of(x, i):
            return jnp.sum(jnp.where(iota(x.shape, 0) == i, x, 0.0), axis=0, keepdims=True)

        for take, copy in zip(taken, copies):
            take.wait()
            copy.start()
        some = pick(early[...], me * e, e)
        down_b[...], gain_m[...], shift_m[...], out_b[...] = (some[i:i + 1] for i in range(4))
        some = pick(late[...], me * e, e)
        gain_a[...], shift_a[...] = some[0:1], some[1:2]
        k = devices // 2
        qv[...] = pick(row_of(late[2:4, :], me // k), me % k * 2 * e, 2 * e)
        k = devices * width // ff
        up_b[...] = pick(row_of(early[4:8, :], me // k), me % k * (ff // devices), ff // devices)
        at = (iota((rows, basis), 1) == iota((rows, basis), 0) + me * rows).astype(F32).astype(BF)
        for out, first in ((mean, 0), (wide, group)):
            x = jnp.concatenate([msum[i + first:i + first + group, :] for i in range(0, 2 * heads, 2 * group)], axis=0)
            out[...] = sum(dot_nt(at, part) for part in thirds(x))
        for copy in copies:
            copy.wait()

    small = [(1, e), (1, e), (1, 2 * e), (1, e), (1, e), (1, e), (1, ff // devices), (1, e), (rows, heads), (rows, heads)]
    return pl.pallas_call(
        kernel,
        out_shape=[jax.ShapeDtypeStruct(a.shape, a.dtype) for a in whole] + [jax.ShapeDtypeStruct(s, F32) for s in small],
        in_specs=[vm] * 3 + [anyw] * n,
        out_specs=[anyw] * n + [vm] * len(small),
        scratch_shapes=[pltpu.VMEM(a.shape, a.dtype) for a in whole] + [pltpu.SemaphoreType.DMA((2 * n,))],
        name="finish",
    )(early, late, msum, *whole)


def gather(x):
    return lax.all_gather(x, AXES, axis=0, tiled=True)


def scatter(x):
    return lax.psum_scatter(x, AXES, scatter_dimension=0, tiled=True)


def shards_plain(
    hidden, grad_out, past_states, old_coeffs, fresh_flags, ridge_map,
    gain_attn, shift_attn, qkv_weight, qv_bias, out_weight, out_bias,
    gain_mlp, shift_mlp, up_weight, up_bias, down_weight, down_bias,
    mean_weight, width_weight,
):
    seqs, length, width = hidden.shape
    heads = mean_weight.shape[1]
    devices = lax.axis_size("dp") * lax.axis_size("fsdp")
    full_qkv, full_out, full_up, full_down = (gather(w) for w in (qkv_weight, out_weight, up_weight, down_weight))
    rows = jnp.zeros((mean_weight.shape[0], 128), BF)
    rows = rows.at[:, 0:heads].set(mean_weight).at[:, 16:16 + heads].set(width_weight)
    wmat = gather(rows)
    full_qv = gather(qv_bias)
    vecs = jnp.stack(
        [gather(gain_attn), gather(shift_attn), full_qv[:width], full_qv[width:],
         gather(out_bias), gather(gain_mlp), gather(shift_mlp), gather(down_bias)]).astype(F32)
    ubias = gather(up_bias).astype(F32).reshape(-1, width)
    ubias = jnp.concatenate([ubias, jnp.zeros((8 - ubias.shape[0], width), F32)], axis=0)

    norm_t, coef_t, qkv, mem, att, lse, ublk, proj = forward_plain_call(
        heads, fresh_flags, hidden, past_states, old_coeffs, ridge_map, wmat, vecs, full_qkv)
    output, gmid, gatt, dout, dup, ddown, vsum_a, usum = middle_call(
        att, hidden, grad_out, full_out, full_up, full_down, vecs, ubias)
    gin, dqkv, vsum_b, msum = backward_plain_call(
        heads, hidden, norm_t, coef_t, qkv, mem, gatt, gmid, lse, ublk, proj, wmat, vecs, full_qkv)

    up_sum = usum.reshape(-1)[:up_bias.shape[0] * devices]
    big = [scatter(a.astype(F32)) for a in (dqkv, dout, dup, ddown)]
    small = [
        scatter(a) for a in (
            vsum_b[2], vsum_b[3], jnp.concatenate([vsum_b[0], vsum_b[1]]), vsum_a[3], vsum_a[1], vsum_a[2],
            up_sum, vsum_a[0], msum[0:heads].T, msum[16:16 + heads].T)
    ]
    return (
        output.reshape(seqs, length, width), gin.reshape(seqs, length, width),
        small[0], small[1], big[0], small[2], big[1], small[3], small[4], small[5],
        big[2], small[6], big[3], small[7], small[8], small[9],
    )


def shards_block(
    hidden, grad_out, past_states, old_coeffs, fresh_flags, ridge_map,
    gain_attn, shift_attn, qkv_weight, qv_bias, out_weight, out_bias,
    gain_mlp, shift_mlp, up_weight, up_bias, down_weight, down_bias,
    mean_weight, width_weight,
):
    seqs, length, width = hidden.shape
    heads = mean_weight.shape[1]
    devices = 32
    ff = up_weight.shape[1]
    e = width // devices
    def put(v, row, col):
        v = v.reshape((1, -1)) if v.ndim == 1 else v
        return jnp.pad(v, ((row, 32 - row - v.shape[0]), (col, 128 - col - v.shape[1])))

    small = (
        put(mean_weight, 0, 0) + put(width_weight, 0, 16)
        + put(gain_attn, 16, 0) + put(shift_attn, 16, e) + put(out_bias, 16, 2 * e) + put(gain_mlp, 16, 3 * e)
        + put(shift_mlp, 17, 0) + put(down_bias, 17, e) + put(qv_bias, 17, 2 * e) + put(up_bias, 18, 0))

    norm_t, coef_t, qkv, mem, output, gmid, gatt, dout, g_up, g_down, wq, lse, ublk, proj, wmat, vecs, vsum_a, usum = forward_call(
        heads, devices, fresh_flags, hidden, past_states, old_coeffs, ridge_map, grad_out, small, qkv_weight, out_weight, up_weight, down_weight)
    gin, d_qkv, d_out, d_up, d_down, early, late, msum = backward_call(
        heads, devices, hidden, norm_t, coef_t, qkv, mem, gatt, gmid, lse, ublk, proj, wmat, vecs, vsum_a, usum, wq,
        dout.reshape(2, 4, 2, width // 16, width), g_up, g_down, ff)

    (output, gin, d_qkv, d_out, d_up, d_down, gain_a, shift_a, qv, out_b, gain_m, shift_m, up_b, down_b, mean, wide) = finish_call(
        heads, devices, ff, early, late, msum, (output, gin, d_qkv, d_out, d_up, d_down))
    flat = lambda v: v.reshape(v.shape[1])
    return (
        output.reshape(seqs, length, width), gin.reshape(seqs, length, width),
        flat(gain_a), flat(shift_a), d_qkv, flat(qv), d_out, flat(out_b), flat(gain_m), flat(shift_m),
        d_up, flat(up_b), d_down, flat(down_b), mean, wide,
    )


def solution(mesh):
    rows = P(AXES, None)
    cube = P(AXES, None, None)
    one = P(AXES)
    in_specs = (cube, cube, cube, cube, one, P(), one, one, rows, one, rows, one, one, one, rows, one, rows, one, rows, rows)
    out_specs = (cube, cube, one, one, rows, one, rows, one, one, one, rows, one, rows, one, rows, rows)
    body = shards_block if mesh.shape["dp"] == 2 and mesh.shape["fsdp"] == 16 else shards_plain
    return jax.shard_map(body, mesh=mesh, in_specs=in_specs, out_specs=out_specs, check_vma=False)
```
